32 devices in a mesh: dp: 2 (over x), expert: 16 (over z, y, core).
Axes of the slice: x: 2, y: 2, z: 4, core: 2. Of those that a mesh axis runs over, the one named last changes fastest.
Arguments:
- tokens: bfloat16 [2, 32, 64, 2048], P(None, ('dp', 'expert')), may hold values from -6 to 6
- cotangent: bfloat16 [2, 32, 64, 2048], P(None, ('dp', 'expert')), may hold values from -6 to 6
- routes: int32 [2, 32, 64, 6], P(None, ('dp', 'expert')), may hold values from 0 to 15, all different within a row; in each aligned block of 64 rows (0 to 63, 64 to 127, ..., all dimensions but the last counted through in order) at most 32 rows name the same one
- segments: int32 [2, 32, 64], P(None, ('dp', 'expert')), may hold values from 0 to 2, never falling along the last dimension, each value on 1 to 32 neighbouring positions
- attn_gain: bfloat16 [2048], P(('dp', 'expert')), may hold values from 0.5 to 1.5
- q_weight: bfloat16 [2048, 3072], P(('dp', 'expert')), may hold values from -0.125 to 0.125
- kv_down: bfloat16 [2048, 576], P(('dp', 'expert')), may hold values from -0.125 to 0.125
- kv_gain: bfloat16 [512], P(('dp', 'expert')), may hold values from 0.5 to 1.5
- kv_up: bfloat16 [512, 4096], P(('dp', 'expert')), may hold values from -0.25 to 0.25
- out_weight: bfloat16 [2048, 2048], P(('dp', 'expert')), may hold values from -0.5 to 0.5
- ffn_gain: bfloat16 [2048], P(('dp', 'expert')), may hold values from 0.5 to 1.5
- router: bfloat16 [2048, 16], P(('dp', 'expert')), may hold values from -0.0625 to 0.0625
- shared_gate: bfloat16 [2048, 2816], P(('dp', 'expert')), may hold values from -0.125 to 0.125
- shared_up: bfloat16 [2048, 2816], P(('dp', 'expert')), may hold values from -0.125 to 0.125
- shared_down: bfloat16 [2816, 2048], P(('dp', 'expert')), may hold values from -0.15625 to 0.15625
- expert_gate: bfloat16 [16, 2048, 1408], P('expert', 'dp'), may hold values from -0.125 to 0.125
- expert_up: bfloat16 [16, 2048, 1408], P('expert', 'dp'), may hold values from -0.125 to 0.125
- expert_down: bfloat16 [16, 1408, 2048], P('expert', None, 'dp'), may hold values from -0.625 to 0.625
Outputs:
- out: bfloat16 [2, 32, 64, 2048], P(None, ('dp', 'expert'))
- tokens_grad: bfloat16 [2, 32, 64, 2048], P(None, ('dp', 'expert'))
- attn_gain_grad: float32 [2048], P(('dp', 'expert'))
- q_weight_grad: float32 [2048, 3072], P(('dp', 'expert'))
- kv_down_grad: float32 [2048, 576], P(('dp', 'expert'))
- kv_gain_grad: float32 [512], P(('dp', 'expert'))
- kv_up_grad: float32 [512, 4096], P(('dp', 'expert'))
- out_weight_grad: float32 [2048, 2048], P(('dp', 'expert'))
- ffn_gain_grad: float32 [2048], P(('dp', 'expert'))
- router_grad: float32 [2048, 16], P(('dp', 'expert'))
- shared_gate_grad: float32 [2048, 2816], P(('dp', 'expert'))
- shared_up_grad: float32 [2048, 2816], P(('dp', 'expert'))
- shared_down_grad: float32 [2816, 2048], P(('dp', 'expert'))
- expert_gate_grad: float32 [16, 2048, 1408], P('expert', 'dp')
- expert_up_grad: float32 [16, 2048, 1408], P('expert', 'dp')
- expert_down_grad: float32 [16, 1408, 2048], P('expert', None, 'dp')
The draws below stay inside these ranges and needn't reach their ends.
Inputs may be any that keep to these rules, and one draw needn't show every extreme that they name: A token's 6 routes are different experts. Within one sequence of one micro-batch no expert is named by more than 32 positions, a bound that some block reaches. `segments`: segment numbers never fall along a sequence.
All inputs are finite; a program needn't handle non-finite values.
Results may differ from the reference program's by a relative error of at most 0.019.
Values may be sent and summed in bfloat16 or wider, within the bound.
A program may use at most 384 MiB of HBM per device.

```python
import math
from functools import partial
import jax
import jax.numpy as jnp
import numpy as np
from jax import lax

D = 2048
HEADS = 16
NOPE = 128
ROPE = 64
VDIM = 128
RANK = 512
EFF = 1408
TOP = 6
SEQ = 64
MICRO = 2
SFF = 2816
EXPERTS = 16
SEQS = 32
CAP = 32


def block_levels(key, dims, pieces, low, largest):
    gain = 1.0
    for dim, shards_of in pieces:
        heights = jax.random.uniform(jax.random.fold_in(jax.random.fold_in(key, 6), dim), (shards_of,), jnp.float32, low / len(pieces), largest / len(pieces))
        gain = gain * jnp.repeat(jnp.exp(heights), dims[dim] // shards_of).reshape((-1,) + (1,) * (len(dims) - 1 - dim))
    return gain


def length_profile(count, total, bound, lean):
    loads = [(1 << 20) // math.isqrt(standing ** lean) + 1 for standing in range(2, count + 1)]
    rest, holding = total - bound - (count - 1), [1] * (count - 1)
    while rest > 0:
        movable = [i for i in range(count - 1) if holding[i] < bound]
        whole, remaining = sum([loads[i] for i in movable]), rest
        for i in movable:
            addition = min(bound - holding[i], max(1, remaining * loads[i] // whole), rest)
            holding[i] = holding[i] + addition
            rest = rest - addition
    return np.array([bound] + holding)


def uneven_parts(key, count, total, limit, skew):
    if count == 2:
        one = jax.random.randint(key, (), max(1, total - limit), min(limit, total - 1) + 1)
        return jnp.stack([one, total - one])
    sizes = jnp.asarray(length_profile(count, total, limit, skew), jnp.int32)
    twos = (count - 1) // 2
    donor, taker = sizes[1:1 + 2 * twos:2], sizes[2:2 + 2 * twos:2]
    room = jnp.minimum(donor - 1, limit - taker)
    passed = jax.random.randint(jax.random.fold_in(key, 1), (twos,), 0, 1 << 20) % (room + 1)
    sizes = sizes.at[1:1 + 2 * twos:2].set(donor - passed).at[2:2 + 2 * twos:2].set(taker + passed)
    return sizes[jax.random.permutation(jax.random.fold_in(key, 2), count)]


def assign_block(own_key, own, number, rows, count, top, most, lean):
    sequence = jax.random.permutation(own_key, count)
    heavy_load, usual = load_shares(count, rows * top, most, lean, True), load_shares(count, rows * top, most, lean, False)
    places = jnp.arange(count)

    def named(tallies, turn):
        used = int((tallies > 0).sum())
        fixed = max(1, used // 4)
        moved = fixed + (places - fixed + turn * (used - fixed)) % max(1, count - fixed)
        return jnp.zeros((count,), jnp.int32).at[sequence[jnp.where(places < fixed, places, moved)]].set(jnp.asarray(tallies, jnp.int32))

    tallies = jnp.where(number % 4 == 0, named(heavy_load, number // 4), named(usual, number - number // 4 - 1))
    mixed = jax.random.permutation(jax.random.fold_in(own, 3), count)
    source_of, receiver = mixed[0:count // 2 * 2:2], mixed[1:count // 2 * 2:2]
    margin = jnp.minimum(tallies[source_of] - 1, most - tallies[receiver]) // 2
    margin = jnp.where((source_of == sequence[0]) | (receiver == sequence[0]) | (tallies[receiver] == 0), 0, jnp.maximum(margin, 0))
    moved = jax.random.randint(jax.random.fold_in(own, 4), (count // 2,), 0, 1 << 20) % (margin + 1)
    tallies = tallies.at[source_of].add(-moved).at[receiver].add(moved)
    members = jnp.searchsorted(jnp.cumsum(tallies), jnp.arange(rows * top), side="right").astype(jnp.int32)
    listing = members.reshape(top, rows).T
    listing = listing[jax.random.permutation(jax.random.fold_in(own, 1), rows)]
    turn = jax.random.randint(jax.random.fold_in(own, 2), (rows, 1), 0, top)
    return jnp.take_along_axis(listing, (jnp.arange(top)[None, :] + turn) % top, axis=1)


def load_shares(amount, total, bound, lean, full):
    portions = [(1 << 20) // math.isqrt(rank ** lean) + 1 for rank in range(1, amount + 1)]
    largest = bound if full else min(bound, max(-(-total // amount), total * portions[0] // sum(portions)))
    least = 1 if total - largest >= amount - 1 else 0
    counts, spare = [largest] + [least] * (amount - 1), total - largest - least * (amount - 1)
    while spare > 0:
        movable = [i for i in range(1, amount) if counts[i] < largest] or [i for i in range(1, amount) if counts[i] < bound]
        whole, left = sum([portions[i] for i in movable]), spare
        for i in movable:
            more = min(bound - counts[i], max(1, left * portions[i] // whole), spare)
            counts[i] = counts[i] + more
            spare = spare - more
    return np.array(counts)


def gaussian(key, extent, deviation, reach, cuts=(), kind=jnp.bfloat16):
    array = jax.random.normal(key, extent, jnp.float32) * deviation
    if len(cuts) > 0:
        array = block_levels(key, extent, cuts, -0.22, 0.18) * array
    return jnp.clip(array, min=-reach, max=reach).astype(kind)


def setup_inputs(seed: int = 0) -> dict:
    keys = jax.random.split(jax.random.key(seed), 19)
    tokens = gaussian(keys[0], (MICRO, SEQS, SEQ, D), 1.0, 6.0, ((1, 32),))
    cotangent = gaussian(keys[1], (MICRO, SEQS, SEQ, D), 1.0, 6.0, ((1, 32),))
    routes_keys = jax.random.split(jax.random.fold_in(keys[2], 1), MICRO * SEQS * SEQ // SEQ)
    routes_turns = jax.random.permutation(jax.random.fold_in(keys[2], 3), MICRO * SEQS * SEQ // SEQ)
    routes = jax.vmap(lambda own, number: assign_block(jax.random.fold_in(keys[2], 2), own, number, SEQ, EXPERTS, TOP, CAP, 1))(routes_keys, routes_turns).reshape((MICRO, SEQS, SEQ, TOP))
    segments = jax.vmap(lambda own: jnp.searchsorted(jnp.cumsum(uneven_parts(own, 3, SEQ, SEQ // 2, 1)), jnp.arange(SEQ), side="right"))(jax.random.split(keys[3], MICRO * SEQS)).reshape((MICRO, SEQS, SEQ)).astype(jnp.int32)
    attn_gain = jnp.clip(1.0 + 0.1 * jax.random.normal(keys[4], (D,), jnp.float32), 0.5, 1.5).astype(jnp.bfloat16)
    q_weight = gaussian(keys[5], (D, HEADS * (NOPE + ROPE)), D ** -0.5, 0.125, ((0, 32),))
    kv_down = gaussian(keys[6], (D, RANK + ROPE), D ** -0.5, 0.125, ((0, 32),))
    kv_gain = jnp.clip(1.0 + 0.1 * jax.random.normal(keys[7], (RANK,), jnp.float32), 0.5, 1.5).astype(jnp.bfloat16)
    kv_up = gaussian(keys[8], (RANK, HEADS * (NOPE + VDIM)), RANK ** -0.5, 0.25, ((0, 32),))
    out_weight = gaussian(keys[9], (HEADS * VDIM, D), (HEADS * VDIM // 16) ** -0.5, 0.5, ((0, 32),))
    ffn_gain = jnp.clip(1.0 + 0.1 * jax.random.normal(keys[10], (D,), jnp.float32), 0.5, 1.5).astype(jnp.bfloat16)
    router = gaussian(keys[11], (D, EXPERTS), (4 * D) ** -0.5, 0.0625, ((0, 32),))
    shared_gate = gaussian(keys[12], (D, SFF), D ** -0.5, 0.125, ((0, 32),))
    shared_up = gaussian(keys[13], (D, SFF), D ** -0.5, 0.125, ((0, 32),))
    shared_down = gaussian(keys[14], (SFF, D), (SFF // 2) ** -0.5, 0.15625, ((0, 32),))
    expert_gate = gaussian(keys[15], (EXPERTS, D, EFF), D ** -0.5, 0.125, ((0, 16), (1, 2)))
    expert_up = gaussian(keys[16], (EXPERTS, D, EFF), D ** -0.5, 0.125, ((0, 16), (1, 2)))
    expert_down = gaussian(keys[17], (EXPERTS, EFF, D), (EFF // 16) ** -0.5, 0.625, ((0, 16), (2, 2)))
    return dict(tokens=tokens, cotangent=cotangent, routes=routes, segments=segments, attn_gain=attn_gain, q_weight=q_weight, kv_down=kv_down, kv_gain=kv_gain, kv_up=kv_up, out_weight=out_weight, ffn_gain=ffn_gain, router=router, shared_gate=shared_gate, shared_up=shared_up, shared_down=shared_down, expert_gate=expert_gate, expert_up=expert_up, expert_down=expert_down)


@jax.custom_vjp
def low(v):
    return lax.optimization_barrier(v.astype(jnp.bfloat16)).astype(jnp.float32)

@jax.custom_vjp
def low_back(v):
    return v

def low_keep(v):
    return (low(v), None)

def low_pass(kept, grad):
    return (grad,)

def back_keep(v):
    return (v, None)

def back_low(kept, grad):
    return (low(grad),)
low.defvjp(low_keep, low_pass)
low_back.defvjp(back_keep, back_low)
EPSILON = 1e-06
ROPE_BASE = 10000.0
MASKED = -1e+30
HIGHEST = lax.Precision.HIGHEST

def normalize(values, gain_row):
    return values * lax.rsqrt(lax.optimization_barrier(jnp.mean(values * values, -1, keepdims=True)) + EPSILON) * gain_row

def rope_tables(length, width):
    half_width = width // 2
    frequency = ROPE_BASE ** (-2.0 * jnp.arange(half_width, dtype=jnp.float32) / width)
    angles = jnp.arange(length, dtype=jnp.float32)[:, None] * frequency[None, :]
    return (jnp.cos(angles), jnp.sin(angles))

def rotate(values, cosine, sine_table):
    half_width = values.shape[-1] // 2
    front_half = values[..., :half_width]
    back_half = values[..., half_width:]
    return jnp.concatenate([front_half * cosine - back_half * sine_table, back_half * cosine + front_half * sine_table], -1)

def assign_slots(route_rows, expert_count):
    route_flat = route_rows.reshape(-1).astype(jnp.int32)
    one_hot = (route_flat[:, None] == jnp.arange(expert_count, dtype=jnp.int32)[None, :]).astype(jnp.int32)
    before = jnp.cumsum(one_hot, 0) - one_hot
    return (route_flat, lax.optimization_barrier(jnp.sum(before * one_hot, 1)).astype(jnp.int32))

def forward(tokens_part, weights, routes_part, segments_part):
    attn_gain, q_weight, kv_down, kv_gain, kv_up, out_weight, ffn_gain, router, shared_gate, shared_up, shared_down, expert_gate, expert_up, expert_down = weights
    expert_count = router.shape[1]
    batch_size = tokens_part.shape[0]
    cosine, sine_table = rope_tables(SEQ, ROPE)
    normed = low(normalize(tokens_part, attn_gain))
    q_raw = low_back(jnp.einsum('bsd,de->bse', normed, q_weight, precision=HIGHEST)).reshape(batch_size, SEQ, HEADS, NOPE + ROPE)
    queries = low(jnp.concatenate([q_raw[..., :NOPE], rotate(q_raw[..., NOPE:], cosine[:, None, :], sine_table[:, None, :])], -1))
    kv_raw = low_back(jnp.einsum('bsd,de->bse', normed, kv_down, precision=HIGHEST))
    latent = low(normalize(kv_raw[..., :RANK], kv_gain))
    key_rope = rotate(kv_raw[..., RANK:], cosine, sine_table)
    kv_full = low_back(jnp.einsum('bsr,re->bse', latent, kv_up, precision=HIGHEST)).reshape(batch_size, SEQ, HEADS, NOPE + VDIM)
    key_rows = low(jnp.concatenate([kv_full[..., :NOPE], jnp.broadcast_to(key_rope[:, :, None, :], (batch_size, SEQ, HEADS, ROPE))], -1))
    value_rows = low(kv_full[..., NOPE:])
    places = jnp.arange(SEQ, dtype=jnp.int32)
    allowed = (places[:, None] >= places[None, :])[None] & (segments_part[:, :, None] == segments_part[:, None, :])
    scores = low_back(jnp.einsum('bqhe,bkhe->bhqk', queries, key_rows, precision=HIGHEST) * (NOPE + ROPE) ** (-0.5))
    scores = jnp.where(allowed[:, None], scores, MASKED)
    exponent = jnp.exp(scores - lax.optimization_barrier(jnp.max(scores, -1, keepdims=True)))
    probability = low(exponent / lax.optimization_barrier(jnp.sum(exponent, -1, keepdims=True)))
    attended = low(low_back(jnp.einsum('bhqk,bkhe->bqhe', probability, value_rows, precision=HIGHEST))).reshape(batch_size, SEQ, HEADS * VDIM)
    mixed_out = low_back(jnp.einsum('bse,ed->bsd', attended, out_weight, precision=HIGHEST))
    residual = tokens_part + mixed_out
    hidden = low(normalize(residual, ffn_gain))
    logits = low_back(jnp.einsum('bsd,de->bse', hidden, router, precision=HIGHEST))
    gate_share = jax.nn.softmax(jnp.take_along_axis(logits, routes_part, axis=-1), -1)
    gate_pre = low_back(jnp.einsum('bsd,df->bsf', hidden, shared_gate, precision=HIGHEST))
    up_pre = low_back(jnp.einsum('bsd,df->bsf', hidden, shared_up, precision=HIGHEST))
    shared_inner = low(jax.nn.silu(gate_pre) * up_pre)
    shared_out = low_back(jnp.einsum('bsf,fd->bsd', shared_inner, shared_down, precision=HIGHEST))
    route_flat, slot_index = jax.vmap(partial(assign_slots, expert_count=expert_count))(routes_part)
    row_index = jnp.arange(batch_size, dtype=jnp.int32)[:, None]
    repeated = jnp.repeat(hidden, TOP, axis=1)
    buffer_rows = jnp.zeros((batch_size, expert_count, CAP, D), jnp.float32).at[row_index, route_flat, slot_index].set(repeated)
    expert_rows = low_back(jnp.transpose(buffer_rows, (1, 0, 2, 3)).reshape(expert_count, batch_size * CAP, D))
    expert_a = low_back(jnp.einsum('end,edf->enf', expert_rows, expert_gate, precision=HIGHEST))
    expert_b = low_back(jnp.einsum('end,edf->enf', expert_rows, expert_up, precision=HIGHEST))
    expert_inner = low(jax.nn.silu(expert_a) * expert_b)
    expert_out = low(low_back(jnp.einsum('enf,efd->end', expert_inner, expert_down, precision=HIGHEST)))
    returned = jnp.transpose(expert_out.reshape(expert_count, batch_size, CAP, D), (1, 0, 2, 3))
    picked = returned[row_index, route_flat, slot_index].reshape(batch_size, SEQ, TOP, D)
    return residual + shared_out + lax.optimization_barrier(jnp.sum(gate_share[..., None] * picked, 2))

def reference(tokens, cotangent, routes, segments, attn_gain, q_weight, kv_down, kv_gain, kv_up, out_weight, ffn_gain, router, shared_gate, shared_up, shared_down, expert_gate, expert_up, expert_down):
    weights = tuple((weight_arg.astype(jnp.float32) for weight_arg in (attn_gain, q_weight, kv_down, kv_gain, kv_up, out_weight, ffn_gain, router, shared_gate, shared_up, shared_down, expert_gate, expert_up, expert_down)))
    outputs = []
    input_grads = []
    totals = None
    for micro_step in range(MICRO):
        result, pullback = jax.vjp(partial(forward, routes_part=routes[micro_step], segments_part=segments[micro_step]), tokens[micro_step].astype(jnp.float32), weights)
        value_grad, weight_grads = pullback(cotangent[micro_step].astype(jnp.float32))
        outputs.append(result)
        input_grads.append(value_grad)
        if totals is None:
            totals = weight_grads
        else:
            totals = tuple((left_sum + right_sum for left_sum, right_sum in zip(totals, weight_grads)))
    return (jnp.stack(outputs).astype(jnp.bfloat16), jnp.stack(input_grads).astype(jnp.bfloat16), totals[0], totals[1], totals[2], totals[3], totals[4], totals[5], totals[6], totals[7], totals[8], totals[9], totals[10], totals[11], totals[12], totals[13])
```

```python
import functools

import jax
import jax.numpy as jnp
from jax import lax
from jax.experimental import pallas as pl
from jax.experimental.pallas import tpu as pltpu
from jax.sharding import PartitionSpec as P

D = 2048
HEADS = 16
NOPE = 128
ROPE = 64
VDIM = 128
RANK = 512
TOP = 6
SEQ = 64
MICRO = 2

EPSILON = 1e-06
ROPE_BASE = 10000.0
MASKED = -1e30
BF = jnp.bfloat16
F32 = jnp.float32

MESH_ID = pl.DeviceIdType.MESH


class Grid:
    def __init__(self, mesh):
        self.experts = mesh.shape["expert"]
        self.size = {"p": mesh.shape["dp"], "r": self.experts // 8, "q": 4}
        self.devices = self.size["p"] * self.experts

    def here(self):
        e = lax.axis_index("expert")
        r_size = self.size["r"]
        return {
            "p": lax.axis_index("dp"),
            "q": lax.div(e, 2 * r_size),
            "r": lax.rem(lax.div(e, 2), r_size),
            "c": lax.rem(e, 2),
        }

    def shift(self, at, offsets):
        moved = dict(at)
        for axis, step in offsets.items():
            if step:
                moved[axis] = lax.rem(at[axis] + step, self.size[axis])
        return moved

    def expert_of(self, at):
        return at["q"] * (2 * self.size["r"]) + at["r"] * 2 + at["c"]

    def number(self, at):
        return at["p"] * self.experts + self.expert_of(at)

    def mesh_id(self, at):
        return (at["p"], self.expert_of(at))

    def partners(self, at):
        found = [{**at, "c": 1 - at["c"]}]
        for axis in "pr":
            found += [self.shift(at, {axis: step}) for step in range(1, self.size[axis])]
        return found


def greet(grid, at):
    barrier = pltpu.get_barrier_semaphore()
    partners = grid.partners(at)
    for partner in partners:
        pl.semaphore_signal(barrier, inc=1, device_id=grid.mesh_id(partner), device_id_type=MESH_ID)
    others = len(partners)
    for step in (-1, 1):
        on_line = jnp.logical_and(at["q"] + step >= 0, at["q"] + step < grid.size["q"])
        others = others + on_line.astype(jnp.int32)

        @pl.when(on_line)
        def _():
            other = grid.mesh_id({**at, "q": at["q"] + step})
            pl.semaphore_signal(barrier, inc=1, device_id=other, device_id_type=MESH_ID)

    pl.semaphore_wait(barrier, others)


ALONG = (0, -1, 1, -2, 2, -3, 3)


def gather_kernel(grid, arrays, items, *refs):
    count = len(items)
    ins, outs = refs[:arrays], refs[arrays : 2 * arrays]
    send_sem, recv_sem, core_send, core_recv, own_sem = refs[2 * arrays :]
    at = grid.here()
    sibling = {**at, "c": 1 - at["c"]}
    q_size = grid.size["q"]
    greet(grid, at)
    pending = []
    own_copies = []
    me = grid.number(at)
    for a in range(arrays):
        own = pltpu.make_async_copy(ins[a], outs[a].at[me], own_sem.at[a])
        own.start()
        own_copies.append(own)

    def spans(axis):
        return ALONG if axis == "q" else tuple(range(grid.size[axis]))

    def inside(step):
        return jnp.logical_and(at["q"] + step >= 0, at["q"] + step < q_size)

    def guarded(step, action):
        if step:
            pl.when(inside(step))(action)
        else:
            action()

    def q_part(i, offset):
        return offset[items[i][3].index("q")]

    def slot(i, offset):
        number = 0
        for axis, part in zip(items[i][3], offset):
            number = number * len(spans(axis)) + spans(axis).index(part)
        return number

    def block_of(i, offset, base):
        moved = dict(base)
        for axis, part in zip(items[i][3], offset):
            if part:
                moved[axis] = (
                    base[axis] + part
                    if axis == "q"
                    else lax.rem(base[axis] + part, grid.size[axis])
                )
        return grid.number(moved)

    def views(i, offset, base):
        a, first, width, order = items[i]
        columns = pl.ds(first, width)
        view = outs[a].at[block_of(i, offset, base), :, columns]
        return (ins[a].at[:, columns] if offset == (0, 0, 0) else view), view

    def send(i, offset, landed, target_step, cond_step):
        number = len(pending)

        def copy():
            source, view = views(i, offset, at)
            return pltpu.make_async_remote_copy(
                src_ref=source,
                dst_ref=view,
                send_sem=send_sem.at[number],
                recv_sem=recv_sem.at[i, slot(i, landed)],
                device_id=grid.mesh_id(target_step()),
                device_id_type=MESH_ID,
            )

        guarded(cond_step, lambda: copy().start())
        pending.append((q_part(i, offset), cond_step, copy))

    def forward(i, offset, stage):
        axis = items[i][3][stage]
        if axis == "q":
            part = offset[stage]
            for step in (1, -1) if part == 0 else (1,) if part < 0 else (-1,):
                if abs(part - step) < q_size:
                    landed = offset[:stage] + (part - step,) + offset[stage + 1 :]
                    send(i, offset, landed, lambda step=step: {**at, "q": at["q"] + step}, step)
            return
        for step in range(1, grid.size[axis]):
            part = (offset[stage] - step) % grid.size[axis]
            landed = offset[:stage] + (part,) + offset[stage + 1 :]
            send(i, offset, landed, lambda step=step: grid.shift(at, {axis: step}), 0)

    def across(i, offset):
        def copy():
            source, view = views(i, offset, at)
            return pltpu.make_async_remote_copy(
                src_ref=source,
                dst_ref=view,
                send_sem=core_send.at[i, slot(i, offset)],
                recv_sem=core_recv.at[i, slot(i, offset)],
                device_id=grid.mesh_id(sibling),
                device_id_type=MESH_ID,
            )

        copy().start()
        pending.append((q_part(i, offset), 0, copy))

    def landed_at(i, offset, base, sem):
        view = views(i, offset, base)[1]
        pltpu.make_async_copy(view, view, sem.at[i, slot(i, offset)]).wait()

    def take(i, offset, stage):
        def action():
            landed_at(i, offset, at, recv_sem)
            if items[i][3][stage] == "q":
                forward(i, offset, stage)
            for later in range(stage + 1, 3):
                forward(i, offset, later)
            across(i, offset)

        guarded(q_part(i, offset), action)

    for i in range(count):
        for stage in range(3):
            forward(i, (0, 0, 0), stage)
        across(i, (0, 0, 0))
    ranges = [[spans(axis) for axis in item[3]] for item in items]
    todo = []
    for i in range(count):
        for u in ranges[i][0]:
            for v in ranges[i][1]:
                for w in ranges[i][2]:
                    stage = 2 if w else 1 if v else 0
                    if u or v or w:
                        todo.append((stage, abs(u), abs(v), abs(w), i, (u, v, w)))
    for stage, _, _, _, i, offset in sorted(todo):
        take(i, offset, stage)
    for own in own_copies:
        own.wait()
    for i in range(count):
        for u in ranges[i][0]:
            for v in ranges[i][1]:
                for w in ranges[i][2]:
                    offset = (u, v, w)
                    guarded(
                        q_part(i, offset),
                        functools.partial(landed_at, i, offset, sibling, core_recv),
                    )
    for q_step, cond_step, copy in pending:
        guarded(q_step, functools.partial(guarded, cond_step, lambda: copy().wait_send()))


def gather_all(grid, arrays, items, collective_id):
    count = len(items)
    slots = grid.devices // 2 // 4 * len(ALONG)
    return pl.pallas_call(
        functools.partial(gather_kernel, grid, len(arrays), items),
        out_shape=[jax.ShapeDtypeStruct((grid.devices,) + a.shape, a.dtype) for a in arrays],
        in_specs=[pl.BlockSpec(memory_space=pl.ANY)] * len(arrays),
        out_specs=[pl.BlockSpec(memory_space=pl.ANY)] * len(arrays),
        scratch_shapes=[
            pltpu.SemaphoreType.DMA((count * slots * 2,)),
            pltpu.SemaphoreType.DMA((count, slots)),
            pltpu.SemaphoreType.DMA((count, slots)),
            pltpu.SemaphoreType.DMA((count, slots)),
            pltpu.SemaphoreType.DMA((len(arrays),)),
        ],
        compiler_params=pltpu.CompilerParams(collective_id=collective_id, has_side_effects=True),
        name="gather_all",
    )(*arrays)


def add_rows(target, *parts):
    rows = target.shape[0]
    step = min(16, rows)

    @pl.loop(0, rows // step)
    def _(k):
        block = pl.ds(pl.multiple_of(k * step, step), step)
        total = parts[0][block, :].astype(jnp.float32)
        for part in parts[1:]:
            total = total + part[block, :].astype(jnp.float32)
        target[block, :] = total.astype(target.dtype)


DEPTH = 2
AHEAD = 6


def scatter_kernel(grid, arrays, items, *refs):
    count = len(items)
    ins, outs = refs[:arrays], refs[arrays : 2 * arrays]
    held, crossed = refs[2 * arrays : 3 * arrays], refs[3 * arrays : 4 * arrays]
    landing = refs[4 * arrays : 4 * arrays + 3 * count]
    load_sem, core_send, core_recv, send_sem, recv_sem, line_send, line_recv = refs[
        4 * arrays + 3 * count :
    ]
    at = grid.here()
    sibling = {**at, "c": 1 - at["c"]}
    size = grid.size
    q_size = size["q"]
    greet(grid, at)

    def flat(block):
        p, r, t = block
        return (p * size["r"] + r) * q_size + t

    def owner(base, block):
        p, r, t = block
        return grid.number({**grid.shift(base, {"p": p, "r": r}), "q": t})

    targets = []
    for t in range(q_size // 2):
        targets += [t, q_size - 1 - t]
    blocks = []
    for t in targets:
        near = [(p, r, t) for p in range(size["p"]) for r in range(size["r"])]
        blocks += sorted(near, key=lambda b: -(b[0] > 0) - (b[1] > 0))

    def load(a, block):
        return pltpu.make_async_copy(
            ins[a].at[owner(at, block)], held[a].at[flat(block)], load_sem.at[a, flat(block)]
        )

    def across(a, block):
        return pltpu.make_async_remote_copy(
            src_ref=ins[a].at[owner(sibling, block)],
            dst_ref=crossed[a].at[flat(block)],
            send_sem=core_send.at[a, flat(block)],
            recv_sem=core_recv.at[a, flat(block)],
            device_id=grid.mesh_id(sibling),
            device_id_type=MESH_ID,
        )

    def begin(number):
        if number < len(blocks):
            for a in range(arrays):
                across(a, blocks[number]).start()
                load(a, blocks[number]).start()

    merged = [0]

    def merge_to(block):
        while merged[0] <= blocks.index(block):
            now = blocks[merged[0]]
            for a in range(arrays):
                load(a, now).wait()
                across(a, now).wait_recv()
                view = held[a].at[flat(now)]
                add_rows(view, view, crossed[a].at[flat(now)])
            begin(merged[0] + AHEAD)
            merged[0] += 1

    def held_view(i, block):
        return held[items[i][0]].at[flat(block), :, pl.ds(items[i][1], items[i][2])]

    def block_at(i, first, second, t):
        part = dict(zip(items[i][3], (first, second)))
        return (part["p"], part["r"], t)

    pending = []

    def send(i, stage, steps, t):
        n1, n2 = (size[axis] for axis in items[i][3])
        step = steps[stage]
        slot = ((steps[0] - 1) * n2 + steps[1]) * q_size + t if stage == 0 else (steps[1] - 1) * q_size + t
        sem = slot if stage == 0 else (n1 - 1) * n2 * q_size + slot
        copy = pltpu.make_async_remote_copy(
            src_ref=held_view(i, block_at(i, *steps, t)),
            dst_ref=landing[3 * i + stage].at[slot],
            send_sem=send_sem.at[i, sem],
            recv_sem=recv_sem.at[i, sem],
            device_id=grid.mesh_id(grid.shift(at, {items[i][3][stage]: step})),
            device_id_type=MESH_ID,
        )
        return copy

    def start(i, stage, steps, t):
        copy = send(i, stage, steps, t)
        copy.start()
        pending.append(copy)

    def receive(i, stage, steps, t):
        send(i, stage, steps, t).wait_recv()
        into = (0, steps[1]) if stage == 0 else (0, 0)
        n2 = size[items[i][3][1]]
        slot = ((steps[0] - 1) * n2 + steps[1]) * q_size + t if stage == 0 else (steps[1] - 1) * q_size + t
        view = held_view(i, block_at(i, *into, t))
        add_rows(view, view, landing[3 * i + stage].at[slot])

    def line(i, t, step):
        side = 0 if step > 0 else 1
        return pltpu.make_async_remote_copy(
            src_ref=held_view(i, (0, 0, t)),
            dst_ref=landing[3 * i + 2].at[side * q_size + t],
            send_sem=line_send.at[i, t],
            recv_sem=line_recv.at[i, side * q_size + t],
            device_id=grid.mesh_id({**at, "q": at["q"] + step}),
            device_id_type=MESH_ID,
        )

    def from_line(i, t, step):
        line(i, t, step).wait_recv()
        side = 0 if step > 0 else 1
        view = held_view(i, (0, 0, t))
        add_rows(view, view, landing[3 * i + 2].at[side * q_size + t])

    def along(t):
        q = at["q"]
        for i in range(count):
            if t > 0:

                @pl.when(jnp.logical_and(q > 0, q <= t))
                def _():
                    from_line(i, t, 1)

                @pl.when(q < t)
                def _():
                    line(i, t, 1).start()

            if t < q_size - 1:

                @pl.when(jnp.logical_and(q < q_size - 1, q >= t))
                def _():
                    from_line(i, t, -1)

                @pl.when(q > t)
                def _():
                    line(i, t, -1).start()

    ticks = []
    for t in targets:
        for far in (True, False):
            turn = []
            for i in range(count):
                n1, n2 = (size[axis] for axis in items[i][3])
                for second in range(1, n2) if far else (0,):
                    for first in range(1, n1):
                        turn.append((i, (first, second), t))
            ticks.append((turn, None if far else t))

    def handle(k):
        turn, done = ticks[k]
        for i, steps, t in turn:
            merge_to(block_at(i, 0, steps[1], t))
            receive(i, 0, steps, t)
            if steps[1] and steps[0] == size[items[i][3][0]] - 1:
                start(i, 1, (0, steps[1]), t)

    def close(t):
        for i in range(count):
            for second in range(1, size[items[i][3][1]]):
                receive(i, 1, (0, second), t)

    for number in range(AHEAD):
        begin(number)
    finished = []
    for k in range(len(ticks) + DEPTH):
        if k < len(ticks):
            for i, steps, t in ticks[k][0]:
                merge_to(block_at(i, *steps, t))
                start(i, 0, steps, t)
        if k >= DEPTH:
            handle(k - DEPTH)
            if ticks[k - DEPTH][1] is not None:
                finished.append(ticks[k - DEPTH][1])
                if len(finished) > 1:
                    close(finished[-2])
                    along(finished[-2])
    close(finished[-1])
    along(finished[-1])
    for a in range(arrays):
        add_rows(outs[a], held[a].at[at["q"]])
    for block in blocks:
        for a in range(arrays):
            across(a, block).wait_send()
    for copy in pending:
        copy.wait_send()
    for t in range(q_size):
        for i in range(count):

            @pl.when(at["q"] < t)
            def _():
                line(i, t, 1).wait_send()

            @pl.when(at["q"] > t)
            def _():
                line(i, t, -1).wait_send()


def sum_scattered(grid, arrays, items, collective_id, dtype=jnp.float32):
    count = len(items)
    chips = grid.devices // 2
    q_size = grid.size["q"]
    scratch = [pltpu.VMEM((chips,) + a.shape[1:], a.dtype) for a in arrays] * 2
    most = 0
    for a, _, width, order in items:
        n1, n2 = (grid.size[axis] for axis in order)
        shares = ((n1 - 1) * n2 * q_size, (n2 - 1) * q_size, 2 * q_size)
        most = max(most, shares[0] + shares[1])
        for share in shares:
            scratch.append(pltpu.VMEM((share, arrays[a].shape[1], width), arrays[a].dtype))
    return pl.pallas_call(
        functools.partial(scatter_kernel, grid, len(arrays), items),
        out_shape=[jax.ShapeDtypeStruct(a.shape[1:], dtype) for a in arrays],
        in_specs=[pl.BlockSpec(memory_space=pl.ANY)] * len(arrays),
        out_specs=[pl.BlockSpec(memory_space=pltpu.VMEM)] * len(arrays),
        scratch_shapes=scratch
        + [
            pltpu.SemaphoreType.DMA((len(arrays), chips)),
            pltpu.SemaphoreType.DMA((len(arrays), chips)),
            pltpu.SemaphoreType.DMA((len(arrays), chips)),
            pltpu.SemaphoreType.DMA((count, most)),
            pltpu.SemaphoreType.DMA((count, most)),
            pltpu.SemaphoreType.DMA((count, q_size)),
            pltpu.SemaphoreType.DMA((count, 2 * q_size)),
        ],
        compiler_params=pltpu.CompilerParams(
            collective_id=collective_id, has_side_effects=True, vmem_limit_bytes=60 * 2**20
        ),
        name="sum_scattered",
    )(*arrays)


def normalize(values, gain_row):
    scale_rows = lax.rsqrt(jnp.mean(values * values, -1, keepdims=True) + EPSILON)
    return (values * scale_rows * gain_row, scale_rows)


def normalize_back(values, scale_rows, gain_row, gradient):
    weighted = gradient * gain_row
    gain_grad = jnp.sum(gradient * values * scale_rows, 0)
    inner_mean = jnp.mean(weighted * values, -1, keepdims=True)
    return (
        scale_rows * weighted - values * scale_rows * scale_rows * scale_rows * inner_mean,
        gain_grad,
    )


def rope_tables(length, width):
    half_width = width // 2
    frequency = ROPE_BASE ** (-2.0 * jnp.arange(half_width, dtype=jnp.float32) / width)
    angles = jnp.arange(length, dtype=jnp.float32)[:, None] * frequency[None, :]
    return (jnp.cos(angles), jnp.sin(angles))


def rotate(values, cosine, sine_table):
    half_width = values.shape[-1] // 2
    front_half = values[..., :half_width]
    back_half = values[..., half_width:]
    return jnp.concatenate(
        [
            front_half * cosine - back_half * sine_table,
            back_half * cosine + front_half * sine_table,
        ],
        -1,
    )


def unrotate(gradient, cosine, sine_table):
    half_width = gradient.shape[-1] // 2
    front_half = gradient[..., :half_width]
    back_half = gradient[..., half_width:]
    return jnp.concatenate(
        [
            front_half * cosine + back_half * sine_table,
            back_half * cosine - front_half * sine_table,
        ],
        -1,
    )


def capacity_for(expert_count):
    return min(SEQ, ((4 * SEQ * TOP + 3 * expert_count - 1) // (3 * expert_count) + 7) // 8 * 8)


def silu_parts(pre_act):
    sigma_rows = jax.nn.sigmoid(pre_act)
    return (pre_act * sigma_rows, sigma_rows * (1.0 + pre_act * (1.0 - sigma_rows)))


def attention_mask(segment_row):
    places = jnp.arange(segment_row.shape[0], dtype=jnp.int32)
    return (places[:, None] >= places[None, :]) & (segment_row[:, None] == segment_row[None, :])


def dot(left, right):
    return jnp.dot(left, right, preferred_element_type=F32)


def dot_t(left, right):
    return lax.dot_general(left, right, (((1,), (1,)), ((), ())), preferred_element_type=F32)


def t_dot(left, right):
    return lax.dot_general(left, right, (((0,), (0,)), ((), ())), preferred_element_type=F32)


def pack(parts, rows):
    flat = jnp.concatenate([part.reshape(rows, -1) for part in parts], 1)
    width = -(-flat.shape[1] // 2048) * 2048
    flat = jnp.pad(flat, ((0, 0), (0, width - flat.shape[1])))
    return flat.reshape(rows, width // 128, 128)


def unpack(block, shapes):
    rows = block.shape[0]
    flat = block.reshape(rows, -1)
    parts, first = [], 0
    for shape in shapes:
        size = 1
        for extent in shape:
            size *= extent
        parts.append(flat[:, first : first + size].reshape((rows,) + shape))
        first += size
    return parts


def swap_windows(pieces, axis_size):
    me = lax.axis_index("dp")
    got = [pieces(me)]
    for step in range(1, axis_size):
        peer = lax.rem(me + step, axis_size)
        perm = [(k, (k + step) % axis_size) for k in range(axis_size)]
        got.append(lax.ppermute(pieces(peer), "dp", perm))
    return got


def in_order(got):
    me = lax.axis_index("dp")
    count = len(got)
    ordered = []
    for k in range(count):
        value = got[0]
        for step in range(1, count):
            value = jnp.where(lax.rem(me - k + count, count) == step, got[step], value)
        ordered.append(value)
    return ordered


def attention_forward(rows, segments, weights, tables):
    attn_gain, q_weight, kv_down, kv_gain, kv_up, out_weight, ffn_gain, router = weights
    cosine, sine_table = tables
    count = rows.shape[0]
    inputs = rows.astype(F32)
    normed_f, scale_one = normalize(inputs, attn_gain)
    normed = normed_f.astype(BF)
    q_raw = dot(normed, q_weight).reshape(MICRO, SEQ, HEADS, NOPE + ROPE)
    turn = (cosine[:, None, :], sine_table[:, None, :])
    queries = jnp.concatenate([q_raw[..., :NOPE], rotate(q_raw[..., NOPE:], *turn)], -1).astype(BF)
    kv_raw = dot(normed, kv_down)
    latent_f, scale_latent = normalize(kv_raw[:, :RANK], kv_gain)
    latent = latent_f.astype(BF)
    key_rope = rotate(kv_raw[:, RANK:].reshape(MICRO, SEQ, ROPE), cosine, sine_table)
    kv_full = dot(latent, kv_up).reshape(MICRO, SEQ, HEADS, NOPE + VDIM)
    shared_key = jnp.broadcast_to(key_rope[:, :, None, :], (MICRO, SEQ, HEADS, ROPE))
    key_rows = jnp.concatenate([kv_full[..., :NOPE], shared_key], -1).astype(BF)
    value_rows = kv_full[..., NOPE:].astype(BF)
    allowed = jax.vmap(attention_mask)(segments)[:, None]
    scores = jnp.einsum("mqhe,mkhe->mhqk", queries, key_rows, preferred_element_type=F32)
    scores = jnp.where(allowed, scores * (NOPE + ROPE) ** (-0.5), MASKED)
    powers = jnp.exp(scores - jnp.max(scores, -1, keepdims=True))
    softmax_rows = powers / jnp.sum(powers, -1, keepdims=True)
    probability = softmax_rows.astype(BF)
    attended = (
        jnp.einsum("mhqk,mkhe->mqhe", probability, value_rows, preferred_element_type=F32)
        .reshape(count, HEADS * VDIM)
        .astype(BF)
    )
    residual = inputs + dot(attended, out_weight)
    hidden_f, scale_two = normalize(residual, ffn_gain)
    hidden = hidden_f.astype(BF)
    saved = (
        inputs, scale_one, normed, queries, kv_raw, scale_latent, latent, key_rows, value_rows,
        softmax_rows, probability, attended, residual, scale_two,
    )
    return hidden, saved


def attention_backward(grad_out, hidden_grad, saved, weights, tables):
    attn_gain, q_weight, kv_down, kv_gain, kv_up, out_weight, ffn_gain, router = weights
    cosine, sine_table = tables
    (
        inputs, scale_one, normed, queries, kv_raw, scale_latent, latent, key_rows, value_rows,
        softmax_rows, probability, attended, residual, scale_two,
    ) = saved
    count = inputs.shape[0]
    turn = (cosine[:, None, :], sine_table[:, None, :])
    residual_part, ffn_gain_grad = normalize_back(residual, scale_two, ffn_gain, hidden_grad)
    residual_grad = grad_out + residual_part
    mixed_grad = residual_grad.astype(BF)
    out_weight_grad = t_dot(attended, mixed_grad)
    attended_grad = dot_t(mixed_grad, out_weight).astype(BF).reshape(MICRO, SEQ, HEADS, VDIM)
    value_grad = jnp.einsum(
        "mhqk,mqhe->mkhe", probability, attended_grad, preferred_element_type=F32
    )
    probs_grad = jnp.einsum(
        "mqhe,mkhe->mhqk", attended_grad, value_rows, preferred_element_type=F32
    )
    inner = jnp.sum(softmax_rows * probs_grad, -1, keepdims=True)
    score_grad = (softmax_rows * (probs_grad - inner)).astype(BF)
    score_scale = (NOPE + ROPE) ** (-0.5)
    query_grad = score_scale * jnp.einsum(
        "mhqk,mkhe->mqhe", score_grad, key_rows, preferred_element_type=F32
    )
    keys_grad = score_scale * jnp.einsum(
        "mhqk,mqhe->mkhe", score_grad, queries, preferred_element_type=F32
    )
    q_raw_grad = (
        jnp.concatenate([query_grad[..., :NOPE], unrotate(query_grad[..., NOPE:], *turn)], -1)
        .reshape(count, HEADS * (NOPE + ROPE))
        .astype(BF)
    )
    q_weight_grad = t_dot(normed, q_raw_grad)
    kv_full_grad = (
        jnp.concatenate([keys_grad[..., :NOPE], value_grad], -1)
        .reshape(count, HEADS * (NOPE + VDIM))
        .astype(BF)
    )
    kv_up_grad = t_dot(latent, kv_full_grad)
    latent_grad = dot_t(kv_full_grad, kv_up)
    latent_part, kv_gain_grad = normalize_back(
        kv_raw[:, :RANK], scale_latent, kv_gain, latent_grad
    )
    rope_grad = unrotate(jnp.sum(keys_grad[..., NOPE:], 2), cosine, sine_table)
    kv_raw_grad = jnp.concatenate([latent_part, rope_grad.reshape(count, ROPE)], -1).astype(BF)
    kv_down_grad = t_dot(normed, kv_raw_grad)
    normed_grad = dot_t(q_raw_grad, q_weight) + dot_t(kv_raw_grad, kv_down)
    input_part, attn_gain_grad = normalize_back(inputs, scale_one, attn_gain, normed_grad)
    tokens_grad = residual_grad + input_part
    return tokens_grad, (
        attn_gain_grad, q_weight_grad, kv_down_grad, kv_gain_grad, kv_up_grad, out_weight_grad,
        ffn_gain_grad,
    )


def experts_step(hidden_all, grad_all, gates, weights, expert_grads):
    gate_part, up_part, down_part, shared_in, shared_down = weights
    devices, tokens, _ = hidden_all.shape
    blocks = devices * tokens // SEQ
    capacity = capacity_for(gates.shape[1])
    expert = lax.axis_index("expert")
    hidden = hidden_all.reshape(blocks, SEQ, D)
    grad = grad_all.reshape(blocks, SEQ, D)
    share = lax.dynamic_index_in_dim(gates, expert, 1, keepdims=False).reshape(blocks, SEQ)
    chosen = share >= 0
    place = jnp.cumsum(chosen.astype(jnp.int32), 1) - 1
    slots = jnp.arange(capacity, dtype=jnp.int32)
    picks = (chosen[:, None, :] & (place[:, None, :] == slots[None, :, None])).astype(BF)
    share_rows = jnp.sum(picks.astype(F32) * share[:, None, :], -1).reshape(-1, 1)
    rows = jnp.einsum("bst,btd->bsd", picks, hidden).reshape(-1, D)
    grad_rows = jnp.einsum("bst,btd->bsd", picks, grad).reshape(-1, D)
    a_pre = dot(rows, gate_part)
    b_pre = dot(rows, up_part)
    act, slope = silu_parts(a_pre)
    inner_f = act * b_pre
    inner = inner_f.astype(BF)
    flow = dot_t(grad_rows, down_part)
    gate_grad_rows = jnp.sum(inner.astype(F32) * flow, -1).reshape(blocks, capacity)
    inner_grad = flow * share_rows
    a_grad = (inner_grad * b_pre * slope).astype(BF)
    b_grad = (inner_grad * act).astype(BF)
    row_grad = (dot_t(a_grad, gate_part) + dot_t(b_grad, up_part)).astype(BF)
    gate_grad = jnp.einsum("bst,bs->bt", picks.astype(F32), gate_grad_rows, precision=lax.Precision.HIGHEST)
    scaled = (inner.astype(F32) * share_rows).astype(BF)
    expert_out = dot(scaled, down_part).astype(BF)
    new_grads = (t_dot(rows, a_grad), t_dot(rows, b_grad), t_dot(scaled, grad_rows))
    if expert_grads is not None:
        new_grads = tuple(x + y for x, y in zip(expert_grads[0], new_grads))

    half = shared_in.shape[1] // 2
    hidden_flat = hidden.reshape(-1, D)
    grad_flat = grad.reshape(-1, D)
    shared_pre = dot(hidden_flat, shared_in)
    shared_act, shared_slope = silu_parts(shared_pre[:, :half])
    shared_b = shared_pre[:, half:]
    shared_inner = (shared_act * shared_b).astype(BF)
    shared_flow = dot_t(grad_flat, shared_down)
    shared_grad = jnp.concatenate(
        [shared_flow * shared_b * shared_slope, shared_flow * shared_act], 1
    ).astype(BF)
    hidden_part = jnp.einsum(
        "bst,bsd->btd", picks, row_grad.reshape(blocks, capacity, D), preferred_element_type=F32
    ) + dot_t(shared_grad, shared_in).reshape(blocks, SEQ, D)
    out_part = jnp.einsum(
        "bst,bsd->btd", picks, expert_out.reshape(blocks, capacity, D), preferred_element_type=F32
    ) + dot(shared_inner, shared_down).reshape(blocks, SEQ, D)
    shared_grads = (t_dot(hidden_flat, shared_grad), t_dot(shared_inner, grad_flat))
    if expert_grads is not None:
        shared_grads = tuple(x + y for x, y in zip(expert_grads[1], shared_grads))
    shape = (devices, tokens, D)
    mine = (jnp.arange(gates.shape[1], dtype=jnp.int32) == expert)[None, :, None]
    gate_grad = jnp.where(mine, gate_grad.reshape(devices, 1, tokens), 0.0)
    return (
        out_part.astype(BF).reshape(shape),
        hidden_part.astype(BF).reshape(shape),
        gate_grad,
        (new_grads, shared_grads),
    )


def body(
    grid,
    tokens,
    cotangent,
    routes,
    segments,
    attn_gain,
    q_weight,
    kv_down,
    kv_gain,
    kv_up,
    out_weight,
    ffn_gain,
    router,
    shared_gate,
    shared_up,
    shared_down,
    expert_gate,
    expert_up,
    expert_down,
):
    devices = grid.devices
    dp_size = grid.size["p"]
    experts = router.shape[1]
    tables = rope_tables(SEQ, ROPE)
    me_dp = lax.axis_index("dp")
    count = MICRO * SEQ
    eff = expert_gate.shape[2]

    window = -(-eff // (128 * dp_size)) * 128
    starts = [min(k * window, eff - window) for k in range(dp_size)]

    def start_of(peer):
        return jnp.minimum(peer * window, eff - window)

    def columns_for(array):
        return lambda peer: lax.dynamic_slice_in_dim(array[0], start_of(peer), window, 1)

    def rows_for(array):
        return lambda peer: lax.dynamic_slice_in_dim(array[0], start_of(peer), window, 0)

    gate_part = jnp.concatenate(in_order(swap_windows(columns_for(expert_gate), dp_size)), 0)
    up_part = jnp.concatenate(in_order(swap_windows(columns_for(expert_up), dp_size)), 0)
    down_part = jnp.concatenate(in_order(swap_windows(rows_for(expert_down), dp_size)), 1)
    fresh = jnp.arange(window, dtype=jnp.int32) + start_of(me_dp) >= me_dp * window
    gate_part = jnp.where(fresh[None, :], gate_part, 0)
    up_part = jnp.where(fresh[None, :], up_part, 0)
    down_part = jnp.where(fresh[:, None], down_part, 0)

    share = shared_gate.shape[1] // devices
    both = jnp.concatenate(
        [shared_gate.reshape(-1, devices, share), shared_up.reshape(-1, devices, share)], 2
    )
    shared_in = lax.all_to_all(
        both.transpose(1, 0, 2), ("dp", "expert"), split_axis=0, concat_axis=0, tiled=True
    ).reshape(D, 2 * share)

    small_shapes = (attn_gain.shape, ffn_gain.shape, kv_gain.shape, router.shape)
    small = pack([attn_gain[None], ffn_gain[None], kv_gain[None], router[None]], 1)[0]
    up_shape = kv_up.shape
    kv_up_sent = kv_up if up_shape[0] % 16 == 0 else kv_up.reshape(16, -1)
    first, second = ("q", "r", "p"), ("q", "p", "r")
    got = gather_all(
        grid,
        [q_weight, kv_down, kv_up_sent, out_weight, small],
        [
            (0, 0, q_weight.shape[1], first),
            (3, 0, out_weight.shape[1], second),
            (2, 0, kv_up_sent.shape[1], second),
            (1, 0, kv_down.shape[1], second),
            (4, 0, 128, first),
        ],
        0,
    )
    gains = unpack(got[4], small_shapes)
    weights = (
        gains[0].reshape(-1).astype(F32),
        got[0].reshape(D, -1),
        got[1].reshape(D, -1),
        gains[2].reshape(-1).astype(F32),
        got[2].reshape(RANK, -1),
        got[3].reshape(-1, D),
        gains[1].reshape(-1).astype(F32),
        gains[3].reshape(D, experts),
    )
    router_full = weights[7]

    token_rows = tokens.reshape(count, D)
    grad_out = cotangent.reshape(count, D)
    route_rows = routes.reshape(count, TOP)
    hidden, saved = attention_forward(token_rows, segments.reshape(MICRO, SEQ), weights, tables)
    logits = dot(hidden, router_full)
    choose = route_rows[:, :, None] == jnp.arange(experts, dtype=jnp.int32)[None, None, :]
    choose = choose.astype(F32)
    gate_share = jax.nn.softmax(jnp.sum(choose * logits[:, None, :], -1), -1)
    dense_share = jnp.sum(choose * gate_share[..., None], 1)
    dense_gates = jnp.where(jnp.sum(choose, 1) > 0, dense_share, -1.0)

    groups = 1 if devices * count <= 8192 else MICRO
    size = count // groups
    half = D // 2
    own_weights = (gate_part, up_part, down_part, shared_in, shared_down)
    outs, hidden_grads, gate_grads = [], [], []
    grads = None
    for g in range(groups):
        piece = slice(g * size, (g + 1) * size)
        sent = [hidden[piece], grad_out[piece], dense_gates[piece].T]
        if g > 0:
            *sent, hidden_grads[-1], outs[-1] = lax.optimization_barrier(
                (*sent, hidden_grads[-1], outs[-1])
            )
        hidden_all, grad_all, gates_all = gather_all(
            grid,
            sent,
            [
                (0, 0, half, first),
                (0, half, half, second),
                (1, 0, half, first),
                (1, half, half, second),
                (2, 0, size, first),
            ],
            1,
        )
        out_part, hidden_part, gate_part_grad, grads = experts_step(
            hidden_all, grad_all, gates_all, own_weights, grads
        )
        hidden_sum, gate_sum = sum_scattered(
            grid,
            [hidden_part, gate_part_grad],
            [(0, 0, half, ("p", "r")), (0, half, half, ("r", "p")), (1, 0, size, ("p", "r"))],
            2,
        )
        (out_sum,) = sum_scattered(
            grid, [out_part], [(0, 0, half, ("p", "r")), (0, half, half, ("r", "p"))], 3
        )
        hidden_grads.append(hidden_sum)
        gate_grads.append(gate_sum.T)
        outs.append(out_sum)
    hidden_sum = jnp.concatenate(hidden_grads, 0)
    gate_grad = jnp.concatenate(gate_grads, 0)
    result = saved[12] + jnp.concatenate(outs, 0)

    dense_share = jnp.maximum(dense_share, 0.0)
    inner = jnp.sum(dense_share * gate_grad, -1, keepdims=True)
    logit_grad = (dense_share * (gate_grad - inner)).astype(BF)
    router_grad = t_dot(hidden, logit_grad)
    hidden_grad = hidden_sum + dot_t(logit_grad, router_full)
    tokens_grad, (
        attn_gain_grad, q_weight_grad, kv_down_grad, kv_gain_grad, kv_up_grad, out_weight_grad,
        ffn_gain_grad,
    ) = attention_backward(grad_out.astype(F32), hidden_grad, saved, weights, tables)

    small_grads = pack(
        [
            attn_gain_grad.reshape(devices, -1),
            ffn_gain_grad.reshape(devices, -1),
            kv_gain_grad.reshape(devices, -1),
            router_grad.reshape(devices, -1),
        ],
        devices,
    )
    q_sum, down_sum, up_sum, out_weight_sum, small_sum = sum_scattered(
        grid,
        [
            q_weight_grad.astype(BF).reshape((devices,) + q_weight.shape),
            kv_down_grad.astype(BF).reshape((devices,) + kv_down.shape),
            kv_up_grad.astype(BF).reshape((devices,) + kv_up_sent.shape),
            out_weight_grad.astype(BF).reshape((devices,) + out_weight.shape),
            small_grads,
        ],
        [
            (0, 0, q_weight.shape[1], ("p", "r")),
            (3, 0, out_weight.shape[1], ("r", "p")),
            (2, 0, kv_up_sent.shape[1], ("r", "p")),
            (1, 0, kv_down.shape[1], ("r", "p")),
            (4, 0, 128, ("p", "r")),
        ],
        4,
    )
    small_sums = unpack(small_sum[None], small_shapes)

    (gate_grad_part, up_grad_part, down_grad_part), (shared_in_grad, shared_down_grad) = grads
    shared_back = lax.all_to_all(
        shared_in_grad.astype(BF).reshape(devices, -1, 2 * share),
        ("dp", "expert"), split_axis=0, concat_axis=0, tiled=True,
    ).astype(F32)
    shared_back = shared_back.transpose(1, 0, 2)
    shared_gate_grad = shared_back[:, :, :share].reshape(shared_gate.shape)
    shared_up_grad = shared_back[:, :, share:].reshape(shared_up.shape)

    def whole(part, axis, other, extent):
        def for_peer(peer):
            return lax.dynamic_slice_in_dim(part, peer * extent, extent, other)

        got_back = swap_windows(lambda peer: for_peer(peer).astype(BF), dp_size)
        got_back = [for_peer(me_dp)] + [piece.astype(F32) for piece in got_back[1:]]
        pieces = []
        for k, piece in enumerate(in_order(got_back)):
            skip = k * window - starts[k]
            pieces.append(lax.slice_in_dim(piece, skip, window, axis=axis))
        return jnp.concatenate(pieces, axis)[None]

    extent = expert_gate.shape[1]
    return (
        result.astype(BF).reshape(tokens.shape),
        tokens_grad.astype(BF).reshape(tokens.shape),
        small_sums[0].reshape(-1),
        q_sum,
        down_sum,
        small_sums[2].reshape(-1),
        up_sum.reshape(up_shape),
        out_weight_sum,
        small_sums[1].reshape(-1),
        small_sums[3].reshape(router.shape),
        shared_gate_grad,
        shared_up_grad,
        shared_down_grad,
        whole(gate_grad_part, 1, 0, extent),
        whole(up_grad_part, 1, 0, extent),
        whole(down_grad_part, 0, 1, extent),
    )


def solution(mesh):
    return jax.shard_map(
        functools.partial(body, Grid(mesh)),
        mesh=mesh,
        in_specs=(
            P(None, ("dp", "expert"), None, None),
            P(None, ("dp", "expert"), None, None),
            P(None, ("dp", "expert"), None, None),
            P(None, ("dp", "expert"), None),
            P(("dp", "expert")),
            P(("dp", "expert"), None),
            P(("dp", "expert"), None),
            P(("dp", "expert")),
            P(("dp", "expert"), None),
            P(("dp", "expert"), None),
            P(("dp", "expert")),
            P(("dp", "expert"), None),
            P(("dp", "expert"), None),
            P(("dp", "expert"), None),
            P(("dp", "expert"), None),
            P("expert", "dp", None),
            P("expert", "dp", None),
            P("expert", None, "dp"),
        ),
        out_specs=(
            P(None, ("dp", "expert"), None, None),
            P(None, ("dp", "expert"), None, None),
            P(("dp", "expert")),
            P(("dp", "expert"), None),
            P(("dp", "expert"), None),
            P(("dp", "expert")),
            P(("dp", "expert"), None),
            P(("dp", "expert"), None),
            P(("dp", "expert")),
            P(("dp", "expert"), None),
            P(("dp", "expert"), None),
            P(("dp", "expert"), None),
            P(("dp", "expert"), None),
            P("expert", "dp", None),
            P("expert", "dp", None),
            P("expert", None, "dp"),
        ),
        check_vma=False,
    )
```

```python
import functools

import jax
import jax.numpy as jnp
from jax import lax
from jax.experimental import pallas as pl
from jax.experimental.pallas import tpu as pltpu
from jax.sharding import PartitionSpec as P

D = 2048
HEADS = 16
NOPE = 128
ROPE = 64
VDIM = 128
RANK = 512
TOP = 6
SEQ = 64
MICRO = 2

EPSILON = 1e-06
ROPE_BASE = 10000.0
MASKED = -1e30
BF = jnp.bfloat16
F32 = jnp.float32

MESH_ID = pl.DeviceIdType.MESH


class Grid:
    def __init__(self, mesh):
        self.experts = mesh.shape["expert"]
        self.size = {"p": mesh.shape["dp"], "r": self.experts // 8, "q": 4}
        self.devices = self.size["p"] * self.experts

    def here(self):
        e = lax.axis_index("expert")
        r_size = self.size["r"]
        return {
            "p": lax.axis_index("dp"),
            "q": lax.div(e, 2 * r_size),
            "r": lax.rem(lax.div(e, 2), r_size),
            "c": lax.rem(e, 2),
        }

    def shift(self, at, offsets):
        moved = dict(at)
        for axis, step in offsets.items():
            if step:
                moved[axis] = lax.rem(at[axis] + step, self.size[axis])
        return moved

    def expert_of(self, at):
        return at["q"] * (2 * self.size["r"]) + at["r"] * 2 + at["c"]

    def number(self, at):
        return at["p"] * self.experts + self.expert_of(at)

    def mesh_id(self, at):
        return (at["p"], self.expert_of(at))

    def partners(self, at):
        found = [{**at, "c": 1 - at["c"]}]
        for axis, size in self.size.items():
            found += [self.shift(at, {axis: step}) for step in range(1, size)]
        return found


def greet(grid, at):
    barrier = pltpu.get_barrier_semaphore()
    partners = grid.partners(at)
    for partner in partners:
        pl.semaphore_signal(barrier, inc=1, device_id=grid.mesh_id(partner), device_id_type=MESH_ID)
    pl.semaphore_wait(barrier, len(partners))


ALONG = (0, -1, 1, -2, 2, -3, 3)


def span_of(grid, axis):
    return ALONG if axis == "q" else tuple(range(grid.size[axis]))


class Gather:
    def __init__(self, grid, arrays, items):
        count = len(items)
        slots = grid.devices // 2 // 4 * len(ALONG)
        self.grid, self.items = grid, items
        self.inputs = list(arrays)
        self.in_specs = [pl.BlockSpec(memory_space=pl.ANY)] * len(arrays)
        self.out_shapes = [
            jax.ShapeDtypeStruct((grid.devices,) + a.shape, a.dtype) for a in arrays
        ]
        self.out_specs = [pl.BlockSpec(memory_space=pl.ANY)] * len(arrays)
        self.scratch = [
            pltpu.SemaphoreType.DMA((count * slots * 2,)),
            pltpu.SemaphoreType.DMA((count, slots)),
            pltpu.SemaphoreType.DMA((count, slots)),
            pltpu.SemaphoreType.DMA((count, slots)),
            pltpu.SemaphoreType.DMA((len(arrays),)),
        ]

    def steps(self, at, ins, outs, scratch):
        grid, items = self.grid, self.items
        count = len(items)
        send_sem, recv_sem, core_send, core_recv, own_sem = scratch
        sibling = {**at, "c": 1 - at["c"]}
        q_size = grid.size["q"]
        pending = []
        me = grid.number(at)

        def inside(step):
            return jnp.logical_and(at["q"] + step >= 0, at["q"] + step < q_size)

        def guarded(step, action):
            if step:
                pl.when(inside(step))(action)
            else:
                action()

        def q_part(i, offset):
            return offset[items[i][3].index("q")]

        def slot(i, offset):
            number = 0
            for axis, part in zip(items[i][3], offset):
                span = span_of(grid, axis)
                number = number * len(span) + span.index(part)
            return number

        def block_of(i, offset, base):
            moved = dict(base)
            for axis, part in zip(items[i][3], offset):
                if part:
                    moved[axis] = (
                        base[axis] + part
                        if axis == "q"
                        else lax.rem(base[axis] + part, grid.size[axis])
                    )
            return grid.number(moved)

        def views(i, offset, base):
            a, first, width, order = items[i]
            columns = pl.ds(first, width)
            view = outs[a].at[block_of(i, offset, base), :, columns]
            return (ins[a].at[:, columns] if offset == (0, 0, 0) else view), view

        def send(i, offset, landed, target_step, cond_step):
            number = len(pending)

            def copy():
                source, view = views(i, offset, at)
                return pltpu.make_async_remote_copy(
                    src_ref=source,
                    dst_ref=view,
                    send_sem=send_sem.at[number],
                    recv_sem=recv_sem.at[i, slot(i, landed)],
                    device_id=grid.mesh_id(target_step()),
                    device_id_type=MESH_ID,
                )

            guarded(cond_step, lambda: copy().start())
            pending.append((q_part(i, offset), cond_step, copy))

        def forward(i, offset, stage):
            axis = items[i][3][stage]
            if axis == "q":
                part = offset[stage]
                for step in (1, -1) if part == 0 else (1,) if part < 0 else (-1,):
                    if abs(part - step) < q_size:
                        landed = offset[:stage] + (part - step,) + offset[stage + 1 :]
                        send(
                            i, offset, landed, lambda step=step: {**at, "q": at["q"] + step}, step
                        )
                return
            for step in range(1, grid.size[axis]):
                part = (offset[stage] - step) % grid.size[axis]
                landed = offset[:stage] + (part,) + offset[stage + 1 :]
                send(i, offset, landed, lambda step=step: grid.shift(at, {axis: step}), 0)

        def across(i, offset):
            def copy():
                source, view = views(i, offset, at)
                return pltpu.make_async_remote_copy(
                    src_ref=source,
                    dst_ref=view,
                    send_sem=core_send.at[i, slot(i, offset)],
                    recv_sem=core_recv.at[i, slot(i, offset)],
                    device_id=grid.mesh_id(sibling),
                    device_id_type=MESH_ID,
                )

            copy().start()
            pending.append((q_part(i, offset), 0, copy))

        def landed_at(i, offset, base, sem):
            view = views(i, offset, base)[1]
            pltpu.make_async_copy(view, view, sem.at[i, slot(i, offset)]).wait()

        def take(i, offset, stage):
            def action():
                landed_at(i, offset, at, recv_sem)
                if items[i][3][stage] == "q":
                    forward(i, offset, stage)
                for later in range(stage + 1, 3):
                    forward(i, offset, later)
                across(i, offset)

            guarded(q_part(i, offset), action)

        ranges = [[span_of(grid, axis) for axis in item[3]] for item in items]
        offsets = [
            (i, (u, v, w))
            for i in range(count)
            for u in ranges[i][0]
            for v in ranges[i][1]
            for w in ranges[i][2]
        ]
        todo = []
        for i, offset in offsets:
            if any(offset):
                stage = max(k for k in range(3) if offset[k])
                todo.append((stage,) + tuple(abs(part) for part in offset) + (i, offset))
        yield len(todo) + 1

        own_copies = []
        for a in range(len(ins)):
            own = pltpu.make_async_copy(ins[a], outs[a].at[me], own_sem.at[a])
            own.start()
            own_copies.append(own)
        for i in range(count):
            for stage in range(3):
                forward(i, (0, 0, 0), stage)
            across(i, (0, 0, 0))
        yield
        for stage, _, _, _, i, offset in sorted(todo):
            take(i, offset, stage)
            yield
        for own in own_copies:
            own.wait()
        for i, offset in offsets:
            guarded(
                q_part(i, offset), functools.partial(landed_at, i, offset, sibling, core_recv)
            )
        for q_step, cond_step, copy in pending:
            guarded(q_step, functools.partial(guarded, cond_step, lambda: copy().wait_send()))


def add_rows(target, *parts):
    rows = target.shape[0]
    step = min(16, rows)

    @pl.loop(0, rows // step)
    def _(k):
        block = pl.ds(pl.multiple_of(k * step, step), step)
        total = parts[0][block, :].astype(F32)
        for part in parts[1:]:
            total = total + part[block, :].astype(F32)
        target[block, :] = total.astype(target.dtype)


DEPTH = 2
AHEAD = 4


class Scatter:
    def __init__(self, grid, arrays, items, rounds):
        count = len(items)
        chips = grid.devices // 2
        q_size = grid.size["q"]
        self.grid, self.items, self.rounds = grid, items, rounds
        self.inputs = list(arrays)
        self.in_specs = [pl.BlockSpec(memory_space=pl.ANY)] * len(arrays)
        self.out_shapes = [jax.ShapeDtypeStruct(a.shape[1:], F32) for a in arrays]
        self.out_specs = [pl.BlockSpec(memory_space=pltpu.VMEM)] * len(arrays)
        scratch = [pltpu.VMEM((chips,) + a.shape[1:], a.dtype) for a in arrays]
        scratch += [pltpu.VMEM((2 * AHEAD,) + a.shape[1:], a.dtype) for a in arrays]
        most = 0
        for a, _, width, order in items:
            n1, n2 = (grid.size[axis] for axis in order)
            shares = ((n1 - 1) * n2 * q_size, (n2 - 1) * q_size, q_size)
            most = max(most, shares[0] + shares[1])
            for share in shares:
                scratch.append(pltpu.VMEM((share, arrays[a].shape[1], width), arrays[a].dtype))
        self.scratch = scratch + [
            pltpu.SemaphoreType.DMA((len(arrays), chips)),
            pltpu.SemaphoreType.DMA((len(arrays), chips)),
            pltpu.SemaphoreType.DMA((len(arrays), chips)),
            pltpu.SemaphoreType.DMA((count, most)),
            pltpu.SemaphoreType.DMA((count, most)),
            pltpu.SemaphoreType.DMA((count, q_size)),
            pltpu.SemaphoreType.DMA((count, q_size)),
        ]

    def steps(self, at, ins, outs, scratch):
        grid, items = self.grid, self.items
        count, arrays = len(items), len(ins)
        held, crossed = scratch[:arrays], scratch[arrays : 2 * arrays]
        landing = scratch[2 * arrays : 2 * arrays + 3 * count]
        load_sem, core_send, core_recv, send_sem, recv_sem, line_send, line_recv = scratch[
            2 * arrays + 3 * count :
        ]
        sibling = {**at, "c": 1 - at["c"]}
        size = grid.size
        q_size = size["q"]

        def flat(block):
            p, r, t = block
            return (p * size["r"] + r) * q_size + t

        def owner(base, block):
            p, r, t = block
            return grid.number({**grid.shift(base, {"p": p, "r": r}), "q": t})

        targets = []
        for t in range(q_size // 2):
            targets += [t, q_size - 1 - t]
        near_blocks = []
        for t in targets:
            near = [(p, r, t) for p in range(size["p"]) for r in range(size["r"])]
            near_blocks += sorted(near, key=lambda b: -(b[0] > 0) - (b[1] > 0))
        blocks = [(n, block) for n in range(len(self.rounds)) for block in near_blocks]
        round_of = {a: n for n, members in enumerate(self.rounds) for a in members}

        def load(a, block):
            return pltpu.make_async_copy(
                ins[a].at[owner(at, block)], held[a].at[flat(block)], load_sem.at[a, flat(block)]
            )

        def crossed_at(a, block):
            return crossed[a].at[near_blocks.index(block) % (2 * AHEAD)]

        def across(a, block):
            return pltpu.make_async_remote_copy(
                src_ref=ins[a].at[owner(sibling, block)],
                dst_ref=crossed_at(a, block),
                send_sem=core_send.at[a, flat(block)],
                recv_sem=core_recv.at[a, flat(block)],
                device_id=grid.mesh_id(sibling),
                device_id_type=MESH_ID,
            )

        def begin(number):
            if number < len(blocks):
                n, block = blocks[number]
                for a in self.rounds[n]:
                    across(a, block).start()
                    load(a, block).start()

        merged = [0]

        def merge_to(n, block):
            while merged[0] <= blocks.index((n, block)):
                turn, now = blocks[merged[0]]
                for a in self.rounds[turn]:
                    load(a, now).wait()
                    across(a, now).wait_recv()
                    view = held[a].at[flat(now)]
                    add_rows(view, view, crossed_at(a, now))
                begin(merged[0] + AHEAD)
                merged[0] += 1

        def held_view(i, block):
            return held[items[i][0]].at[flat(block), :, pl.ds(items[i][1], items[i][2])]

        def block_at(i, first, second, t):
            part = dict(zip(items[i][3], (first, second)))
            return (part["p"], part["r"], t)

        def landing_slot(i, stage, steps, t):
            n2 = size[items[i][3][1]]
            if stage == 0:
                return ((steps[0] - 1) * n2 + steps[1]) * q_size + t
            return (steps[1] - 1) * q_size + t

        pending = []

        def send(i, stage, steps, t):
            n1, n2 = (size[axis] for axis in items[i][3])
            slot = landing_slot(i, stage, steps, t)
            sem = slot if stage == 0 else (n1 - 1) * n2 * q_size + slot
            return pltpu.make_async_remote_copy(
                src_ref=held_view(i, block_at(i, *steps, t)),
                dst_ref=landing[3 * i + stage].at[slot],
                send_sem=send_sem.at[i, sem],
                recv_sem=recv_sem.at[i, sem],
                device_id=grid.mesh_id(grid.shift(at, {items[i][3][stage]: steps[stage]})),
                device_id_type=MESH_ID,
            )

        def start(i, stage, steps, t):
            copy = send(i, stage, steps, t)
            copy.start()
            pending.append(copy)

        def receive(i, stage, steps, t):
            send(i, stage, steps, t).wait_recv()
            into = (0, steps[1]) if stage == 0 else (0, 0)
            view = held_view(i, block_at(i, *into, t))
            add_rows(view, view, landing[3 * i + stage].at[landing_slot(i, stage, steps, t)])

        def line(i, t):
            return pltpu.make_async_remote_copy(
                src_ref=held_view(i, (0, 0, t)),
                dst_ref=landing[3 * i + 2].at[at["q"]],
                send_sem=line_send.at[i, t],
                recv_sem=line_recv.at[i, at["q"]],
                device_id=grid.mesh_id({**at, "q": t}),
                device_id_type=MESH_ID,
            )

        def close(i, t):
            for second in range(1, size[items[i][3][1]]):
                receive(i, 1, (0, second), t)
            pl.when(at["q"] != t)(lambda: line(i, t).start())

        def finish(i):
            a, first, width, _ = items[i]
            parts = [held[a].at[at["q"], :, pl.ds(first, width)]]
            for step in range(1, q_size):
                source = lax.rem(at["q"] + step, q_size)
                view = landing[3 * i + 2].at[source]
                pltpu.make_async_copy(view, view, line_recv.at[i, source]).wait()
                parts.append(view)
            add_rows(outs[a].at[:, pl.ds(first, width)], *parts)

        ticks = []
        for n, members in enumerate(self.rounds):
            mine = [i for i in range(count) if items[i][0] in members]
            for t in targets:
                for far in (True, False):
                    turn = []
                    for i in mine:
                        n1, n2 = (size[axis] for axis in items[i][3])
                        for second in range(1, n2) if far else (0,):
                            for first in range(1, n1):
                                turn.append((i, (first, second), t))
                    ticks.append((n, turn, None if far else (mine, t)))
        yield sum(2 * len(turn) for _, turn, _ in ticks) + q_size * count + count

        for number in range(AHEAD):
            begin(number)
        closing, finishing = [], []
        for k in range(len(ticks) + DEPTH):
            if k < len(ticks):
                n, turn, _ = ticks[k]
                for i, steps, t in turn:
                    merge_to(n, block_at(i, *steps, t))
                    start(i, 0, steps, t)
                    yield
            if k >= DEPTH:
                n, turn, done = ticks[k - DEPTH]
                for i, steps, t in turn:
                    merge_to(n, block_at(i, 0, steps[1], t))
                    receive(i, 0, steps, t)
                    if steps[1] and steps[0] == size[items[i][3][0]] - 1:
                        start(i, 1, (0, steps[1]), t)
                    yield
                if closing and done is None:
                    for i in closing[0][0]:
                        close(i, closing[0][1])
                        yield
                    if closing[0][1] == targets[-1]:
                        finishing.append(closing[0][0])
                    closing.pop()
                    if len(finishing) > 1:
                        for i in finishing.pop(0):
                            finish(i)
                            yield
                if done is not None:
                    closing.append(done)
        for mine, t in closing:
            for i in mine:
                close(i, t)
                yield
            finishing.append(mine)
        for mine in finishing:
            for i in mine:
                finish(i)
                yield
        for n, block in blocks:
            for a in self.rounds[n]:
                across(a, block).wait_send()
        for copy in pending:
            copy.wait_send()
        for i in range(count):
            for t in range(q_size):
                pl.when(at["q"] != t)(lambda: line(i, t).wait_send())


def together(grid, parts, collective_id, name):
    def kernel(*refs):
        at = grid.here()
        if collective_id is not None:
            greet(grid, at)
        ins, outs, scratch = [], [], []
        for list_of, key in ((ins, "inputs"), (outs, "out_shapes"), (scratch, "scratch")):
            for part in parts:
                count = len(getattr(part, key))
                list_of.append(refs[:count])
                refs = refs[count:]
        running = []
        for part, *its in zip(parts, ins, outs, scratch):
            steps = part.steps(at, *its)
            running.append([steps, next(steps), 0])
        while running:
            now = min(running, key=lambda entry: entry[2] / entry[1])
            now[2] += 1
            if next(now[0], "end") == "end":
                running.remove(now)

    outs = pl.pallas_call(
        kernel,
        out_shape=[shape for part in parts for shape in part.out_shapes],
        in_specs=[spec for part in parts for spec in part.in_specs],
        out_specs=[spec for part in parts for spec in part.out_specs],
        scratch_shapes=[entry for part in parts for entry in part.scratch],
        compiler_params=pltpu.CompilerParams(
            collective_id=collective_id,
            has_side_effects=collective_id is not None,
            vmem_limit_bytes=62 * 2**20,
        ),
        name=name,
    )(*[array for part in parts for array in part.inputs])
    split = []
    for part in parts:
        split.append(outs[: len(part.out_shapes)])
        outs = outs[len(part.out_shapes) :]
    return split


GROUP = 256


def tiles(extent, width):
    def wrap(action):
        width_now = min(width, extent)

        @pl.loop(0, extent // width_now)
        def _(k):
            action(pl.ds(pl.multiple_of(k * width_now, width_now), width_now))

    return wrap


class Experts:
    def __init__(self, hidden, grad, share, weights, capacity):
        gate, up, down, shared_in, shared_down = weights
        count = hidden.shape[0]
        window = gate.shape[1]
        self.supers = count // (2 * GROUP)
        self.slots = GROUP // SEQ * capacity
        self.capacity = capacity
        self.window = window
        rows = 2 * self.slots
        total = self.supers * rows
        groups = count // GROUP
        self.inputs = [hidden, grad, share, gate, up, down, shared_in, shared_down]
        hbm = pl.BlockSpec(memory_space=pl.ANY)
        vmem = pl.BlockSpec(memory_space=pltpu.VMEM)
        self.in_specs = [hbm, hbm] + [vmem] * 6
        shared_width = shared_in.shape[1]
        kept = [(rows, D), (rows, D), (rows, 2 * window), (rows, window)]
        kept += [(2 * GROUP, shared_width), (2 * GROUP, shared_width // 2)]
        self.out_shapes = [
            jax.ShapeDtypeStruct((count, D), BF),
            jax.ShapeDtypeStruct((count, D), BF),
            jax.ShapeDtypeStruct((groups, GROUP), F32),
        ] + [jax.ShapeDtypeStruct((self.supers * r, c), BF) for r, c in kept]
        self.out_specs = [hbm, hbm, vmem] + [hbm] * len(kept)
        self.scratch = (
            [pltpu.VMEM((2 * GROUP, D), BF)] * 2
            + [pltpu.VMEM((2, r, c), BF) for r, c in kept]
            + [pltpu.VMEM((2, GROUP, D), BF)] * 2
            + [pltpu.VMEM((rows, window), F32)] * 3
            + [pltpu.VMEM((rows, D), BF)] * 2
            + [
                pltpu.VMEM((groups, GROUP), F32),
                pltpu.VMEM((2, self.slots, GROUP), BF),
                pltpu.VMEM((2, GROUP, self.slots), BF),
                pltpu.VMEM((rows, 1), F32),
                pltpu.VMEM((rows, 1), F32),
                pltpu.VMEM((2 * GROUP, shared_width), F32),
                pltpu.SemaphoreType.DMA((2,)),
                pltpu.SemaphoreType.DMA((len(kept), 2)),
                pltpu.SemaphoreType.DMA((2, 2)),
            ]
        )

    def steps(self, at, ins, outs, scratch):
        hidden, grad, share, gate, up, down, shared_in, shared_down = ins
        hidden_out, out_out, gate_grad = outs[:3]
        kept_out = outs[3:]
        hidden_in, grad_in = scratch[:2]
        kept = scratch[2:8]
        parts = scratch[8:10]
        a_pre, b_pre, flow = scratch[10:13]
        row_grad, expert_out = scratch[13:15]
        keys, picks, picks_t, share_rows, gate_rows, shared_pre = scratch[15:21]
        load_sem, keep_sem, part_sem = scratch[21:]
        slots, window, supers = self.slots, self.window, self.supers
        rows = 2 * slots
        half = shared_in.shape[1] // 2
        yield supers * 12

        def load(k):
            piece = pl.ds(k * 2 * GROUP, 2 * GROUP)
            return (
                pltpu.make_async_copy(hidden.at[piece, :], hidden_in, load_sem.at[0]),
                pltpu.make_async_copy(grad.at[piece, :], grad_in, load_sem.at[1]),
            )

        def keep(n, k):
            extent = kept[n].shape[1]
            return pltpu.make_async_copy(
                kept[n].at[k % 2],
                kept_out[n].at[pl.ds(k * extent, extent), :],
                keep_sem.at[n, k % 2],
            )

        def put(n, k, j):
            target = (hidden_out, out_out)[n]
            piece = pl.ds((2 * k + j) * GROUP, GROUP)
            return pltpu.make_async_copy(parts[n].at[j], target.at[piece, :], part_sem.at[n, j])

        for copy in load(0):
            copy.start()
        row_of = lax.broadcasted_iota(jnp.int32, (GROUP, GROUP), 0)
        column_of = lax.broadcasted_iota(jnp.int32, (GROUP, GROUP), 1)
        same = lax.div(row_of, SEQ) == lax.div(column_of, SEQ)
        earlier = jnp.logical_and(same, row_of < column_of).astype(BF)
        chosen = (share[...] >= 0).astype(F32)
        place = jnp.dot(chosen.astype(BF), earlier, preferred_element_type=F32)
        sequence = lax.div(lax.broadcasted_iota(jnp.int32, place.shape, 1), SEQ).astype(F32)
        keys[...] = jnp.where(chosen > 0, place + sequence * self.capacity, -1.0)

        for k in range(supers):
            slot = k % 2
            rows_in, grad_rows, ab_grad, scaled, shared_grad, shared_inner = (
                buffer.at[slot] for buffer in kept
            )
            if k >= 2:
                for n in range(len(kept)):
                    keep(n, k - 2).wait()
            for j in range(2):
                key = keys[pl.ds(2 * k + j, 1), :]
                number = lax.broadcasted_iota(jnp.int32, (slots, GROUP), 0).astype(F32)
                pick = (number == key).astype(F32)
                picks[j] = pick.astype(BF)
                picks_t[j] = pick.T.astype(BF)
                weight = share[pl.ds(2 * k + j, 1), :]
                share_rows[pl.ds(j * slots, slots), :] = jnp.sum(
                    pick * weight, axis=1, keepdims=True
                )
            for copy in load(k):
                copy.wait()
            for source, target in ((hidden_in, rows_in), (grad_in, grad_rows)):
                for j in range(2):

                    @tiles(D, 512)
                    def _(columns):
                        target[pl.ds(j * slots, slots), columns] = jnp.dot(
                            picks[j],
                            source[pl.ds(j * GROUP, GROUP), columns],
                            preferred_element_type=F32,
                        ).astype(BF)

                yield
            for weight, target in ((gate, a_pre), (up, b_pre)):

                @tiles(window, 256)
                def _(columns):
                    target[:, columns] = jnp.dot(
                        rows_in[...], weight[:, columns], preferred_element_type=F32
                    )

                yield

            @tiles(window, 256)
            def _(columns):
                flow[:, columns] = dot_t(grad_rows[...], down[columns, :])

            yield

            @tiles(rows, 32)
            def _(block):
                a = a_pre[block, :]
                b = b_pre[block, :]
                u = flow[block, :]
                weight = share_rows[block, :]
                sigma = jax.nn.sigmoid(a)
                act = a * sigma
                inner = (act * b).astype(BF).astype(F32)
                gate_rows[block, :] = jnp.sum(inner * u, axis=1, keepdims=True)
                scaled[block, :] = (inner * weight).astype(BF)
                u = u * weight
                ab_grad[block, pl.ds(0, window)] = (
                    u * b * (sigma * (1.0 + a * (1.0 - sigma)))
                ).astype(BF)
                ab_grad[block, pl.ds(window, window)] = (u * act).astype(BF)

            for j in range(2):
                pick = picks[j].astype(F32)
                gate_grad[pl.ds(2 * k + j, 1), :] = jnp.sum(
                    pick * gate_rows[pl.ds(j * slots, slots), :], axis=0, keepdims=True
                )
            yield

            @tiles(D, 256)
            def _(columns):
                row_grad[:, columns] = (
                    dot_t(ab_grad[:, pl.ds(0, window)], gate[columns, :])
                    + dot_t(ab_grad[:, pl.ds(window, window)], up[columns, :])
                ).astype(BF)

            yield

            @tiles(D, 512)
            def _(columns):
                expert_out[:, columns] = jnp.dot(
                    scaled[...], down[:, columns], preferred_element_type=F32
                ).astype(BF)

            yield

            @tiles(2 * GROUP, GROUP)
            def _(block):
                shared_pre[block, :] = jnp.dot(
                    hidden_in[block, :], shared_in[...], preferred_element_type=F32
                )

            yield

            @tiles(2 * GROUP, GROUP)
            def _(block):
                u = dot_t(grad_in[block, :], shared_down[...])
                a = shared_pre[block, pl.ds(0, half)]
                b = shared_pre[block, pl.ds(half, half)]
                sigma = jax.nn.sigmoid(a)
                act = a * sigma
                shared_inner[block, :] = (act * b).astype(BF)
                shared_grad[block, pl.ds(0, half)] = (
                    u * b * (sigma * (1.0 + a * (1.0 - sigma)))
                ).astype(BF)
                shared_grad[block, pl.ds(half, half)] = (u * act).astype(BF)

            for n in range(len(kept)):
                keep(n, k).start()
            if k + 1 < supers:
                for copy in load(k + 1):
                    copy.start()
            yield
            for j in range(2):
                if k:
                    put(0, k - 1, j).wait()

                @tiles(D, 256)
                def _(columns):
                    parts[0][j, :, columns] = (
                        jnp.dot(
                            picks_t[j],
                            row_grad[pl.ds(j * slots, slots), columns],
                            preferred_element_type=F32,
                        )
                        + dot_t(shared_grad[pl.ds(j * GROUP, GROUP), :], shared_in[columns, :])
                    ).astype(BF)

                put(0, k, j).start()
            yield
            for j in range(2):
                if k:
                    put(1, k - 1, j).wait()

                @tiles(D, 256)
                def _(columns):
                    parts[1][j, :, columns] = (
                        jnp.dot(
                            picks_t[j],
                            expert_out[pl.ds(j * slots, slots), columns],
                            preferred_element_type=F32,
                        )
                        + jnp.dot(
                            shared_inner[pl.ds(j * GROUP, GROUP), :],
                            shared_down[:, columns],
                            preferred_element_type=F32,
                        )
                    ).astype(BF)

                put(1, k, j).start()
            yield
        for k in range(max(0, supers - 2), supers):
            for n in range(len(kept)):
                keep(n, k).wait()
        for n in range(2):
            for j in range(2):
                put(n, supers - 1, j).wait()


def gather_all(grid, arrays, items, collective_id):
    return together(grid, [Gather(grid, arrays, items)], collective_id, "gather_all")[0]


def sum_scattered(grid, arrays, items, rounds, collective_id):
    part = Scatter(grid, arrays, items, rounds)
    return together(grid, [part], collective_id, "sum_scattered")[0]


def normalize(values, gain_row):
    scale_rows = lax.rsqrt(jnp.mean(values * values, -1, keepdims=True) + EPSILON)
    return (values * scale_rows * gain_row, scale_rows)


def normalize_back(values, scale_rows, gain_row, gradient):
    weighted = gradient * gain_row
    gain_grad = jnp.sum(gradient * values * scale_rows, 0)
    inner_mean = jnp.mean(weighted * values, -1, keepdims=True)
    return (
        scale_rows * weighted - values * scale_rows * scale_rows * scale_rows * inner_mean,
        gain_grad,
    )


def rope_tables(length, width):
    half_width = width // 2
    frequency = ROPE_BASE ** (-2.0 * jnp.arange(half_width, dtype=jnp.float32) / width)
    angles = jnp.arange(length, dtype=jnp.float32)[:, None] * frequency[None, :]
    return (jnp.cos(angles), jnp.sin(angles))


def rotate(values, cosine, sine_table):
    half_width = values.shape[-1] // 2
    front_half = values[..., :half_width]
    back_half = values[..., half_width:]
    return jnp.concatenate(
        [
            front_half * cosine - back_half * sine_table,
            back_half * cosine + front_half * sine_table,
        ],
        -1,
    )


def unrotate(gradient, cosine, sine_table):
    half_width = gradient.shape[-1] // 2
    front_half = gradient[..., :half_width]
    back_half = gradient[..., half_width:]
    return jnp.concatenate(
        [
            front_half * cosine + back_half * sine_table,
            back_half * cosine - front_half * sine_table,
        ],
        -1,
    )


def capacity_for(expert_count):
    return min(SEQ, ((4 * SEQ * TOP + 3 * expert_count - 1) // (3 * expert_count) + 7) // 8 * 8)


def silu_parts(pre_act):
    sigma_rows = jax.nn.sigmoid(pre_act)
    return (pre_act * sigma_rows, sigma_rows * (1.0 + pre_act * (1.0 - sigma_rows)))


def attention_mask(segment_row):
    places = jnp.arange(segment_row.shape[0], dtype=jnp.int32)
    return (places[:, None] >= places[None, :]) & (segment_row[:, None] == segment_row[None, :])


def dot(left, right):
    return jnp.dot(left, right, preferred_element_type=F32)


def dot_t(left, right):
    return lax.dot_general(left, right, (((1,), (1,)), ((), ())), preferred_element_type=F32)


def t_dot(left, right):
    return lax.dot_general(left, right, (((0,), (0,)), ((), ())), preferred_element_type=F32)


def pack(parts, rows):
    flat = jnp.concatenate([part.reshape(rows, -1) for part in parts], 1)
    width = -(-flat.shape[1] // 2048) * 2048
    flat = jnp.pad(flat, ((0, 0), (0, width - flat.shape[1])))
    return flat.reshape(rows, width // 128, 128)


def unpack(block, shapes):
    rows = block.shape[0]
    flat = block.reshape(rows, -1)
    parts, first = [], 0
    for shape in shapes:
        size = 1
        for extent in shape:
            size *= extent
        parts.append(flat[:, first : first + size].reshape((rows,) + shape))
        first += size
    return parts


def swap_windows(pieces, axis_size):
    me = lax.axis_index("dp")
    got = [pieces(me)]
    for step in range(1, axis_size):
        peer = lax.rem(me + step, axis_size)
        perm = [(k, (k + step) % axis_size) for k in range(axis_size)]
        got.append(lax.ppermute(pieces(peer), "dp", perm))
    return got


def in_order(got):
    me = lax.axis_index("dp")
    count = len(got)
    ordered = []
    for k in range(count):
        value = got[0]
        for step in range(1, count):
            value = jnp.where(lax.rem(me - k + count, count) == step, got[step], value)
        ordered.append(value)
    return ordered


def attention_forward(rows, segments, weights, tables):
    attn_gain, q_weight, kv_down, kv_gain, kv_up, out_weight, ffn_gain, router = weights
    cosine, sine_table = tables
    count = rows.shape[0]
    inputs = rows.astype(F32)
    normed_f, scale_one = normalize(inputs, attn_gain)
    normed = normed_f.astype(BF)
    q_raw = dot(normed, q_weight).reshape(MICRO, SEQ, HEADS, NOPE + ROPE)
    turn = (cosine[:, None, :], sine_table[:, None, :])
    queries = jnp.concatenate([q_raw[..., :NOPE], rotate(q_raw[..., NOPE:], *turn)], -1).astype(BF)
    kv_raw = dot(normed, kv_down)
    latent_f, scale_latent = normalize(kv_raw[:, :RANK], kv_gain)
    latent = latent_f.astype(BF)
    key_rope = rotate(kv_raw[:, RANK:].reshape(MICRO, SEQ, ROPE), cosine, sine_table)
    kv_full = dot(latent, kv_up).reshape(MICRO, SEQ, HEADS, NOPE + VDIM)
    shared_key = jnp.broadcast_to(key_rope[:, :, None, :], (MICRO, SEQ, HEADS, ROPE))
    key_rows = jnp.concatenate([kv_full[..., :NOPE], shared_key], -1).astype(BF)
    value_rows = kv_full[..., NOPE:].astype(BF)
    allowed = jax.vmap(attention_mask)(segments)[:, None]
    scores = jnp.einsum("mqhe,mkhe->mhqk", queries, key_rows, preferred_element_type=F32)
    scores = jnp.where(allowed, scores * (NOPE + ROPE) ** (-0.5), MASKED)
    powers = jnp.exp(scores - jnp.max(scores, -1, keepdims=True))
    softmax_rows = powers / jnp.sum(powers, -1, keepdims=True)
    probability = softmax_rows.astype(BF)
    attended = (
        jnp.einsum("mhqk,mkhe->mqhe", probability, value_rows, preferred_element_type=F32)
        .reshape(count, HEADS * VDIM)
        .astype(BF)
    )
    residual = inputs + dot(attended, out_weight)
    hidden_f, scale_two = normalize(residual, ffn_gain)
    hidden = hidden_f.astype(BF)
    saved = (
        inputs, scale_one, normed, queries, kv_raw, scale_latent, latent, key_rows, value_rows,
        softmax_rows, probability, attended, residual, scale_two,
    )
    return hidden, saved


def attention_backward(grad_out, hidden_grad, saved, weights, tables):
    attn_gain, q_weight, kv_down, kv_gain, kv_up, out_weight, ffn_gain, router = weights
    cosine, sine_table = tables
    (
        inputs, scale_one, normed, queries, kv_raw, scale_latent, latent, key_rows, value_rows,
        softmax_rows, probability, attended, residual, scale_two,
    ) = saved
    count = inputs.shape[0]
    turn = (cosine[:, None, :], sine_table[:, None, :])
    residual_part, ffn_gain_grad = normalize_back(residual, scale_two, ffn_gain, hidden_grad)
    residual_grad = grad_out + residual_part
    mixed_grad = residual_grad.astype(BF)
    out_weight_grad = t_dot(attended, mixed_grad)
    attended_grad = dot_t(mixed_grad, out_weight).astype(BF).reshape(MICRO, SEQ, HEADS, VDIM)
    value_grad = jnp.einsum(
        "mhqk,mqhe->mkhe", probability, attended_grad, preferred_element_type=F32
    )
    probs_grad = jnp.einsum(
        "mqhe,mkhe->mhqk", attended_grad, value_rows, preferred_element_type=F32
    )
    inner = jnp.sum(softmax_rows * probs_grad, -1, keepdims=True)
    score_grad = (softmax_rows * (probs_grad - inner)).astype(BF)
    score_scale = (NOPE + ROPE) ** (-0.5)
    query_grad = score_scale * jnp.einsum(
        "mhqk,mkhe->mqhe", score_grad, key_rows, preferred_element_type=F32
    )
    keys_grad = score_scale * jnp.einsum(
        "mhqk,mqhe->mkhe", score_grad, queries, preferred_element_type=F32
    )
    q_raw_grad = (
        jnp.concatenate([query_grad[..., :NOPE], unrotate(query_grad[..., NOPE:], *turn)], -1)
        .reshape(count, HEADS * (NOPE + ROPE))
        .astype(BF)
    )
    q_weight_grad = t_dot(normed, q_raw_grad)
    kv_full_grad = (
        jnp.concatenate([keys_grad[..., :NOPE], value_grad], -1)
        .reshape(count, HEADS * (NOPE + VDIM))
        .astype(BF)
    )
    kv_up_grad = t_dot(latent, kv_full_grad)
    latent_grad = dot_t(kv_full_grad, kv_up)
    latent_part, kv_gain_grad = normalize_back(
        kv_raw[:, :RANK], scale_latent, kv_gain, latent_grad
    )
    rope_grad = unrotate(jnp.sum(keys_grad[..., NOPE:], 2), cosine, sine_table)
    kv_raw_grad = jnp.concatenate([latent_part, rope_grad.reshape(count, ROPE)], -1).astype(BF)
    kv_down_grad = t_dot(normed, kv_raw_grad)
    normed_grad = dot_t(q_raw_grad, q_weight) + dot_t(kv_raw_grad, kv_down)
    input_part, attn_gain_grad = normalize_back(inputs, scale_one, attn_gain, normed_grad)
    tokens_grad = residual_grad + input_part
    return tokens_grad, (
        attn_gain_grad, q_weight_grad, kv_down_grad, kv_gain_grad, kv_up_grad, out_weight_grad,
        ffn_gain_grad,
    )


def body(
    grid,
    tokens,
    cotangent,
    routes,
    segments,
    attn_gain,
    q_weight,
    kv_down,
    kv_gain,
    kv_up,
    out_weight,
    ffn_gain,
    router,
    shared_gate,
    shared_up,
    shared_down,
    expert_gate,
    expert_up,
    expert_down,
):
    devices = grid.devices
    dp_size = grid.size["p"]
    experts = router.shape[1]
    tables = rope_tables(SEQ, ROPE)
    me_dp = lax.axis_index("dp")
    count = MICRO * SEQ
    eff = expert_gate.shape[2]

    window = -(-eff // (128 * dp_size)) * 128
    starts = [min(k * window, eff - window) for k in range(dp_size)]

    def start_of(peer):
        return jnp.minimum(peer * window, eff - window)

    def columns_for(array):
        return lambda peer: lax.dynamic_slice_in_dim(array[0], start_of(peer), window, 1)

    def rows_for(array):
        return lambda peer: lax.dynamic_slice_in_dim(array[0], start_of(peer), window, 0)

    gate_part = jnp.concatenate(in_order(swap_windows(columns_for(expert_gate), dp_size)), 0)
    up_part = jnp.concatenate(in_order(swap_windows(columns_for(expert_up), dp_size)), 0)
    down_part = jnp.concatenate(in_order(swap_windows(rows_for(expert_down), dp_size)), 1)
    fresh = jnp.arange(window, dtype=jnp.int32) + start_of(me_dp) >= me_dp * window
    gate_part = jnp.where(fresh[None, :], gate_part, 0)
    up_part = jnp.where(fresh[None, :], up_part, 0)
    down_part = jnp.where(fresh[:, None], down_part, 0)

    share = shared_gate.shape[1] // devices
    both = jnp.concatenate(
        [shared_gate.reshape(-1, devices, share), shared_up.reshape(-1, devices, share)], 2
    )
    shared_in = lax.all_to_all(
        both.transpose(1, 0, 2), ("dp", "expert"), split_axis=0, concat_axis=0, tiled=True
    ).reshape(D, 2 * share)
    room = -(-share // 128) * 128
    shared_in = jnp.concatenate(
        [
            jnp.pad(shared_in[:, :share], ((0, 0), (0, room - share))),
            jnp.pad(shared_in[:, share:], ((0, 0), (0, room - share))),
        ],
        1,
    )
    shared_part = jnp.pad(shared_down, ((0, room - share), (0, 0)))

    small_shapes = (attn_gain.shape, ffn_gain.shape, kv_gain.shape, router.shape)
    small = pack([attn_gain[None], ffn_gain[None], kv_gain[None], router[None]], 1)[0]
    up_shape = kv_up.shape
    kv_up_sent = kv_up if up_shape[0] % 16 == 0 else kv_up.reshape(16, -1)
    first, second = ("q", "r", "p"), ("q", "p", "r")
    got = gather_all(
        grid,
        [q_weight, kv_down, kv_up_sent, out_weight, small],
        [
            (0, 0, q_weight.shape[1], first),
            (3, 0, out_weight.shape[1], second),
            (2, 0, kv_up_sent.shape[1], second),
            (1, 0, kv_down.shape[1], second),
            (4, 0, 128, first),
        ],
        0,
    )
    gains = unpack(got[4], small_shapes)
    weights = (
        gains[0].reshape(-1).astype(F32),
        got[0].reshape(D, -1),
        got[1].reshape(D, -1),
        gains[2].reshape(-1).astype(F32),
        got[2].reshape(RANK, -1),
        got[3].reshape(-1, D),
        gains[1].reshape(-1).astype(F32),
        gains[3].reshape(D, experts),
    )
    router_full = weights[7]

    token_rows = tokens.reshape(count, D)
    grad_out = cotangent.reshape(count, D)
    route_rows = routes.reshape(count, TOP)
    hidden, saved = attention_forward(token_rows, segments.reshape(MICRO, SEQ), weights, tables)
    logits = dot(hidden, router_full)
    choose = route_rows[:, :, None] == jnp.arange(experts, dtype=jnp.int32)[None, None, :]
    choose = choose.astype(F32)
    gate_share = jax.nn.softmax(jnp.sum(choose * logits[:, None, :], -1), -1)
    dense_share = jnp.sum(choose * gate_share[..., None], 1)
    dense_gates = jnp.where(jnp.sum(choose, 1) > 0, dense_share, -1.0)

    half = D // 2
    capacity = capacity_for(experts)
    expert = lax.axis_index("expert")
    own_weights = (gate_part, up_part, down_part, shared_in, shared_part)

    def gather_of(chunk):
        piece = slice(chunk * SEQ, (chunk + 1) * SEQ)
        sent = [hidden[piece], grad_out[piece], dense_gates[piece].T]
        orders = [(0, 0, half, first), (0, half, half, second)]
        orders += [(1, 0, half, first), (1, half, half, second), (2, 0, SEQ, first)]
        return Gather(grid, sent, orders)

    kept_hidden, kept_grad = [], []

    def experts_of(gathered):
        hidden_all, grad_all, gates_all = gathered
        kept_hidden.append(hidden_all)
        kept_grad.append(grad_all)
        share = lax.dynamic_index_in_dim(gates_all, expert, 1, keepdims=False)
        return Experts(
            hidden_all.reshape(-1, D),
            grad_all.reshape(-1, D),
            share.reshape(-1, GROUP),
            own_weights,
            capacity,
        )

    def sums_of(done):
        hidden_part, out_part, gate_grad = done[:3]
        mine = (jnp.arange(experts, dtype=jnp.int32) == expert)[None, :, None]
        gate_grad = jnp.where(mine, gate_grad.reshape(devices, 1, SEQ), 0.0)
        shape = (devices, SEQ, D)
        return [hidden_part.reshape(shape), gate_grad, out_part.reshape(shape)]

    over = [(0, 0, half, ("p", "r")), (0, half, half, ("r", "p"))]
    over_gates = [(1, 0, SEQ, ("p", "r"))]
    over_out = [(2, 0, half, ("p", "r")), (2, half, half, ("r", "p"))]
    if devices <= 32:
        (gathered,) = together(grid, [gather_of(0)], 1, "gather_first")
        gathered, done_0 = together(
            grid, [gather_of(1), experts_of(gathered)], 2, "gather_second_experts_first"
        )
        everything = over + over_gates + over_out
        sums_0, done_1 = together(
            grid,
            [Scatter(grid, sums_of(done_0), everything, [[0, 1], [2]]), experts_of(gathered)],
            3,
            "scatter_first_experts_second",
        )
        (sums_1,) = together(
            grid, [Scatter(grid, sums_of(done_1), everything, [[0, 1], [2]])], 4, "scatter_second"
        )
        sums, done = (sums_0, sums_1), (done_0, done_1)
    else:
        sums, done = [], []
        for chunk in range(MICRO):
            part = gather_of(chunk)
            if chunk:
                before = tuple(sums[-1])
                *part.inputs, sums[-1] = lax.optimization_barrier((*part.inputs, before))
            (gathered,) = together(grid, [part], 1, "gather")
            part = experts_of(gathered)
            (now,) = together(grid, [part], None, "experts")
            parts = sums_of(now)
            (hidden_gates,) = together(
                grid, [Scatter(grid, parts[:2], over + over_gates, [[0, 1]])], 2, "scatter_hidden"
            )
            (out_sum,) = together(grid, [Scatter(grid, parts[2:], over, [[0]])], 3, "scatter_out")
            sums.append((*hidden_gates, *out_sum))
            done.append(now)
    hidden_sum = jnp.concatenate([entry[0] for entry in sums], 0)
    gate_grad = jnp.concatenate([entry[1].T for entry in sums], 0)
    result = saved[12] + jnp.concatenate([entry[2] for entry in sums], 0)

    dense_share = jnp.maximum(dense_share, 0.0)
    inner = jnp.sum(dense_share * gate_grad, -1, keepdims=True)
    logit_grad = (dense_share * (gate_grad - inner)).astype(BF)
    router_grad = t_dot(hidden, logit_grad)
    hidden_grad = hidden_sum + dot_t(logit_grad, router_full)
    tokens_grad, (
        attn_gain_grad, q_weight_grad, kv_down_grad, kv_gain_grad, kv_up_grad, out_weight_grad,
        ffn_gain_grad,
    ) = attention_backward(grad_out.astype(F32), hidden_grad, saved, weights, tables)

    small_grads = pack(
        [
            attn_gain_grad.reshape(devices, -1),
            ffn_gain_grad.reshape(devices, -1),
            kv_gain_grad.reshape(devices, -1),
            router_grad.reshape(devices, -1),
        ],
        devices,
    )
    def halves(a, columns):
        part = columns // 256 * 128
        return [(a, 0, part, ("p", "r")), (a, part, columns - part, ("r", "p"))]

    q_sum, down_sum, up_sum, out_weight_sum, small_sum = sum_scattered(
        grid,
        [
            q_weight_grad.astype(BF).reshape((devices,) + q_weight.shape),
            kv_down_grad.astype(BF).reshape((devices,) + kv_down.shape),
            kv_up_grad.astype(BF).reshape((devices,) + kv_up_sent.shape),
            out_weight_grad.astype(BF).reshape((devices,) + out_weight.shape),
            small_grads,
        ],
        halves(0, q_weight.shape[1])
        + halves(1, kv_down.shape[1])
        + halves(2, kv_up_sent.shape[1])
        + halves(3, out_weight.shape[1])
        + [(4, 0, 128, ("p", "r"))],
        [[3], [2, 1], [0, 4]],
        5,
    )
    small_sums = unpack(small_sum[None], small_shapes)

    def total(pairs):
        return functools.reduce(jnp.add, [t_dot(left, right) for left, right in pairs])

    kept = [entry[3:] for entry in done]
    chunks = range(MICRO)
    both_grad = total([(kept[c][0], kept[c][2]) for c in chunks])
    gate_grad_part, up_grad_part = both_grad[:, :window], both_grad[:, window:]
    down_grad_part = total([(kept[c][3], kept[c][1]) for c in chunks])
    hidden_rows = [kept_hidden[c].reshape(-1, D) for c in chunks]
    grad_rows = [kept_grad[c].reshape(-1, D) for c in chunks]
    shared_in_grad = total([(hidden_rows[c], kept[c][4]) for c in chunks])
    shared_down_grad = total([(kept[c][5], grad_rows[c]) for c in chunks])[:share]
    shared_in_grad = jnp.concatenate(
        [shared_in_grad[:, :share], shared_in_grad[:, room : room + share]], 1
    )
    shared_back = lax.all_to_all(
        shared_in_grad.astype(BF).reshape(devices, -1, 2 * share),
        ("dp", "expert"), split_axis=0, concat_axis=0, tiled=True,
    ).astype(F32)
    shared_back = shared_back.transpose(1, 0, 2)
    shared_gate_grad = shared_back[:, :, :share].reshape(shared_gate.shape)
    shared_up_grad = shared_back[:, :, share:].reshape(shared_up.shape)

    def whole(part, axis, other, extent):
        def for_peer(peer):
            return lax.dynamic_slice_in_dim(part, peer * extent, extent, other)

        got_back = swap_windows(lambda peer: for_peer(peer).astype(BF), dp_size)
        got_back = [for_peer(me_dp)] + [piece.astype(F32) for piece in got_back[1:]]
        pieces = []
        for k, piece in enumerate(in_order(got_back)):
            skip = k * window - starts[k]
            pieces.append(lax.slice_in_dim(piece, skip, window, axis=axis))
        return jnp.concatenate(pieces, axis)[None]

    extent = expert_gate.shape[1]
    return (
        result.astype(BF).reshape(tokens.shape),
        tokens_grad.astype(BF).reshape(tokens.shape),
        small_sums[0].reshape(-1),
        q_sum,
        down_sum,
        small_sums[2].reshape(-1),
        up_sum.reshape(up_shape),
        out_weight_sum,
        small_sums[1].reshape(-1),
        small_sums[3].reshape(router.shape),
        shared_gate_grad,
        shared_up_grad,
        shared_down_grad,
        whole(gate_grad_part, 1, 0, extent),
        whole(up_grad_part, 1, 0, extent),
        whole(down_grad_part, 0, 1, extent),
    )


def solution(mesh):
    return jax.shard_map(
        functools.partial(body, Grid(mesh)),
        mesh=mesh,
        in_specs=(
            P(None, ("dp", "expert"), None, None),
            P(None, ("dp", "expert"), None, None),
            P(None, ("dp", "expert"), None, None),
            P(None, ("dp", "expert"), None),
            P(("dp", "expert")),
            P(("dp", "expert"), None),
            P(("dp", "expert"), None),
            P(("dp", "expert")),
            P(("dp", "expert"), None),
            P(("dp", "expert"), None),
            P(("dp", "expert")),
            P(("dp", "expert"), None),
            P(("dp", "expert"), None),
            P(("dp", "expert"), None),
            P(("dp", "expert"), None),
            P("expert", "dp", None),
            P("expert", "dp", None),
            P("expert", None, "dp"),
        ),
        out_specs=(
            P(None, ("dp", "expert"), None, None),
            P(None, ("dp", "expert"), None, None),
            P(("dp", "expert")),
            P(("dp", "expert"), None),
            P(("dp", "expert"), None),
            P(("dp", "expert")),
            P(("dp", "expert"), None),
            P(("dp", "expert"), None),
            P(("dp", "expert")),
            P(("dp", "expert"), None),
            P(("dp", "expert"), None),
            P(("dp", "expert"), None),
            P(("dp", "expert"), None),
            P("expert", "dp", None),
            P("expert", "dp", None),
            P("expert", None, "dp"),
        ),
        check_vma=False,
    )
```

```python
import functools

import jax
import jax.numpy as jnp
import numpy as np
from jax import lax
from jax.experimental import pallas as pl
from jax.experimental.pallas import tpu as pltpu
from jax.sharding import PartitionSpec as P

D = 2048
HEADS = 16
NOPE = 128
ROPE = 64
VDIM = 128
RANK = 512
TOP = 6
SEQ = 64
MICRO = 2

EPSILON = 1e-06
ROPE_BASE = 10000.0
MASKED = -1e30
BF = jnp.bfloat16
F32 = jnp.float32

MESH_ID = pl.DeviceIdType.MESH


class Grid:
    def __init__(self, mesh):
        self.experts = mesh.shape["expert"]
        self.size = {"p": mesh.shape["dp"], "r": self.experts // 8, "q": 4}
        self.devices = self.size["p"] * self.experts

    def here(self):
        e = lax.axis_index("expert")
        r_size = self.size["r"]
        return {
            "p": lax.axis_index("dp"),
            "q": lax.div(e, 2 * r_size),
            "r": lax.rem(lax.div(e, 2), r_size),
            "c": lax.rem(e, 2),
        }

    def shift(self, at, offsets):
        moved = dict(at)
        for axis, step in offsets.items():
            if step:
                moved[axis] = lax.rem(at[axis] + step, self.size[axis])
        return moved

    def expert_of(self, at):
        return at["q"] * (2 * self.size["r"]) + at["r"] * 2 + at["c"]

    def number(self, at):
        return at["p"] * self.experts + self.expert_of(at)

    def mesh_id(self, at):
        return (at["p"], self.expert_of(at))

    def partners(self, at):
        found = [{**at, "c": 1 - at["c"]}]
        for axis, size in self.size.items():
            found += [self.shift(at, {axis: step}) for step in range(1, size)]
        return found


def greet(grid, at):
    barrier = pltpu.get_barrier_semaphore()
    partners = grid.partners(at)
    for partner in partners:
        pl.semaphore_signal(barrier, inc=1, device_id=grid.mesh_id(partner), device_id_type=MESH_ID)
    pl.semaphore_wait(barrier, len(partners))


ALONG = (0, -1, 1, -2, 2, -3, 3)


def span_of(grid, axis):
    return ALONG if axis == "q" else tuple(range(grid.size[axis]))


class Gather:
    def __init__(self, grid, arrays, items):
        count = len(items)
        slots = grid.devices // 2 // 4 * len(ALONG)
        self.grid, self.items = grid, items
        self.inputs = list(arrays)
        self.in_specs = [pl.BlockSpec(memory_space=pl.ANY)] * len(arrays)
        self.out_shapes = [
            jax.ShapeDtypeStruct((grid.devices,) + a.shape, a.dtype) for a in arrays
        ]
        self.out_specs = [pl.BlockSpec(memory_space=pl.ANY)] * len(arrays)
        self.scratch = [
            pltpu.SemaphoreType.DMA((count * slots * 2,)),
            pltpu.SemaphoreType.DMA((count, slots)),
            pltpu.SemaphoreType.DMA((count, slots)),
            pltpu.SemaphoreType.DMA((count, slots)),
            pltpu.SemaphoreType.DMA((len(arrays),)),
        ]

    def steps(self, at, ins, outs, scratch):
        grid, items = self.grid, self.items
        count = len(items)
        send_sem, recv_sem, core_send, core_recv, own_sem = scratch
        sibling = {**at, "c": 1 - at["c"]}
        q_size = grid.size["q"]
        pending = []
        me = grid.number(at)

        def inside(step):
            return jnp.logical_and(at["q"] + step >= 0, at["q"] + step < q_size)

        def guarded(step, action):
            if step:
                pl.when(inside(step))(action)
            else:
                action()

        def q_part(i, offset):
            return offset[items[i][3].index("q")]

        def slot(i, offset):
            number = 0
            for axis, part in zip(items[i][3], offset):
                span = span_of(grid, axis)
                number = number * len(span) + span.index(part)
            return number

        def block_of(i, offset, base):
            moved = dict(base)
            for axis, part in zip(items[i][3], offset):
                if part:
                    moved[axis] = (
                        base[axis] + part
                        if axis == "q"
                        else lax.rem(base[axis] + part, grid.size[axis])
                    )
            return grid.number(moved)

        def views(i, offset, base):
            a, first, width, order = items[i]
            columns = pl.ds(first, width)
            view = outs[a].at[block_of(i, offset, base), :, columns]
            return (ins[a].at[:, columns] if offset == (0, 0, 0) else view), view

        def send(i, offset, landed, target_step, cond_step):
            number = len(pending)

            def copy():
                source, view = views(i, offset, at)
                return pltpu.make_async_remote_copy(
                    src_ref=source,
                    dst_ref=view,
                    send_sem=send_sem.at[number],
                    recv_sem=recv_sem.at[i, slot(i, landed)],
                    device_id=grid.mesh_id(target_step()),
                    device_id_type=MESH_ID,
                )

            guarded(cond_step, lambda: copy().start())
            pending.append((q_part(i, offset), cond_step, copy))

        def forward(i, offset, stage):
            axis = items[i][3][stage]
            if axis == "q":
                part = offset[stage]
                for step in (1, -1) if part == 0 else (1,) if part < 0 else (-1,):
                    if abs(part - step) < q_size:
                        landed = offset[:stage] + (part - step,) + offset[stage + 1 :]
                        send(
                            i, offset, landed, lambda step=step: {**at, "q": at["q"] + step}, step
                        )
                return
            for step in range(1, grid.size[axis]):
                part = (offset[stage] - step) % grid.size[axis]
                landed = offset[:stage] + (part,) + offset[stage + 1 :]
                send(i, offset, landed, lambda step=step: grid.shift(at, {axis: step}), 0)

        def across(i, offset):
            def copy():
                source, view = views(i, offset, at)
                return pltpu.make_async_remote_copy(
                    src_ref=source,
                    dst_ref=view,
                    send_sem=core_send.at[i, slot(i, offset)],
                    recv_sem=core_recv.at[i, slot(i, offset)],
                    device_id=grid.mesh_id(sibling),
                    device_id_type=MESH_ID,
                )

            copy().start()
            pending.append((q_part(i, offset), 0, copy))

        def landed_at(i, offset, base, sem):
            view = views(i, offset, base)[1]
            pltpu.make_async_copy(view, view, sem.at[i, slot(i, offset)]).wait()

        def take(i, offset, stage):
            def action():
                landed_at(i, offset, at, recv_sem)
                if items[i][3][stage] == "q":
                    forward(i, offset, stage)
                for later in range(stage + 1, 3):
                    forward(i, offset, later)
                across(i, offset)

            guarded(q_part(i, offset), action)

        ranges = [[span_of(grid, axis) for axis in item[3]] for item in items]
        offsets = [
            (i, (u, v, w))
            for i in range(count)
            for u in ranges[i][0]
            for v in ranges[i][1]
            for w in ranges[i][2]
        ]
        todo = []
        for i, offset in offsets:
            if any(offset):
                stage = max(k for k in range(3) if offset[k])
                todo.append((stage,) + tuple(abs(part) for part in offset) + (i, offset))
        yield len(todo) + 1

        own_copies = []
        for a in range(len(ins)):
            own = pltpu.make_async_copy(ins[a], outs[a].at[me], own_sem.at[a])
            own.start()
            own_copies.append(own)
        for i in range(count):
            for stage in range(3):
                forward(i, (0, 0, 0), stage)
            across(i, (0, 0, 0))
        yield
        for stage, _, _, _, i, offset in sorted(todo):
            take(i, offset, stage)
            yield
        for own in own_copies:
            own.wait()
        for i, offset in offsets:
            guarded(
                q_part(i, offset), functools.partial(landed_at, i, offset, sibling, core_recv)
            )
        for q_step, cond_step, copy in pending:
            guarded(q_step, functools.partial(guarded, cond_step, lambda: copy().wait_send()))


def add_rows(target, *parts):
    rows = target.shape[0]
    step = min(16, rows)

    @pl.loop(0, rows // step)
    def _(k):
        block = pl.ds(pl.multiple_of(k * step, step), step)
        total = parts[0][block, :].astype(F32)
        for part in parts[1:]:
            total = total + part[block, :].astype(F32)
        target[block, :] = total.astype(target.dtype)


DEPTH = 2
AHEAD = 4


class Scatter:
    def __init__(self, grid, arrays, items, rounds):
        count = len(items)
        chips = grid.devices // 2
        q_size = grid.size["q"]
        self.grid, self.items, self.rounds = grid, items, rounds
        self.inputs = list(arrays)
        self.in_specs = [pl.BlockSpec(memory_space=pl.ANY)] * len(arrays)
        self.out_shapes = [jax.ShapeDtypeStruct(a.shape[1:], F32) for a in arrays]
        self.out_specs = [pl.BlockSpec(memory_space=pltpu.VMEM)] * len(arrays)
        scratch = [pltpu.VMEM((chips,) + a.shape[1:], a.dtype) for a in arrays]
        scratch += [pltpu.VMEM((2 * AHEAD,) + a.shape[1:], a.dtype) for a in arrays]
        most = 0
        for a, _, width, order in items:
            n1, n2 = (grid.size[axis] for axis in order)
            shares = ((n1 - 1) * n2 * q_size, (n2 - 1) * q_size, q_size)
            most = max(most, shares[0] + shares[1])
            for share in shares:
                scratch.append(pltpu.VMEM((share, arrays[a].shape[1], width), arrays[a].dtype))
        self.scratch = scratch + [
            pltpu.SemaphoreType.DMA((len(arrays), chips)),
            pltpu.SemaphoreType.DMA((len(arrays), chips)),
            pltpu.SemaphoreType.DMA((len(arrays), chips)),
            pltpu.SemaphoreType.DMA((count, most)),
            pltpu.SemaphoreType.DMA((count, most)),
            pltpu.SemaphoreType.DMA((count, q_size)),
            pltpu.SemaphoreType.DMA((count, q_size)),
        ]

    def steps(self, at, ins, outs, scratch):
        grid, items = self.grid, self.items
        count, arrays = len(items), len(ins)
        held, crossed = scratch[:arrays], scratch[arrays : 2 * arrays]
        landing = scratch[2 * arrays : 2 * arrays + 3 * count]
        load_sem, core_send, core_recv, send_sem, recv_sem, line_send, line_recv = scratch[
            2 * arrays + 3 * count :
        ]
        sibling = {**at, "c": 1 - at["c"]}
        size = grid.size
        q_size = size["q"]

        def flat(block):
            p, r, t = block
            return (p * size["r"] + r) * q_size + t

        def owner(base, block):
            p, r, t = block
            return grid.number({**grid.shift(base, {"p": p, "r": r}), "q": t})

        targets = []
        for t in range(q_size // 2):
            targets += [t, q_size - 1 - t]
        near_blocks = []
        for t in targets:
            near = [(p, r, t) for p in range(size["p"]) for r in range(size["r"])]
            near_blocks += sorted(near, key=lambda b: -(b[0] > 0) - (b[1] > 0))
        blocks = [(n, block) for n in range(len(self.rounds)) for block in near_blocks]
        round_of = {a: n for n, members in enumerate(self.rounds) for a in members}

        def load(a, block):
            return pltpu.make_async_copy(
                ins[a].at[owner(at, block)], held[a].at[flat(block)], load_sem.at[a, flat(block)]
            )

        def crossed_at(a, block):
            return crossed[a].at[near_blocks.index(block) % (2 * AHEAD)]

        def across(a, block):
            return pltpu.make_async_remote_copy(
                src_ref=ins[a].at[owner(sibling, block)],
                dst_ref=crossed_at(a, block),
                send_sem=core_send.at[a, flat(block)],
                recv_sem=core_recv.at[a, flat(block)],
                device_id=grid.mesh_id(sibling),
                device_id_type=MESH_ID,
            )

        def begin(number):
            if number < len(blocks):
                n, block = blocks[number]
                for a in self.rounds[n]:
                    across(a, block).start()
                    load(a, block).start()

        merged = [0]

        def merge_to(n, block):
            while merged[0] <= blocks.index((n, block)):
                turn, now = blocks[merged[0]]
                for a in self.rounds[turn]:
                    load(a, now).wait()
                    across(a, now).wait_recv()
                    view = held[a].at[flat(now)]
                    add_rows(view, view, crossed_at(a, now))
                begin(merged[0] + AHEAD)
                merged[0] += 1

        def held_view(i, block):
            return held[items[i][0]].at[flat(block), :, pl.ds(items[i][1], items[i][2])]

        def block_at(i, first, second, t):
            part = dict(zip(items[i][3], (first, second)))
            return (part["p"], part["r"], t)

        def landing_slot(i, stage, steps, t):
            n2 = size[items[i][3][1]]
            if stage == 0:
                return ((steps[0] - 1) * n2 + steps[1]) * q_size + t
            return (steps[1] - 1) * q_size + t

        pending = []

        def send(i, stage, steps, t):
            n1, n2 = (size[axis] for axis in items[i][3])
            slot = landing_slot(i, stage, steps, t)
            sem = slot if stage == 0 else (n1 - 1) * n2 * q_size + slot
            return pltpu.make_async_remote_copy(
                src_ref=held_view(i, block_at(i, *steps, t)),
                dst_ref=landing[3 * i + stage].at[slot],
                send_sem=send_sem.at[i, sem],
                recv_sem=recv_sem.at[i, sem],
                device_id=grid.mesh_id(grid.shift(at, {items[i][3][stage]: steps[stage]})),
                device_id_type=MESH_ID,
            )

        def start(i, stage, steps, t):
            copy = send(i, stage, steps, t)
            copy.start()
            pending.append(copy)

        def receive(i, stage, steps, t):
            send(i, stage, steps, t).wait_recv()
            into = (0, steps[1]) if stage == 0 else (0, 0)
            view = held_view(i, block_at(i, *into, t))
            add_rows(view, view, landing[3 * i + stage].at[landing_slot(i, stage, steps, t)])

        def line(i, t):
            return pltpu.make_async_remote_copy(
                src_ref=held_view(i, (0, 0, t)),
                dst_ref=landing[3 * i + 2].at[at["q"]],
                send_sem=line_send.at[i, t],
                recv_sem=line_recv.at[i, at["q"]],
                device_id=grid.mesh_id({**at, "q": t}),
                device_id_type=MESH_ID,
            )

        def close(i, t):
            for second in range(1, size[items[i][3][1]]):
                receive(i, 1, (0, second), t)
            pl.when(at["q"] != t)(lambda: line(i, t).start())

        def finish(i):
            a, first, width, _ = items[i]
            parts = [held[a].at[at["q"], :, pl.ds(first, width)]]
            for step in range(1, q_size):
                source = lax.rem(at["q"] + step, q_size)
                view = landing[3 * i + 2].at[source]
                pltpu.make_async_copy(view, view, line_recv.at[i, source]).wait()
                parts.append(view)
            add_rows(outs[a].at[:, pl.ds(first, width)], *parts)

        ticks = []
        for n, members in enumerate(self.rounds):
            mine = [i for i in range(count) if items[i][0] in members]
            for t in targets:
                for far in (True, False):
                    turn = []
                    for i in mine:
                        n1, n2 = (size[axis] for axis in items[i][3])
                        for second in range(1, n2) if far else (0,):
                            for first in range(1, n1):
                                turn.append((i, (first, second), t))
                    ticks.append((n, turn, None if far else (mine, t)))
        yield sum(2 * len(turn) for _, turn, _ in ticks) + q_size * count + count

        for number in range(AHEAD):
            begin(number)
        closing, finishing = [], []
        for k in range(len(ticks) + DEPTH):
            if k < len(ticks):
                n, turn, _ = ticks[k]
                for i, steps, t in turn:
                    merge_to(n, block_at(i, *steps, t))
                    start(i, 0, steps, t)
                    yield
            if k >= DEPTH:
                n, turn, done = ticks[k - DEPTH]
                for i, steps, t in turn:
                    merge_to(n, block_at(i, 0, steps[1], t))
                    receive(i, 0, steps, t)
                    if steps[1] and steps[0] == size[items[i][3][0]] - 1:
                        start(i, 1, (0, steps[1]), t)
                    yield
                if closing and done is None:
                    for i in closing[0][0]:
                        close(i, closing[0][1])
                        yield
                    if closing[0][1] == targets[-1]:
                        finishing.append(closing[0][0])
                    closing.pop()
                    if len(finishing) > 1:
                        for i in finishing.pop(0):
                            finish(i)
                            yield
                if done is not None:
                    closing.append(done)
        for mine, t in closing:
            for i in mine:
                close(i, t)
                yield
            finishing.append(mine)
        for mine in finishing:
            for i in mine:
                finish(i)
                yield
        for n, block in blocks:
            for a in self.rounds[n]:
                across(a, block).wait_send()
        for copy in pending:
            copy.wait_send()
        for i in range(count):
            for t in range(q_size):
                pl.when(at["q"] != t)(lambda: line(i, t).wait_send())


def together(grid, parts, collective_id, name):
    def kernel(*refs):
        at = grid.here()
        if collective_id is not None:
            greet(grid, at)
        ins, outs, scratch = [], [], []
        for list_of, key in ((ins, "inputs"), (outs, "out_shapes"), (scratch, "scratch")):
            for part in parts:
                count = len(getattr(part, key))
                list_of.append(refs[:count])
                refs = refs[count:]
        running = []
        for part, *its in zip(parts, ins, outs, scratch):
            steps = part.steps(at, *its)
            running.append([steps, next(steps), 0])
        while running:
            now = min(running, key=lambda entry: entry[2] / entry[1])
            now[2] += 1
            if next(now[0], "end") == "end":
                running.remove(now)

    outs = pl.pallas_call(
        kernel,
        out_shape=[shape for part in parts for shape in part.out_shapes],
        in_specs=[spec for part in parts for spec in part.in_specs],
        out_specs=[spec for part in parts for spec in part.out_specs],
        scratch_shapes=[entry for part in parts for entry in part.scratch],
        compiler_params=pltpu.CompilerParams(
            collective_id=collective_id,
            has_side_effects=collective_id is not None,
            vmem_limit_bytes=62 * 2**20,
        ),
        name=name,
    )(*[array for part in parts for array in part.inputs])
    split = []
    for part in parts:
        split.append(outs[: len(part.out_shapes)])
        outs = outs[len(part.out_shapes) :]
    return split


GROUP = 256


def tiles(extent, width):
    def wrap(action):
        width_now = min(width, extent)

        @pl.loop(0, extent // width_now)
        def _(k):
            action(pl.ds(pl.multiple_of(k * width_now, width_now), width_now))

    return wrap


def window_start(peer, peers, window, eff):
    return pl.multiple_of(peer * window - lax.div(peer, peers - 1) * (peers * window - eff), 128)


class Experts:
    def __init__(self, grid, hidden, grad, share, weights, capacity):
        own, got, shared_in, shared_down = weights
        self.grid = grid
        self.peers = grid.size["p"]
        self.eff = own[0].shape[1]
        self.extent = own[0].shape[0]
        count = hidden.shape[0]
        window = got[0].shape[2]
        self.supers = count // (2 * GROUP)
        self.slots = GROUP // SEQ * capacity
        self.capacity = capacity
        self.window = window
        rows = 2 * self.slots
        total = self.supers * rows
        groups = count // GROUP
        self.inputs = [hidden, grad, share, *own, *got, shared_in, shared_down]
        hbm = pl.BlockSpec(memory_space=pl.ANY)
        vmem = pl.BlockSpec(memory_space=pltpu.VMEM)
        self.in_specs = [hbm, hbm, vmem] + [hbm] * 6 + [vmem] * 2
        shared_width = shared_in.shape[1]
        kept = [(rows, D), (rows, D), (rows, 2 * window), (rows, window)]
        kept += [(2 * GROUP, shared_width), (2 * GROUP, shared_width // 2)]
        self.out_shapes = [
            jax.ShapeDtypeStruct((count, D), BF),
            jax.ShapeDtypeStruct((count, D), BF),
            jax.ShapeDtypeStruct((groups, GROUP), F32),
        ] + [jax.ShapeDtypeStruct((self.supers * r, c), BF) for r, c in kept]
        self.out_specs = [hbm, hbm, vmem] + [hbm] * len(kept)
        self.scratch = (
            [pltpu.VMEM((2 * GROUP, D), BF)] * 2
            + [pltpu.VMEM((2, r, c), BF) for r, c in kept]
            + [pltpu.VMEM((2, GROUP, D), BF)] * 2
            + [pltpu.VMEM((rows, window), F32)] * 3
            + [pltpu.VMEM((rows, D), BF)] * 2
            + [
                pltpu.VMEM((groups, GROUP), F32),
                pltpu.VMEM((2, self.slots, GROUP), BF),
                pltpu.VMEM((2, GROUP, self.slots), BF),
                pltpu.VMEM((rows, 1), F32),
                pltpu.VMEM((rows, 1), F32),
                pltpu.VMEM((2 * GROUP, shared_width), F32),
                pltpu.SemaphoreType.DMA((2,)),
                pltpu.SemaphoreType.DMA((len(kept), 2)),
                pltpu.SemaphoreType.DMA((2, 2)),
                pltpu.VMEM((D, window), BF),
                pltpu.VMEM((D, window), BF),
                pltpu.VMEM((window, D), BF),
                pltpu.SemaphoreType.DMA((3, self.peers)),
            ]
        )

    def steps(self, at, ins, outs, scratch):
        hidden, grad, share = ins[:3]
        own, got = ins[3:6], ins[6:9]
        shared_in, shared_down = ins[9:]
        hidden_out, out_out, gate_grad = outs[:3]
        kept_out = outs[3:]
        hidden_in, grad_in = scratch[:2]
        kept = scratch[2:8]
        parts = scratch[8:10]
        a_pre, b_pre, flow = scratch[10:13]
        row_grad, expert_out = scratch[13:15]
        keys, picks, picks_t, share_rows, gate_rows, shared_pre = scratch[15:21]
        load_sem, keep_sem, part_sem, gate, up, down, weight_sem = scratch[21:]
        slots, window, supers = self.slots, self.window, self.supers
        rows = 2 * slots
        half = shared_in.shape[1] // 2
        yield supers * 12

        def load(k):
            piece = pl.ds(k * 2 * GROUP, 2 * GROUP)
            return (
                pltpu.make_async_copy(hidden.at[piece, :], hidden_in, load_sem.at[0]),
                pltpu.make_async_copy(grad.at[piece, :], grad_in, load_sem.at[1]),
            )

        def keep(n, k):
            extent = kept[n].shape[1]
            return pltpu.make_async_copy(
                kept[n].at[k % 2],
                kept_out[n].at[pl.ds(k * extent, extent), :],
                keep_sem.at[n, k % 2],
            )

        def put(n, k, j):
            target = (hidden_out, out_out)[n]
            piece = pl.ds((2 * k + j) * GROUP, GROUP)
            return pltpu.make_async_copy(parts[n].at[j], target.at[piece, :], part_sem.at[n, j])

        me, peers, extent = at["p"], self.peers, self.extent
        first = window_start(me, peers, window, self.eff)
        weight_copies = []
        for n, weight in enumerate((gate, up, down)):
            for step in range(peers):
                peer = lax.rem(me + peers - step, peers)
                share_of_d = pl.ds(pl.multiple_of(peer * extent, extent), extent)
                target = weight.at[:, share_of_d] if n == 2 else weight.at[share_of_d, :]
                if step:
                    source = got[n].at[step - 1]
                else:
                    units = pl.ds(first, window)
                    source = own[n].at[units, :] if n == 2 else own[n].at[:, units]
                weight_copies.append(
                    pltpu.make_async_copy(source, target, weight_sem.at[n, step])
                )
        for copy in load(0):
            copy.start()
        for copy in weight_copies:
            copy.start()
        row_of = lax.broadcasted_iota(jnp.int32, (GROUP, GROUP), 0)
        column_of = lax.broadcasted_iota(jnp.int32, (GROUP, GROUP), 1)
        same = lax.div(row_of, SEQ) == lax.div(column_of, SEQ)
        earlier = jnp.logical_and(same, row_of < column_of).astype(BF)
        chosen = (share[...] >= 0).astype(F32)
        place = jnp.dot(chosen.astype(BF), earlier, preferred_element_type=F32)
        sequence = lax.div(lax.broadcasted_iota(jnp.int32, place.shape, 1), SEQ).astype(F32)
        keys[...] = jnp.where(chosen > 0, place + sequence * self.capacity, -1.0)
        for copy in weight_copies:
            copy.wait()
        twice = peers * window - self.eff
        if twice:

            @pl.when(me == peers - 1)
            def _():
                gate[:, pl.ds(0, twice)] = jnp.zeros((D, twice), BF)
                up[:, pl.ds(0, twice)] = jnp.zeros((D, twice), BF)
                down[pl.ds(0, twice), :] = jnp.zeros((twice, D), BF)

        for k in range(supers):
            slot = k % 2
            rows_in, grad_rows, ab_grad, scaled, shared_grad, shared_inner = (
                buffer.at[slot] for buffer in kept
            )
            if k >= 2:
                for n in range(len(kept)):
                    keep(n, k - 2).wait()
            for j in range(2):
                key = keys[pl.ds(2 * k + j, 1), :]
                number = lax.broadcasted_iota(jnp.int32, (slots, GROUP), 0).astype(F32)
                pick = (number == key).astype(F32)
                picks[j] = pick.astype(BF)
                picks_t[j] = pick.T.astype(BF)
                weight = share[pl.ds(2 * k + j, 1), :]
                share_rows[pl.ds(j * slots, slots), :] = jnp.sum(
                    pick * weight, axis=1, keepdims=True
                )
            for copy in load(k):
                copy.wait()
            for source, target in ((hidden_in, rows_in), (grad_in, grad_rows)):
                for j in range(2):

                    @tiles(D, 512)
                    def _(columns):
                        target[pl.ds(j * slots, slots), columns] = jnp.dot(
                            picks[j],
                            source[pl.ds(j * GROUP, GROUP), columns],
                            preferred_element_type=F32,
                        ).astype(BF)

                yield
            for weight, target in ((gate, a_pre), (up, b_pre)):

                @tiles(window, 256)
                def _(columns):
                    target[:, columns] = jnp.dot(
                        rows_in[...], weight[:, columns], preferred_element_type=F32
                    )

                yield

            @tiles(window, 256)
            def _(columns):
                flow[:, columns] = dot_t(grad_rows[...], down[columns, :])

            yield

            @tiles(rows, 32)
            def _(block):
                a = a_pre[block, :]
                b = b_pre[block, :]
                u = flow[block, :]
                weight = share_rows[block, :]
                sigma = jax.nn.sigmoid(a)
                act = a * sigma
                inner = (act * b).astype(BF).astype(F32)
                gate_rows[block, :] = jnp.sum(inner * u, axis=1, keepdims=True)
                scaled[block, :] = (inner * weight).astype(BF)
                u = u * weight
                ab_grad[block, pl.ds(0, window)] = (
                    u * b * (sigma * (1.0 + a * (1.0 - sigma)))
                ).astype(BF)
                ab_grad[block, pl.ds(window, window)] = (u * act).astype(BF)

            for j in range(2):
                pick = picks[j].astype(F32)
                gate_grad[pl.ds(2 * k + j, 1), :] = jnp.sum(
                    pick * gate_rows[pl.ds(j * slots, slots), :], axis=0, keepdims=True
                )
            yield

            @tiles(D, 256)
            def _(columns):
                row_grad[:, columns] = (
                    dot_t(ab_grad[:, pl.ds(0, window)], gate[columns, :])
                    + dot_t(ab_grad[:, pl.ds(window, window)], up[columns, :])
                ).astype(BF)

            yield

            @tiles(D, 512)
            def _(columns):
                expert_out[:, columns] = jnp.dot(
                    scaled[...], down[:, columns], preferred_element_type=F32
                ).astype(BF)

            yield

            @tiles(2 * GROUP, GROUP)
            def _(block):
                shared_pre[block, :] = jnp.dot(
                    hidden_in[block, :], shared_in[...], preferred_element_type=F32
                )

            yield

            @tiles(2 * GROUP, GROUP)
            def _(block):
                u = dot_t(grad_in[block, :], shared_down[...])
                a = shared_pre[block, pl.ds(0, half)]
                b = shared_pre[block, pl.ds(half, half)]
                sigma = jax.nn.sigmoid(a)
                act = a * sigma
                shared_inner[block, :] = (act * b).astype(BF)
                shared_grad[block, pl.ds(0, half)] = (
                    u * b * (sigma * (1.0 + a * (1.0 - sigma)))
                ).astype(BF)
                shared_grad[block, pl.ds(half, half)] = (u * act).astype(BF)

            for n in range(len(kept)):
                keep(n, k).start()
            if k + 1 < supers:
                for copy in load(k + 1):
                    copy.start()
            yield
            for j in range(2):
                if k:
                    put(0, k - 1, j).wait()

                @tiles(D, 256)
                def _(columns):
                    parts[0][j, :, columns] = (
                        jnp.dot(
                            picks_t[j],
                            row_grad[pl.ds(j * slots, slots), columns],
                            preferred_element_type=F32,
                        )
                        + dot_t(shared_grad[pl.ds(j * GROUP, GROUP), :], shared_in[columns, :])
                    ).astype(BF)

                put(0, k, j).start()
            yield
            for j in range(2):
                if k:
                    put(1, k - 1, j).wait()

                @tiles(D, 256)
                def _(columns):
                    parts[1][j, :, columns] = (
                        jnp.dot(
                            picks_t[j],
                            expert_out[pl.ds(j * slots, slots), columns],
                            preferred_element_type=F32,
                        )
                        + jnp.dot(
                            shared_inner[pl.ds(j * GROUP, GROUP), :],
                            shared_down[:, columns],
                            preferred_element_type=F32,
                        )
                    ).astype(BF)

                put(1, k, j).start()
            yield
        for k in range(max(0, supers - 2), supers):
            for n in range(len(kept)):
                keep(n, k).wait()
        for n in range(2):
            for j in range(2):
                put(n, supers - 1, j).wait()


class Exchange:
    def __init__(self, grid, arrays, views, shapes):
        self.grid, self.views = grid, views
        self.peers = grid.size["p"]
        self.inputs = list(arrays)
        hbm = pl.BlockSpec(memory_space=pl.ANY)
        self.in_specs = [hbm] * len(arrays)
        self.out_shapes = [
            jax.ShapeDtypeStruct((self.peers - 1,) + shape, a.dtype)
            for a, shape in zip(arrays, shapes)
        ]
        self.out_specs = [hbm] * len(arrays)
        self.scratch = [pltpu.SemaphoreType.DMA((len(arrays), self.peers - 1))] * 2

    def steps(self, at, ins, outs, scratch):
        send_sem, recv_sem = scratch
        yield 1
        copies = []
        for n, view in enumerate(self.views):
            for step in range(1, self.peers):
                there = self.grid.shift(at, {"p": step})
                copy = pltpu.make_async_remote_copy(
                    src_ref=view(ins[n], there["p"], step),
                    dst_ref=outs[n].at[step - 1],
                    send_sem=send_sem.at[n, step - 1],
                    recv_sem=recv_sem.at[n, step - 1],
                    device_id=self.grid.mesh_id(there),
                    device_id_type=MESH_ID,
                )
                copy.start()
                copies.append(copy)
        yield
        for copy in copies:
            copy.wait()


SCALE = (NOPE + ROPE) ** (-0.5)
HALF = ROPE // 2
TURN = HEADS * HALF
WIDE = HEADS * NOPE


def spread():
    row = lax.broadcasted_iota(jnp.int32, (128, TURN), 0)
    lane = lax.broadcasted_iota(jnp.int32, (128, TURN), 1)
    return (lax.rem(lane, HALF) == row).astype(BF)


def of_head(h):
    lane = lax.broadcasted_iota(jnp.int32, (MICRO * SEQ, 2 * TURN), 1)
    return jnp.bitwise_and(jnp.right_shift(lane, 5), HEADS - 1) == h


def rms_scale(values):
    return lax.rsqrt(jnp.mean(values * values, -1, keepdims=True) + EPSILON)


class AttentionForward:
    def __init__(self, tokens, routes, allowed, tables, gains, weights, experts):
        count = MICRO * SEQ
        self.experts = experts
        self.inputs = [tokens, routes, allowed, *tables, *gains, *weights]
        vmem = pl.BlockSpec(memory_space=pltpu.VMEM)
        hbm = pl.BlockSpec(memory_space=pl.ANY)
        self.in_specs = [vmem] * 8 + [hbm] * 5
        shapes = [
            ((count, D), BF), ((experts, count), F32),
            ((count, D), BF), ((count, WIDE), BF), ((count, 2 * TURN), BF), ((count, RANK), F32),
            ((count, RANK), BF), ((count, 2 * TURN), BF), ((count, 2 * WIDE), BF),
            ((HEADS, count, count), F32), ((count, WIDE), BF), ((count, D), F32),
        ]
        self.out_shapes = [jax.ShapeDtypeStruct(shape, kind) for shape, kind in shapes]
        self.out_specs = [vmem] * len(shapes)
        self.scratch = [pltpu.VMEM(w.shape, BF) for w in weights] + [
            pltpu.VMEM((count, RANK + 256), F32),
            pltpu.VMEM((count, 2 * TURN), F32),
            pltpu.SemaphoreType.DMA((5,)),
        ]

    def steps(self, at, ins, outs, scratch):
        tokens, routes, allowed, cosine, sine, attn_gain, kv_gain, ffn_gain = ins[:8]
        (
            hidden, gates, normed, q_plain, q_turned, kv_low, latent, k_turned, kv, chances,
            attended, residual,
        ) = outs
        q_weight, kv_down, kv_up, out_weight, router = scratch[:5]
        kv_raw, q_raw, sem = scratch[5:]
        yield 9
        loads = [
            pltpu.make_async_copy(ins[8 + n], scratch[n], sem.at[n]) for n in range(5)
        ]
        for n in (1, 0, 2, 3, 4):
            loads[n].start()
        values = tokens[...].astype(F32)
        normed[...] = (values * rms_scale(values) * attn_gain[...]).astype(BF)
        yield
        loads[1].wait()

        @tiles(RANK + 256, 256)
        def _(columns):
            kv_raw[:, columns] = dot(normed[...], kv_down[:, columns])

        low = kv_raw[:, pl.ds(0, RANK)]
        kv_low[...] = low
        latent[...] = (low * rms_scale(low) * kv_gain[...]).astype(BF)
        first, second = kv_raw[:, pl.ds(RANK, 128)], kv_raw[:, pl.ds(RANK + 128, 128)]
        c, s = cosine[:, pl.ds(0, 128)], sine[:, pl.ds(0, 128)]
        lay = spread()
        k_turned[:, pl.ds(0, TURN)] = dot((first * c - second * s).astype(BF), lay).astype(BF)
        k_turned[:, pl.ds(TURN, TURN)] = dot((second * c + first * s).astype(BF), lay).astype(BF)
        yield
        loads[0].wait()

        @tiles(WIDE, 256)
        def _(columns):
            q_plain[:, columns] = dot(normed[...], q_weight[:, columns]).astype(BF)

        yield
        for n in range(4):
            columns = pl.ds(n * 256, 256)
            q_raw[:, columns] = dot(normed[...], q_weight[:, pl.ds(WIDE + n * 256, 256)])
        first, second = q_raw[:, pl.ds(0, TURN)], q_raw[:, pl.ds(TURN, TURN)]
        q_turned[:, pl.ds(0, TURN)] = (first * cosine[...] - second * sine[...]).astype(BF)
        q_turned[:, pl.ds(TURN, TURN)] = (second * cosine[...] + first * sine[...]).astype(BF)
        yield
        loads[2].wait()

        @tiles(2 * WIDE, 256)
        def _(columns):
            kv[:, columns] = dot(latent[...], kv_up[:, columns]).astype(BF)

        yield

        @pl.loop(0, HEADS)
        def _(h):
            plain = pl.ds(pl.multiple_of(h * NOPE, NOPE), NOPE)
            keys = pl.ds(pl.multiple_of(h * 2 * NOPE, NOPE), NOPE)
            both = pl.ds(pl.multiple_of(h * 2 * NOPE + NOPE, NOPE), VDIM)
            turned = jnp.where(of_head(h), q_turned[...].astype(F32), 0.0).astype(BF)
            scores = dot_t(q_plain[:, plain], kv[:, keys]) + dot_t(turned, k_turned[...])
            scores = jnp.where(allowed[...] > 0, scores * SCALE, MASKED)
            powers = jnp.exp(scores - jnp.max(scores, -1, keepdims=True))
            chance = powers / jnp.sum(powers, -1, keepdims=True)
            chances[h] = chance
            attended[:, plain] = dot(chance.astype(BF), kv[:, both]).astype(BF)

        yield
        loads[3].wait()

        @tiles(D, 256)
        def _(columns):
            residual[:, columns] = tokens[:, columns].astype(F32) + dot(
                attended[...], out_weight[:, columns]
            )

        yield
        values = residual[...]
        hidden[...] = (values * rms_scale(values) * ffn_gain[...]).astype(BF)
        loads[4].wait()
        logits = dot(hidden[...], router[...])
        lane = lax.broadcasted_iota(jnp.int32, logits.shape, 1)
        chosen = lane < 0
        for k in range(TOP):
            chosen = jnp.logical_or(chosen, routes[:, pl.ds(k, 1)] == lane)
        logits = jnp.where(chosen, logits, MASKED)
        powers = jnp.where(chosen, jnp.exp(logits - jnp.max(logits, -1, keepdims=True)), 0.0)
        share = powers / jnp.sum(powers, -1, keepdims=True)
        gates[...] = jnp.where(chosen, share, -1.0).T[: self.experts]
        yield


class AttentionBackward:
    def __init__(self, cotangent, hidden_sum, gate_grad, saved, tokens, tables, gains, weights):
        count = MICRO * SEQ
        self.experts = gate_grad.shape[0]
        self.inputs = [cotangent, hidden_sum, gate_grad, *tables, *gains, *saved, tokens, *weights]
        vmem = pl.BlockSpec(memory_space=pltpu.VMEM)
        hbm = pl.BlockSpec(memory_space=pl.ANY)
        self.in_specs = [vmem] * (8 + 12 + 1) + [hbm] * 5
        self.grads = [(WIDE, D), (RANK, 2 * WIDE), (D, WIDE + 2 * TURN), (D, RANK + 256)]
        self.out_shapes = [jax.ShapeDtypeStruct(shape, BF) for shape in self.grads] + [
            jax.ShapeDtypeStruct((count, D), BF),
            jax.ShapeDtypeStruct((1, D), F32),
            jax.ShapeDtypeStruct((1, RANK), F32),
            jax.ShapeDtypeStruct((1, D), F32),
            jax.ShapeDtypeStruct((D, 128), F32),
        ]
        self.out_specs = [hbm] * 4 + [vmem] * 5
        self.scratch = [pltpu.VMEM(w.shape, BF) for w in weights] + [
            pltpu.VMEM((2, 256, 2 * WIDE), BF),
            pltpu.VMEM((count, 128), F32),
            pltpu.VMEM((count, D), F32),
            pltpu.VMEM((count, D), F32),
            pltpu.VMEM((count, D), BF),
            pltpu.VMEM((count, WIDE), BF),
            pltpu.VMEM((count, WIDE + 2 * TURN), BF),
            pltpu.VMEM((count, 2 * WIDE), BF),
            pltpu.VMEM((count, RANK + 256), BF),
            pltpu.VMEM((count, 2 * TURN), F32),
            pltpu.VMEM((count, 2 * TURN), F32),
            pltpu.SemaphoreType.DMA((5,)),
            pltpu.SemaphoreType.DMA((2,)),
        ]

    def steps(self, at, ins, outs, scratch):
        cotangent, hidden_sum, gate_grad, cosine, sine, attn_gain, kv_gain, ffn_gain = ins[:8]
        (
            hidden, gates, normed, q_plain, q_turned, kv_low, latent, k_turned, kv, chances,
            attended, residual,
        ) = ins[8:20]
        tokens_grad, attn_gain_grad, kv_gain_grad, ffn_gain_grad, router_grad = outs[4:]
        q_weight, kv_down, kv_up, out_weight, router = scratch[:5]
        (
            buffers, turned_gates, hidden_grad, residual_grad, mixed, attended_grad, q_grad, kv_grad,
            kv_raw_grad, q_turn_grad, k_turn_grad, sem, out_sem,
        ) = scratch[5:]
        experts = self.experts
        yield 4 + sum(shape[0] // 256 for shape in self.grads)
        loads = [
            pltpu.make_async_copy(ins[21 + n], scratch[n], sem.at[n]) for n in range(5)
        ]
        for n in (4, 3, 2, 0, 1):
            loads[n].start()
        share = jnp.maximum(gates[...], 0.0)
        inner = jnp.sum(share * gate_grad[...], 0, keepdims=True)
        turned_gates[...] = jnp.zeros_like(turned_gates)
        turned_gates[pl.ds(0, experts), :] = share * (gate_grad[...] - inner)
        logit_grad = turned_gates[...].T.astype(BF)
        loads[4].wait()

        @tiles(D, 256)
        def _(columns):
            router_grad[columns, :] = t_dot(hidden[:, columns], logit_grad)
            hidden_grad[:, columns] = hidden_sum[:, columns] + dot_t(
                logit_grad, router[columns, :]
            )

        def norm_back(values, gain, gradient):
            scale = rms_scale(values)
            weighted = gradient * gain
            mean = jnp.mean(weighted * values, -1, keepdims=True)
            gain_grad = jnp.sum(gradient * values * scale, 0, keepdims=True)
            return scale * weighted - values * (scale * scale * scale * mean), gain_grad

        part, ffn_gain_grad[...] = norm_back(residual[...], ffn_gain[...], hidden_grad[...])
        total = cotangent[...].astype(F32) + part
        residual_grad[...] = total
        mixed[...] = total.astype(BF)
        yield
        loads[3].wait()

        @tiles(WIDE, 256)
        def _(columns):
            attended_grad[:, columns] = dot_t(mixed[...], out_weight[columns, :]).astype(BF)

        yield
        turn = [0]
        stores = {}

        def weight_grad(n, left, right):
            rows, width = self.grads[n]
            for k in range(rows // 256):
                slot = turn[0] % 2
                turn[0] += 1
                if slot in stores:
                    stores[slot].wait()
                piece = pl.ds(k * 256, 256)

                @tiles(width, 256)
                def _(columns):
                    buffers[slot, :, columns] = t_dot(left[:, piece], right[:, columns]).astype(BF)

                stores[slot] = pltpu.make_async_copy(
                    buffers.at[slot, :, pl.ds(0, width)], outs[n].at[piece, :], out_sem.at[slot]
                )
                stores[slot].start()
                yield

        yield from weight_grad(0, attended, mixed)
        q_turn_grad[...] = jnp.zeros_like(q_turn_grad)
        k_turn_grad[...] = jnp.zeros_like(k_turn_grad)

        @pl.loop(0, HEADS)
        def _(h):
            plain = pl.ds(pl.multiple_of(h * NOPE, NOPE), NOPE)
            keys = pl.ds(pl.multiple_of(h * 2 * NOPE, NOPE), NOPE)
            both = pl.ds(pl.multiple_of(h * 2 * NOPE + NOPE, NOPE), VDIM)
            chance = chances[h]
            grads = attended_grad[:, plain]
            kv_grad[:, both] = t_dot(chance.astype(BF), grads).astype(BF)
            chance_grad = dot_t(grads, kv[:, both])
            mean = jnp.sum(chance * chance_grad, -1, keepdims=True)
            score_grad = (chance * (chance_grad - mean)).astype(BF)
            q_grad[:, plain] = (dot(score_grad, kv[:, keys]) * SCALE).astype(BF)
            kv_grad[:, keys] = (t_dot(score_grad, q_plain[:, plain]) * SCALE).astype(BF)
            mine = of_head(h)
            turned = jnp.where(mine, q_turned[...].astype(F32), 0.0).astype(BF)
            q_turn_grad[...] += jnp.where(mine, dot(score_grad, k_turned[...]), 0.0) * SCALE
            k_turn_grad[...] += t_dot(score_grad, turned) * SCALE

        yield
        first, second = q_turn_grad[:, pl.ds(0, TURN)], q_turn_grad[:, pl.ds(TURN, TURN)]
        c, s = cosine[...], sine[...]
        q_grad[:, pl.ds(WIDE, TURN)] = (first * c + second * s).astype(BF)
        q_grad[:, pl.ds(WIDE + TURN, TURN)] = (second * c - first * s).astype(BF)
        lay = spread()

        def gathered(columns):
            values = k_turn_grad[:, columns]
            high = values.astype(BF)
            low = (values - high.astype(F32)).astype(BF)
            return dot_t(high, lay) + dot_t(low, lay)

        first, second = gathered(pl.ds(0, TURN)), gathered(pl.ds(TURN, TURN))
        c, s = cosine[:, pl.ds(0, 128)], sine[:, pl.ds(0, 128)]
        kv_raw_grad[:, pl.ds(RANK, 128)] = (first * c + second * s).astype(BF)
        kv_raw_grad[:, pl.ds(RANK + 128, 128)] = (second * c - first * s).astype(BF)
        loads[2].wait()
        latent_grad = dot_t(kv_grad[...], kv_up[...])
        part, kv_gain_grad[...] = norm_back(kv_low[...], kv_gain[...], latent_grad)
        kv_raw_grad[:, pl.ds(0, RANK)] = part.astype(BF)
        yield from weight_grad(1, latent, kv_grad)
        yield from weight_grad(2, normed, q_grad)
        yield from weight_grad(3, normed, kv_raw_grad)
        loads[0].wait()
        loads[1].wait()

        @tiles(D, 256)
        def _(columns):
            hidden_grad[:, columns] = dot_t(q_grad[...], q_weight[columns, :]) + dot_t(
                kv_raw_grad[...], kv_down[columns, :]
            )

        part, attn_gain_grad[...] = norm_back(
            ins[20][...].astype(F32), attn_gain[...], hidden_grad[...]
        )
        tokens_grad[...] = (residual_grad[...] + part).astype(BF)
        yield
        for store in stores.values():
            store.wait()


class WeightGrads:
    TILE = 256

    def __init__(self, grid, kept, extent):
        self.grid, self.extent, self.chunks = grid, extent, len(kept)
        self.inputs = [array for entry in kept for array in entry]
        rows, grad_rows, ab_grad, scaled, shared_grad, shared_inner, hidden, grad = kept[0]
        self.window = scaled.shape[1]
        hbm = pl.BlockSpec(memory_space=pl.ANY)
        self.in_specs = [hbm] * len(self.inputs)
        peers = grid.size["p"]
        window, tile = self.window, self.TILE
        self.out_shapes = [
            jax.ShapeDtypeStruct((extent, 2 * window), F32),
            jax.ShapeDtypeStruct((window, extent), F32),
            jax.ShapeDtypeStruct((peers - 1, extent, 2 * window), BF),
            jax.ShapeDtypeStruct((peers - 1, window, extent), BF),
            jax.ShapeDtypeStruct((D, shared_grad.shape[1]), BF),
            jax.ShapeDtypeStruct((shared_inner.shape[1], D), F32),
        ]
        self.out_specs = [hbm] * 6
        self.jobs = [(0, 2, True), (1, 3, False), (6, 4, True), (7, 5, False)]
        self.scratch = []
        for streamed, resident, left in self.jobs:
            a, b = kept[0][streamed], kept[0][resident]
            self.scratch.append(pltpu.VMEM((self.chunks,) + b.shape, BF))
            self.scratch.append(pltpu.VMEM((2, self.chunks, a.shape[0], tile), BF))
            shape = (tile, b.shape[1]) if left else (b.shape[1], tile)
            self.scratch.append(pltpu.VMEM((2,) + shape, F32))
            self.scratch.append(pltpu.VMEM((2,) + shape, BF))
        self.scratch += [
            pltpu.SemaphoreType.DMA((4, self.chunks)),
            pltpu.SemaphoreType.DMA((4, 2, self.chunks)),
            pltpu.SemaphoreType.DMA((4, 2)),
        ]

    def steps(self, at, ins, outs, scratch):
        tile, extent, chunks = self.TILE, self.extent, self.chunks
        peers = self.grid.size["p"]
        kept = [ins[c * 8 : (c + 1) * 8] for c in range(chunks)]
        whole_sem, tile_sem, out_sem = scratch[16:]
        own_ab, own_down, sent_ab, sent_down, shared_in, shared_down = outs

        def whole(job, c):
            return pltpu.make_async_copy(
                kept[c][self.jobs[job][1]], scratch[4 * job].at[c], whole_sem.at[job, c]
            )

        work = []
        per_peer = extent // tile
        for step in range(peers):
            for job in range(2):
                for k in range(per_peer):
                    piece = pl.ds(k * tile, tile)
                    if step == 0:
                        target = own_ab.at[piece, :] if job == 0 else own_down.at[:, piece]
                    elif job == 0:
                        target = sent_ab.at[step - 1, piece, :]
                    else:
                        target = sent_down.at[step - 1, :, piece]
                    peer = self.grid.shift(at, {"p": step})["p"]
                    first = pl.multiple_of(peer * extent + k * tile, tile)
                    work.append((job, first, target, step == 0))
        for k in range(D // tile):
            piece = pl.ds(k * tile, tile)
            work.append((2, k * tile, shared_in.at[piece, :], False))
            work.append((3, k * tile, shared_down.at[:, piece], True))
        work.sort(key=lambda entry: entry[0] >= 2)
        turns = [0] * 4
        numbered = []
        for job, first, target, wide in work:
            numbered.append((job, first, target, wide, turns[job]))
            turns[job] += 1
        yield len(work)

        def fetch(number, c):
            job, first, _, _, turn = numbered[number]
            return pltpu.make_async_copy(
                kept[c][self.jobs[job][0]].at[:, pl.ds(first, tile)],
                scratch[4 * job + 1].at[turn % 2, c],
                tile_sem.at[job, turn % 2, c],
            )

        def store(number):
            job, _, target, wide, turn = numbered[number]
            source = scratch[4 * job + (2 if wide else 3)].at[turn % 2]
            return pltpu.make_async_copy(source, target, out_sem.at[job, turn % 2])

        for c in range(chunks):
            for job in range(2):
                whole(job, c).start()
            fetch(0, c).start()
            for job in range(2, 4):
                whole(job, c).start()
        begun = set()
        last = {}
        for number, (job, _, _, wide, turn) in enumerate(numbered):
            if number + 1 < len(numbered):
                for c in range(chunks):
                    fetch(number + 1, c).start()
            if job not in begun:
                begun.add(job)
                for c in range(chunks):
                    whole(job, c).wait()
            for c in range(chunks):
                fetch(number, c).wait()
            if (job, turn % 2) in last:
                store(last[job, turn % 2]).wait()
            last[job, turn % 2] = number
            resident, streamed = scratch[4 * job], scratch[4 * job + 1].at[turn % 2]
            result = scratch[4 * job + (2 if wide else 3)].at[turn % 2]
            left = self.jobs[job][2]

            @tiles(resident.shape[2], 256)
            def _(columns):
                total = None
                for c in range(chunks):
                    if left:
                        term = t_dot(streamed[c], resident[c, :, columns])
                    else:
                        term = t_dot(resident[c, :, columns], streamed[c])
                    total = term if total is None else total + term
                if left:
                    result[:, columns] = total.astype(result.dtype)
                else:
                    result[columns, :] = total.astype(result.dtype)

            store(number).start()
            yield
        for number in last.values():
            store(number).wait()


class Assemble:
    TILE = 128

    def __init__(self, grid, own_ab, own_down, got_ab, got_down, eff):
        self.grid, self.eff = grid, eff
        self.extent = own_ab.shape[0]
        self.window = own_down.shape[0]
        self.peers = 1 + len(got_ab)
        self.inputs = [own_ab, own_down, *got_ab, *got_down]
        hbm = pl.BlockSpec(memory_space=pl.ANY)
        self.in_specs = [hbm] * len(self.inputs)
        self.out_shapes = [
            jax.ShapeDtypeStruct((self.extent, eff), F32),
            jax.ShapeDtypeStruct((self.extent, eff), F32),
            jax.ShapeDtypeStruct((eff, self.extent), F32),
        ]
        self.out_specs = [hbm] * 3
        tile, window = self.TILE, self.window
        self.scratch = [
            pltpu.VMEM((2, tile, 2 * window), F32),
            pltpu.VMEM((2, window, tile), F32),
            pltpu.VMEM((2, self.peers - 1, tile, 2 * window), BF),
            pltpu.VMEM((2, self.peers - 1, window, tile), BF),
            pltpu.VMEM((2, 2, tile, eff), F32),
            pltpu.VMEM((2, eff, tile), F32),
            pltpu.SemaphoreType.DMA((2, 2, self.peers)),
            pltpu.SemaphoreType.DMA((2, 3)),
        ]

    def steps(self, at, ins, outs, scratch):
        tile, window, peers, eff = self.TILE, self.window, self.peers, self.eff
        own = ins[:2]
        got = (ins[2 : 1 + peers], ins[1 + peers :])
        own_tiles, got_tiles = scratch[:2], scratch[2:4]
        both, down, in_sem, out_sem = scratch[4:]
        count = self.extent // tile
        yield 2 * count
        work = [(job, k) for job in range(2) for k in range(count)]

        def piece_of(array, job, k):
            piece = pl.ds(k * tile, tile)
            return array.at[piece, :] if job == 0 else array.at[:, piece]

        def fetch(job, k):
            copies = []
            for source in range(peers):
                array = own[job] if source == 0 else got[job][source - 1]
                target = own_tiles[job].at[k % 2]
                if source:
                    target = got_tiles[job].at[k % 2, source - 1]
                copies.append(
                    pltpu.make_async_copy(
                        piece_of(array, job, k), target, in_sem.at[job, k % 2, source]
                    )
                )
            return copies

        def store(job, k):
            if job:
                return [
                    pltpu.make_async_copy(
                        down.at[k % 2], piece_of(outs[2], 1, k), out_sem.at[k % 2, 2]
                    )
                ]
            return [
                pltpu.make_async_copy(
                    both.at[k % 2, n], piece_of(outs[n], 0, k), out_sem.at[k % 2, n]
                )
                for n in range(2)
            ]

        for copy in fetch(*work[0]):
            copy.start()
        for number, (job, k) in enumerate(work):
            if number + 1 < len(work):
                for copy in fetch(*work[number + 1]):
                    copy.start()
            for copy in fetch(job, k):
                copy.wait()
            if k >= 2:
                for copy in store(job, k - 2):
                    copy.wait()
            for peer in range(peers):
                first = peer * window
                width = min(window, eff - first)
                skip = window - width
                for source in range(peers):

                    @pl.when(lax.rem(at["p"] - peer + peers, peers) == source)
                    def _():
                        if source:
                            view = got_tiles[job].at[k % 2, source - 1]
                        else:
                            view = own_tiles[job].at[k % 2]
                        if job:
                            down[k % 2, pl.ds(first, width), :] = view[
                                pl.ds(skip, width), :
                            ].astype(F32)
                        else:
                            for n in range(2):
                                both[k % 2, n, :, pl.ds(first, width)] = view[
                                    :, pl.ds(n * window + skip, width)
                                ].astype(F32)

            for copy in store(job, k):
                copy.start()
            yield
        for job in range(2):
            for k in range(max(0, count - 2), count):
                for copy in store(job, k):
                    copy.wait()


def gather_all(grid, arrays, items, collective_id):
    return together(grid, [Gather(grid, arrays, items)], collective_id, "gather_all")[0]


def position_tables():
    frequency = ROPE_BASE ** (-2.0 * np.arange(HALF) / ROPE)
    angles = np.tile(np.arange(SEQ)[:, None] * frequency[None, :], (MICRO, HEADS))
    return [jnp.asarray(np.cos(angles), F32), jnp.asarray(np.sin(angles), F32)]


def capacity_for(expert_count):
    return min(SEQ, ((4 * SEQ * TOP + 3 * expert_count - 1) // (3 * expert_count) + 7) // 8 * 8)


def dot(left, right):
    return jnp.dot(left, right, preferred_element_type=F32)


def dot_t(left, right):
    return lax.dot_general(left, right, (((1,), (1,)), ((), ())), preferred_element_type=F32)


def t_dot(left, right):
    return lax.dot_general(left, right, (((0,), (0,)), ((), ())), preferred_element_type=F32)


def pack(parts, rows):
    flat = jnp.concatenate([part.reshape(rows, -1) for part in parts], 1)
    width = -(-flat.shape[1] // 2048) * 2048
    flat = jnp.pad(flat, ((0, 0), (0, width - flat.shape[1])))
    return flat.reshape(rows, width // 128, 128)


def unpack(block, shapes):
    rows = block.shape[0]
    flat = block.reshape(rows, -1)
    parts, first = [], 0
    for shape in shapes:
        size = 1
        for extent in shape:
            size *= extent
        parts.append(flat[:, first : first + size].reshape((rows,) + shape))
        first += size
    return parts


def plain_weight_grads(grid, kept, extent):
    me = lax.axis_index("dp")
    peers = grid.size["p"]

    def total(left, right):
        return functools.reduce(jnp.add, [t_dot(entry[left], entry[right]) for entry in kept])

    def share_of(array, step, axis):
        peer = lax.rem(me + step, peers)
        return lax.dynamic_slice_in_dim(array, peer * extent, extent, axis)

    both, down = total(0, 2), total(3, 1)
    steps = range(1, peers)
    return (
        share_of(both, 0, 0),
        share_of(down, 0, 1),
        jnp.stack([share_of(both, step, 0) for step in steps]).astype(BF),
        jnp.stack([share_of(down, step, 1) for step in steps]).astype(BF),
        total(6, 4).astype(BF),
        total(5, 7),
    )


def body(
    grid,
    tokens,
    cotangent,
    routes,
    segments,
    attn_gain,
    q_weight,
    kv_down,
    kv_gain,
    kv_up,
    out_weight,
    ffn_gain,
    router,
    shared_gate,
    shared_up,
    shared_down,
    expert_gate,
    expert_up,
    expert_down,
):
    devices = grid.devices
    dp_size = grid.size["p"]
    experts = router.shape[1]
    count = MICRO * SEQ
    eff = expert_gate.shape[2]
    extent = expert_gate.shape[1]
    window = -(-eff // (128 * dp_size)) * 128
    own = (expert_gate[0], expert_up[0], expert_down[0])

    rows = q_weight.shape[0]
    q_heads = q_weight.reshape(rows, HEADS, NOPE + ROPE)
    q_sent = jnp.concatenate(
        [
            q_heads[:, :, :NOPE].reshape(rows, WIDE),
            q_heads[:, :, NOPE : NOPE + HALF].reshape(rows, TURN),
            q_heads[:, :, NOPE + HALF :].reshape(rows, TURN),
        ],
        1,
    )
    gap = jnp.zeros((rows, 128 - HALF), BF)
    down_sent = jnp.concatenate(
        [kv_down[:, : RANK + HALF], gap, kv_down[:, RANK + HALF :], gap], 1
    )
    small_shapes = (attn_gain.shape, ffn_gain.shape, kv_gain.shape, router.shape)
    small = pack([attn_gain[None], ffn_gain[None], kv_gain[None], router[None]], 1)[0]
    up_shape = kv_up.shape
    up_sent = kv_up if up_shape[0] % 16 == 0 else kv_up.reshape(16, -1)
    first, second, third = ("q", "r", "p"), ("q", "p", "r"), ("p", "q", "r")

    def columns_of(ref, peer, step):
        return ref.at[:, pl.ds(window_start(peer, dp_size, window, eff), window)]

    def rows_of(ref, peer, step):
        return ref.at[pl.ds(window_start(peer, dp_size, window, eff), window), :]

    gathered, windows = together(
        grid,
        [
            Gather(
                grid,
                [q_sent, down_sent, up_sent, out_weight, small],
                [
                    (0, 0, q_sent.shape[1], third),
                    (1, 0, down_sent.shape[1], third),
                    (2, 0, up_sent.shape[1], ("r", "p", "q")),
                    (3, 0, out_weight.shape[1], first),
                    (4, 0, 128, first),
                ],
            ),
            Exchange(grid, own[:2], [columns_of] * 2, [(extent, window)] * 2),
        ],
        0,
        "gather_attention",
    )
    parts = unpack(gathered[4], small_shapes)
    gains = [parts[n].reshape(1, -1).astype(F32) for n in (0, 2, 1)]
    weights = [
        gathered[0].reshape(D, -1),
        gathered[1].reshape(D, -1),
        gathered[2].reshape(RANK, -1),
        gathered[3].reshape(-1, D),
        jnp.pad(parts[3].reshape(D, experts), ((0, 0), (0, 128 - experts))),
    ]

    token_rows = tokens.reshape(count, D)
    grad_out = cotangent.reshape(count, D)
    tables = position_tables()
    numbers = segments.reshape(1, -1) + 4 * (jnp.arange(count, dtype=jnp.int32) // SEQ)[None, :]
    places = jnp.arange(count, dtype=jnp.int32)
    allowed = (numbers == numbers.T) & (places[:, None] >= places[None, :])

    def half_orders(a):
        return [(a, 0, D // 2, first), (a, D // 2, D // 2, second)]

    (grad_first,), saved, windows_down = together(
        grid,
        [
            Gather(grid, [grad_out[:SEQ]], [(0, 0, D // 2, third), (0, D // 2, D // 2, second)]),
            AttentionForward(
                token_rows,
                routes.reshape(count, TOP),
                allowed.astype(F32),
                tables,
                gains,
                weights,
                experts,
            ),
            Exchange(grid, own[2:], [rows_of], [(window, extent)]),
        ],
        6,
        "attention_forward",
    )
    hidden, dense_gates, residual = saved[0], saved[1], saved[11]

    share = shared_gate.shape[1] // devices
    both = jnp.concatenate(
        [shared_gate.reshape(-1, devices, share), shared_up.reshape(-1, devices, share)], 2
    )
    shared_in = lax.all_to_all(
        both.transpose(1, 0, 2), ("dp", "expert"), split_axis=0, concat_axis=0, tiled=True
    ).reshape(D, 2 * share)
    room = -(-share // 128) * 128
    shared_in = jnp.concatenate(
        [
            jnp.pad(shared_in[:, :share], ((0, 0), (0, room - share))),
            jnp.pad(shared_in[:, share:], ((0, 0), (0, room - share))),
        ],
        1,
    )
    shared_part = jnp.pad(shared_down, ((0, room - share), (0, 0)))

    half = D // 2
    capacity = capacity_for(experts)
    expert = lax.axis_index("expert")
    own_weights = (own, (*windows, *windows_down), shared_in, shared_part)

    def gather_of(chunk):
        piece = slice(chunk * SEQ, (chunk + 1) * SEQ)
        sent = [hidden[piece], dense_gates[:, piece]]
        orders = half_orders(0) + [(1, 0, SEQ, first)]
        if chunk:
            sent.append(grad_out[piece])
            orders += half_orders(2)
        return Gather(grid, sent, orders)

    kept_hidden, kept_grad = [], []

    def experts_of(hidden_all, gates_all, grad_all):
        kept_hidden.append(hidden_all)
        kept_grad.append(grad_all)
        share = lax.dynamic_index_in_dim(gates_all, expert, 1, keepdims=False)
        return Experts(
            grid,
            hidden_all.reshape(-1, D),
            grad_all.reshape(-1, D),
            share.reshape(-1, GROUP),
            own_weights,
            capacity,
        )

    def sums_of(done):
        hidden_part, out_part, gate_grad = done[:3]
        mine = (jnp.arange(experts, dtype=jnp.int32) == expert)[None, :, None]
        gate_grad = jnp.where(mine, gate_grad.reshape(devices, 1, SEQ), 0.0)
        shape = (devices, SEQ, D)
        return [hidden_part.reshape(shape), gate_grad, out_part.reshape(shape)]

    def kept_of(done):
        flat = [(h.reshape(-1, D), g.reshape(-1, D)) for h, g in zip(kept_hidden, kept_grad)]
        return [tuple(entry[3:]) + pair for entry, pair in zip(done, flat)]

    over = [(0, 0, half, ("p", "r")), (0, half, half, ("r", "p"))]
    over_gates = [(1, 0, SEQ, ("p", "r"))]
    over_out = [(2, 0, half, ("p", "r")), (2, half, half, ("r", "p"))]
    if devices <= 32:
        (gathered,) = together(grid, [gather_of(0)], 1, "gather_first")
        gathered, done_0 = together(
            grid,
            [gather_of(1), experts_of(*gathered, grad_first)],
            2,
            "gather_second_experts_first",
        )
        everything = over + over_gates + over_out
        sums_0, done_1 = together(
            grid,
            [Scatter(grid, sums_of(done_0), everything, [[0, 1], [2]]), experts_of(*gathered)],
            3,
            "scatter_first_experts_second",
        )
        kept = kept_of((done_0, done_1))
        sums_1, weight_grads = together(
            grid,
            [
                Scatter(grid, sums_of(done_1), everything, [[0, 1], [2]]),
                WeightGrads(grid, kept, extent),
            ],
            4,
            "scatter_second_weight_grads",
        )
        sums = (sums_0, sums_1)
    else:
        sums, done = [], []
        for chunk in range(MICRO):
            part = gather_of(chunk)
            if chunk:
                before = tuple(sums[-1])
                *part.inputs, sums[-1] = lax.optimization_barrier((*part.inputs, before))
            (gathered,) = together(grid, [part], 1 + 7 * chunk, "gather")
            part = experts_of(*gathered, *([] if chunk else [grad_first]))
            (now,) = together(grid, [part], None, "experts")
            parts = sums_of(now)
            (hidden_gates,) = together(
                grid, [Scatter(grid, parts[:2], over + over_gates, [[0, 1]])], 2, "scatter_hidden"
            )
            (out_sum,) = together(grid, [Scatter(grid, parts[2:], over, [[0]])], 3, "scatter_out")
            sums.append((*hidden_gates, *out_sum))
            done.append(now)
        weight_grads = plain_weight_grads(grid, kept_of(done), extent)
    hidden_sum = jnp.concatenate([entry[0] for entry in sums], 0)
    gate_grad = jnp.concatenate([entry[1] for entry in sums], 1)
    result = residual + jnp.concatenate([entry[2] for entry in sums], 0)
    own_ab, own_down, sent_ab, sent_down, shared_in_grad, shared_down_grad = weight_grads

    def sent_to(ref, peer, step):
        return ref.at[step - 1]

    attention_grads, (got_ab, got_down) = together(
        grid,
        [
            AttentionBackward(
                grad_out, hidden_sum, gate_grad, saved, token_rows, tables, gains, weights
            ),
            Exchange(
                grid,
                [sent_ab, sent_down],
                [sent_to] * 2,
                [(extent, 2 * window), (window, extent)],
            ),
        ],
        7,
        "attention_backward",
    )
    (
        out_weight_grad, kv_up_grad, q_weight_grad, kv_down_grad, tokens_grad, attn_gain_grad,
        kv_gain_grad, ffn_gain_grad, router_grad,
    ) = attention_grads
    shared_down_grad = shared_down_grad[:share]
    shared_in_grad = jnp.concatenate(
        [shared_in_grad[:, :share], shared_in_grad[:, room : room + share]], 1
    )
    small_grads = pack(
        [
            attn_gain_grad.reshape(devices, -1),
            ffn_gain_grad.reshape(devices, -1),
            kv_gain_grad.reshape(devices, -1),
            router_grad[:, :experts].reshape(devices, -1),
        ],
        devices,
    )

    def halves(a, columns):
        part = columns // 256 * 128
        return [(a, 0, part, ("p", "r")), (a, part, columns - part, ("r", "p"))]

    attention_sums = Scatter(
        grid,
        [
            q_weight_grad.reshape((devices,) + q_sent.shape),
            kv_down_grad.reshape((devices,) + down_sent.shape),
            kv_up_grad.reshape((devices,) + up_sent.shape),
            out_weight_grad.reshape((devices,) + out_weight.shape),
            small_grads,
        ],
        halves(0, q_sent.shape[1])
        + halves(1, down_sent.shape[1])
        + halves(2, up_sent.shape[1])
        + halves(3, out_weight.shape[1])
        + [(4, 0, 128, ("p", "r"))],
        [[3], [2, 1], [0, 4]],
    )
    experts_grads = Assemble(
        grid,
        own_ab,
        own_down,
        [got_ab[step] for step in range(dp_size - 1)],
        [got_down[step] for step in range(dp_size - 1)],
        eff,
    )
    (q_sum, down_sum, up_sum, out_weight_sum, small_sum), experts_grads = together(
        grid, [attention_sums, experts_grads], 5, "scatter_attention_assemble"
    )
    small_sums = unpack(small_sum[None], small_shapes)
    q_sum = jnp.concatenate(
        [
            q_sum[:, :WIDE].reshape(rows, HEADS, NOPE),
            q_sum[:, WIDE : WIDE + TURN].reshape(rows, HEADS, HALF),
            q_sum[:, WIDE + TURN :].reshape(rows, HEADS, HALF),
        ],
        2,
    ).reshape(q_weight.shape)
    down_sum = jnp.concatenate(
        [down_sum[:, : RANK + HALF], down_sum[:, RANK + 128 : RANK + 128 + HALF]], 1
    )

    shared_back = lax.all_to_all(
        shared_in_grad.reshape(devices, -1, 2 * share),
        ("dp", "expert"), split_axis=0, concat_axis=0, tiled=True,
    ).astype(F32)
    shared_back = shared_back.transpose(1, 0, 2)
    shared_gate_grad = shared_back[:, :, :share].reshape(shared_gate.shape)
    shared_up_grad = shared_back[:, :, share:].reshape(shared_up.shape)

    return (
        result.astype(BF).reshape(tokens.shape),
        tokens_grad.reshape(tokens.shape),
        small_sums[0].reshape(-1),
        q_sum,
        down_sum,
        small_sums[2].reshape(-1),
        up_sum.reshape(up_shape),
        out_weight_sum,
        small_sums[1].reshape(-1),
        small_sums[3].reshape(router.shape),
        shared_gate_grad,
        shared_up_grad,
        shared_down_grad,
        experts_grads[0][None],
        experts_grads[1][None],
        experts_grads[2][None],
    )


def solution(mesh):
    return jax.shard_map(
        functools.partial(body, Grid(mesh)),
        mesh=mesh,
        in_specs=(
            P(None, ("dp", "expert"), None, None),
            P(None, ("dp", "expert"), None, None),
            P(None, ("dp", "expert"), None, None),
            P(None, ("dp", "expert"), None),
            P(("dp", "expert")),
            P(("dp", "expert"), None),
            P(("dp", "expert"), None),
            P(("dp", "expert")),
            P(("dp", "expert"), None),
            P(("dp", "expert"), None),
            P(("dp", "expert")),
            P(("dp", "expert"), None),
            P(("dp", "expert"), None),
            P(("dp", "expert"), None),
            P(("dp", "expert"), None),
            P("expert", "dp", None),
            P("expert", "dp", None),
            P("expert", None, "dp"),
        ),
        out_specs=(
            P(None, ("dp", "expert"), None, None),
            P(None, ("dp", "expert"), None, None),
            P(("dp", "expert")),
            P(("dp", "expert"), None),
            P(("dp", "expert"), None),
            P(("dp", "expert")),
            P(("dp", "expert"), None),
            P(("dp", "expert"), None),
            P(("dp", "expert")),
            P(("dp", "expert"), None),
            P(("dp", "expert"), None),
            P(("dp", "expert"), None),
            P(("dp", "expert"), None),
            P("expert", "dp", None),
            P("expert", "dp", None),
            P("expert", None, "dp"),
        ),
        check_vma=False,
    )
```

```python
import functools

import jax
import jax.numpy as jnp
import numpy as np
from jax import lax
from jax.experimental import pallas as pl
from jax.experimental.pallas import tpu as pltpu
from jax.sharding import PartitionSpec as P

D = 2048
HEADS = 16
NOPE = 128
ROPE = 64
VDIM = 128
RANK = 512
TOP = 6
SEQ = 64
MICRO = 2

EPSILON = 1e-06
ROPE_BASE = 10000.0
MASKED = -1e30
BF = jnp.bfloat16
F32 = jnp.float32

MESH_ID = pl.DeviceIdType.MESH


class Grid:
    def __init__(self, mesh):
        self.experts = mesh.shape["expert"]
        self.size = {"p": mesh.shape["dp"], "r": self.experts // 8, "q": 4}
        self.devices = self.size["p"] * self.experts

    def here(self):
        e = lax.axis_index("expert")
        r_size = self.size["r"]
        return {
            "p": lax.axis_index("dp"),
            "q": lax.div(e, 2 * r_size),
            "r": lax.rem(lax.div(e, 2), r_size),
            "c": lax.rem(e, 2),
        }

    def shift(self, at, offsets):
        moved = dict(at)
        for axis, step in offsets.items():
            if step:
                moved[axis] = lax.rem(at[axis] + step, self.size[axis])
        return moved

    def expert_of(self, at):
        return at["q"] * (2 * self.size["r"]) + at["r"] * 2 + at["c"]

    def number(self, at):
        return at["p"] * self.experts + self.expert_of(at)

    def mesh_id(self, at):
        return (at["p"], self.expert_of(at))

    def device_id(self, number):
        return (lax.div(number, self.experts), lax.rem(number, self.experts))

    def partners(self, at):
        found = [{**at, "c": 1 - at["c"]}]
        for axis, size in self.size.items():
            found += [self.shift(at, {axis: step}) for step in range(1, size)]
        return found


def greet(grid, at, everyone):
    barrier = pltpu.get_barrier_semaphore()
    partners = [grid.mesh_id(partner) for partner in grid.partners(at)]
    if everyone:
        me = grid.number(at)
        partners = [
            grid.device_id(lax.rem(me + step, grid.devices)) for step in range(1, grid.devices)
        ]
    for partner in partners:
        pl.semaphore_signal(barrier, inc=1, device_id=partner, device_id_type=MESH_ID)
    pl.semaphore_wait(barrier, len(partners))


ALONG = (0, -1, 1, -2, 2, -3, 3)


def span_of(grid, axis):
    return ALONG if axis == "q" else tuple(range(grid.size[axis]))


class Gather:
    def __init__(self, grid, arrays, items):
        count = len(items)
        slots = grid.devices // 2 // 4 * len(ALONG)
        self.grid, self.items = grid, items
        self.inputs = list(arrays)
        self.in_specs = [pl.BlockSpec(memory_space=pl.ANY)] * len(arrays)
        self.out_shapes = [
            jax.ShapeDtypeStruct((grid.devices,) + a.shape, a.dtype) for a in arrays
        ]
        self.out_specs = [pl.BlockSpec(memory_space=pl.ANY)] * len(arrays)
        self.scratch = [
            pltpu.SemaphoreType.DMA((count * slots * 2,)),
            pltpu.SemaphoreType.DMA((count, slots)),
            pltpu.SemaphoreType.DMA((count, slots)),
            pltpu.SemaphoreType.DMA((count, slots)),
            pltpu.SemaphoreType.DMA((len(arrays),)),
        ]

    def steps(self, at, ins, outs, scratch):
        grid, items = self.grid, self.items
        count = len(items)
        send_sem, recv_sem, core_send, core_recv, own_sem = scratch
        sibling = {**at, "c": 1 - at["c"]}
        q_size = grid.size["q"]
        pending = []
        me = grid.number(at)

        def inside(step):
            return jnp.logical_and(at["q"] + step >= 0, at["q"] + step < q_size)

        def guarded(step, action):
            if step:
                pl.when(inside(step))(action)
            else:
                action()

        def q_part(i, offset):
            return offset[items[i][3].index("q")]

        def slot(i, offset):
            number = 0
            for axis, part in zip(items[i][3], offset):
                span = span_of(grid, axis)
                number = number * len(span) + span.index(part)
            return number

        def block_of(i, offset, base):
            moved = dict(base)
            for axis, part in zip(items[i][3], offset):
                if part:
                    moved[axis] = (
                        base[axis] + part
                        if axis == "q"
                        else lax.rem(base[axis] + part, grid.size[axis])
                    )
            return grid.number(moved)

        def views(i, offset, base):
            a, first, width, order = items[i]
            columns = pl.ds(first, width)
            view = outs[a].at[block_of(i, offset, base), :, columns]
            return (ins[a].at[:, columns] if offset == (0, 0, 0) else view), view

        def send(i, offset, landed, target_step, cond_step):
            number = len(pending)

            def copy():
                source, view = views(i, offset, at)
                return pltpu.make_async_remote_copy(
                    src_ref=source,
                    dst_ref=view,
                    send_sem=send_sem.at[number],
                    recv_sem=recv_sem.at[i, slot(i, landed)],
                    device_id=grid.mesh_id(target_step()),
                    device_id_type=MESH_ID,
                )

            guarded(cond_step, lambda: copy().start())
            pending.append((q_part(i, offset), cond_step, copy))

        def forward(i, offset, stage):
            axis = items[i][3][stage]
            if axis == "q":
                part = offset[stage]
                for step in (1, -1) if part == 0 else (1,) if part < 0 else (-1,):
                    if abs(part - step) < q_size:
                        landed = offset[:stage] + (part - step,) + offset[stage + 1 :]
                        send(
                            i, offset, landed, lambda step=step: {**at, "q": at["q"] + step}, step
                        )
                return
            for step in range(1, grid.size[axis]):
                part = (offset[stage] - step) % grid.size[axis]
                landed = offset[:stage] + (part,) + offset[stage + 1 :]
                send(i, offset, landed, lambda step=step: grid.shift(at, {axis: step}), 0)

        def across(i, offset):
            def copy():
                source, view = views(i, offset, at)
                return pltpu.make_async_remote_copy(
                    src_ref=source,
                    dst_ref=view,
                    send_sem=core_send.at[i, slot(i, offset)],
                    recv_sem=core_recv.at[i, slot(i, offset)],
                    device_id=grid.mesh_id(sibling),
                    device_id_type=MESH_ID,
                )

            copy().start()
            pending.append((q_part(i, offset), 0, copy))

        def landed_at(i, offset, base, sem):
            view = views(i, offset, base)[1]
            pltpu.make_async_copy(view, view, sem.at[i, slot(i, offset)]).wait()

        def take(i, offset, stage):
            def action():
                landed_at(i, offset, at, recv_sem)
                if items[i][3][stage] == "q":
                    forward(i, offset, stage)
                for later in range(stage + 1, 3):
                    forward(i, offset, later)
                across(i, offset)

            guarded(q_part(i, offset), action)

        ranges = [[span_of(grid, axis) for axis in item[3]] for item in items]
        offsets = [
            (i, (u, v, w))
            for i in range(count)
            for u in ranges[i][0]
            for v in ranges[i][1]
            for w in ranges[i][2]
        ]
        todo = []
        for i, offset in offsets:
            if any(offset):
                stage = max(k for k in range(3) if offset[k])
                todo.append((stage,) + tuple(abs(part) for part in offset) + (i, offset))
        yield len(todo) + 1

        own_copies = []
        for a in range(len(ins)):
            own = pltpu.make_async_copy(ins[a], outs[a].at[me], own_sem.at[a])
            own.start()
            own_copies.append(own)
        for i in range(count):
            for stage in range(3):
                forward(i, (0, 0, 0), stage)
            across(i, (0, 0, 0))
        yield
        for stage, _, _, _, i, offset in sorted(todo):
            take(i, offset, stage)
            yield
        for own in own_copies:
            own.wait()
        for i, offset in offsets:
            guarded(
                q_part(i, offset), functools.partial(landed_at, i, offset, sibling, core_recv)
            )
        for q_step, cond_step, copy in pending:
            guarded(q_step, functools.partial(guarded, cond_step, lambda: copy().wait_send()))


def add_rows(target, *parts):
    rows = target.shape[0]
    step = min(16, rows)

    @pl.loop(0, rows // step)
    def _(k):
        block = pl.ds(pl.multiple_of(k * step, step), step)
        total = parts[0][block, :].astype(F32)
        for part in parts[1:]:
            total = total + part[block, :].astype(F32)
        target[block, :] = total.astype(target.dtype)


DEPTH = 2
AHEAD = 4


class Scatter:
    def __init__(self, grid, arrays, items, rounds):
        count = len(items)
        chips = grid.devices // 2
        q_size = grid.size["q"]
        self.grid, self.items, self.rounds = grid, items, rounds
        self.inputs = list(arrays)
        self.in_specs = [pl.BlockSpec(memory_space=pl.ANY)] * len(arrays)
        self.out_shapes = [jax.ShapeDtypeStruct(a.shape[1:], F32) for a in arrays]
        self.out_specs = [pl.BlockSpec(memory_space=pltpu.VMEM)] * len(arrays)
        scratch = [pltpu.VMEM((chips,) + a.shape[1:], a.dtype) for a in arrays]
        scratch += [pltpu.VMEM((2 * AHEAD,) + a.shape[1:], a.dtype) for a in arrays]
        most = 0
        for a, _, width, order in items:
            n1, n2 = (grid.size[axis] for axis in order)
            shares = ((n1 - 1) * n2 * q_size, (n2 - 1) * q_size, q_size)
            most = max(most, shares[0] + shares[1])
            for share in shares:
                scratch.append(pltpu.VMEM((share, arrays[a].shape[1], width), arrays[a].dtype))
        self.scratch = scratch + [
            pltpu.SemaphoreType.DMA((len(arrays), chips)),
            pltpu.SemaphoreType.DMA((len(arrays), chips)),
            pltpu.SemaphoreType.DMA((len(arrays), chips)),
            pltpu.SemaphoreType.DMA((count, most)),
            pltpu.SemaphoreType.DMA((count, most)),
            pltpu.SemaphoreType.DMA((count, q_size)),
            pltpu.SemaphoreType.DMA((count, q_size)),
        ]

    def steps(self, at, ins, outs, scratch):
        grid, items = self.grid, self.items
        count, arrays = len(items), len(ins)
        held, crossed = scratch[:arrays], scratch[arrays : 2 * arrays]
        landing = scratch[2 * arrays : 2 * arrays + 3 * count]
        load_sem, core_send, core_recv, send_sem, recv_sem, line_send, line_recv = scratch[
            2 * arrays + 3 * count :
        ]
        sibling = {**at, "c": 1 - at["c"]}
        size = grid.size
        q_size = size["q"]

        def flat(block):
            p, r, t = block
            return (p * size["r"] + r) * q_size + t

        def owner(base, block):
            p, r, t = block
            return grid.number({**grid.shift(base, {"p": p, "r": r}), "q": t})

        targets = []
        for t in range(q_size // 2):
            targets += [t, q_size - 1 - t]
        near_blocks = []
        for t in targets:
            near = [(p, r, t) for p in range(size["p"]) for r in range(size["r"])]
            near_blocks += sorted(near, key=lambda b: -(b[0] > 0) - (b[1] > 0))
        blocks = [(n, block) for n in range(len(self.rounds)) for block in near_blocks]
        round_of = {a: n for n, members in enumerate(self.rounds) for a in members}

        def load(a, block):
            return pltpu.make_async_copy(
                ins[a].at[owner(at, block)], held[a].at[flat(block)], load_sem.at[a, flat(block)]
            )

        def crossed_at(a, block):
            return crossed[a].at[near_blocks.index(block) % (2 * AHEAD)]

        def across(a, block):
            return pltpu.make_async_remote_copy(
                src_ref=ins[a].at[owner(sibling, block)],
                dst_ref=crossed_at(a, block),
                send_sem=core_send.at[a, flat(block)],
                recv_sem=core_recv.at[a, flat(block)],
                device_id=grid.mesh_id(sibling),
                device_id_type=MESH_ID,
            )

        def begin(number):
            if number < len(blocks):
                n, block = blocks[number]
                for a in self.rounds[n]:
                    across(a, block).start()
                    load(a, block).start()

        merged = [0]

        def merge_to(n, block):
            while merged[0] <= blocks.index((n, block)):
                turn, now = blocks[merged[0]]
                for a in self.rounds[turn]:
                    load(a, now).wait()
                    across(a, now).wait_recv()
                    view = held[a].at[flat(now)]
                    add_rows(view, view, crossed_at(a, now))
                begin(merged[0] + AHEAD)
                merged[0] += 1

        def held_view(i, block):
            return held[items[i][0]].at[flat(block), :, pl.ds(items[i][1], items[i][2])]

        def block_at(i, first, second, t):
            part = dict(zip(items[i][3], (first, second)))
            return (part["p"], part["r"], t)

        def landing_slot(i, stage, steps, t):
            n2 = size[items[i][3][1]]
            if stage == 0:
                return ((steps[0] - 1) * n2 + steps[1]) * q_size + t
            return (steps[1] - 1) * q_size + t

        pending = []

        def send(i, stage, steps, t):
            n1, n2 = (size[axis] for axis in items[i][3])
            slot = landing_slot(i, stage, steps, t)
            sem = slot if stage == 0 else (n1 - 1) * n2 * q_size + slot
            return pltpu.make_async_remote_copy(
                src_ref=held_view(i, block_at(i, *steps, t)),
                dst_ref=landing[3 * i + stage].at[slot],
                send_sem=send_sem.at[i, sem],
                recv_sem=recv_sem.at[i, sem],
                device_id=grid.mesh_id(grid.shift(at, {items[i][3][stage]: steps[stage]})),
                device_id_type=MESH_ID,
            )

        def start(i, stage, steps, t):
            copy = send(i, stage, steps, t)
            copy.start()
            pending.append(copy)

        def receive(i, stage, steps, t):
            send(i, stage, steps, t).wait_recv()
            into = (0, steps[1]) if stage == 0 else (0, 0)
            view = held_view(i, block_at(i, *into, t))
            add_rows(view, view, landing[3 * i + stage].at[landing_slot(i, stage, steps, t)])

        def line(i, t):
            return pltpu.make_async_remote_copy(
                src_ref=held_view(i, (0, 0, t)),
                dst_ref=landing[3 * i + 2].at[at["q"]],
                send_sem=line_send.at[i, t],
                recv_sem=line_recv.at[i, at["q"]],
                device_id=grid.mesh_id({**at, "q": t}),
                device_id_type=MESH_ID,
            )

        def close(i, t):
            for second in range(1, size[items[i][3][1]]):
                receive(i, 1, (0, second), t)
            pl.when(at["q"] != t)(lambda: line(i, t).start())

        def finish(i):
            a, first, width, _ = items[i]
            parts = [held[a].at[at["q"], :, pl.ds(first, width)]]
            for step in range(1, q_size):
                source = lax.rem(at["q"] + step, q_size)
                view = landing[3 * i + 2].at[source]
                pltpu.make_async_copy(view, view, line_recv.at[i, source]).wait()
                parts.append(view)
            add_rows(outs[a].at[:, pl.ds(first, width)], *parts)

        ticks = []
        for n, members in enumerate(self.rounds):
            mine = [i for i in range(count) if items[i][0] in members]
            for t in targets:
                for far in (True, False):
                    turn = []
                    for i in mine:
                        n1, n2 = (size[axis] for axis in items[i][3])
                        for second in range(1, n2) if far else (0,):
                            for first in range(1, n1):
                                turn.append((i, (first, second), t))
                    ticks.append((n, turn, None if far else (mine, t)))
        yield sum(2 * len(turn) for _, turn, _ in ticks) + q_size * count + count

        for number in range(AHEAD):
            begin(number)
        closing, finishing = [], []
        for k in range(len(ticks) + DEPTH):
            if k < len(ticks):
                n, turn, _ = ticks[k]
                for i, steps, t in turn:
                    merge_to(n, block_at(i, *steps, t))
                    start(i, 0, steps, t)
                    yield
            if k >= DEPTH:
                n, turn, done = ticks[k - DEPTH]
                for i, steps, t in turn:
                    merge_to(n, block_at(i, 0, steps[1], t))
                    receive(i, 0, steps, t)
                    if steps[1] and steps[0] == size[items[i][3][0]] - 1:
                        start(i, 1, (0, steps[1]), t)
                    yield
                if closing and done is None:
                    for i in closing[0][0]:
                        close(i, closing[0][1])
                        yield
                    if closing[0][1] == targets[-1]:
                        finishing.append(closing[0][0])
                    closing.pop()
                    if len(finishing) > 1:
                        for i in finishing.pop(0):
                            finish(i)
                            yield
                if done is not None:
                    closing.append(done)
        for mine, t in closing:
            for i in mine:
                close(i, t)
                yield
            finishing.append(mine)
        for mine in finishing:
            for i in mine:
                finish(i)
                yield
        for n, block in blocks:
            for a in self.rounds[n]:
                across(a, block).wait_send()
        for copy in pending:
            copy.wait_send()
        for i in range(count):
            for t in range(q_size):
                pl.when(at["q"] != t)(lambda: line(i, t).wait_send())


def together(grid, parts, collective_id, name):
    def kernel(*refs):
        at = grid.here()
        if collective_id is not None:
            greet(grid, at, any(isinstance(part, AllToAll) for part in parts))
        ins, outs, scratch = [], [], []
        for list_of, key in ((ins, "inputs"), (outs, "out_shapes"), (scratch, "scratch")):
            for part in parts:
                count = len(getattr(part, key))
                list_of.append(refs[:count])
                refs = refs[count:]
        running = []
        for part, *its in zip(parts, ins, outs, scratch):
            steps = part.steps(at, *its)
            running.append([steps, next(steps), 0])
        while running:
            now = min(running, key=lambda entry: entry[2] / entry[1])
            now[2] += 1
            if next(now[0], "end") == "end":
                running.remove(now)

    outs = pl.pallas_call(
        kernel,
        out_shape=[shape for part in parts for shape in part.out_shapes],
        in_specs=[spec for part in parts for spec in part.in_specs],
        out_specs=[spec for part in parts for spec in part.out_specs],
        scratch_shapes=[entry for part in parts for entry in part.scratch],
        compiler_params=pltpu.CompilerParams(
            collective_id=collective_id,
            has_side_effects=collective_id is not None,
            vmem_limit_bytes=62 * 2**20,
        ),
        name=name,
    )(*[array for part in parts for array in part.inputs])
    split = []
    for part in parts:
        split.append(outs[: len(part.out_shapes)])
        outs = outs[len(part.out_shapes) :]
    return split


GROUP = 256


def tiles(extent, width):
    def wrap(action):
        width_now = min(width, extent)

        @pl.loop(0, extent // width_now)
        def _(k):
            action(pl.ds(pl.multiple_of(k * width_now, width_now), width_now))

    return wrap


def window_start(peer, peers, window, eff):
    return pl.multiple_of(peer * window - lax.div(peer, peers - 1) * (peers * window - eff), 128)


class Experts:
    def __init__(self, grid, hidden, grad, share, weights, capacity):
        own, got, shared_in, shared_down = weights
        self.grid = grid
        self.peers = grid.size["p"]
        self.eff = own[0].shape[1]
        self.extent = own[0].shape[0]
        count = hidden.shape[0]
        window = got[0].shape[2]
        self.supers = count // (2 * GROUP)
        self.slots = GROUP // SEQ * capacity
        self.capacity = capacity
        self.window = window
        rows = 2 * self.slots
        total = self.supers * rows
        groups = count // GROUP
        self.inputs = [hidden, grad, share, *own, *got, shared_in, shared_down]
        hbm = pl.BlockSpec(memory_space=pl.ANY)
        vmem = pl.BlockSpec(memory_space=pltpu.VMEM)
        self.in_specs = [hbm, hbm, vmem] + [hbm] * 6 + [vmem] * 2
        shared_width = shared_in.shape[1]
        kept = [(rows, D), (rows, D), (rows, 2 * window), (rows, window)]
        kept += [(2 * GROUP, shared_width), (2 * GROUP, shared_width // 2)]
        self.out_shapes = [
            jax.ShapeDtypeStruct((count, D), BF),
            jax.ShapeDtypeStruct((count, D), BF),
            jax.ShapeDtypeStruct((groups, GROUP), F32),
        ] + [jax.ShapeDtypeStruct((self.supers * r, c), BF) for r, c in kept]
        self.out_specs = [hbm, hbm, vmem] + [hbm] * len(kept)
        self.scratch = (
            [pltpu.VMEM((2 * GROUP, D), BF)] * 2
            + [pltpu.VMEM((2, r, c), BF) for r, c in kept]
            + [pltpu.VMEM((2, GROUP, D), BF)] * 2
            + [pltpu.VMEM((rows, window), F32)] * 3
            + [pltpu.VMEM((rows, D), BF)] * 2
            + [
                pltpu.VMEM((groups, GROUP), F32),
                pltpu.VMEM((2, self.slots, GROUP), BF),
                pltpu.VMEM((2, GROUP, self.slots), BF),
                pltpu.VMEM((rows, 1), F32),
                pltpu.VMEM((rows, 1), F32),
                pltpu.VMEM((2 * GROUP, shared_width), F32),
                pltpu.SemaphoreType.DMA((2,)),
                pltpu.SemaphoreType.DMA((len(kept), 2)),
                pltpu.SemaphoreType.DMA((2, 2)),
                pltpu.VMEM((D, window), BF),
                pltpu.VMEM((D, window), BF),
                pltpu.VMEM((window, D), BF),
                pltpu.SemaphoreType.DMA((3, self.peers)),
            ]
        )

    def steps(self, at, ins, outs, scratch):
        hidden, grad, share = ins[:3]
        own, got = ins[3:6], ins[6:9]
        shared_in, shared_down = ins[9:]
        hidden_out, out_out, gate_grad = outs[:3]
        kept_out = outs[3:]
        hidden_in, grad_in = scratch[:2]
        kept = scratch[2:8]
        parts = scratch[8:10]
        a_pre, b_pre, flow = scratch[10:13]
        row_grad, expert_out = scratch[13:15]
        keys, picks, picks_t, share_rows, gate_rows, shared_pre = scratch[15:21]
        load_sem, keep_sem, part_sem, gate, up, down, weight_sem = scratch[21:]
        slots, window, supers = self.slots, self.window, self.supers
        rows = 2 * slots
        half = shared_in.shape[1] // 2
        yield supers * 12

        def load(k):
            piece = pl.ds(k * 2 * GROUP, 2 * GROUP)
            return (
                pltpu.make_async_copy(hidden.at[piece, :], hidden_in, load_sem.at[0]),
                pltpu.make_async_copy(grad.at[piece, :], grad_in, load_sem.at[1]),
            )

        def keep(n, k):
            extent = kept[n].shape[1]
            return pltpu.make_async_copy(
                kept[n].at[k % 2],
                kept_out[n].at[pl.ds(k * extent, extent), :],
                keep_sem.at[n, k % 2],
            )

        def put(n, k, j):
            target = (hidden_out, out_out)[n]
            piece = pl.ds((2 * k + j) * GROUP, GROUP)
            return pltpu.make_async_copy(parts[n].at[j], target.at[piece, :], part_sem.at[n, j])

        me, peers, extent = at["p"], self.peers, self.extent
        first = window_start(me, peers, window, self.eff)
        weight_copies = []
        for n, weight in enumerate((gate, up, down)):
            for step in range(peers):
                peer = lax.rem(me + peers - step, peers)
                share_of_d = pl.ds(pl.multiple_of(peer * extent, extent), extent)
                target = weight.at[:, share_of_d] if n == 2 else weight.at[share_of_d, :]
                if step:
                    source = got[n].at[step - 1]
                else:
                    units = pl.ds(first, window)
                    source = own[n].at[units, :] if n == 2 else own[n].at[:, units]
                weight_copies.append(
                    pltpu.make_async_copy(source, target, weight_sem.at[n, step])
                )
        for copy in load(0):
            copy.start()
        for copy in weight_copies:
            copy.start()
        row_of = lax.broadcasted_iota(jnp.int32, (GROUP, GROUP), 0)
        column_of = lax.broadcasted_iota(jnp.int32, (GROUP, GROUP), 1)
        same = lax.div(row_of, SEQ) == lax.div(column_of, SEQ)
        earlier = jnp.logical_and(same, row_of < column_of).astype(BF)
        chosen = (share[...] >= 0).astype(F32)
        place = jnp.dot(chosen.astype(BF), earlier, preferred_element_type=F32)
        sequence = lax.div(lax.broadcasted_iota(jnp.int32, place.shape, 1), SEQ).astype(F32)
        keys[...] = jnp.where(chosen > 0, place + sequence * self.capacity, -1.0)
        for copy in weight_copies:
            copy.wait()
        twice = peers * window - self.eff
        if twice:

            @pl.when(me == peers - 1)
            def _():
                gate[:, pl.ds(0, twice)] = jnp.zeros((D, twice), BF)
                up[:, pl.ds(0, twice)] = jnp.zeros((D, twice), BF)
                down[pl.ds(0, twice), :] = jnp.zeros((twice, D), BF)

        for k in range(supers):
            slot = k % 2
            rows_in, grad_rows, ab_grad, scaled, shared_grad, shared_inner = (
                buffer.at[slot] for buffer in kept
            )
            if k >= 2:
                for n in range(len(kept)):
                    keep(n, k - 2).wait()
            for j in range(2):
                key = keys[pl.ds(2 * k + j, 1), :]
                number = lax.broadcasted_iota(jnp.int32, (slots, GROUP), 0).astype(F32)
                pick = (number == key).astype(F32)
                picks[j] = pick.astype(BF)
                picks_t[j] = pick.T.astype(BF)
                weight = share[pl.ds(2 * k + j, 1), :]
                share_rows[pl.ds(j * slots, slots), :] = jnp.sum(
                    pick * weight, axis=1, keepdims=True
                )
            for copy in load(k):
                copy.wait()
            for source, target in ((hidden_in, rows_in), (grad_in, grad_rows)):
                for j in range(2):

                    @tiles(D, 2048)
                    def _(columns):
                        target[pl.ds(j * slots, slots), columns] = jnp.dot(
                            picks[j],
                            source[pl.ds(j * GROUP, GROUP), columns],
                            preferred_element_type=F32,
                        ).astype(BF)

                yield
            for weight, target in ((gate, a_pre), (up, b_pre)):

                @tiles(window, window)
                def _(columns):
                    target[:, columns] = jnp.dot(
                        rows_in[...], weight[:, columns], preferred_element_type=F32
                    )

                yield

            @tiles(window, window)
            def _(columns):
                flow[:, columns] = dot_t(grad_rows[...], down[columns, :])

            yield

            @tiles(rows, 32)
            def _(block):
                a = a_pre[block, :]
                b = b_pre[block, :]
                u = flow[block, :]
                weight = share_rows[block, :]
                sigma = jax.nn.sigmoid(a)
                act = a * sigma
                inner = (act * b).astype(BF).astype(F32)
                gate_rows[block, :] = jnp.sum(inner * u, axis=1, keepdims=True)
                scaled[block, :] = (inner * weight).astype(BF)
                u = u * weight
                ab_grad[block, pl.ds(0, window)] = (
                    u * b * (sigma * (1.0 + a * (1.0 - sigma)))
                ).astype(BF)
                ab_grad[block, pl.ds(window, window)] = (u * act).astype(BF)

            for j in range(2):
                pick = picks[j].astype(F32)
                gate_grad[pl.ds(2 * k + j, 1), :] = jnp.sum(
                    pick * gate_rows[pl.ds(j * slots, slots), :], axis=0, keepdims=True
                )
            yield

            @tiles(D, 1024)
            def _(columns):
                row_grad[:, columns] = (
                    dot_t(ab_grad[:, pl.ds(0, window)], gate[columns, :])
                    + dot_t(ab_grad[:, pl.ds(window, window)], up[columns, :])
                ).astype(BF)

            yield

            @tiles(D, 2048)
            def _(columns):
                expert_out[:, columns] = jnp.dot(
                    scaled[...], down[:, columns], preferred_element_type=F32
                ).astype(BF)

            yield

            @tiles(2 * GROUP, 2 * GROUP)
            def _(block):
                shared_pre[block, :] = jnp.dot(
                    hidden_in[block, :], shared_in[...], preferred_element_type=F32
                )

            yield

            @tiles(2 * GROUP, GROUP)
            def _(block):
                u = dot_t(grad_in[block, :], shared_down[...])
                a = shared_pre[block, pl.ds(0, half)]
                b = shared_pre[block, pl.ds(half, half)]
                sigma = jax.nn.sigmoid(a)
                act = a * sigma
                shared_inner[block, :] = (act * b).astype(BF)
                shared_grad[block, pl.ds(0, half)] = (
                    u * b * (sigma * (1.0 + a * (1.0 - sigma)))
                ).astype(BF)
                shared_grad[block, pl.ds(half, half)] = (u * act).astype(BF)

            for n in range(len(kept)):
                keep(n, k).start()
            if k + 1 < supers:
                for copy in load(k + 1):
                    copy.start()
            yield
            for j in range(2):
                if k:
                    put(0, k - 1, j).wait()

                @tiles(D, 1024)
                def _(columns):
                    parts[0][j, :, columns] = (
                        jnp.dot(
                            picks_t[j],
                            row_grad[pl.ds(j * slots, slots), columns],
                            preferred_element_type=F32,
                        )
                        + dot_t(shared_grad[pl.ds(j * GROUP, GROUP), :], shared_in[columns, :])
                    ).astype(BF)

                put(0, k, j).start()
            yield
            for j in range(2):
                if k:
                    put(1, k - 1, j).wait()

                @tiles(D, 1024)
                def _(columns):
                    parts[1][j, :, columns] = (
                        jnp.dot(
                            picks_t[j],
                            expert_out[pl.ds(j * slots, slots), columns],
                            preferred_element_type=F32,
                        )
                        + jnp.dot(
                            shared_inner[pl.ds(j * GROUP, GROUP), :],
                            shared_down[:, columns],
                            preferred_element_type=F32,
                        )
                    ).astype(BF)

                put(1, k, j).start()
            yield
        for k in range(max(0, supers - 2), supers):
            for n in range(len(kept)):
                keep(n, k).wait()
        for n in range(2):
            for j in range(2):
                put(n, supers - 1, j).wait()


class AllToAll:
    def __init__(self, grid, array):
        self.grid = grid
        self.inputs = [array]
        hbm = pl.BlockSpec(memory_space=pl.ANY)
        self.in_specs, self.out_specs = [hbm], [hbm]
        self.out_shapes = [jax.ShapeDtypeStruct(array.shape, array.dtype)]
        self.scratch = [pltpu.SemaphoreType.DMA((grid.devices,))] * 2

    def steps(self, at, ins, outs, scratch):
        grid, (send_sem, recv_sem) = self.grid, scratch
        me = grid.number(at)
        yield 8

        def copy(step):
            there = lax.rem(me + step, grid.devices)
            return pltpu.make_async_remote_copy(
                src_ref=ins[0].at[there],
                dst_ref=outs[0].at[me],
                send_sem=send_sem.at[step],
                recv_sem=recv_sem.at[step],
                device_id=grid.device_id(there),
                device_id_type=MESH_ID,
            )

        own = pltpu.make_async_copy(ins[0].at[me], outs[0].at[me], recv_sem.at[0])
        own.start()
        for k in range(8):
            for step in range(1 + k, grid.devices, 8):
                copy(step).start()
            yield
        own.wait()
        for step in range(1, grid.devices):
            copy(step).wait_send()
            back = outs[0].at[lax.rem(me - step + grid.devices, grid.devices)]
            pltpu.make_async_copy(back, back, recv_sem.at[step]).wait()


class Exchange:
    def __init__(self, grid, arrays, views, shapes, begins=(0, 0)):
        self.grid, self.views, self.begins = grid, views, begins
        self.peers = grid.size["p"]
        self.inputs = list(arrays)
        hbm = pl.BlockSpec(memory_space=pl.ANY)
        self.in_specs = [hbm] * len(arrays)
        self.out_shapes = [
            jax.ShapeDtypeStruct((self.peers - 1,) + shape, a.dtype)
            for a, shape in zip(arrays, shapes)
        ]
        self.out_specs = [hbm] * len(arrays)
        self.scratch = [pltpu.SemaphoreType.DMA((len(arrays), self.peers - 1))] * 2

    def steps(self, at, ins, outs, scratch):
        send_sem, recv_sem = scratch
        yield 20
        copies = []
        for k in range(20):
            for n, view in enumerate(self.views):
                if self.begins[n] != k:
                    continue
                for step in range(1, self.peers):
                    there = self.grid.shift(at, {"p": step})
                    copy = pltpu.make_async_remote_copy(
                        src_ref=view(ins[n], there["p"], step),
                        dst_ref=outs[n].at[step - 1],
                        send_sem=send_sem.at[n, step - 1],
                        recv_sem=recv_sem.at[n, step - 1],
                        device_id=self.grid.mesh_id(there),
                        device_id_type=MESH_ID,
                    )
                    copy.start()
                    copies.append(copy)
            yield
        for copy in copies:
            copy.wait()


SCALE = (NOPE + ROPE) ** (-0.5)
HALF = ROPE // 2
TURN = HEADS * HALF
WIDE = HEADS * NOPE


def spread():
    row = lax.broadcasted_iota(jnp.int32, (128, TURN), 0)
    lane = lax.broadcasted_iota(jnp.int32, (128, TURN), 1)
    return (lax.rem(lane, HALF) == row).astype(BF)


def of_head(h):
    lane = lax.broadcasted_iota(jnp.int32, (MICRO * SEQ, 2 * TURN), 1)
    return jnp.bitwise_and(jnp.right_shift(lane, 5), HEADS - 1) == h


def rms_scale(values):
    return lax.rsqrt(jnp.mean(values * values, -1, keepdims=True) + EPSILON)


QUERY = WIDE + 2 * TURN
ATTN_LANE, FFN_LANE = 126, 127


def weight_buffers(weights):
    q_weight, kv_down, kv_up, out_weight = weights
    shapes = [(D, QUERY), kv_down.shape, kv_up.shape, out_weight.shape, (D, 128)]
    return [pltpu.VMEM(shape, BF) for shape in shapes] + [pltpu.SemaphoreType.DMA((5,))]


def weight_loads(sources, scratch):
    q_weight, kv_down, kv_up, out_weight = sources
    views = [q_weight.at[:, pl.ds(0, QUERY)], kv_down, kv_up, out_weight]
    views.append(q_weight.at[:, pl.ds(QUERY, 128)])
    return [
        pltpu.make_async_copy(view, scratch[n], scratch[5].at[n]) for n, view in enumerate(views)
    ]


def gain_rows(router):
    turned = router[...].astype(F32).T
    return turned[ATTN_LANE : ATTN_LANE + 1], turned[FFN_LANE : FFN_LANE + 1]


def kv_gain_row(kv_up):
    return kv_up[:, pl.ds(2 * WIDE, 128)].astype(F32).T[:1]


class AttentionForward:
    def __init__(self, tokens, routes, allowed, tables, weights, experts):
        count = MICRO * SEQ
        self.experts = experts
        self.inputs = [tokens, routes, allowed, *tables, *weights]
        vmem = pl.BlockSpec(memory_space=pltpu.VMEM)
        hbm = pl.BlockSpec(memory_space=pl.ANY)
        self.in_specs = [vmem] * 5 + [hbm] * 4
        shapes = [
            ((count, D), BF), ((experts, count), F32),
            ((count, D), BF), ((count, WIDE), BF), ((count, 2 * TURN), BF), ((count, RANK), F32),
            ((count, RANK), BF), ((count, 2 * TURN), BF), ((count, 2 * WIDE), BF),
            ((HEADS, count, count), F32), ((count, WIDE), BF), ((count, D), F32),
        ]
        self.out_shapes = [jax.ShapeDtypeStruct(shape, kind) for shape, kind in shapes]
        self.out_specs = [vmem] * len(shapes)
        self.scratch = weight_buffers(weights) + [
            pltpu.VMEM((count, RANK + 256), F32),
            pltpu.VMEM((count, 2 * TURN), F32),
        ]

    def steps(self, at, ins, outs, scratch):
        tokens, routes, allowed, cosine, sine = ins[:5]
        (
            hidden, gates, normed, q_plain, q_turned, kv_low, latent, k_turned, kv, chances,
            attended, residual,
        ) = outs
        q_weight, kv_down, kv_up, out_weight, router = scratch[:5]
        kv_raw, q_raw = scratch[6:]
        yield 16
        loads = weight_loads(ins[5:], scratch)
        for n in (4, 1, 0, 2, 3):
            loads[n].start()
        loads[4].wait()
        attn_gain, ffn_gain = gain_rows(router)
        values = tokens[...].astype(F32)
        normed[...] = (values * rms_scale(values) * attn_gain).astype(BF)
        yield
        loads[1].wait()

        @tiles(RANK + 256, RANK + 256)
        def _(columns):
            kv_raw[:, columns] = dot(normed[...], kv_down[:, columns])

        low = kv_raw[:, pl.ds(0, RANK)]
        kv_low[...] = low
        loads[2].wait()
        kv_gain = kv_gain_row(kv_up)
        latent[...] = (low * rms_scale(low) * kv_gain).astype(BF)
        first, second = kv_raw[:, pl.ds(RANK, 128)], kv_raw[:, pl.ds(RANK + 128, 128)]
        c, s = cosine[:, pl.ds(0, 128)], sine[:, pl.ds(0, 128)]
        lay = spread()
        k_turned[:, pl.ds(0, TURN)] = dot((first * c - second * s).astype(BF), lay).astype(BF)
        k_turned[:, pl.ds(TURN, TURN)] = dot((second * c + first * s).astype(BF), lay).astype(BF)
        yield
        loads[0].wait()

        for k in range(2):
            columns = pl.ds(k * WIDE // 2, WIDE // 2)
            q_plain[:, columns] = dot(normed[...], q_weight[:, columns]).astype(BF)
            yield
        q_raw[...] = dot(normed[...], q_weight[:, pl.ds(WIDE, 2 * TURN)])
        first, second = q_raw[:, pl.ds(0, TURN)], q_raw[:, pl.ds(TURN, TURN)]
        q_turned[:, pl.ds(0, TURN)] = (first * cosine[...] - second * sine[...]).astype(BF)
        q_turned[:, pl.ds(TURN, TURN)] = (second * cosine[...] + first * sine[...]).astype(BF)
        yield

        @tiles(2 * WIDE, 2048)
        def _(columns):
            kv[:, columns] = dot(latent[...], kv_up[:, columns]).astype(BF)

        yield

        def head(h):
            plain = pl.ds(pl.multiple_of(h * NOPE, NOPE), NOPE)
            keys = pl.ds(pl.multiple_of(h * 2 * NOPE, NOPE), NOPE)
            both = pl.ds(pl.multiple_of(h * 2 * NOPE + NOPE, NOPE), VDIM)
            turned = jnp.where(of_head(h), q_turned[...].astype(F32), 0.0).astype(BF)
            scores = dot_t(q_plain[:, plain], kv[:, keys]) + dot_t(turned, k_turned[...])
            scores = jnp.where(allowed[...] > 0, scores * SCALE, MASKED)
            powers = jnp.exp(scores - jnp.max(scores, -1, keepdims=True))
            chance = powers / jnp.sum(powers, -1, keepdims=True)
            chances[h] = chance
            attended[:, plain] = dot(chance.astype(BF), kv[:, both]).astype(BF)

        for k in range(0, HEADS, 4):
            pl.loop(k, k + 4)(head)
            yield
        loads[3].wait()
        for k in range(2):
            columns = pl.ds(k * D // 2, D // 2)
            residual[:, columns] = tokens[:, columns].astype(F32) + dot(
                attended[...], out_weight[:, columns]
            )
            yield
        values = residual[...]
        hidden[...] = (values * rms_scale(values) * ffn_gain).astype(BF)
        logits = dot(hidden[...], router[...])
        lane = lax.broadcasted_iota(jnp.int32, logits.shape, 1)
        chosen = lane < 0
        for k in range(TOP):
            chosen = jnp.logical_or(chosen, routes[:, pl.ds(k, 1)] == lane)
        logits = jnp.where(chosen, logits, MASKED)
        powers = jnp.where(chosen, jnp.exp(logits - jnp.max(logits, -1, keepdims=True)), 0.0)
        share = powers / jnp.sum(powers, -1, keepdims=True)
        gates[...] = jnp.where(chosen, share, -1.0).T[: self.experts]
        yield


class AttentionBackward:
    def __init__(self, cotangent, hidden_sum, gate_grad, saved, tokens, tables, weights):
        count = MICRO * SEQ
        self.experts = gate_grad.shape[0]
        self.inputs = [cotangent, hidden_sum, gate_grad, *tables, *saved, tokens, *weights]
        vmem = pl.BlockSpec(memory_space=pltpu.VMEM)
        hbm = pl.BlockSpec(memory_space=pl.ANY)
        self.in_specs = [vmem] * (5 + 12 + 1) + [hbm] * 4
        self.grads = [weights[n].shape for n in (3, 2, 0, 1)]
        self.out_shapes = [jax.ShapeDtypeStruct(shape, BF) for shape in self.grads] + [
            jax.ShapeDtypeStruct((count, D), BF)
        ]
        self.out_specs = [hbm] * 4 + [vmem]
        widest = max(width for _, width in self.grads)
        self.scratch = weight_buffers(weights) + [
            pltpu.VMEM((2, 256, widest), BF),
            pltpu.VMEM((count, 128), F32),
            pltpu.VMEM((count, D), F32),
            pltpu.VMEM((count, D), F32),
            pltpu.VMEM((count, D), BF),
            pltpu.VMEM((count, WIDE), BF),
            pltpu.VMEM((count, QUERY), BF),
            pltpu.VMEM((count, 2 * WIDE), BF),
            pltpu.VMEM((count, RANK + 256), BF),
            pltpu.VMEM((count, 2 * TURN), F32),
            pltpu.VMEM((count, 2 * TURN), F32),
            pltpu.VMEM((D, 128), F32),
            pltpu.VMEM((128, D), F32),
            pltpu.VMEM((128, RANK), F32),
            pltpu.SemaphoreType.DMA((2,)),
        ]

    def steps(self, at, ins, outs, scratch):
        cotangent, hidden_sum, gate_grad, cosine, sine = ins[:5]
        (
            hidden, gates, normed, q_plain, q_turned, kv_low, latent, k_turned, kv, chances,
            attended, residual,
        ) = ins[5:17]
        tokens, tokens_grad = ins[17], outs[4]
        q_weight, kv_down, kv_up, out_weight, router = scratch[:5]
        (
            buffers, turned_gates, hidden_grad, residual_grad, mixed, attended_grad, q_grad, kv_grad,
            kv_raw_grad, q_turn_grad, k_turn_grad, router_grad, gain_grads, kv_gain_grads, out_sem,
        ) = scratch[6:]
        experts = self.experts
        yield 7 + sum(shape[0] // 256 for shape in self.grads)
        loads = weight_loads(ins[18:], scratch)
        for n in (4, 3, 2, 0, 1):
            loads[n].start()
        gain_grads[...] = jnp.zeros_like(gain_grads)
        kv_gain_grads[...] = jnp.zeros_like(kv_gain_grads)
        share = jnp.maximum(gates[...], 0.0)
        inner = jnp.sum(share * gate_grad[...], 0, keepdims=True)
        turned_gates[...] = jnp.zeros_like(turned_gates)
        turned_gates[pl.ds(0, experts), :] = share * (gate_grad[...] - inner)
        logit_grad = turned_gates[...].T.astype(BF)
        loads[4].wait()
        attn_gain, ffn_gain = gain_rows(router)

        @tiles(D, 1024)
        def _(columns):
            router_grad[columns, :] = t_dot(hidden[:, columns], logit_grad)
            hidden_grad[:, columns] = hidden_sum[:, columns] + dot_t(
                logit_grad, router[columns, :]
            )

        def norm_back(values, gain, gradient):
            scale = rms_scale(values)
            weighted = gradient * gain
            mean = jnp.mean(weighted * values, -1, keepdims=True)
            gain_grad = jnp.sum(gradient * values * scale, 0, keepdims=True)
            return scale * weighted - values * (scale * scale * scale * mean), gain_grad

        part, gain_grads[pl.ds(FFN_LANE, 1), :] = norm_back(
            residual[...], ffn_gain, hidden_grad[...]
        )
        total = cotangent[...].astype(F32) + part
        residual_grad[...] = total
        mixed[...] = total.astype(BF)
        yield
        loads[3].wait()

        @tiles(WIDE, 1024)
        def _(columns):
            attended_grad[:, columns] = dot_t(mixed[...], out_weight[columns, :]).astype(BF)

        yield
        turn = [0]
        stores = {}

        def weight_grad(n, left, right, width, beside=None):
            rows, whole = self.grads[n]
            for k in range(rows // 256):
                slot = turn[0] % 2
                turn[0] += 1
                if slot in stores:
                    stores[slot].wait()
                piece = pl.ds(k * 256, 256)

                @tiles(width, width if width < 1024 else 1024)
                def _(columns):
                    buffers[slot, :, columns] = t_dot(left[:, piece], right[:, columns]).astype(BF)

                if beside is not None:
                    lanes = beside[k * 256 : (k + 1) * 256, :]
                    buffers[slot, :, pl.ds(width, 128)] = lanes.astype(BF)
                if whole > width + 128:
                    rest = pl.ds(width + 128, whole - width - 128)
                    buffers[slot, :, rest] = jnp.zeros((256, whole - width - 128), BF)
                stores[slot] = pltpu.make_async_copy(
                    buffers.at[slot, :, pl.ds(0, whole)], outs[n].at[piece, :], out_sem.at[slot]
                )
                stores[slot].start()
                yield

        yield from weight_grad(0, attended, mixed, D)
        q_turn_grad[...] = jnp.zeros_like(q_turn_grad)
        k_turn_grad[...] = jnp.zeros_like(k_turn_grad)

        def head(h):
            plain = pl.ds(pl.multiple_of(h * NOPE, NOPE), NOPE)
            keys = pl.ds(pl.multiple_of(h * 2 * NOPE, NOPE), NOPE)
            both = pl.ds(pl.multiple_of(h * 2 * NOPE + NOPE, NOPE), VDIM)
            chance = chances[h]
            grads = attended_grad[:, plain]
            kv_grad[:, both] = t_dot(chance.astype(BF), grads).astype(BF)
            chance_grad = dot_t(grads, kv[:, both])
            mean = jnp.sum(chance * chance_grad, -1, keepdims=True)
            score_grad = (chance * (chance_grad - mean)).astype(BF)
            q_grad[:, plain] = (dot(score_grad, kv[:, keys]) * SCALE).astype(BF)
            kv_grad[:, keys] = (t_dot(score_grad, q_plain[:, plain]) * SCALE).astype(BF)
            mine = of_head(h)
            turned = jnp.where(mine, q_turned[...].astype(F32), 0.0).astype(BF)
            q_turn_grad[...] += jnp.where(mine, dot(score_grad, k_turned[...]), 0.0) * SCALE
            k_turn_grad[...] += t_dot(score_grad, turned) * SCALE

        for k in range(0, HEADS, 4):
            pl.loop(k, k + 4)(head)
            yield
        first, second = q_turn_grad[:, pl.ds(0, TURN)], q_turn_grad[:, pl.ds(TURN, TURN)]
        c, s = cosine[...], sine[...]
        q_grad[:, pl.ds(WIDE, TURN)] = (first * c + second * s).astype(BF)
        q_grad[:, pl.ds(WIDE + TURN, TURN)] = (second * c - first * s).astype(BF)
        lay = spread()

        def gathered(columns):
            values = k_turn_grad[:, columns]
            high = values.astype(BF)
            low = (values - high.astype(F32)).astype(BF)
            return dot_t(high, lay) + dot_t(low, lay)

        first, second = gathered(pl.ds(0, TURN)), gathered(pl.ds(TURN, TURN))
        c, s = cosine[:, pl.ds(0, 128)], sine[:, pl.ds(0, 128)]
        kv_raw_grad[:, pl.ds(RANK, 128)] = (first * c + second * s).astype(BF)
        kv_raw_grad[:, pl.ds(RANK + 128, 128)] = (second * c - first * s).astype(BF)
        loads[2].wait()
        latent_grad = dot_t(kv_grad[...], kv_up[:, pl.ds(0, 2 * WIDE)])
        part, kv_gain_grads[pl.ds(0, 1), :] = norm_back(
            kv_low[...], kv_gain_row(kv_up), latent_grad
        )
        kv_raw_grad[:, pl.ds(0, RANK)] = part.astype(BF)
        loads[0].wait()
        loads[1].wait()

        @tiles(D, 512)
        def _(columns):
            hidden_grad[:, columns] = dot_t(q_grad[...], q_weight[columns, :]) + dot_t(
                kv_raw_grad[...], kv_down[columns, :]
            )

        yield
        part, gain_grads[pl.ds(ATTN_LANE, 1), :] = norm_back(
            tokens[...].astype(F32), attn_gain, hidden_grad[...]
        )
        tokens_grad[...] = (residual_grad[...] + part).astype(BF)
        router_grad[...] += gain_grads[...].T
        yield from weight_grad(1, latent, kv_grad, 2 * WIDE, kv_gain_grads[...].T)
        yield from weight_grad(2, normed, q_grad, QUERY, router_grad)
        yield from weight_grad(3, normed, kv_raw_grad, RANK + 256)
        for store in stores.values():
            store.wait()


class WeightGrads:
    TILE = 256

    def __init__(self, grid, kept, extent):
        self.grid, self.extent, self.chunks = grid, extent, len(kept)
        self.inputs = [array for entry in kept for array in entry]
        rows, grad_rows, ab_grad, scaled, shared_grad, shared_inner, hidden, grad = kept[0]
        self.window = scaled.shape[1]
        hbm = pl.BlockSpec(memory_space=pl.ANY)
        self.in_specs = [hbm] * len(self.inputs)
        peers = grid.size["p"]
        window, tile = self.window, self.TILE
        self.out_shapes = [
            jax.ShapeDtypeStruct((extent, 2 * window), F32),
            jax.ShapeDtypeStruct((window, extent), F32),
            jax.ShapeDtypeStruct((peers - 1, extent, 2 * window), BF),
            jax.ShapeDtypeStruct((peers - 1, window, extent), BF),
            jax.ShapeDtypeStruct((D, shared_grad.shape[1]), BF),
            jax.ShapeDtypeStruct((shared_inner.shape[1], D), F32),
        ]
        self.out_specs = [hbm] * 6
        self.jobs = [(0, 2, True), (1, 3, False), (6, 4, True), (7, 5, False)]
        self.scratch = []
        for streamed, resident, left in self.jobs:
            a, b = kept[0][streamed], kept[0][resident]
            self.scratch.append(pltpu.VMEM((self.chunks,) + b.shape, BF))
            self.scratch.append(pltpu.VMEM((2, self.chunks, a.shape[0], tile), BF))
            shape = (tile, b.shape[1]) if left else (b.shape[1], tile)
            self.scratch.append(pltpu.VMEM((2,) + shape, F32))
            self.scratch.append(pltpu.VMEM((2,) + shape, BF))
        self.scratch += [
            pltpu.SemaphoreType.DMA((4, self.chunks)),
            pltpu.SemaphoreType.DMA((4, 2, self.chunks)),
            pltpu.SemaphoreType.DMA((4, 2)),
        ]

    def steps(self, at, ins, outs, scratch):
        tile, extent, chunks = self.TILE, self.extent, self.chunks
        peers = self.grid.size["p"]
        kept = [ins[c * 8 : (c + 1) * 8] for c in range(chunks)]
        whole_sem, tile_sem, out_sem = scratch[16:]
        own_ab, own_down, sent_ab, sent_down, shared_in, shared_down = outs

        def whole(job, c):
            return pltpu.make_async_copy(
                kept[c][self.jobs[job][1]], scratch[4 * job].at[c], whole_sem.at[job, c]
            )

        work = []
        per_peer = extent // tile
        for step in range(peers):
            for job in range(2):
                for k in range(per_peer):
                    piece = pl.ds(k * tile, tile)
                    if step == 0:
                        target = own_ab.at[piece, :] if job == 0 else own_down.at[:, piece]
                    elif job == 0:
                        target = sent_ab.at[step - 1, piece, :]
                    else:
                        target = sent_down.at[step - 1, :, piece]
                    peer = self.grid.shift(at, {"p": step})["p"]
                    first = pl.multiple_of(peer * extent + k * tile, tile)
                    work.append((job, first, target, step == 0))
        for k in range(D // tile):
            piece = pl.ds(k * tile, tile)
            work.append((2, k * tile, shared_in.at[piece, :], False))
            work.append((3, k * tile, shared_down.at[:, piece], True))
        work.sort(key=lambda entry: entry[0] >= 2)
        turns = [0] * 4
        numbered = []
        for job, first, target, wide in work:
            numbered.append((job, first, target, wide, turns[job]))
            turns[job] += 1
        yield len(work)

        def fetch(number, c):
            job, first, _, _, turn = numbered[number]
            return pltpu.make_async_copy(
                kept[c][self.jobs[job][0]].at[:, pl.ds(first, tile)],
                scratch[4 * job + 1].at[turn % 2, c],
                tile_sem.at[job, turn % 2, c],
            )

        def store(number):
            job, _, target, wide, turn = numbered[number]
            source = scratch[4 * job + (2 if wide else 3)].at[turn % 2]
            return pltpu.make_async_copy(source, target, out_sem.at[job, turn % 2])

        for c in range(chunks):
            for job in range(2):
                whole(job, c).start()
            fetch(0, c).start()
            for job in range(2, 4):
                whole(job, c).start()
        begun = set()
        last = {}
        for number, (job, _, _, wide, turn) in enumerate(numbered):
            if number + 1 < len(numbered):
                for c in range(chunks):
                    fetch(number + 1, c).start()
            if job not in begun:
                begun.add(job)
                for c in range(chunks):
                    whole(job, c).wait()
            for c in range(chunks):
                fetch(number, c).wait()
            if (job, turn % 2) in last:
                store(last[job, turn % 2]).wait()
            last[job, turn % 2] = number
            resident, streamed = scratch[4 * job], scratch[4 * job + 1].at[turn % 2]
            result = scratch[4 * job + (2 if wide else 3)].at[turn % 2]
            left = self.jobs[job][2]

            @tiles(resident.shape[2], 256)
            def _(columns):
                total = None
                for c in range(chunks):
                    if left:
                        term = t_dot(streamed[c], resident[c, :, columns])
                    else:
                        term = t_dot(resident[c, :, columns], streamed[c])
                    total = term if total is None else total + term
                if left:
                    result[:, columns] = total.astype(result.dtype)
                else:
                    result[columns, :] = total.astype(result.dtype)

            store(number).start()
            yield
        for number in last.values():
            store(number).wait()


class Assemble:
    TILE = 128

    def __init__(self, grid, own_ab, own_down, got_ab, got_down, eff):
        self.grid, self.eff = grid, eff
        self.extent = own_ab.shape[0]
        self.window = own_down.shape[0]
        self.peers = 1 + len(got_ab)
        self.inputs = [own_ab, own_down, *got_ab, *got_down]
        hbm = pl.BlockSpec(memory_space=pl.ANY)
        self.in_specs = [hbm] * len(self.inputs)
        self.out_shapes = [
            jax.ShapeDtypeStruct((self.extent, eff), F32),
            jax.ShapeDtypeStruct((self.extent, eff), F32),
            jax.ShapeDtypeStruct((eff, self.extent), F32),
        ]
        self.out_specs = [hbm] * 3
        tile, window = self.TILE, self.window
        self.scratch = [
            pltpu.VMEM((2, tile, 2 * window), F32),
            pltpu.VMEM((2, window, tile), F32),
            pltpu.VMEM((2, self.peers - 1, tile, 2 * window), BF),
            pltpu.VMEM((2, self.peers - 1, window, tile), BF),
            pltpu.VMEM((2, 2, tile, eff), F32),
            pltpu.VMEM((2, eff, tile), F32),
            pltpu.SemaphoreType.DMA((2, 2, self.peers)),
            pltpu.SemaphoreType.DMA((2, 3)),
        ]

    def steps(self, at, ins, outs, scratch):
        tile, window, peers, eff = self.TILE, self.window, self.peers, self.eff
        own = ins[:2]
        got = (ins[2 : 1 + peers], ins[1 + peers :])
        own_tiles, got_tiles = scratch[:2], scratch[2:4]
        both, down, in_sem, out_sem = scratch[4:]
        count = self.extent // tile
        yield 2 * count
        work = [(job, k) for job in range(2) for k in range(count)]

        def piece_of(array, job, k):
            piece = pl.ds(k * tile, tile)
            return array.at[piece, :] if job == 0 else array.at[:, piece]

        def fetch(job, k):
            copies = []
            for source in range(peers):
                array = own[job] if source == 0 else got[job][source - 1]
                target = own_tiles[job].at[k % 2]
                if source:
                    target = got_tiles[job].at[k % 2, source - 1]
                copies.append(
                    pltpu.make_async_copy(
                        piece_of(array, job, k), target, in_sem.at[job, k % 2, source]
                    )
                )
            return copies

        def store(job, k):
            if job:
                return [
                    pltpu.make_async_copy(
                        down.at[k % 2], piece_of(outs[2], 1, k), out_sem.at[k % 2, 2]
                    )
                ]
            return [
                pltpu.make_async_copy(
                    both.at[k % 2, n], piece_of(outs[n], 0, k), out_sem.at[k % 2, n]
                )
                for n in range(2)
            ]

        for copy in fetch(*work[0]):
            copy.start()
        for number, (job, k) in enumerate(work):
            if number + 1 < len(work):
                for copy in fetch(*work[number + 1]):
                    copy.start()
            for copy in fetch(job, k):
                copy.wait()
            if k >= 2:
                for copy in store(job, k - 2):
                    copy.wait()
            for peer in range(peers):
                first = peer * window
                width = min(window, eff - first)
                skip = window - width
                for source in range(peers):

                    @pl.when(lax.rem(at["p"] - peer + peers, peers) == source)
                    def _():
                        if source:
                            view = got_tiles[job].at[k % 2, source - 1]
                        else:
                            view = own_tiles[job].at[k % 2]
                        if job:
                            down[k % 2, pl.ds(first, width), :] = view[
                                pl.ds(skip, width), :
                            ].astype(F32)
                        else:
                            for n in range(2):
                                both[k % 2, n, :, pl.ds(first, width)] = view[
                                    :, pl.ds(n * window + skip, width)
                                ].astype(F32)

            for copy in store(job, k):
                copy.start()
            yield
        for job in range(2):
            for k in range(max(0, count - 2), count):
                for copy in store(job, k):
                    copy.wait()


def gather_all(grid, arrays, items, collective_id):
    return together(grid, [Gather(grid, arrays, items)], collective_id, "gather_all")[0]


def position_tables():
    frequency = ROPE_BASE ** (-2.0 * np.arange(HALF) / ROPE)
    angles = np.tile(np.arange(SEQ)[:, None] * frequency[None, :], (MICRO, HEADS))
    return [jnp.asarray(np.cos(angles), F32), jnp.asarray(np.sin(angles), F32)]


def capacity_for(expert_count):
    return min(SEQ, ((4 * SEQ * TOP + 3 * expert_count - 1) // (3 * expert_count) + 7) // 8 * 8)


def dot(left, right):
    return jnp.dot(left, right, preferred_element_type=F32)


def dot_t(left, right):
    return lax.dot_general(left, right, (((1,), (1,)), ((), ())), preferred_element_type=F32)


def t_dot(left, right):
    return lax.dot_general(left, right, (((0,), (0,)), ((), ())), preferred_element_type=F32)


def plain_weight_grads(grid, kept, extent):
    me = lax.axis_index("dp")
    peers = grid.size["p"]

    def total(left, right):
        return functools.reduce(jnp.add, [t_dot(entry[left], entry[right]) for entry in kept])

    def share_of(array, step, axis):
        peer = lax.rem(me + step, peers)
        return lax.dynamic_slice_in_dim(array, peer * extent, extent, axis)

    both, down = total(0, 2), total(3, 1)
    steps = range(1, peers)
    return (
        share_of(both, 0, 0),
        share_of(down, 0, 1),
        jnp.stack([share_of(both, step, 0) for step in steps]).astype(BF),
        jnp.stack([share_of(down, step, 1) for step in steps]).astype(BF),
        total(6, 4).astype(BF),
        total(5, 7),
    )


def body(
    grid,
    tokens,
    cotangent,
    routes,
    segments,
    attn_gain,
    q_weight,
    kv_down,
    kv_gain,
    kv_up,
    out_weight,
    ffn_gain,
    router,
    shared_gate,
    shared_up,
    shared_down,
    expert_gate,
    expert_up,
    expert_down,
):
    devices = grid.devices
    dp_size = grid.size["p"]
    experts = router.shape[1]
    count = MICRO * SEQ
    eff = expert_gate.shape[2]
    extent = expert_gate.shape[1]
    window = -(-eff // (128 * dp_size)) * 128
    own = (expert_gate[0], expert_up[0], expert_down[0])

    rows = q_weight.shape[0]
    q_heads = q_weight.reshape(rows, HEADS, NOPE + ROPE)
    beside = jnp.concatenate(
        [
            router,
            jnp.zeros((rows, ATTN_LANE - experts), BF),
            attn_gain[:, None],
            ffn_gain[:, None],
        ],
        1,
    )
    q_sent = jnp.concatenate(
        [
            q_heads[:, :, :NOPE].reshape(rows, WIDE),
            q_heads[:, :, NOPE : NOPE + HALF].reshape(rows, TURN),
            q_heads[:, :, NOPE + HALF :].reshape(rows, TURN),
            beside,
        ],
        1,
    )
    gap = jnp.zeros((rows, 128 - HALF), BF)
    down_sent = jnp.concatenate(
        [kv_down[:, : RANK + HALF], gap, kv_down[:, RANK + HALF :], gap], 1
    )
    up_rows = kv_up.shape[0]
    up_room = 128 * max(1, 16 // up_rows)
    up_wide = jnp.concatenate(
        [kv_up, kv_gain[:, None], jnp.zeros((up_rows, up_room - 1), BF)], 1
    )
    up_sent = up_wide if up_rows % 16 == 0 else up_wide.reshape(16, -1)

    share = shared_gate.shape[1] // devices
    room = -(-share // 128) * 128
    shared_sent = jnp.concatenate(
        [
            jnp.pad(
                half.reshape(rows, devices, share).transpose(1, 0, 2),
                ((0, 0), (0, 0), (0, room - share)),
            )
            for half in (shared_gate, shared_up)
        ],
        2,
    )
    first, second, third = ("q", "r", "p"), ("q", "p", "r"), ("p", "q", "r")

    def columns_of(ref, peer, step):
        return ref.at[:, pl.ds(window_start(peer, dp_size, window, eff), window)]

    def rows_of(ref, peer, step):
        return ref.at[pl.ds(window_start(peer, dp_size, window, eff), window), :]

    gathered, windows = together(
        grid,
        [
            Gather(
                grid,
                [q_sent, down_sent, up_sent, out_weight],
                [
                    (0, 0, q_sent.shape[1], third),
                    (1, 0, down_sent.shape[1], third),
                    (2, 0, up_sent.shape[1], ("r", "p", "q")),
                    (3, 0, D // 2, first),
                    (3, D // 2, D // 2, second),
                ],
            ),
            Exchange(grid, own[:2], [columns_of] * 2, [(extent, window)] * 2, (2, 5)),
        ],
        0,
        "gather_attention",
    )
    weights = [
        gathered[0].reshape(D, -1),
        gathered[1].reshape(D, -1),
        gathered[2].reshape(RANK, -1),
        gathered[3].reshape(-1, D),
    ]

    token_rows = tokens.reshape(count, D)
    grad_out = cotangent.reshape(count, D)
    tables = position_tables()
    numbers = segments.reshape(1, -1) + 4 * (jnp.arange(count, dtype=jnp.int32) // SEQ)[None, :]
    places = jnp.arange(count, dtype=jnp.int32)
    allowed = (numbers == numbers.T) & (places[:, None] >= places[None, :])

    def half_orders(a):
        return [(a, 0, D // 2, first), (a, D // 2, D // 2, second)]

    (grad_first,), saved, windows_down, (shared_in,) = together(
        grid,
        [
            Gather(
                grid, [grad_out[:SEQ]], [(0, 0, 1536, third), (0, 1536, 512, ("p", "r", "q"))]
            ),
            AttentionForward(
                token_rows,
                routes.reshape(count, TOP),
                allowed.astype(F32),
                tables,
                weights,
                experts,
            ),
            Exchange(grid, own[2:], [rows_of], [(window, extent)], (2,)),
            AllToAll(grid, shared_sent),
        ],
        6,
        "attention_forward",
    )
    hidden, dense_gates, residual = saved[0], saved[1], saved[11]

    shared_in = shared_in.reshape(D, 2 * room)
    shared_part = jnp.pad(shared_down, ((0, room - share), (0, 0)))

    half = D // 2
    capacity = capacity_for(experts)
    expert = lax.axis_index("expert")
    own_weights = (own, (*windows, *windows_down), shared_in, shared_part)

    def gather_of(chunk):
        piece = slice(chunk * SEQ, (chunk + 1) * SEQ)
        sent = [hidden[piece], dense_gates[:, piece]]
        orders = half_orders(0) + [(1, 0, SEQ, first)]
        if chunk:
            sent.append(grad_out[piece])
            orders += half_orders(2)
        return Gather(grid, sent, orders)

    kept_hidden, kept_grad = [], []

    def experts_of(hidden_all, gates_all, grad_all):
        kept_hidden.append(hidden_all)
        kept_grad.append(grad_all)
        share = lax.dynamic_index_in_dim(gates_all, expert, 1, keepdims=False)
        return Experts(
            grid,
            hidden_all.reshape(-1, D),
            grad_all.reshape(-1, D),
            share.reshape(-1, GROUP),
            own_weights,
            capacity,
        )

    def sums_of(done):
        hidden_part, out_part, gate_grad = done[:3]
        mine = (jnp.arange(experts, dtype=jnp.int32) == expert)[None, :, None]
        gate_grad = jnp.where(mine, gate_grad.reshape(devices, 1, SEQ), 0.0)
        shape = (devices, SEQ, D)
        return [hidden_part.reshape(shape), gate_grad, out_part.reshape(shape)]

    def kept_of(done):
        flat = [(h.reshape(-1, D), g.reshape(-1, D)) for h, g in zip(kept_hidden, kept_grad)]
        return [tuple(entry[3:]) + pair for entry, pair in zip(done, flat)]

    over = [(0, 0, half, ("p", "r")), (0, half, half, ("r", "p"))]
    over_gates = [(1, 0, SEQ, ("p", "r"))]
    over_out = [(2, 0, half, ("p", "r")), (2, half, half, ("r", "p"))]
    if devices <= 32:
        (gathered,) = together(grid, [gather_of(0)], 1, "gather_first")
        gathered, done_0 = together(
            grid,
            [gather_of(1), experts_of(*gathered, grad_first)],
            2,
            "gather_second_experts_first",
        )
        everything = over + over_gates + over_out
        sums_0, done_1 = together(
            grid,
            [Scatter(grid, sums_of(done_0), everything, [[0, 1], [2]]), experts_of(*gathered)],
            3,
            "scatter_first_experts_second",
        )
        kept = kept_of((done_0, done_1))
        sums_1, weight_grads = together(
            grid,
            [
                Scatter(grid, sums_of(done_1), everything, [[0, 1], [2]]),
                WeightGrads(grid, kept, extent),
            ],
            4,
            "scatter_second_weight_grads",
        )
        sums = (sums_0, sums_1)
    else:
        sums, done = [], []
        for chunk in range(MICRO):
            part = gather_of(chunk)
            if chunk:
                before = tuple(sums[-1])
                *part.inputs, sums[-1] = lax.optimization_barrier((*part.inputs, before))
            (gathered,) = together(grid, [part], 1 + 7 * chunk, "gather")
            part = experts_of(*gathered, *([] if chunk else [grad_first]))
            (now,) = together(grid, [part], None, "experts")
            parts = sums_of(now)
            (hidden_gates,) = together(
                grid, [Scatter(grid, parts[:2], over + over_gates, [[0, 1]])], 2, "scatter_hidden"
            )
            (out_sum,) = together(grid, [Scatter(grid, parts[2:], over, [[0]])], 3, "scatter_out")
            sums.append((*hidden_gates, *out_sum))
            done.append(now)
        weight_grads = plain_weight_grads(grid, kept_of(done), extent)
    hidden_sum = jnp.concatenate([entry[0] for entry in sums], 0)
    gate_grad = jnp.concatenate([entry[1] for entry in sums], 1)
    result = residual + jnp.concatenate([entry[2] for entry in sums], 0)
    own_ab, own_down, sent_ab, sent_down, shared_in_grad, shared_down_grad = weight_grads

    def sent_to(ref, peer, step):
        return ref.at[step - 1]

    attention_grads, (got_ab, got_down), (shared_back,) = together(
        grid,
        [
            AttentionBackward(
                grad_out, hidden_sum, gate_grad, saved, token_rows, tables, weights
            ),
            Exchange(
                grid,
                [sent_ab, sent_down],
                [sent_to] * 2,
                [(extent, 2 * window), (window, extent)],
            ),
            AllToAll(grid, shared_in_grad.reshape(devices, -1, 2 * room)),
        ],
        7,
        "attention_backward",
    )
    out_weight_grad, kv_up_grad, q_weight_grad, kv_down_grad, tokens_grad = attention_grads
    shared_down_grad = shared_down_grad[:share]

    def halves(a, columns):
        part = columns // 256 * 128
        return [(a, 0, part, ("p", "r")), (a, part, columns - part, ("r", "p"))]

    attention_sums = Scatter(
        grid,
        [
            q_weight_grad.reshape((devices,) + q_sent.shape),
            kv_down_grad.reshape((devices,) + down_sent.shape),
            kv_up_grad.reshape((devices,) + up_sent.shape),
            out_weight_grad.reshape((devices,) + out_weight.shape),
        ],
        halves(0, q_sent.shape[1])
        + halves(1, down_sent.shape[1])
        + halves(2, up_sent.shape[1])
        + halves(3, out_weight.shape[1]),
        [[3], [2, 1], [0]],
    )
    experts_grads = Assemble(
        grid,
        own_ab,
        own_down,
        [got_ab[step] for step in range(dp_size - 1)],
        [got_down[step] for step in range(dp_size - 1)],
        eff,
    )
    (q_sum, down_sum, up_sum, out_weight_sum), experts_grads = together(
        grid, [attention_sums, experts_grads], 5, "scatter_attention_assemble"
    )
    up_sum = up_sum.reshape(up_rows, -1)
    beside_sum = q_sum[:, QUERY:]
    q_sum = jnp.concatenate(
        [
            q_sum[:, :WIDE].reshape(rows, HEADS, NOPE),
            q_sum[:, WIDE : WIDE + TURN].reshape(rows, HEADS, HALF),
            q_sum[:, WIDE + TURN : QUERY].reshape(rows, HEADS, HALF),
        ],
        2,
    ).reshape(q_weight.shape)
    down_sum = jnp.concatenate(
        [down_sum[:, : RANK + HALF], down_sum[:, RANK + 128 : RANK + 128 + HALF]], 1
    )

    shared_back = shared_back.astype(F32).transpose(1, 0, 2)
    shared_gate_grad = shared_back[:, :, :share].reshape(shared_gate.shape)
    shared_up_grad = shared_back[:, :, room : room + share].reshape(shared_up.shape)
    return (
        result.astype(BF).reshape(tokens.shape),
        tokens_grad.reshape(tokens.shape),
        beside_sum[:, ATTN_LANE],
        q_sum,
        down_sum,
        up_sum[:, 2 * WIDE],
        up_sum[:, : 2 * WIDE],
        out_weight_sum,
        beside_sum[:, FFN_LANE],
        beside_sum[:, :experts],
        shared_gate_grad,
        shared_up_grad,
        shared_down_grad,
        experts_grads[0][None],
        experts_grads[1][None],
        experts_grads[2][None],
    )


def solution(mesh):
    return jax.shard_map(
        functools.partial(body, Grid(mesh)),
        mesh=mesh,
        in_specs=(
            P(None, ("dp", "expert"), None, None),
            P(None, ("dp", "expert"), None, None),
            P(None, ("dp", "expert"), None, None),
            P(None, ("dp", "expert"), None),
            P(("dp", "expert")),
            P(("dp", "expert"), None),
            P(("dp", "expert"), None),
            P(("dp", "expert")),
            P(("dp", "expert"), None),
            P(("dp", "expert"), None),
            P(("dp", "expert")),
            P(("dp", "expert"), None),
            P(("dp", "expert"), None),
            P(("dp", "expert"), None),
            P(("dp", "expert"), None),
            P("expert", "dp", None),
            P("expert", "dp", None),
            P("expert", None, "dp"),
        ),
        out_specs=(
            P(None, ("dp", "expert"), None, None),
            P(None, ("dp", "expert"), None, None),
            P(("dp", "expert")),
            P(("dp", "expert"), None),
            P(("dp", "expert"), None),
            P(("dp", "expert")),
            P(("dp", "expert"), None),
            P(("dp", "expert"), None),
            P(("dp", "expert")),
            P(("dp", "expert"), None),
            P(("dp", "expert"), None),
            P(("dp", "expert"), None),
            P(("dp", "expert"), None),
            P("expert", "dp", None),
            P("expert", "dp", None),
            P("expert", None, "dp"),
        ),
        check_vma=False,
    )
```

```python
import functools

import jax
import jax.numpy as jnp
import numpy as np
from jax import lax
from jax.experimental import pallas as pl
from jax.experimental.pallas import tpu as pltpu
from jax.sharding import PartitionSpec as P

D = 2048
HEADS = 16
NOPE = 128
ROPE = 64
VDIM = 128
RANK = 512
TOP = 6
SEQ = 64
MICRO = 2

EPSILON = 1e-06
ROPE_BASE = 10000.0
MASKED = -1e30
BF = jnp.bfloat16
F32 = jnp.float32

MESH_ID = pl.DeviceIdType.MESH


class Grid:
    def __init__(self, mesh):
        self.experts = mesh.shape["expert"]
        self.size = {"p": mesh.shape["dp"], "r": self.experts // 8, "q": 4}
        self.devices = self.size["p"] * self.experts

    def here(self):
        e = lax.axis_index("expert")
        r_size = self.size["r"]
        return {
            "p": lax.axis_index("dp"),
            "q": lax.div(e, 2 * r_size),
            "r": lax.rem(lax.div(e, 2), r_size),
            "c": lax.rem(e, 2),
        }

    def shift(self, at, offsets):
        moved = dict(at)
        for axis, step in offsets.items():
            if step:
                moved[axis] = lax.rem(at[axis] + step, self.size[axis])
        return moved

    def expert_of(self, at):
        return at["q"] * (2 * self.size["r"]) + at["r"] * 2 + at["c"]

    def number(self, at):
        return at["p"] * self.experts + self.expert_of(at)

    def mesh_id(self, at):
        return (at["p"], self.expert_of(at))

    def device_id(self, number):
        return (lax.div(number, self.experts), lax.rem(number, self.experts))

    def partners(self, at):
        found = [{**at, "c": 1 - at["c"]}]
        for axis, size in self.size.items():
            found += [self.shift(at, {axis: step}) for step in range(1, size)]
        return found


def greet(grid, at, everyone):
    barrier = pltpu.get_barrier_semaphore()
    partners = [grid.mesh_id(partner) for partner in grid.partners(at)]
    if everyone:
        me = grid.number(at)
        partners = [
            grid.device_id(lax.rem(me + step, grid.devices)) for step in range(1, grid.devices)
        ]
    for partner in partners:
        pl.semaphore_signal(barrier, inc=1, device_id=partner, device_id_type=MESH_ID)
    pl.semaphore_wait(barrier, len(partners))


ALONG = (0, -1, 1, -2, 2, -3, 3)


def span_of(grid, axis):
    return ALONG if axis == "q" else tuple(range(grid.size[axis]))


class Gather:
    def __init__(self, grid, arrays, items):
        count = len(items)
        slots = grid.devices // 2 // 4 * len(ALONG)
        self.grid, self.items = grid, items
        self.inputs = list(arrays)
        self.in_specs = [pl.BlockSpec(memory_space=pl.ANY)] * len(arrays)
        self.out_shapes = [
            jax.ShapeDtypeStruct((grid.devices,) + a.shape, a.dtype) for a in arrays
        ]
        self.out_specs = [pl.BlockSpec(memory_space=pl.ANY)] * len(arrays)
        self.scratch = [
            pltpu.SemaphoreType.DMA((count * slots * 2,)),
            pltpu.SemaphoreType.DMA((count, slots)),
            pltpu.SemaphoreType.DMA((count, slots)),
            pltpu.SemaphoreType.DMA((count, slots)),
            pltpu.SemaphoreType.DMA((len(arrays),)),
        ]

    def steps(self, at, ins, outs, scratch):
        grid, items = self.grid, self.items
        count = len(items)
        send_sem, recv_sem, core_send, core_recv, own_sem = scratch
        sibling = {**at, "c": 1 - at["c"]}
        q_size = grid.size["q"]
        pending = []
        me = grid.number(at)

        def inside(step):
            return jnp.logical_and(at["q"] + step >= 0, at["q"] + step < q_size)

        def guarded(step, action):
            if step:
                pl.when(inside(step))(action)
            else:
                action()

        def q_part(i, offset):
            return offset[items[i][3].index("q")]

        def slot(i, offset):
            number = 0
            for axis, part in zip(items[i][3], offset):
                span = span_of(grid, axis)
                number = number * len(span) + span.index(part)
            return number

        def block_of(i, offset, base):
            moved = dict(base)
            for axis, part in zip(items[i][3], offset):
                if part:
                    moved[axis] = (
                        base[axis] + part
                        if axis == "q"
                        else lax.rem(base[axis] + part, grid.size[axis])
                    )
            return grid.number(moved)

        def views(i, offset, base):
            a, first, width, order = items[i]
            columns = pl.ds(first, width)
            view = outs[a].at[block_of(i, offset, base), :, columns]
            return (ins[a].at[:, columns] if offset == (0, 0, 0) else view), view

        def send(i, offset, landed, target_step, cond_step):
            number = len(pending)

            def copy():
                source, view = views(i, offset, at)
                return pltpu.make_async_remote_copy(
                    src_ref=source,
                    dst_ref=view,
                    send_sem=send_sem.at[number],
                    recv_sem=recv_sem.at[i, slot(i, landed)],
                    device_id=grid.mesh_id(target_step()),
                    device_id_type=MESH_ID,
                )

            guarded(cond_step, lambda: copy().start())
            pending.append((q_part(i, offset), cond_step, copy))

        def forward(i, offset, stage):
            axis = items[i][3][stage]
            if axis == "q":
                part = offset[stage]
                for step in (1, -1) if part == 0 else (1,) if part < 0 else (-1,):
                    if abs(part - step) < q_size:
                        landed = offset[:stage] + (part - step,) + offset[stage + 1 :]
                        send(
                            i, offset, landed, lambda step=step: {**at, "q": at["q"] + step}, step
                        )
                return
            for step in range(1, grid.size[axis]):
                part = (offset[stage] - step) % grid.size[axis]
                landed = offset[:stage] + (part,) + offset[stage + 1 :]
                send(i, offset, landed, lambda step=step: grid.shift(at, {axis: step}), 0)

        def across(i, offset):
            def copy():
                source, view = views(i, offset, at)
                return pltpu.make_async_remote_copy(
                    src_ref=source,
                    dst_ref=view,
                    send_sem=core_send.at[i, slot(i, offset)],
                    recv_sem=core_recv.at[i, slot(i, offset)],
                    device_id=grid.mesh_id(sibling),
                    device_id_type=MESH_ID,
                )

            copy().start()
            pending.append((q_part(i, offset), 0, copy))

        def landed_at(i, offset, base, sem):
            view = views(i, offset, base)[1]
            pltpu.make_async_copy(view, view, sem.at[i, slot(i, offset)]).wait()

        def take(i, offset, stage):
            def action():
                landed_at(i, offset, at, recv_sem)
                if items[i][3][stage] == "q":
                    forward(i, offset, stage)
                for later in range(stage + 1, 3):
                    forward(i, offset, later)
                across(i, offset)

            guarded(q_part(i, offset), action)

        ranges = [[span_of(grid, axis) for axis in item[3]] for item in items]
        offsets = [
            (i, (u, v, w))
            for i in range(count)
            for u in ranges[i][0]
            for v in ranges[i][1]
            for w in ranges[i][2]
        ]
        todo = []
        for i, offset in offsets:
            if any(offset):
                stage = max(k for k in range(3) if offset[k])
                todo.append((stage,) + tuple(abs(part) for part in offset) + (i, offset))
        yield len(todo) + 1

        own_copies = []
        for a in range(len(ins)):
            own = pltpu.make_async_copy(ins[a], outs[a].at[me], own_sem.at[a])
            own.start()
            own_copies.append(own)
        for i in range(count):
            for stage in range(3):
                forward(i, (0, 0, 0), stage)
            across(i, (0, 0, 0))
        yield
        for stage, _, _, _, i, offset in sorted(todo):
            take(i, offset, stage)
            yield
        for own in own_copies:
            own.wait()
        for i, offset in offsets:
            guarded(
                q_part(i, offset), functools.partial(landed_at, i, offset, sibling, core_recv)
            )
        for q_step, cond_step, copy in pending:
            guarded(q_step, functools.partial(guarded, cond_step, lambda: copy().wait_send()))


def add_rows(target, *parts):
    rows = target.shape[0]
    step = min(16, rows)

    @pl.loop(0, rows // step)
    def _(k):
        block = pl.ds(pl.multiple_of(k * step, step), step)
        total = parts[0][block, :].astype(F32)
        for part in parts[1:]:
            total = total + part[block, :].astype(F32)
        target[block, :] = total.astype(target.dtype)


DEPTH = 2
AHEAD = 4


class Scatter:
    def __init__(self, grid, arrays, items, rounds):
        count = len(items)
        chips = grid.devices // 2
        q_size = grid.size["q"]
        self.grid, self.items, self.rounds = grid, items, rounds
        self.inputs = list(arrays)
        self.in_specs = [pl.BlockSpec(memory_space=pl.ANY)] * len(arrays)
        self.out_shapes = [jax.ShapeDtypeStruct(a.shape[1:], F32) for a in arrays]
        self.out_specs = [pl.BlockSpec(memory_space=pltpu.VMEM)] * len(arrays)
        scratch = [pltpu.VMEM((chips,) + a.shape[1:], a.dtype) for a in arrays]
        scratch += [pltpu.VMEM((2 * AHEAD,) + a.shape[1:], a.dtype) for a in arrays]
        most = 0
        for a, _, width, order in items:
            n1, n2 = (grid.size[axis] for axis in order)
            shares = ((n1 - 1) * n2 * q_size, (n2 - 1) * q_size, q_size)
            most = max(most, shares[0] + shares[1])
            for share in shares:
                scratch.append(pltpu.VMEM((share, arrays[a].shape[1], width), arrays[a].dtype))
        self.scratch = scratch + [
            pltpu.SemaphoreType.DMA((len(arrays), chips)),
            pltpu.SemaphoreType.DMA((len(arrays), chips)),
            pltpu.SemaphoreType.DMA((len(arrays), chips)),
            pltpu.SemaphoreType.DMA((count, most)),
            pltpu.SemaphoreType.DMA((count, most)),
            pltpu.SemaphoreType.DMA((count, q_size)),
            pltpu.SemaphoreType.DMA((count, q_size)),
        ]

    def steps(self, at, ins, outs, scratch):
        grid, items = self.grid, self.items
        count, arrays = len(items), len(ins)
        held, crossed = scratch[:arrays], scratch[arrays : 2 * arrays]
        landing = scratch[2 * arrays : 2 * arrays + 3 * count]
        load_sem, core_send, core_recv, send_sem, recv_sem, line_send, line_recv = scratch[
            2 * arrays + 3 * count :
        ]
        sibling = {**at, "c": 1 - at["c"]}
        size = grid.size
        q_size = size["q"]

        def flat(block):
            p, r, t = block
            return (p * size["r"] + r) * q_size + t

        def owner(base, block):
            p, r, t = block
            return grid.number({**grid.shift(base, {"p": p, "r": r}), "q": t})

        targets = []
        for t in range(q_size // 2):
            targets += [t, q_size - 1 - t]
        near_blocks = []
        for t in targets:
            near = [(p, r, t) for p in range(size["p"]) for r in range(size["r"])]
            near_blocks += sorted(near, key=lambda b: -(b[0] > 0) - (b[1] > 0))
        blocks = [(n, block) for n in range(len(self.rounds)) for block in near_blocks]
        round_of = {a: n for n, members in enumerate(self.rounds) for a in members}

        def load(a, block):
            return pltpu.make_async_copy(
                ins[a].at[owner(at, block)], held[a].at[flat(block)], load_sem.at[a, flat(block)]
            )

        def crossed_at(a, block):
            return crossed[a].at[near_blocks.index(block) % (2 * AHEAD)]

        def across(a, block):
            return pltpu.make_async_remote_copy(
                src_ref=ins[a].at[owner(sibling, block)],
                dst_ref=crossed_at(a, block),
                send_sem=core_send.at[a, flat(block)],
                recv_sem=core_recv.at[a, flat(block)],
                device_id=grid.mesh_id(sibling),
                device_id_type=MESH_ID,
            )

        def begin(number):
            if number < len(blocks):
                n, block = blocks[number]
                for a in self.rounds[n]:
                    across(a, block).start()
                    load(a, block).start()

        merged = [0]

        def merge_to(n, block):
            while merged[0] <= blocks.index((n, block)):
                turn, now = blocks[merged[0]]
                for a in self.rounds[turn]:
                    load(a, now).wait()
                    across(a, now).wait_recv()
                    view = held[a].at[flat(now)]
                    add_rows(view, view, crossed_at(a, now))
                begin(merged[0] + AHEAD)
                merged[0] += 1

        def held_view(i, block):
            return held[items[i][0]].at[flat(block), :, pl.ds(items[i][1], items[i][2])]

        def block_at(i, first, second, t):
            part = dict(zip(items[i][3], (first, second)))
            return (part["p"], part["r"], t)

        def landing_slot(i, stage, steps, t):
            n2 = size[items[i][3][1]]
            if stage == 0:
                return ((steps[0] - 1) * n2 + steps[1]) * q_size + t
            return (steps[1] - 1) * q_size + t

        pending = []

        def send(i, stage, steps, t):
            n1, n2 = (size[axis] for axis in items[i][3])
            slot = landing_slot(i, stage, steps, t)
            sem = slot if stage == 0 else (n1 - 1) * n2 * q_size + slot
            return pltpu.make_async_remote_copy(
                src_ref=held_view(i, block_at(i, *steps, t)),
                dst_ref=landing[3 * i + stage].at[slot],
                send_sem=send_sem.at[i, sem],
                recv_sem=recv_sem.at[i, sem],
                device_id=grid.mesh_id(grid.shift(at, {items[i][3][stage]: steps[stage]})),
                device_id_type=MESH_ID,
            )

        def start(i, stage, steps, t):
            copy = send(i, stage, steps, t)
            copy.start()
            pending.append(copy)

        def receive(i, stage, steps, t):
            send(i, stage, steps, t).wait_recv()
            into = (0, steps[1]) if stage == 0 else (0, 0)
            view = held_view(i, block_at(i, *into, t))
            add_rows(view, view, landing[3 * i + stage].at[landing_slot(i, stage, steps, t)])

        def line(i, t):
            return pltpu.make_async_remote_copy(
                src_ref=held_view(i, (0, 0, t)),
                dst_ref=landing[3 * i + 2].at[at["q"]],
                send_sem=line_send.at[i, t],
                recv_sem=line_recv.at[i, at["q"]],
                device_id=grid.mesh_id({**at, "q": t}),
                device_id_type=MESH_ID,
            )

        def close(i, t):
            for second in range(1, size[items[i][3][1]]):
                receive(i, 1, (0, second), t)
            pl.when(at["q"] != t)(lambda: line(i, t).start())

        def finish(i):
            a, first, width, _ = items[i]
            parts = [held[a].at[at["q"], :, pl.ds(first, width)]]
            for step in range(1, q_size):
                source = lax.rem(at["q"] + step, q_size)
                view = landing[3 * i + 2].at[source]
                pltpu.make_async_copy(view, view, line_recv.at[i, source]).wait()
                parts.append(view)
            add_rows(outs[a].at[:, pl.ds(first, width)], *parts)

        ticks = []
        for n, members in enumerate(self.rounds):
            mine = [i for i in range(count) if items[i][0] in members]
            for t in targets:
                for far in (True, False):
                    turn = []
                    for i in mine:
                        n1, n2 = (size[axis] for axis in items[i][3])
                        for second in range(1, n2) if far else (0,):
                            for first in range(1, n1):
                                turn.append((i, (first, second), t))
                    ticks.append((n, turn, None if far else (mine, t)))
        yield sum(2 * len(turn) for _, turn, _ in ticks) + q_size * count + count

        for number in range(AHEAD):
            begin(number)
        closing, finishing = [], []
        for k in range(len(ticks) + DEPTH):
            if k < len(ticks):
                n, turn, _ = ticks[k]
                for i, steps, t in turn:
                    merge_to(n, block_at(i, *steps, t))
                    start(i, 0, steps, t)
                    yield
            if k >= DEPTH:
                n, turn, done = ticks[k - DEPTH]
                for i, steps, t in turn:
                    merge_to(n, block_at(i, 0, steps[1], t))
                    receive(i, 0, steps, t)
                    if steps[1] and steps[0] == size[items[i][3][0]] - 1:
                        start(i, 1, (0, steps[1]), t)
                    yield
                if closing and done is None:
                    for i in closing[0][0]:
                        close(i, closing[0][1])
                        yield
                    if closing[0][1] == targets[-1]:
                        finishing.append(closing[0][0])
                    closing.pop()
                    if len(finishing) > 1:
                        for i in finishing.pop(0):
                            finish(i)
                            yield
                if done is not None:
                    closing.append(done)
        for mine, t in closing:
            for i in mine:
                close(i, t)
                yield
            finishing.append(mine)
        for mine in finishing:
            for i in mine:
                finish(i)
                yield
        for n, block in blocks:
            for a in self.rounds[n]:
                across(a, block).wait_send()
        for copy in pending:
            copy.wait_send()
        for i in range(count):
            for t in range(q_size):
                pl.when(at["q"] != t)(lambda: line(i, t).wait_send())


def together(grid, parts, collective_id, name):
    def kernel(*refs):
        at = grid.here()
        if collective_id is not None:
            greet(grid, at, any(isinstance(part, AllToAll) for part in parts))
        ins, outs, scratch = [], [], []
        for list_of, key in ((ins, "inputs"), (outs, "out_shapes"), (scratch, "scratch")):
            for part in parts:
                count = len(getattr(part, key))
                list_of.append(refs[:count])
                refs = refs[count:]
        running = []
        for part, *its in zip(parts, ins, outs, scratch):
            steps = part.steps(at, *its)
            running.append([steps, next(steps), 0])
        while running:
            now = min(running, key=lambda entry: entry[2] / entry[1])
            now[2] += 1
            if next(now[0], "end") == "end":
                running.remove(now)

    outs = pl.pallas_call(
        kernel,
        out_shape=[shape for part in parts for shape in part.out_shapes],
        in_specs=[spec for part in parts for spec in part.in_specs],
        out_specs=[spec for part in parts for spec in part.out_specs],
        scratch_shapes=[entry for part in parts for entry in part.scratch],
        compiler_params=pltpu.CompilerParams(
            collective_id=collective_id,
            has_side_effects=collective_id is not None,
            vmem_limit_bytes=62 * 2**20,
        ),
        name=name,
    )(*[array for part in parts for array in part.inputs])
    split = []
    for part in parts:
        split.append(outs[: len(part.out_shapes)])
        outs = outs[len(part.out_shapes) :]
    return split


GROUP = 256


def tiles(extent, width):
    def wrap(action):
        width_now = min(width, extent)

        @pl.loop(0, extent // width_now)
        def _(k):
            action(pl.ds(pl.multiple_of(k * width_now, width_now), width_now))

    return wrap


def window_start(peer, peers, window, eff):
    return pl.multiple_of(peer * window - lax.div(peer, peers - 1) * (peers * window - eff), 128)


class Experts:
    def __init__(self, grid, hidden, grad, share, weights, capacity):
        own, got, shared_in, shared_down = weights
        self.grid = grid
        self.peers = grid.size["p"]
        self.eff = own[0].shape[1]
        self.extent = own[0].shape[0]
        count = hidden.shape[0]
        window = got[0].shape[2]
        self.supers = count // (2 * GROUP)
        self.slots = GROUP // SEQ * capacity
        self.capacity = capacity
        self.window = window
        rows = 2 * self.slots
        total = self.supers * rows
        groups = count // GROUP
        self.inputs = [hidden, grad, share, *own, *got, shared_in, shared_down]
        hbm = pl.BlockSpec(memory_space=pl.ANY)
        vmem = pl.BlockSpec(memory_space=pltpu.VMEM)
        self.in_specs = [hbm, hbm, vmem] + [hbm] * 6 + [vmem] * 2
        shared_width = shared_in.shape[1]
        kept = [(rows, D), (rows, D), (rows, 2 * window), (rows, window)]
        kept += [(2 * GROUP, shared_width), (2 * GROUP, shared_width // 2)]
        self.out_shapes = [
            jax.ShapeDtypeStruct((count, D), BF),
            jax.ShapeDtypeStruct((count, D), BF),
            jax.ShapeDtypeStruct((groups, GROUP), F32),
        ] + [jax.ShapeDtypeStruct((self.supers * r, c), BF) for r, c in kept]
        self.out_specs = [hbm, hbm, vmem] + [hbm] * len(kept)
        self.scratch = (
            [pltpu.VMEM((2 * GROUP, D), BF)] * 2
            + [pltpu.VMEM((2, r, c), BF) for r, c in kept]
            + [pltpu.VMEM((2, GROUP, D), BF)] * 2
            + [pltpu.VMEM((rows, window), F32)] * 3
            + [pltpu.VMEM((rows, D), BF)] * 2
            + [
                pltpu.VMEM((groups, GROUP), F32),
                pltpu.VMEM((2, self.slots, GROUP), BF),
                pltpu.VMEM((2, GROUP, self.slots), BF),
                pltpu.VMEM((rows, 1), F32),
                pltpu.VMEM((rows, 1), F32),
                pltpu.VMEM((2 * GROUP, shared_width), F32),
                pltpu.SemaphoreType.DMA((2,)),
                pltpu.SemaphoreType.DMA((len(kept), 2)),
                pltpu.SemaphoreType.DMA((2, 2)),
                pltpu.VMEM((D, window), BF),
                pltpu.VMEM((D, window), BF),
                pltpu.VMEM((window, D), BF),
                pltpu.SemaphoreType.DMA((3, self.peers)),
            ]
        )

    def steps(self, at, ins, outs, scratch):
        hidden, grad, share = ins[:3]
        own, got = ins[3:6], ins[6:9]
        shared_in, shared_down = ins[9:]
        hidden_out, out_out, gate_grad = outs[:3]
        kept_out = outs[3:]
        hidden_in, grad_in = scratch[:2]
        kept = scratch[2:8]
        parts = scratch[8:10]
        a_pre, b_pre, flow = scratch[10:13]
        row_grad, expert_out = scratch[13:15]
        keys, picks, picks_t, share_rows, gate_rows, shared_pre = scratch[15:21]
        load_sem, keep_sem, part_sem, gate, up, down, weight_sem = scratch[21:]
        slots, window, supers = self.slots, self.window, self.supers
        rows = 2 * slots
        half = shared_in.shape[1] // 2
        yield supers * 12

        def load(k):
            piece = pl.ds(k * 2 * GROUP, 2 * GROUP)
            return (
                pltpu.make_async_copy(hidden.at[piece, :], hidden_in, load_sem.at[0]),
                pltpu.make_async_copy(grad.at[piece, :], grad_in, load_sem.at[1]),
            )

        def keep(n, k):
            extent = kept[n].shape[1]
            return pltpu.make_async_copy(
                kept[n].at[k % 2],
                kept_out[n].at[pl.ds(k * extent, extent), :],
                keep_sem.at[n, k % 2],
            )

        def put(n, k, j):
            target = (hidden_out, out_out)[n]
            piece = pl.ds((2 * k + j) * GROUP, GROUP)
            return pltpu.make_async_copy(parts[n].at[j], target.at[piece, :], part_sem.at[n, j])

        me, peers, extent = at["p"], self.peers, self.extent
        first = window_start(me, peers, window, self.eff)
        weight_copies = []
        for n, weight in enumerate((gate, up, down)):
            for step in range(peers):
                peer = lax.rem(me + peers - step, peers)
                share_of_d = pl.ds(pl.multiple_of(peer * extent, extent), extent)
                target = weight.at[:, share_of_d] if n == 2 else weight.at[share_of_d, :]
                if step:
                    source = got[n].at[step - 1]
                else:
                    units = pl.ds(first, window)
                    source = own[n].at[units, :] if n == 2 else own[n].at[:, units]
                weight_copies.append(
                    pltpu.make_async_copy(source, target, weight_sem.at[n, step])
                )
        for copy in load(0):
            copy.start()
        for copy in weight_copies:
            copy.start()
        row_of = lax.broadcasted_iota(jnp.int32, (GROUP, GROUP), 0)
        column_of = lax.broadcasted_iota(jnp.int32, (GROUP, GROUP), 1)
        same = lax.div(row_of, SEQ) == lax.div(column_of, SEQ)
        earlier = jnp.logical_and(same, row_of < column_of).astype(BF)
        chosen = (share[...] >= 0).astype(F32)
        place = jnp.dot(chosen.astype(BF), earlier, preferred_element_type=F32)
        sequence = lax.div(lax.broadcasted_iota(jnp.int32, place.shape, 1), SEQ).astype(F32)
        keys[...] = jnp.where(chosen > 0, place + sequence * self.capacity, -1.0)
        for copy in weight_copies:
            copy.wait()
        twice = peers * window - self.eff
        if twice:

            @pl.when(me == peers - 1)
            def _():
                gate[:, pl.ds(0, twice)] = jnp.zeros((D, twice), BF)
                up[:, pl.ds(0, twice)] = jnp.zeros((D, twice), BF)
                down[pl.ds(0, twice), :] = jnp.zeros((twice, D), BF)

        for k in range(supers):
            slot = k % 2
            rows_in, grad_rows, ab_grad, scaled, shared_grad, shared_inner = (
                buffer.at[slot] for buffer in kept
            )
            if k >= 2:
                for n in range(len(kept)):
                    keep(n, k - 2).wait()
            for j in range(2):
                key = keys[pl.ds(2 * k + j, 1), :]
                number = lax.broadcasted_iota(jnp.int32, (slots, GROUP), 0).astype(F32)
                pick = (number == key).astype(F32)
                picks[j] = pick.astype(BF)
                picks_t[j] = pick.T.astype(BF)
                weight = share[pl.ds(2 * k + j, 1), :]
                share_rows[pl.ds(j * slots, slots), :] = jnp.sum(
                    pick * weight, axis=1, keepdims=True
                )
            for copy in load(k):
                copy.wait()
            for source, target in ((hidden_in, rows_in), (grad_in, grad_rows)):
                for j in range(2):

                    @tiles(D, 2048)
                    def _(columns):
                        target[pl.ds(j * slots, slots), columns] = jnp.dot(
                            picks[j],
                            source[pl.ds(j * GROUP, GROUP), columns],
                            preferred_element_type=F32,
                        ).astype(BF)

                yield
            for weight, target in ((gate, a_pre), (up, b_pre)):

                @tiles(window, window)
                def _(columns):
                    target[:, columns] = jnp.dot(
                        rows_in[...], weight[:, columns], preferred_element_type=F32
                    )

                yield

            @tiles(window, window)
            def _(columns):
                flow[:, columns] = dot_t(grad_rows[...], down[columns, :])

            yield

            @tiles(rows, 32)
            def _(block):
                a = a_pre[block, :]
                b = b_pre[block, :]
                u = flow[block, :]
                weight = share_rows[block, :]
                sigma = jax.nn.sigmoid(a)
                act = a * sigma
                inner = (act * b).astype(BF).astype(F32)
                gate_rows[block, :] = jnp.sum(inner * u, axis=1, keepdims=True)
                scaled[block, :] = (inner * weight).astype(BF)
                u = u * weight
                ab_grad[block, pl.ds(0, window)] = (
                    u * b * (sigma * (1.0 + a * (1.0 - sigma)))
                ).astype(BF)
                ab_grad[block, pl.ds(window, window)] = (u * act).astype(BF)

            for j in range(2):
                pick = picks[j].astype(F32)
                gate_grad[pl.ds(2 * k + j, 1), :] = jnp.sum(
                    pick * gate_rows[pl.ds(j * slots, slots), :], axis=0, keepdims=True
                )
            yield

            @tiles(D, 1024)
            def _(columns):
                row_grad[:, columns] = (
                    dot_t(ab_grad[:, pl.ds(0, window)], gate[columns, :])
                    + dot_t(ab_grad[:, pl.ds(window, window)], up[columns, :])
                ).astype(BF)

            yield

            @tiles(D, 2048)
            def _(columns):
                expert_out[:, columns] = jnp.dot(
                    scaled[...], down[:, columns], preferred_element_type=F32
                ).astype(BF)

            yield

            @tiles(2 * GROUP, 2 * GROUP)
            def _(block):
                shared_pre[block, :] = jnp.dot(
                    hidden_in[block, :], shared_in[...], preferred_element_type=F32
                )

            yield

            @tiles(2 * GROUP, GROUP)
            def _(block):
                u = dot_t(grad_in[block, :], shared_down[...])
                a = shared_pre[block, pl.ds(0, half)]
                b = shared_pre[block, pl.ds(half, half)]
                sigma = jax.nn.sigmoid(a)
                act = a * sigma
                shared_inner[block, :] = (act * b).astype(BF)
                shared_grad[block, pl.ds(0, half)] = (
                    u * b * (sigma * (1.0 + a * (1.0 - sigma)))
                ).astype(BF)
                shared_grad[block, pl.ds(half, half)] = (u * act).astype(BF)

            for n in range(len(kept)):
                keep(n, k).start()
            if k + 1 < supers:
                for copy in load(k + 1):
                    copy.start()
            yield
            for j in range(2):
                if k:
                    put(0, k - 1, j).wait()

                @tiles(D, 1024)
                def _(columns):
                    parts[0][j, :, columns] = (
                        jnp.dot(
                            picks_t[j],
                            row_grad[pl.ds(j * slots, slots), columns],
                            preferred_element_type=F32,
                        )
                        + dot_t(shared_grad[pl.ds(j * GROUP, GROUP), :], shared_in[columns, :])
                    ).astype(BF)

                put(0, k, j).start()
            yield
            for j in range(2):
                if k:
                    put(1, k - 1, j).wait()

                @tiles(D, 1024)
                def _(columns):
                    parts[1][j, :, columns] = (
                        jnp.dot(
                            picks_t[j],
                            expert_out[pl.ds(j * slots, slots), columns],
                            preferred_element_type=F32,
                        )
                        + jnp.dot(
                            shared_inner[pl.ds(j * GROUP, GROUP), :],
                            shared_down[:, columns],
                            preferred_element_type=F32,
                        )
                    ).astype(BF)

                put(1, k, j).start()
            yield
        for k in range(max(0, supers - 2), supers):
            for n in range(len(kept)):
                keep(n, k).wait()
        for n in range(2):
            for j in range(2):
                put(n, supers - 1, j).wait()


class AllToAll:
    def __init__(self, grid, array):
        self.grid = grid
        self.inputs = [array]
        hbm = pl.BlockSpec(memory_space=pl.ANY)
        self.in_specs, self.out_specs = [hbm], [hbm]
        self.out_shapes = [jax.ShapeDtypeStruct(array.shape, array.dtype)]
        self.scratch = [pltpu.SemaphoreType.DMA((grid.devices,))] * 2

    def steps(self, at, ins, outs, scratch):
        grid, (send_sem, recv_sem) = self.grid, scratch
        me = grid.number(at)
        yield 8

        def copy(step):
            there = lax.rem(me + step, grid.devices)
            return pltpu.make_async_remote_copy(
                src_ref=ins[0].at[there],
                dst_ref=outs[0].at[me],
                send_sem=send_sem.at[step],
                recv_sem=recv_sem.at[step],
                device_id=grid.device_id(there),
                device_id_type=MESH_ID,
            )

        own = pltpu.make_async_copy(ins[0].at[me], outs[0].at[me], recv_sem.at[0])
        own.start()
        for k in range(8):
            for step in range(1 + k, grid.devices, 8):
                copy(step).start()
            yield
        own.wait()
        for step in range(1, grid.devices):
            copy(step).wait_send()
            back = outs[0].at[lax.rem(me - step + grid.devices, grid.devices)]
            pltpu.make_async_copy(back, back, recv_sem.at[step]).wait()


def chosen_lanes(height, shift, share):
    row = lax.broadcasted_iota(jnp.int32, (height, 128), 0)
    lane = lax.broadcasted_iota(jnp.int32, (height, 128), 1)
    return jnp.logical_and(row - lane == shift, lane < share).astype(BF)


class SharedColumns:
    def __init__(self, arrays, devices):
        rows, self.width = arrays[0].shape
        self.devices, self.share = devices, self.width // devices
        vmem = pl.BlockSpec(memory_space=pltpu.VMEM)
        self.inputs = list(arrays)
        self.in_specs = [vmem] * len(arrays)
        self.out_shapes = [jax.ShapeDtypeStruct((devices, rows, 128 * len(arrays)), BF)]
        self.out_specs = [vmem]
        self.scratch = []

    def steps(self, at, ins, outs, scratch):
        share = self.share
        yield self.devices
        for k in range(self.devices):
            first = share * k // 128 * 128
            width = min(256, self.width - first)
            lanes = chosen_lanes(width, share * k - first, share)
            for n, array in enumerate(ins):
                outs[0][k, :, pl.ds(128 * n, 128)] = dot(
                    array[:, pl.ds(first, width)], lanes
                ).astype(BF)
            yield


class SharedRows:
    def __init__(self, array, width):
        devices, rows, lanes = array.shape
        self.devices, self.width, self.share = devices, width, width // devices
        vmem = pl.BlockSpec(memory_space=pltpu.VMEM)
        self.inputs, self.in_specs = [array], [vmem]
        self.out_shapes = [jax.ShapeDtypeStruct((rows, width), F32)] * (lanes // 128)
        self.out_specs = [vmem] * (lanes // 128)
        self.scratch = []

    def steps(self, at, ins, outs, scratch):
        share = self.share
        yield self.width // 128
        for w in range(self.width // 128):
            totals = [None] * len(outs)
            for k in range(128 * w // share, (128 * w + 127) // share + 1):
                row = lax.broadcasted_iota(jnp.int32, (128, 128), 0)
                lane = lax.broadcasted_iota(jnp.int32, (128, 128), 1)
                place = jnp.logical_and(row - lane == 128 * w - share * k, row < share).astype(BF)
                for n in range(len(outs)):
                    term = dot(ins[0][k, :, pl.ds(128 * n, 128)], place)
                    totals[n] = term if totals[n] is None else totals[n] + term
            for out, total in zip(outs, totals):
                out[:, pl.ds(128 * w, 128)] = total
            yield


class Exchange:
    def __init__(self, grid, arrays, views, shapes, begins=(0, 0)):
        self.grid, self.views, self.begins = grid, views, begins
        self.peers = grid.size["p"]
        self.inputs = list(arrays)
        hbm = pl.BlockSpec(memory_space=pl.ANY)
        self.in_specs = [hbm] * len(arrays)
        self.out_shapes = [
            jax.ShapeDtypeStruct((self.peers - 1,) + shape, a.dtype)
            for a, shape in zip(arrays, shapes)
        ]
        self.out_specs = [hbm] * len(arrays)
        self.scratch = [pltpu.SemaphoreType.DMA((len(arrays), self.peers - 1))] * 2

    def steps(self, at, ins, outs, scratch):
        send_sem, recv_sem = scratch
        yield 20
        copies = []
        for k in range(20):
            for n, view in enumerate(self.views):
                if self.begins[n] != k:
                    continue
                for step in range(1, self.peers):
                    there = self.grid.shift(at, {"p": step})
                    copy = pltpu.make_async_remote_copy(
                        src_ref=view(ins[n], there["p"], step),
                        dst_ref=outs[n].at[step - 1],
                        send_sem=send_sem.at[n, step - 1],
                        recv_sem=recv_sem.at[n, step - 1],
                        device_id=self.grid.mesh_id(there),
                        device_id_type=MESH_ID,
                    )
                    copy.start()
                    copies.append(copy)
            yield
        for copy in copies:
            copy.wait()


SCALE = (NOPE + ROPE) ** (-0.5)
HALF = ROPE // 2
TURN = HEADS * HALF
WIDE = HEADS * NOPE


def spread():
    row = lax.broadcasted_iota(jnp.int32, (128, TURN), 0)
    lane = lax.broadcasted_iota(jnp.int32, (128, TURN), 1)
    return (lax.rem(lane, HALF) == row).astype(BF)


def of_head(h):
    lane = lax.broadcasted_iota(jnp.int32, (MICRO * SEQ, 2 * TURN), 1)
    return jnp.bitwise_and(jnp.right_shift(lane, 5), HEADS - 1) == h


def rms_scale(values):
    return lax.rsqrt(jnp.mean(values * values, -1, keepdims=True) + EPSILON)


QUERY = WIDE + 2 * TURN
ATTN_LANE, FFN_LANE = 126, 127


def weight_buffers(weights):
    q_weight, kv_down, kv_up, out_weight = weights
    shapes = [(D, QUERY), kv_down.shape, kv_up.shape, out_weight.shape, (D, 128)]
    return [pltpu.VMEM(shape, BF) for shape in shapes] + [pltpu.SemaphoreType.DMA((5,))]


def weight_loads(sources, scratch):
    q_weight, kv_down, kv_up, out_weight = sources
    views = [q_weight.at[:, pl.ds(0, QUERY)], kv_down, kv_up, out_weight]
    views.append(q_weight.at[:, pl.ds(QUERY, 128)])
    return [
        pltpu.make_async_copy(view, scratch[n], scratch[5].at[n]) for n, view in enumerate(views)
    ]


def gain_rows(router):
    turned = router[...].astype(F32).T
    return turned[ATTN_LANE : ATTN_LANE + 1], turned[FFN_LANE : FFN_LANE + 1]


def kv_gain_row(kv_up):
    return kv_up[:, pl.ds(2 * WIDE, 128)].astype(F32).T[:1]


class AttentionForward:
    def __init__(self, tokens, routes, allowed, tables, weights, experts):
        count = MICRO * SEQ
        self.experts = experts
        self.inputs = [tokens, routes, allowed, *tables, *weights]
        vmem = pl.BlockSpec(memory_space=pltpu.VMEM)
        hbm = pl.BlockSpec(memory_space=pl.ANY)
        self.in_specs = [vmem] * 5 + [hbm] * 4
        shapes = [
            ((count, D), BF), ((experts, count), F32),
            ((count, D), BF), ((count, WIDE), BF), ((count, 2 * TURN), BF), ((count, RANK), F32),
            ((count, RANK), BF), ((count, 2 * TURN), BF), ((count, 2 * WIDE), BF),
            ((HEADS, count, count), F32), ((count, WIDE), BF), ((count, D), F32),
        ]
        self.out_shapes = [jax.ShapeDtypeStruct(shape, kind) for shape, kind in shapes]
        self.out_specs = [vmem] * len(shapes)
        self.scratch = weight_buffers(weights) + [
            pltpu.VMEM((count, RANK + 256), F32),
            pltpu.VMEM((count, 2 * TURN), F32),
        ]

    def steps(self, at, ins, outs, scratch):
        tokens, routes, allowed, cosine, sine = ins[:5]
        (
            hidden, gates, normed, q_plain, q_turned, kv_low, latent, k_turned, kv, chances,
            attended, residual,
        ) = outs
        q_weight, kv_down, kv_up, out_weight, router = scratch[:5]
        kv_raw, q_raw = scratch[6:]
        yield 16
        loads = weight_loads(ins[5:], scratch)
        for n in (4, 1, 0, 2, 3):
            loads[n].start()
        loads[4].wait()
        attn_gain, ffn_gain = gain_rows(router)
        values = tokens[...].astype(F32)
        normed[...] = (values * rms_scale(values) * attn_gain).astype(BF)
        yield
        loads[1].wait()

        @tiles(RANK + 256, RANK + 256)
        def _(columns):
            kv_raw[:, columns] = dot(normed[...], kv_down[:, columns])

        low = kv_raw[:, pl.ds(0, RANK)]
        kv_low[...] = low
        loads[2].wait()
        kv_gain = kv_gain_row(kv_up)
        latent[...] = (low * rms_scale(low) * kv_gain).astype(BF)
        first, second = kv_raw[:, pl.ds(RANK, 128)], kv_raw[:, pl.ds(RANK + 128, 128)]
        c, s = cosine[:, pl.ds(0, 128)], sine[:, pl.ds(0, 128)]
        lay = spread()
        k_turned[:, pl.ds(0, TURN)] = dot((first * c - second * s).astype(BF), lay).astype(BF)
        k_turned[:, pl.ds(TURN, TURN)] = dot((second * c + first * s).astype(BF), lay).astype(BF)
        yield
        loads[0].wait()

        for k in range(2):
            columns = pl.ds(k * WIDE // 2, WIDE // 2)
            q_plain[:, columns] = dot(normed[...], q_weight[:, columns]).astype(BF)
            yield
        q_raw[...] = dot(normed[...], q_weight[:, pl.ds(WIDE, 2 * TURN)])
        first, second = q_raw[:, pl.ds(0, TURN)], q_raw[:, pl.ds(TURN, TURN)]
        q_turned[:, pl.ds(0, TURN)] = (first * cosine[...] - second * sine[...]).astype(BF)
        q_turned[:, pl.ds(TURN, TURN)] = (second * cosine[...] + first * sine[...]).astype(BF)
        yield

        @tiles(2 * WIDE, 2048)
        def _(columns):
            kv[:, columns] = dot(latent[...], kv_up[:, columns]).astype(BF)

        yield

        def head(h):
            plain = pl.ds(pl.multiple_of(h * NOPE, NOPE), NOPE)
            keys = pl.ds(pl.multiple_of(h * 2 * NOPE, NOPE), NOPE)
            both = pl.ds(pl.multiple_of(h * 2 * NOPE + NOPE, NOPE), VDIM)
            turned = jnp.where(of_head(h), q_turned[...].astype(F32), 0.0).astype(BF)
            scores = dot_t(q_plain[:, plain], kv[:, keys]) + dot_t(turned, k_turned[...])
            scores = jnp.where(allowed[...] > 0, scores * SCALE, MASKED)
            powers = jnp.exp(scores - jnp.max(scores, -1, keepdims=True))
            chance = powers / jnp.sum(powers, -1, keepdims=True)
            chances[h] = chance
            attended[:, plain] = dot(chance.astype(BF), kv[:, both]).astype(BF)

        for k in range(0, HEADS, 4):
            pl.loop(k, k + 4)(head)
            yield
        loads[3].wait()
        for k in range(2):
            columns = pl.ds(k * D // 2, D // 2)
            residual[:, columns] = tokens[:, columns].astype(F32) + dot(
                attended[...], out_weight[:, columns]
            )
            yield
        values = residual[...]
        hidden[...] = (values * rms_scale(values) * ffn_gain).astype(BF)
        logits = dot(hidden[...], router[...])
        lane = lax.broadcasted_iota(jnp.int32, logits.shape, 1)
        chosen = lane < 0
        for k in range(TOP):
            chosen = jnp.logical_or(chosen, routes[:, pl.ds(k, 1)] == lane)
        logits = jnp.where(chosen, logits, MASKED)
        powers = jnp.where(chosen, jnp.exp(logits - jnp.max(logits, -1, keepdims=True)), 0.0)
        share = powers / jnp.sum(powers, -1, keepdims=True)
        gates[...] = jnp.where(chosen, share, -1.0).T[: self.experts]
        yield


class AttentionBackward:
    def __init__(self, cotangent, hidden_sum, gate_grad, out_sums, saved, tokens, tables, weights):
        count = MICRO * SEQ
        self.experts = gate_grad.shape[0]
        self.inputs = [cotangent, hidden_sum, gate_grad, *tables, *saved, tokens, *out_sums]
        self.inputs += weights
        vmem = pl.BlockSpec(memory_space=pltpu.VMEM)
        hbm = pl.BlockSpec(memory_space=pl.ANY)
        self.in_specs = [vmem] * (5 + 12 + 1 + MICRO) + [hbm] * 4
        self.grads = [weights[n].shape for n in (3, 2, 0, 1)]
        self.out_shapes = [jax.ShapeDtypeStruct(shape, BF) for shape in self.grads] + [
            jax.ShapeDtypeStruct((count, D), BF)
        ] * 2
        self.out_specs = [hbm] * 4 + [vmem] * 2
        widest = max(width for _, width in self.grads)
        self.scratch = weight_buffers(weights) + [
            pltpu.VMEM((2, 256, widest), BF),
            pltpu.VMEM((count, 128), F32),
            pltpu.VMEM((count, D), F32),
            pltpu.VMEM((count, D), F32),
            pltpu.VMEM((count, D), BF),
            pltpu.VMEM((count, WIDE), BF),
            pltpu.VMEM((count, QUERY), BF),
            pltpu.VMEM((count, 2 * WIDE), BF),
            pltpu.VMEM((count, RANK + 256), BF),
            pltpu.VMEM((count, 2 * TURN), F32),
            pltpu.VMEM((count, 2 * TURN), F32),
            pltpu.VMEM((D, 128), F32),
            pltpu.VMEM((128, D), F32),
            pltpu.VMEM((128, RANK), F32),
            pltpu.SemaphoreType.DMA((2,)),
        ]

    def steps(self, at, ins, outs, scratch):
        cotangent, hidden_sum, gate_grad, cosine, sine = ins[:5]
        (
            hidden, gates, normed, q_plain, q_turned, kv_low, latent, k_turned, kv, chances,
            attended, residual,
        ) = ins[5:17]
        tokens, (tokens_grad, result) = ins[17], outs[4:]
        q_weight, kv_down, kv_up, out_weight, router = scratch[:5]
        (
            buffers, turned_gates, hidden_grad, residual_grad, mixed, attended_grad, q_grad, kv_grad,
            kv_raw_grad, q_turn_grad, k_turn_grad, router_grad, gain_grads, kv_gain_grads, out_sem,
        ) = scratch[6:]
        experts = self.experts
        yield 7 + sum(shape[0] // 256 for shape in self.grads)
        loads = weight_loads(ins[18 + MICRO :], scratch)
        for n in (4, 3, 2, 0, 1):
            loads[n].start()
        for k in range(MICRO):
            piece = pl.ds(k * SEQ, SEQ)
            result[piece, :] = (residual[piece, :] + ins[18 + k][...]).astype(BF)
        gain_grads[...] = jnp.zeros_like(gain_grads)
        kv_gain_grads[...] = jnp.zeros_like(kv_gain_grads)
        share = jnp.maximum(gates[...], 0.0)
        inner = jnp.sum(share * gate_grad[...], 0, keepdims=True)
        turned_gates[...] = jnp.zeros_like(turned_gates)
        turned_gates[pl.ds(0, experts), :] = share * (gate_grad[...] - inner)
        logit_grad = turned_gates[...].T.astype(BF)
        loads[4].wait()
        attn_gain, ffn_gain = gain_rows(router)

        @tiles(D, 1024)
        def _(columns):
            router_grad[columns, :] = t_dot(hidden[:, columns], logit_grad)
            hidden_grad[:, columns] = hidden_sum[:, columns] + dot_t(
                logit_grad, router[columns, :]
            )

        def norm_back(values, gain, gradient):
            scale = rms_scale(values)
            weighted = gradient * gain
            mean = jnp.mean(weighted * values, -1, keepdims=True)
            gain_grad = jnp.sum(gradient * values * scale, 0, keepdims=True)
            return scale * weighted - values * (scale * scale * scale * mean), gain_grad

        part, gain_grads[pl.ds(FFN_LANE, 1), :] = norm_back(
            residual[...], ffn_gain, hidden_grad[...]
        )
        total = cotangent[...].astype(F32) + part
        residual_grad[...] = total
        mixed[...] = total.astype(BF)
        yield
        loads[3].wait()

        @tiles(WIDE, 1024)
        def _(columns):
            attended_grad[:, columns] = dot_t(mixed[...], out_weight[columns, :]).astype(BF)

        yield
        turn = [0]
        stores = {}

        def weight_grad(n, left, right, width, beside=None):
            rows, whole = self.grads[n]
            for k in range(rows // 256):
                slot = turn[0] % 2
                turn[0] += 1
                if slot in stores:
                    stores[slot].wait()
                piece = pl.ds(k * 256, 256)

                @tiles(width, width if width < 1024 else 1024)
                def _(columns):
                    buffers[slot, :, columns] = t_dot(left[:, piece], right[:, columns]).astype(BF)

                if beside is not None:
                    lanes = beside[k * 256 : (k + 1) * 256, :]
                    buffers[slot, :, pl.ds(width, 128)] = lanes.astype(BF)
                if whole > width + 128:
                    rest = pl.ds(width + 128, whole - width - 128)
                    buffers[slot, :, rest] = jnp.zeros((256, whole - width - 128), BF)
                stores[slot] = pltpu.make_async_copy(
                    buffers.at[slot, :, pl.ds(0, whole)], outs[n].at[piece, :], out_sem.at[slot]
                )
                stores[slot].start()
                yield

        yield from weight_grad(0, attended, mixed, D)
        q_turn_grad[...] = jnp.zeros_like(q_turn_grad)
        k_turn_grad[...] = jnp.zeros_like(k_turn_grad)

        def head(h):
            plain = pl.ds(pl.multiple_of(h * NOPE, NOPE), NOPE)
            keys = pl.ds(pl.multiple_of(h * 2 * NOPE, NOPE), NOPE)
            both = pl.ds(pl.multiple_of(h * 2 * NOPE + NOPE, NOPE), VDIM)
            chance = chances[h]
            grads = attended_grad[:, plain]
            kv_grad[:, both] = t_dot(chance.astype(BF), grads).astype(BF)
            chance_grad = dot_t(grads, kv[:, both])
            mean = jnp.sum(chance * chance_grad, -1, keepdims=True)
            score_grad = (chance * (chance_grad - mean)).astype(BF)
            q_grad[:, plain] = (dot(score_grad, kv[:, keys]) * SCALE).astype(BF)
            kv_grad[:, keys] = (t_dot(score_grad, q_plain[:, plain]) * SCALE).astype(BF)
            mine = of_head(h)
            turned = jnp.where(mine, q_turned[...].astype(F32), 0.0).astype(BF)
            q_turn_grad[...] += jnp.where(mine, dot(score_grad, k_turned[...]), 0.0) * SCALE
            k_turn_grad[...] += t_dot(score_grad, turned) * SCALE

        for k in range(0, HEADS, 4):
            pl.loop(k, k + 4)(head)
            yield
        first, second = q_turn_grad[:, pl.ds(0, TURN)], q_turn_grad[:, pl.ds(TURN, TURN)]
        c, s = cosine[...], sine[...]
        q_grad[:, pl.ds(WIDE, TURN)] = (first * c + second * s).astype(BF)
        q_grad[:, pl.ds(WIDE + TURN, TURN)] = (second * c - first * s).astype(BF)
        lay = spread()

        def gathered(columns):
            values = k_turn_grad[:, columns]
            high = values.astype(BF)
            low = (values - high.astype(F32)).astype(BF)
            return dot_t(high, lay) + dot_t(low, lay)

        first, second = gathered(pl.ds(0, TURN)), gathered(pl.ds(TURN, TURN))
        c, s = cosine[:, pl.ds(0, 128)], sine[:, pl.ds(0, 128)]
        kv_raw_grad[:, pl.ds(RANK, 128)] = (first * c + second * s).astype(BF)
        kv_raw_grad[:, pl.ds(RANK + 128, 128)] = (second * c - first * s).astype(BF)
        loads[2].wait()
        latent_grad = dot_t(kv_grad[...], kv_up[:, pl.ds(0, 2 * WIDE)])
        part, kv_gain_grads[pl.ds(0, 1), :] = norm_back(
            kv_low[...], kv_gain_row(kv_up), latent_grad
        )
        kv_raw_grad[:, pl.ds(0, RANK)] = part.astype(BF)
        loads[0].wait()
        loads[1].wait()

        @tiles(D, 512)
        def _(columns):
            hidden_grad[:, columns] = dot_t(q_grad[...], q_weight[columns, :]) + dot_t(
                kv_raw_grad[...], kv_down[columns, :]
            )

        yield
        part, gain_grads[pl.ds(ATTN_LANE, 1), :] = norm_back(
            tokens[...].astype(F32), attn_gain, hidden_grad[...]
        )
        tokens_grad[...] = (residual_grad[...] + part).astype(BF)
        router_grad[...] += gain_grads[...].T
        yield from weight_grad(1, latent, kv_grad, 2 * WIDE, kv_gain_grads[...].T)
        yield from weight_grad(2, normed, q_grad, QUERY, router_grad)
        yield from weight_grad(3, normed, kv_raw_grad, RANK + 256)
        for store in stores.values():
            store.wait()


class WeightGrads:
    TILE = 256

    def __init__(self, grid, kept, extent):
        self.grid, self.extent, self.chunks = grid, extent, len(kept)
        self.inputs = [array for entry in kept for array in entry]
        rows, grad_rows, ab_grad, scaled, shared_grad, shared_inner, hidden, grad = kept[0]
        self.window = scaled.shape[1]
        hbm = pl.BlockSpec(memory_space=pl.ANY)
        self.in_specs = [hbm] * len(self.inputs)
        peers = grid.size["p"]
        window, tile = self.window, self.TILE
        self.out_shapes = [
            jax.ShapeDtypeStruct((extent, 2 * window), F32),
            jax.ShapeDtypeStruct((window, extent), F32),
            jax.ShapeDtypeStruct((peers - 1, extent, 2 * window), BF),
            jax.ShapeDtypeStruct((peers - 1, window, extent), BF),
            jax.ShapeDtypeStruct((D, shared_grad.shape[1]), BF),
            jax.ShapeDtypeStruct((shared_inner.shape[1], D), F32),
        ]
        self.out_specs = [hbm] * 6
        self.jobs = [(0, 2, True), (1, 3, False), (6, 4, True), (7, 5, False)]
        self.scratch = []
        for streamed, resident, left in self.jobs:
            a, b = kept[0][streamed], kept[0][resident]
            self.scratch.append(pltpu.VMEM((self.chunks,) + b.shape, BF))
            self.scratch.append(pltpu.VMEM((2, self.chunks, a.shape[0], tile), BF))
            shape = (tile, b.shape[1]) if left else (b.shape[1], tile)
            self.scratch.append(pltpu.VMEM((2,) + shape, F32))
            self.scratch.append(pltpu.VMEM((2,) + shape, BF))
        self.scratch += [
            pltpu.SemaphoreType.DMA((4, self.chunks)),
            pltpu.SemaphoreType.DMA((4, 2, self.chunks)),
            pltpu.SemaphoreType.DMA((4, 2)),
        ]

    def steps(self, at, ins, outs, scratch):
        tile, extent, chunks = self.TILE, self.extent, self.chunks
        peers = self.grid.size["p"]
        kept = [ins[c * 8 : (c + 1) * 8] for c in range(chunks)]
        whole_sem, tile_sem, out_sem = scratch[16:]
        own_ab, own_down, sent_ab, sent_down, shared_in, shared_down = outs

        def whole(job, c):
            return pltpu.make_async_copy(
                kept[c][self.jobs[job][1]], scratch[4 * job].at[c], whole_sem.at[job, c]
            )

        work = []
        per_peer = extent // tile
        for step in range(peers):
            for job in range(2):
                for k in range(per_peer):
                    piece = pl.ds(k * tile, tile)
                    if step == 0:
                        target = own_ab.at[piece, :] if job == 0 else own_down.at[:, piece]
                    elif job == 0:
                        target = sent_ab.at[step - 1, piece, :]
                    else:
                        target = sent_down.at[step - 1, :, piece]
                    peer = self.grid.shift(at, {"p": step})["p"]
                    first = pl.multiple_of(peer * extent + k * tile, tile)
                    work.append((job, first, target, step == 0))
        for k in range(D // tile):
            piece = pl.ds(k * tile, tile)
            work.append((2, k * tile, shared_in.at[piece, :], False))
            work.append((3, k * tile, shared_down.at[:, piece], True))
        work.sort(key=lambda entry: entry[0] >= 2)
        turns = [0] * 4
        numbered = []
        for job, first, target, wide in work:
            numbered.append((job, first, target, wide, turns[job]))
            turns[job] += 1
        yield len(work)

        def fetch(number, c):
            job, first, _, _, turn = numbered[number]
            return pltpu.make_async_copy(
                kept[c][self.jobs[job][0]].at[:, pl.ds(first, tile)],
                scratch[4 * job + 1].at[turn % 2, c],
                tile_sem.at[job, turn % 2, c],
            )

        def store(number):
            job, _, target, wide, turn = numbered[number]
            source = scratch[4 * job + (2 if wide else 3)].at[turn % 2]
            return pltpu.make_async_copy(source, target, out_sem.at[job, turn % 2])

        for c in range(chunks):
            for job in range(2):
                whole(job, c).start()
            fetch(0, c).start()
            for job in range(2, 4):
                whole(job, c).start()
        begun = set()
        last = {}
        for number, (job, _, _, wide, turn) in enumerate(numbered):
            if number + 1 < len(numbered):
                for c in range(chunks):
                    fetch(number + 1, c).start()
            if job not in begun:
                begun.add(job)
                for c in range(chunks):
                    whole(job, c).wait()
            for c in range(chunks):
                fetch(number, c).wait()
            if (job, turn % 2) in last:
                store(last[job, turn % 2]).wait()
            last[job, turn % 2] = number
            resident, streamed = scratch[4 * job], scratch[4 * job + 1].at[turn % 2]
            result = scratch[4 * job + (2 if wide else 3)].at[turn % 2]
            left = self.jobs[job][2]

            @tiles(resident.shape[2], 256)
            def _(columns):
                total = None
                for c in range(chunks):
                    if left:
                        term = t_dot(streamed[c], resident[c, :, columns])
                    else:
                        term = t_dot(resident[c, :, columns], streamed[c])
                    total = term if total is None else total + term
                if left:
                    result[:, columns] = total.astype(result.dtype)
                else:
                    result[columns, :] = total.astype(result.dtype)

            store(number).start()
            yield
        for number in last.values():
            store(number).wait()


class Assemble:
    TILE = 128

    def __init__(self, grid, own_ab, own_down, got_ab, got_down, eff):
        self.grid, self.eff = grid, eff
        self.extent = own_ab.shape[0]
        self.window = own_down.shape[0]
        self.peers = 1 + len(got_ab)
        self.inputs = [own_ab, own_down, *got_ab, *got_down]
        hbm = pl.BlockSpec(memory_space=pl.ANY)
        self.in_specs = [hbm] * len(self.inputs)
        self.out_shapes = [
            jax.ShapeDtypeStruct((self.extent, eff), F32),
            jax.ShapeDtypeStruct((self.extent, eff), F32),
            jax.ShapeDtypeStruct((eff, self.extent), F32),
        ]
        self.out_specs = [hbm] * 3
        tile, window = self.TILE, self.window
        self.scratch = [
            pltpu.VMEM((2, tile, 2 * window), F32),
            pltpu.VMEM((2, window, tile), F32),
            pltpu.VMEM((2, self.peers - 1, tile, 2 * window), BF),
            pltpu.VMEM((2, self.peers - 1, window, tile), BF),
            pltpu.VMEM((2, 2, tile, eff), F32),
            pltpu.VMEM((2, eff, tile), F32),
            pltpu.SemaphoreType.DMA((2, 2, self.peers)),
            pltpu.SemaphoreType.DMA((2, 3)),
        ]

    def steps(self, at, ins, outs, scratch):
        tile, window, peers, eff = self.TILE, self.window, self.peers, self.eff
        own = ins[:2]
        got = (ins[2 : 1 + peers], ins[1 + peers :])
        own_tiles, got_tiles = scratch[:2], scratch[2:4]
        both, down, in_sem, out_sem = scratch[4:]
        count = self.extent // tile
        yield 2 * count
        work = [(job, k) for job in range(2) for k in range(count)]

        def piece_of(array, job, k):
            piece = pl.ds(k * tile, tile)
            return array.at[piece, :] if job == 0 else array.at[:, piece]

        def fetch(job, k):
            copies = []
            for source in range(peers):
                array = own[job] if source == 0 else got[job][source - 1]
                target = own_tiles[job].at[k % 2]
                if source:
                    target = got_tiles[job].at[k % 2, source - 1]
                copies.append(
                    pltpu.make_async_copy(
                        piece_of(array, job, k), target, in_sem.at[job, k % 2, source]
                    )
                )
            return copies

        def store(job, k):
            if job:
                return [
                    pltpu.make_async_copy(
                        down.at[k % 2], piece_of(outs[2], 1, k), out_sem.at[k % 2, 2]
                    )
                ]
            return [
                pltpu.make_async_copy(
                    both.at[k % 2, n], piece_of(outs[n], 0, k), out_sem.at[k % 2, n]
                )
                for n in range(2)
            ]

        for copy in fetch(*work[0]):
            copy.start()
        for number, (job, k) in enumerate(work):
            if number + 1 < len(work):
                for copy in fetch(*work[number + 1]):
                    copy.start()
            for copy in fetch(job, k):
                copy.wait()
            if k >= 2:
                for copy in store(job, k - 2):
                    copy.wait()
            for peer in range(peers):
                first = peer * window
                width = min(window, eff - first)
                skip = window - width
                for source in range(peers):

                    @pl.when(lax.rem(at["p"] - peer + peers, peers) == source)
                    def _():
                        if source:
                            view = got_tiles[job].at[k % 2, source - 1]
                        else:
                            view = own_tiles[job].at[k % 2]
                        if job:
                            down[k % 2, pl.ds(first, width), :] = view[
                                pl.ds(skip, width), :
                            ].astype(F32)
                        else:
                            for n in range(2):
                                both[k % 2, n, :, pl.ds(first, width)] = view[
                                    :, pl.ds(n * window + skip, width)
                                ].astype(F32)

            for copy in store(job, k):
                copy.start()
            yield
        for job in range(2):
            for k in range(max(0, count - 2), count):
                for copy in store(job, k):
                    copy.wait()


def gather_all(grid, arrays, items, collective_id):
    return together(grid, [Gather(grid, arrays, items)], collective_id, "gather_all")[0]


def position_tables():
    frequency = ROPE_BASE ** (-2.0 * np.arange(HALF) / ROPE)
    angles = np.tile(np.arange(SEQ)[:, None] * frequency[None, :], (MICRO, HEADS))
    return [jnp.asarray(np.cos(angles), F32), jnp.asarray(np.sin(angles), F32)]


def capacity_for(expert_count):
    return min(SEQ, ((4 * SEQ * TOP + 3 * expert_count - 1) // (3 * expert_count) + 7) // 8 * 8)


def dot(left, right):
    return jnp.dot(left, right, preferred_element_type=F32)


def dot_t(left, right):
    return lax.dot_general(left, right, (((1,), (1,)), ((), ())), preferred_element_type=F32)


def t_dot(left, right):
    return lax.dot_general(left, right, (((0,), (0,)), ((), ())), preferred_element_type=F32)


PIECES = 4


def finish_kernel(copied, experts, *refs):
    q_sum, down_sum, up_sum = refs[:3]
    sources = refs[3 : 3 + copied]
    q_out, down_out, up_out, gains_out, kv_gain_out, router_out = refs[3 + copied : 9 + copied]
    targets = refs[9 + copied : 9 + 2 * copied]
    held = refs[9 + 2 * copied : 9 + 3 * copied]
    in_sem, out_sem = refs[9 + 3 * copied :]
    arriving, leaving = [], []
    for n, source in enumerate(sources):
        part = source.shape[0] // PIECES
        for k in range(PIECES):
            piece = pl.ds(k * part, part)
            into = pltpu.make_async_copy(source.at[piece, :], held[n].at[piece, :], in_sem.at[n, k])
            into.start()
            arriving.append(into)
            leaving.append(
                pltpu.make_async_copy(
                    held[n].at[piece, :], targets[n].at[piece, :], out_sem.at[n, k]
                )
            )
    for h in range(0, HEADS, 2):
        pieces = []
        for head in (h, h + 1):
            pieces.append(q_sum[:, head * NOPE : (head + 1) * NOPE])
            for half in range(2):
                first = WIDE + half * TURN + head * HALF
                pieces.append(q_sum[:, first : first + HALF])
        width = 2 * (NOPE + ROPE)
        q_out[:, pl.ds(h * (NOPE + ROPE), width)] = jnp.concatenate(pieces, 1)
    down_out[...] = jnp.concatenate(
        [down_sum[:, : RANK + HALF], down_sum[:, RANK + 128 : RANK + 128 + HALF]], 1
    )
    up_out[...] = up_sum[:, : 2 * WIDE]
    beside = q_sum[:, QUERY:].T
    gains_out[...] = beside[ATTN_LANE:]
    router_out[...] = beside[:experts]
    kv_gain_out[...] = up_sum[:, 2 * WIDE : 2 * WIDE + 128].T[:1]
    for into, out in zip(arriving, leaving):
        into.wait()
        out.start()
    for out in leaving:
        out.wait()


def finished(q_sum, down_sum, up_sum, plain, experts):
    rows, up_rows = q_sum.shape[0], up_sum.shape[0]
    vmem = pl.BlockSpec(memory_space=pltpu.VMEM)
    hbm = pl.BlockSpec(memory_space=pl.ANY)
    shapes = [
        (rows, HEADS * (NOPE + ROPE)), (rows, RANK + ROPE), (up_rows, 2 * WIDE), (2, rows),
        (1, up_rows), (experts, rows),
    ]
    return pl.pallas_call(
        functools.partial(finish_kernel, len(plain), experts),
        out_shape=[jax.ShapeDtypeStruct(shape, F32) for shape in shapes]
        + [jax.ShapeDtypeStruct(array.shape, array.dtype) for array in plain],
        in_specs=[vmem] * 3 + [hbm] * len(plain),
        out_specs=[vmem] * 6 + [hbm] * len(plain),
        scratch_shapes=[pltpu.VMEM(array.shape, array.dtype) for array in plain]
        + [pltpu.SemaphoreType.DMA((len(plain), PIECES))] * 2,
        compiler_params=pltpu.CompilerParams(vmem_limit_bytes=62 * 2**20),
        name="finish",
    )(q_sum, down_sum, up_sum, *plain)


def prepare_kernel(q_weight, kv_down, kv_up, router, gains, kv_gain, shared_down, q_out, down_out, up_out, shared_out):
    rows = q_weight.shape[0]
    values = q_weight[...].astype(F32)
    head = NOPE + ROPE
    for h in range(0, HEADS, 2):
        pair = [values[:, k * head : k * head + NOPE] for k in (h, h + 1)]
        q_out[:, pl.ds(h * NOPE, 2 * NOPE)] = jnp.concatenate(pair, 1).astype(BF)
    for half in range(2):
        for h in range(0, HEADS, 4):
            starts = [k * head + NOPE + half * HALF for k in range(h, h + 4)]
            pieces = [values[:, start : start + HALF] for start in starts]
            first = WIDE + half * TURN + h * HALF
            q_out[:, pl.ds(first, 4 * HALF)] = jnp.concatenate(pieces, 1).astype(BF)
    experts = router.shape[1]
    beside = [
        router[...].astype(F32),
        jnp.zeros((rows, ATTN_LANE - experts), F32),
        gains[...].astype(F32).T,
    ]
    q_out[:, pl.ds(QUERY, 128)] = jnp.concatenate(beside, 1).astype(BF)
    low = kv_down[...].astype(F32)
    gap = jnp.zeros((rows, 128 - HALF), F32)
    down_out[:, pl.ds(0, RANK)] = kv_down[:, pl.ds(0, RANK)]
    for half in range(2):
        first = RANK + half * HALF
        down_out[:, pl.ds(RANK + half * 128, 128)] = jnp.concatenate(
            [low[:, first : first + HALF], gap], 1
        ).astype(BF)
    up_out[:, pl.ds(0, 2 * WIDE)] = kv_up[...]
    up_rows, room = kv_up.shape[0], up_out.shape[1] - 2 * WIDE
    up_out[:, pl.ds(2 * WIDE, room)] = jnp.concatenate(
        [kv_gain[...].astype(F32).T, jnp.zeros((up_rows, room - 1), F32)], 1
    ).astype(BF)
    share = shared_down.shape[0]
    shared_out[pl.ds(0, share), :] = shared_down[...]
    left = shared_out.shape[0] - share
    shared_out[pl.ds(share, left), :] = jnp.zeros((left, D), BF)


def prepared(q_weight, kv_down, kv_up, router, gains, kv_gain, shared_down, up_room, room):
    rows, up_rows = q_weight.shape[0], kv_up.shape[0]
    vmem = pl.BlockSpec(memory_space=pltpu.VMEM)
    shapes = [
        (rows, QUERY + 128), (rows, RANK + 256), (up_rows, 2 * WIDE + up_room), (room, D),
    ]
    return pl.pallas_call(
        prepare_kernel,
        out_shape=[jax.ShapeDtypeStruct(shape, BF) for shape in shapes],
        in_specs=[vmem] * 7,
        out_specs=[vmem] * 4,
        compiler_params=pltpu.CompilerParams(vmem_limit_bytes=62 * 2**20),
        name="prepare",
    )(q_weight, kv_down, kv_up, router, gains, kv_gain, shared_down)


def plain_weight_grads(grid, kept, extent):
    me = lax.axis_index("dp")
    peers = grid.size["p"]

    def total(left, right):
        return functools.reduce(jnp.add, [t_dot(entry[left], entry[right]) for entry in kept])

    def share_of(array, step, axis):
        peer = lax.rem(me + step, peers)
        return lax.dynamic_slice_in_dim(array, peer * extent, extent, axis)

    both, down = total(0, 2), total(3, 1)
    steps = range(1, peers)
    return (
        share_of(both, 0, 0),
        share_of(down, 0, 1),
        jnp.stack([share_of(both, step, 0) for step in steps]).astype(BF),
        jnp.stack([share_of(down, step, 1) for step in steps]).astype(BF),
        total(6, 4).astype(BF),
        total(5, 7),
    )


def body(
    grid,
    tokens,
    cotangent,
    routes,
    segments,
    attn_gain,
    q_weight,
    kv_down,
    kv_gain,
    kv_up,
    out_weight,
    ffn_gain,
    router,
    shared_gate,
    shared_up,
    shared_down,
    expert_gate,
    expert_up,
    expert_down,
):
    devices = grid.devices
    dp_size = grid.size["p"]
    experts = router.shape[1]
    count = MICRO * SEQ
    eff = expert_gate.shape[2]
    extent = expert_gate.shape[1]
    window = -(-eff // (128 * dp_size)) * 128
    own = (expert_gate[0], expert_up[0], expert_down[0])

    rows = q_weight.shape[0]
    up_rows = kv_up.shape[0]
    up_room = 128 * max(1, 16 // up_rows)
    room = 128
    q_sent, down_sent, up_wide, shared_part = prepared(
        q_weight,
        kv_down,
        kv_up,
        router,
        jnp.stack([attn_gain, ffn_gain]),
        kv_gain[None],
        shared_down,
        up_room,
        room,
    )
    up_sent = up_wide if up_rows % 16 == 0 else up_wide.reshape(16, -1)

    share = shared_gate.shape[1] // devices
    first, second, third = ("q", "r", "p"), ("q", "p", "r"), ("p", "q", "r")

    def columns_of(ref, peer, step):
        return ref.at[:, pl.ds(window_start(peer, dp_size, window, eff), window)]

    def rows_of(ref, peer, step):
        return ref.at[pl.ds(window_start(peer, dp_size, window, eff), window), :]

    gathered, windows, (shared_sent,) = together(
        grid,
        [
            Gather(
                grid,
                [q_sent, down_sent, up_sent, out_weight],
                [
                    (0, 0, q_sent.shape[1], third),
                    (1, 0, down_sent.shape[1], third),
                    (2, 0, up_sent.shape[1], ("r", "p", "q")),
                    (3, 0, D // 2, first),
                    (3, D // 2, D // 2, second),
                ],
            ),
            Exchange(grid, own[:2], [columns_of] * 2, [(extent, window)] * 2, (2, 5)),
            SharedColumns([shared_gate, shared_up], devices),
        ],
        0,
        "gather_attention",
    )
    weights = [
        gathered[0].reshape(D, -1),
        gathered[1].reshape(D, -1),
        gathered[2].reshape(RANK, -1),
        gathered[3].reshape(-1, D),
    ]

    token_rows = tokens.reshape(count, D)
    grad_out = cotangent.reshape(count, D)
    tables = position_tables()
    numbers = segments.reshape(1, -1) + 4 * (jnp.arange(count, dtype=jnp.int32) // SEQ)[None, :]
    places = jnp.arange(count, dtype=jnp.int32)
    allowed = (numbers == numbers.T) & (places[:, None] >= places[None, :])

    def half_orders(a):
        return [(a, 0, D // 2, first), (a, D // 2, D // 2, second)]

    (grad_first,), saved, windows_down, (shared_in,) = together(
        grid,
        [
            Gather(
                grid, [grad_out[:SEQ]], [(0, 0, 1536, third), (0, 1536, 512, ("p", "r", "q"))]
            ),
            AttentionForward(
                token_rows,
                routes.reshape(count, TOP),
                allowed.astype(F32),
                tables,
                weights,
                experts,
            ),
            Exchange(grid, own[2:], [rows_of], [(window, extent)], (2,)),
            AllToAll(grid, shared_sent),
        ],
        6,
        "attention_forward",
    )
    hidden, dense_gates = saved[0], saved[1]

    shared_in = shared_in.reshape(D, 2 * room)

    half = D // 2
    capacity = capacity_for(experts)
    expert = lax.axis_index("expert")
    own_weights = (own, (*windows, *windows_down), shared_in, shared_part)

    def gather_of(chunk):
        piece = slice(chunk * SEQ, (chunk + 1) * SEQ)
        sent = [hidden[piece], dense_gates[:, piece]]
        orders = half_orders(0) + [(1, 0, SEQ, first)]
        if chunk:
            sent.append(grad_out[piece])
            orders += half_orders(2)
        return Gather(grid, sent, orders)

    kept_hidden, kept_grad = [], []

    def experts_of(hidden_all, gates_all, grad_all):
        kept_hidden.append(hidden_all)
        kept_grad.append(grad_all)
        share = lax.dynamic_index_in_dim(gates_all, expert, 1, keepdims=False)
        return Experts(
            grid,
            hidden_all.reshape(-1, D),
            grad_all.reshape(-1, D),
            share.reshape(-1, GROUP),
            own_weights,
            capacity,
        )

    def sums_of(done):
        hidden_part, out_part, gate_grad = done[:3]
        mine = (jnp.arange(experts, dtype=jnp.int32) == expert)[None, :, None]
        gate_grad = jnp.where(mine, gate_grad.reshape(devices, 1, SEQ), 0.0)
        shape = (devices, SEQ, D)
        return [hidden_part.reshape(shape), gate_grad, out_part.reshape(shape)]

    def kept_of(done):
        flat = [(h.reshape(-1, D), g.reshape(-1, D)) for h, g in zip(kept_hidden, kept_grad)]
        return [tuple(entry[3:]) + pair for entry, pair in zip(done, flat)]

    over = [(0, 0, half, ("p", "r")), (0, half, half, ("r", "p"))]
    over_gates = [(1, 0, SEQ, ("p", "r"))]
    over_out = [(2, 0, half, ("p", "r")), (2, half, half, ("r", "p"))]
    if devices <= 32:
        (gathered,) = together(grid, [gather_of(0)], 1, "gather_first")
        gathered, done_0 = together(
            grid,
            [gather_of(1), experts_of(*gathered, grad_first)],
            2,
            "gather_second_experts_first",
        )
        everything = over + over_gates + over_out
        sums_0, done_1 = together(
            grid,
            [Scatter(grid, sums_of(done_0), everything, [[0, 1], [2]]), experts_of(*gathered)],
            3,
            "scatter_first_experts_second",
        )
        kept = kept_of((done_0, done_1))
        sums_1, weight_grads = together(
            grid,
            [
                Scatter(grid, sums_of(done_1), everything, [[0, 1], [2]]),
                WeightGrads(grid, kept, extent),
            ],
            4,
            "scatter_second_weight_grads",
        )
        sums = (sums_0, sums_1)
    else:
        sums, done = [], []
        for chunk in range(MICRO):
            part = gather_of(chunk)
            if chunk:
                before = tuple(sums[-1])
                *part.inputs, sums[-1] = lax.optimization_barrier((*part.inputs, before))
            (gathered,) = together(grid, [part], 1 + 7 * chunk, "gather")
            part = experts_of(*gathered, *([] if chunk else [grad_first]))
            (now,) = together(grid, [part], None, "experts")
            parts = sums_of(now)
            (hidden_gates,) = together(
                grid, [Scatter(grid, parts[:2], over + over_gates, [[0, 1]])], 2, "scatter_hidden"
            )
            (out_sum,) = together(grid, [Scatter(grid, parts[2:], over, [[0]])], 3, "scatter_out")
            sums.append((*hidden_gates, *out_sum))
            done.append(now)
        weight_grads = plain_weight_grads(grid, kept_of(done), extent)
    hidden_sum = jnp.concatenate([entry[0] for entry in sums], 0)
    gate_grad = jnp.concatenate([entry[1] for entry in sums], 1)
    out_sums = [entry[2] for entry in sums]
    own_ab, own_down, sent_ab, sent_down, shared_in_grad, shared_down_grad = weight_grads

    def sent_to(ref, peer, step):
        return ref.at[step - 1]

    attention_grads, (got_ab, got_down), (shared_back,) = together(
        grid,
        [
            AttentionBackward(
                grad_out, hidden_sum, gate_grad, out_sums, saved, token_rows, tables, weights
            ),
            Exchange(
                grid,
                [sent_ab, sent_down],
                [sent_to] * 2,
                [(extent, 2 * window), (window, extent)],
            ),
            AllToAll(grid, shared_in_grad.reshape(devices, -1, 2 * room)),
        ],
        7,
        "attention_backward",
    )
    (
        out_weight_grad, kv_up_grad, q_weight_grad, kv_down_grad, tokens_grad, result,
    ) = attention_grads
    shared_down_grad = shared_down_grad[:share]

    def halves(a, columns):
        part = columns // 256 * 128
        return [(a, 0, part, ("p", "r")), (a, part, columns - part, ("r", "p"))]

    attention_sums = Scatter(
        grid,
        [
            q_weight_grad.reshape((devices,) + q_sent.shape),
            kv_down_grad.reshape((devices,) + down_sent.shape),
            kv_up_grad.reshape((devices,) + up_sent.shape),
            out_weight_grad.reshape((devices,) + out_weight.shape),
        ],
        halves(0, q_sent.shape[1])
        + halves(1, down_sent.shape[1])
        + halves(2, up_sent.shape[1])
        + halves(3, out_weight.shape[1]),
        [[0], [3], [2], [1]],
    )
    experts_grads = Assemble(
        grid,
        own_ab,
        own_down,
        [got_ab[step] for step in range(dp_size - 1)],
        [got_down[step] for step in range(dp_size - 1)],
        eff,
    )
    (
        (q_sum, down_sum, up_sum, out_weight_sum), experts_grads,
        (shared_gate_grad, shared_up_grad),
    ) = together(
        grid,
        [attention_sums, experts_grads, SharedRows(shared_back, shared_gate.shape[1])],
        5,
        "scatter_attention_assemble",
    )
    (
        q_grad, down_grad, up_grad, gain_grads, kv_gain_grad, router_grad, result, tokens_grad,
        out_weight_grad, shared_gate_grad, shared_up_grad, gate_grad, expert_up_grad,
        expert_down_grad,
    ) = finished(
        q_sum,
        down_sum,
        up_sum.reshape(up_rows, -1),
        [
            result, tokens_grad, out_weight_sum, shared_gate_grad, shared_up_grad, *experts_grads,
        ],
        experts,
    )
    return (
        result.reshape(tokens.shape),
        tokens_grad.reshape(tokens.shape),
        gain_grads[0],
        q_grad,
        down_grad,
        kv_gain_grad[0],
        up_grad,
        out_weight_grad,
        gain_grads[1],
        router_grad.T,
        shared_gate_grad,
        shared_up_grad,
        shared_down_grad,
        gate_grad[None],
        expert_up_grad[None],
        expert_down_grad[None],
    )


def solution(mesh):
    return jax.shard_map(
        functools.partial(body, Grid(mesh)),
        mesh=mesh,
        in_specs=(
            P(None, ("dp", "expert"), None, None),
            P(None, ("dp", "expert"), None, None),
            P(None, ("dp", "expert"), None, None),
            P(None, ("dp", "expert"), None),
            P(("dp", "expert")),
            P(("dp", "expert"), None),
            P(("dp", "expert"), None),
            P(("dp", "expert")),
            P(("dp", "expert"), None),
            P(("dp", "expert"), None),
            P(("dp", "expert")),
            P(("dp", "expert"), None),
            P(("dp", "expert"), None),
            P(("dp", "expert"), None),
            P(("dp", "expert"), None),
            P("expert", "dp", None),
            P("expert", "dp", None),
            P("expert", None, "dp"),
        ),
        out_specs=(
            P(None, ("dp", "expert"), None, None),
            P(None, ("dp", "expert"), None, None),
            P(("dp", "expert")),
            P(("dp", "expert"), None),
            P(("dp", "expert"), None),
            P(("dp", "expert")),
            P(("dp", "expert"), None),
            P(("dp", "expert"), None),
            P(("dp", "expert")),
            P(("dp", "expert"), None),
            P(("dp", "expert"), None),
            P(("dp", "expert"), None),
            P(("dp", "expert"), None),
            P("expert", "dp", None),
            P("expert", "dp", None),
            P("expert", None, "dp"),
        ),
        check_vma=False,
    )
```

```python
import functools

import jax
import jax.numpy as jnp
import numpy as np
from jax import lax
from jax.experimental import pallas as pl
from jax.experimental.pallas import tpu as pltpu
from jax.sharding import PartitionSpec as P

D = 2048
HEADS = 16
NOPE = 128
ROPE = 64
VDIM = 128
RANK = 512
TOP = 6
SEQ = 64
MICRO = 2

EPSILON = 1e-06
ROPE_BASE = 10000.0
MASKED = -1e30
BF = jnp.bfloat16
F32 = jnp.float32

MESH_ID = pl.DeviceIdType.MESH


class Grid:
    def __init__(self, mesh):
        self.experts = mesh.shape["expert"]
        self.size = {"p": mesh.shape["dp"], "r": self.experts // 8, "q": 4}
        self.devices = self.size["p"] * self.experts

    def here(self):
        e = lax.axis_index("expert")
        r_size = self.size["r"]
        return {
            "p": lax.axis_index("dp"),
            "q": lax.div(e, 2 * r_size),
            "r": lax.rem(lax.div(e, 2), r_size),
            "c": lax.rem(e, 2),
        }

    def shift(self, at, offsets):
        moved = dict(at)
        for axis, step in offsets.items():
            if step:
                moved[axis] = lax.rem(at[axis] + step, self.size[axis])
        return moved

    def expert_of(self, at):
        return at["q"] * (2 * self.size["r"]) + at["r"] * 2 + at["c"]

    def number(self, at):
        return at["p"] * self.experts + self.expert_of(at)

    def mesh_id(self, at):
        return (at["p"], self.expert_of(at))

    def device_id(self, number):
        return (lax.div(number, self.experts), lax.rem(number, self.experts))

    def partners(self, at):
        found = [{**at, "c": 1 - at["c"]}]
        for axis, size in self.size.items():
            found += [self.shift(at, {axis: step}) for step in range(1, size)]
        return found


def greet(grid, at, everyone):
    barrier = pltpu.get_barrier_semaphore()
    partners = [grid.mesh_id(partner) for partner in grid.partners(at)]
    if everyone:
        me = grid.number(at)
        partners = [
            grid.device_id(lax.rem(me + step, grid.devices)) for step in range(1, grid.devices)
        ]
    for partner in partners:
        pl.semaphore_signal(barrier, inc=1, device_id=partner, device_id_type=MESH_ID)
    pl.semaphore_wait(barrier, len(partners))


ALONG = (0, -1, 1, -2, 2, -3, 3)


def span_of(grid, axis):
    return ALONG if axis == "q" else tuple(range(grid.size[axis]))


class Gather:
    def __init__(self, grid, arrays, items):
        count = len(items)
        slots = grid.devices // 2 // 4 * len(ALONG)
        self.grid, self.items = grid, items
        self.inputs = list(arrays)
        self.in_specs = [pl.BlockSpec(memory_space=pl.ANY)] * len(arrays)
        self.out_shapes = [
            jax.ShapeDtypeStruct((grid.devices,) + a.shape, a.dtype) for a in arrays
        ]
        self.out_specs = [pl.BlockSpec(memory_space=pl.ANY)] * len(arrays)
        self.scratch = [
            pltpu.SemaphoreType.DMA((count * slots * 2,)),
            pltpu.SemaphoreType.DMA((count, slots)),
            pltpu.SemaphoreType.DMA((count, slots)),
            pltpu.SemaphoreType.DMA((count, slots)),
            pltpu.SemaphoreType.DMA((len(arrays),)),
        ]

    def steps(self, at, ins, outs, scratch):
        grid, items = self.grid, self.items
        count = len(items)
        send_sem, recv_sem, core_send, core_recv, own_sem = scratch
        sibling = {**at, "c": 1 - at["c"]}
        q_size = grid.size["q"]
        pending = []
        me = grid.number(at)

        def inside(step):
            return jnp.logical_and(at["q"] + step >= 0, at["q"] + step < q_size)

        def guarded(step, action):
            if step:
                pl.when(inside(step))(action)
            else:
                action()

        def q_part(i, offset):
            return offset[items[i][3].index("q")]

        def slot(i, offset):
            number = 0
            for axis, part in zip(items[i][3], offset):
                span = span_of(grid, axis)
                number = number * len(span) + span.index(part)
            return number

        def block_of(i, offset, base):
            moved = dict(base)
            for axis, part in zip(items[i][3], offset):
                if part:
                    moved[axis] = (
                        base[axis] + part
                        if axis == "q"
                        else lax.rem(base[axis] + part, grid.size[axis])
                    )
            return grid.number(moved)

        def views(i, offset, base):
            a, first, width, order = items[i]
            columns = pl.ds(first, width)
            view = outs[a].at[block_of(i, offset, base), :, columns]
            return (ins[a].at[:, columns] if offset == (0, 0, 0) else view), view

        def send(i, offset, landed, target_step, cond_step):
            number = len(pending)

            def copy():
                source, view = views(i, offset, at)
                return pltpu.make_async_remote_copy(
                    src_ref=source,
                    dst_ref=view,
                    send_sem=send_sem.at[number],
                    recv_sem=recv_sem.at[i, slot(i, landed)],
                    device_id=grid.mesh_id(target_step()),
                    device_id_type=MESH_ID,
                )

            guarded(cond_step, lambda: copy().start())
            pending.append((q_part(i, offset), cond_step, copy))

        def forward(i, offset, stage):
            axis = items[i][3][stage]
            if axis == "q":
                part = offset[stage]
                for step in (1, -1) if part == 0 else (1,) if part < 0 else (-1,):
                    if abs(part - step) < q_size:
                        landed = offset[:stage] + (part - step,) + offset[stage + 1 :]
                        send(
                            i, offset, landed, lambda step=step: {**at, "q": at["q"] + step}, step
                        )
                return
            for step in range(1, grid.size[axis]):
                part = (offset[stage] - step) % grid.size[axis]
                landed = offset[:stage] + (part,) + offset[stage + 1 :]
                send(i, offset, landed, lambda step=step: grid.shift(at, {axis: step}), 0)

        def across(i, offset):
            def copy():
                source, view = views(i, offset, at)
                return pltpu.make_async_remote_copy(
                    src_ref=source,
                    dst_ref=view,
                    send_sem=core_send.at[i, slot(i, offset)],
                    recv_sem=core_recv.at[i, slot(i, offset)],
                    device_id=grid.mesh_id(sibling),
                    device_id_type=MESH_ID,
                )

            copy().start()
            pending.append((q_part(i, offset), 0, copy))

        def landed_at(i, offset, base, sem):
            view = views(i, offset, base)[1]
            pltpu.make_async_copy(view, view, sem.at[i, slot(i, offset)]).wait()

        def take(i, offset, stage):
            def action():
                landed_at(i, offset, at, recv_sem)
                if items[i][3][stage] == "q":
                    forward(i, offset, stage)
                for later in range(stage + 1, 3):
                    forward(i, offset, later)
                across(i, offset)

            guarded(q_part(i, offset), action)

        ranges = [[span_of(grid, axis) for axis in item[3]] for item in items]
        offsets = [
            (i, (u, v, w))
            for i in range(count)
            for u in ranges[i][0]
            for v in ranges[i][1]
            for w in ranges[i][2]
        ]
        todo = []
        for i, offset in offsets:
            if any(offset):
                stage = max(k for k in range(3) if offset[k])
                todo.append((stage,) + tuple(abs(part) for part in offset) + (i, offset))
        yield len(todo) + 1

        own_copies = []
        for a in range(len(ins)):
            own = pltpu.make_async_copy(ins[a], outs[a].at[me], own_sem.at[a])
            own.start()
            own_copies.append(own)
        for i in range(count):
            for stage in range(3):
                forward(i, (0, 0, 0), stage)
            across(i, (0, 0, 0))
        yield
        for stage, _, _, _, i, offset in sorted(todo):
            take(i, offset, stage)
            yield
        for own in own_copies:
            own.wait()
        for i, offset in offsets:
            guarded(
                q_part(i, offset), functools.partial(landed_at, i, offset, sibling, core_recv)
            )
        for q_step, cond_step, copy in pending:
            guarded(q_step, functools.partial(guarded, cond_step, lambda: copy().wait_send()))


def add_rows(target, *parts):
    rows = target.shape[0]
    step = min(16, rows)

    @pl.loop(0, rows // step)
    def _(k):
        block = pl.ds(pl.multiple_of(k * step, step), step)
        total = parts[0][block, :].astype(F32)
        for part in parts[1:]:
            total = total + part[block, :].astype(F32)
        target[block, :] = total.astype(target.dtype)


DEPTH = 2
AHEAD = 4


class Scatter:
    def __init__(self, grid, arrays, items, rounds, windows=None):
        count = len(items)
        self.windows = windows or [(n, 0, a.shape[2]) for n, a in enumerate(arrays)]
        chips = grid.devices // 2
        q_size = grid.size["q"]
        self.grid, self.items, self.rounds = grid, items, rounds
        self.inputs = list(arrays)
        self.in_specs = [pl.BlockSpec(memory_space=pl.ANY)] * len(arrays)
        self.out_shapes = [jax.ShapeDtypeStruct(a.shape[1:], F32) for a in arrays]
        self.out_specs = [pl.BlockSpec(memory_space=pltpu.VMEM)] * len(arrays)
        blocks = [((arrays[n].shape[1], width), arrays[n].dtype) for n, _, width in self.windows]
        scratch = [pltpu.VMEM((chips,) + shape, kind) for shape, kind in blocks]
        scratch += [pltpu.VMEM((2 * AHEAD,) + shape, kind) for shape, kind in blocks]
        most = 0
        for a, _, width, order in items:
            n1, n2 = (grid.size[axis] for axis in order)
            shares = ((n1 - 1) * n2 * q_size, (n2 - 1) * q_size, q_size)
            most = max(most, shares[0] + shares[1])
            for share in shares:
                scratch.append(pltpu.VMEM((share, blocks[a][0][0], width), blocks[a][1]))
        self.scratch = scratch + [
            pltpu.SemaphoreType.DMA((len(blocks), chips)),
            pltpu.SemaphoreType.DMA((len(blocks), chips)),
            pltpu.SemaphoreType.DMA((len(blocks), chips)),
            pltpu.SemaphoreType.DMA((count, most)),
            pltpu.SemaphoreType.DMA((count, most)),
            pltpu.SemaphoreType.DMA((count, q_size)),
            pltpu.SemaphoreType.DMA((count, q_size)),
        ]

    def steps(self, at, ins, outs, scratch):
        grid, items = self.grid, self.items
        count, arrays = len(items), len(self.windows)
        held, crossed = scratch[:arrays], scratch[arrays : 2 * arrays]
        landing = scratch[2 * arrays : 2 * arrays + 3 * count]
        load_sem, core_send, core_recv, send_sem, recv_sem, line_send, line_recv = scratch[
            2 * arrays + 3 * count :
        ]
        sibling = {**at, "c": 1 - at["c"]}
        size = grid.size
        q_size = size["q"]

        def flat(block):
            p, r, t = block
            return (p * size["r"] + r) * q_size + t

        def owner(base, block):
            p, r, t = block
            return grid.number({**grid.shift(base, {"p": p, "r": r}), "q": t})

        targets = []
        for t in range(q_size // 2):
            targets += [t, q_size - 1 - t]
        near_blocks = []
        for t in targets:
            near = [(p, r, t) for p in range(size["p"]) for r in range(size["r"])]
            near_blocks += sorted(near, key=lambda b: -(b[0] > 0) - (b[1] > 0))
        blocks = [(n, block) for n in range(len(self.rounds)) for block in near_blocks]
        round_of = {a: n for n, members in enumerate(self.rounds) for a in members}

        def source(a, number):
            array, first, width = self.windows[a]
            return ins[array].at[number, :, pl.ds(first, width)]

        def load(a, block):
            return pltpu.make_async_copy(
                source(a, owner(at, block)), held[a].at[flat(block)], load_sem.at[a, flat(block)]
            )

        def crossed_at(a, block):
            return crossed[a].at[near_blocks.index(block) % (2 * AHEAD)]

        def across(a, block):
            return pltpu.make_async_remote_copy(
                src_ref=source(a, owner(sibling, block)),
                dst_ref=crossed_at(a, block),
                send_sem=core_send.at[a, flat(block)],
                recv_sem=core_recv.at[a, flat(block)],
                device_id=grid.mesh_id(sibling),
                device_id_type=MESH_ID,
            )

        def begin(number):
            if number < len(blocks):
                n, block = blocks[number]
                for a in self.rounds[n]:
                    across(a, block).start()
                    load(a, block).start()

        merged = [0]

        def merge_to(n, block):
            while merged[0] <= blocks.index((n, block)):
                turn, now = blocks[merged[0]]
                for a in self.rounds[turn]:
                    load(a, now).wait()
                    across(a, now).wait_recv()
                    view = held[a].at[flat(now)]
                    add_rows(view, view, crossed_at(a, now))
                begin(merged[0] + AHEAD)
                merged[0] += 1

        def held_view(i, block):
            return held[items[i][0]].at[flat(block), :, pl.ds(items[i][1], items[i][2])]

        def block_at(i, first, second, t):
            part = dict(zip(items[i][3], (first, second)))
            return (part["p"], part["r"], t)

        def landing_slot(i, stage, steps, t):
            n2 = size[items[i][3][1]]
            if stage == 0:
                return ((steps[0] - 1) * n2 + steps[1]) * q_size + t
            return (steps[1] - 1) * q_size + t

        pending = []

        def send(i, stage, steps, t):
            n1, n2 = (size[axis] for axis in items[i][3])
            slot = landing_slot(i, stage, steps, t)
            sem = slot if stage == 0 else (n1 - 1) * n2 * q_size + slot
            return pltpu.make_async_remote_copy(
                src_ref=held_view(i, block_at(i, *steps, t)),
                dst_ref=landing[3 * i + stage].at[slot],
                send_sem=send_sem.at[i, sem],
                recv_sem=recv_sem.at[i, sem],
                device_id=grid.mesh_id(grid.shift(at, {items[i][3][stage]: steps[stage]})),
                device_id_type=MESH_ID,
            )

        def start(i, stage, steps, t):
            copy = send(i, stage, steps, t)
            copy.start()
            pending.append(copy)

        def receive(i, stage, steps, t):
            send(i, stage, steps, t).wait_recv()
            into = (0, steps[1]) if stage == 0 else (0, 0)
            view = held_view(i, block_at(i, *into, t))
            add_rows(view, view, landing[3 * i + stage].at[landing_slot(i, stage, steps, t)])

        def line(i, t):
            return pltpu.make_async_remote_copy(
                src_ref=held_view(i, (0, 0, t)),
                dst_ref=landing[3 * i + 2].at[at["q"]],
                send_sem=line_send.at[i, t],
                recv_sem=line_recv.at[i, at["q"]],
                device_id=grid.mesh_id({**at, "q": t}),
                device_id_type=MESH_ID,
            )

        def close(i, t):
            for second in range(1, size[items[i][3][1]]):
                receive(i, 1, (0, second), t)
            pl.when(at["q"] != t)(lambda: line(i, t).start())

        def finish(i):
            a, first, width, _ = items[i]
            parts = [held[a].at[at["q"], :, pl.ds(first, width)]]
            for step in range(1, q_size):
                back = lax.rem(at["q"] + step, q_size)
                view = landing[3 * i + 2].at[back]
                pltpu.make_async_copy(view, view, line_recv.at[i, back]).wait()
                parts.append(view)
            array, window_first, _ = self.windows[a]
            add_rows(outs[array].at[:, pl.ds(window_first + first, width)], *parts)

        ticks = []
        for n, members in enumerate(self.rounds):
            mine = [i for i in range(count) if items[i][0] in members]
            for t in targets:
                for far in (True, False):
                    turn = []
                    for i in mine:
                        n1, n2 = (size[axis] for axis in items[i][3])
                        for second in range(1, n2) if far else (0,):
                            for first in range(1, n1):
                                turn.append((i, (first, second), t))
                    ticks.append((n, turn, None if far else (mine, t)))
        yield sum(2 * len(turn) for _, turn, _ in ticks) + q_size * count + count

        for number in range(AHEAD):
            begin(number)
        closing, finishing = [], []
        for k in range(len(ticks) + DEPTH):
            if k < len(ticks):
                n, turn, _ = ticks[k]
                for i, steps, t in turn:
                    merge_to(n, block_at(i, *steps, t))
                    start(i, 0, steps, t)
                    yield
            if k >= DEPTH:
                n, turn, done = ticks[k - DEPTH]
                for i, steps, t in turn:
                    merge_to(n, block_at(i, 0, steps[1], t))
                    receive(i, 0, steps, t)
                    if steps[1] and steps[0] == size[items[i][3][0]] - 1:
                        start(i, 1, (0, steps[1]), t)
                    yield
                if closing and done is None:
                    for i in closing[0][0]:
                        close(i, closing[0][1])
                        yield
                    if closing[0][1] == targets[-1]:
                        finishing.append(closing[0][0])
                    closing.pop()
                    if len(finishing) > 1:
                        for i in finishing.pop(0):
                            finish(i)
                            yield
                if done is not None:
                    closing.append(done)
        for mine, t in closing:
            for i in mine:
                close(i, t)
                yield
            finishing.append(mine)
        for mine in finishing:
            for i in mine:
                finish(i)
                yield
        for n, block in blocks:
            for a in self.rounds[n]:
                across(a, block).wait_send()
        for copy in pending:
            copy.wait_send()
        for i in range(count):
            for t in range(q_size):
                pl.when(at["q"] != t)(lambda: line(i, t).wait_send())


def together(grid, parts, collective_id, name):
    def kernel(*refs):
        at = grid.here()
        if collective_id is not None:
            greet(grid, at, any(isinstance(part, AllToAll) for part in parts))
        ins, outs, scratch = [], [], []
        for list_of, key in ((ins, "inputs"), (outs, "out_shapes"), (scratch, "scratch")):
            for part in parts:
                count = len(getattr(part, key))
                list_of.append(refs[:count])
                refs = refs[count:]
        running = []
        for part, *its in zip(parts, ins, outs, scratch):
            steps = part.steps(at, *its)
            running.append([steps, next(steps), 0])
        while running:
            now = min(running, key=lambda entry: entry[2] / entry[1])
            now[2] += 1
            if next(now[0], "end") == "end":
                running.remove(now)

    outs = pl.pallas_call(
        kernel,
        out_shape=[shape for part in parts for shape in part.out_shapes],
        in_specs=[spec for part in parts for spec in part.in_specs],
        out_specs=[spec for part in parts for spec in part.out_specs],
        scratch_shapes=[entry for part in parts for entry in part.scratch],
        compiler_params=pltpu.CompilerParams(
            collective_id=collective_id,
            has_side_effects=collective_id is not None,
            vmem_limit_bytes=62 * 2**20,
        ),
        name=name,
    )(*[array for part in parts for array in part.inputs])
    split = []
    for part in parts:
        split.append(outs[: len(part.out_shapes)])
        outs = outs[len(part.out_shapes) :]
    return split


GROUP = 256


def tiles(extent, width):
    def wrap(action):
        width_now = min(width, extent)

        @pl.loop(0, extent // width_now)
        def _(k):
            action(pl.ds(pl.multiple_of(k * width_now, width_now), width_now))

    return wrap


def window_start(peer, peers, window, eff):
    return pl.multiple_of(peer * window - lax.div(peer, peers - 1) * (peers * window - eff), 128)


class Experts:
    def __init__(self, grid, hidden, grad, share, weights, capacity):
        own, got, shared_in, shared_down = weights
        self.grid = grid
        self.peers = grid.size["p"]
        self.eff = own[0].shape[1]
        self.extent = own[0].shape[0]
        count = hidden.shape[0]
        window = got[0].shape[2]
        self.supers = count // (2 * GROUP)
        self.slots = GROUP // SEQ * capacity
        self.capacity = capacity
        self.window = window
        rows = 2 * self.slots
        total = self.supers * rows
        groups = count // GROUP
        self.inputs = [hidden, grad, share, *own, *got, shared_in, shared_down]
        hbm = pl.BlockSpec(memory_space=pl.ANY)
        vmem = pl.BlockSpec(memory_space=pltpu.VMEM)
        self.in_specs = [hbm, hbm, vmem] + [hbm] * 6 + [vmem] * 2
        shared_width = shared_in.shape[1]
        kept = [(rows, D), (rows, D), (rows, 2 * window), (rows, window)]
        kept += [(2 * GROUP, shared_width), (2 * GROUP, shared_width // 2)]
        self.out_shapes = [
            jax.ShapeDtypeStruct((count, D), BF),
            jax.ShapeDtypeStruct((count, D), BF),
            jax.ShapeDtypeStruct((groups, GROUP), F32),
        ] + [jax.ShapeDtypeStruct((self.supers * r, c), BF) for r, c in kept]
        self.out_specs = [hbm, hbm, vmem] + [hbm] * len(kept)
        self.scratch = (
            [pltpu.VMEM((2 * GROUP, D), BF)] * 2
            + [pltpu.VMEM((2, r, c), BF) for r, c in kept]
            + [pltpu.VMEM((2, GROUP, D), BF)] * 2
            + [pltpu.VMEM((rows, window), F32)] * 3
            + [pltpu.VMEM((rows, D), BF)] * 2
            + [
                pltpu.VMEM((groups, GROUP), F32),
                pltpu.VMEM((2, self.slots, GROUP), BF),
                pltpu.VMEM((2, GROUP, self.slots), BF),
                pltpu.VMEM((rows, 1), F32),
                pltpu.VMEM((rows, 1), F32),
                pltpu.VMEM((2 * GROUP, shared_width), F32),
                pltpu.SemaphoreType.DMA((2,)),
                pltpu.SemaphoreType.DMA((len(kept), 2)),
                pltpu.SemaphoreType.DMA((2, 2)),
                pltpu.VMEM((D, window), BF),
                pltpu.VMEM((D, window), BF),
                pltpu.VMEM((window, D), BF),
                pltpu.SemaphoreType.DMA((3, self.peers)),
            ]
        )

    def steps(self, at, ins, outs, scratch):
        hidden, grad, share = ins[:3]
        own, got = ins[3:6], ins[6:9]
        shared_in, shared_down = ins[9:]
        hidden_out, out_out, gate_grad = outs[:3]
        kept_out = outs[3:]
        hidden_in, grad_in = scratch[:2]
        kept = scratch[2:8]
        parts = scratch[8:10]
        a_pre, b_pre, flow = scratch[10:13]
        row_grad, expert_out = scratch[13:15]
        keys, picks, picks_t, share_rows, gate_rows, shared_pre = scratch[15:21]
        load_sem, keep_sem, part_sem, gate, up, down, weight_sem = scratch[21:]
        slots, window, supers = self.slots, self.window, self.supers
        rows = 2 * slots
        half = shared_in.shape[1] // 2
        yield supers * 12

        def load(k):
            piece = pl.ds(k * 2 * GROUP, 2 * GROUP)
            return (
                pltpu.make_async_copy(hidden.at[piece, :], hidden_in, load_sem.at[0]),
                pltpu.make_async_copy(grad.at[piece, :], grad_in, load_sem.at[1]),
            )

        def keep(n, k):
            extent = kept[n].shape[1]
            return pltpu.make_async_copy(
                kept[n].at[k % 2],
                kept_out[n].at[pl.ds(k * extent, extent), :],
                keep_sem.at[n, k % 2],
            )

        def put(n, k, j):
            target = (hidden_out, out_out)[n]
            piece = pl.ds((2 * k + j) * GROUP, GROUP)
            return pltpu.make_async_copy(parts[n].at[j], target.at[piece, :], part_sem.at[n, j])

        me, peers, extent = at["p"], self.peers, self.extent
        first = window_start(me, peers, window, self.eff)
        weight_copies = []
        for n, weight in enumerate((gate, up, down)):
            for step in range(peers):
                peer = lax.rem(me + peers - step, peers)
                share_of_d = pl.ds(pl.multiple_of(peer * extent, extent), extent)
                target = weight.at[:, share_of_d] if n == 2 else weight.at[share_of_d, :]
                if step:
                    source = got[n].at[step - 1]
                else:
                    units = pl.ds(first, window)
                    source = own[n].at[units, :] if n == 2 else own[n].at[:, units]
                weight_copies.append(
                    pltpu.make_async_copy(source, target, weight_sem.at[n, step])
                )
        for copy in load(0):
            copy.start()
        for copy in weight_copies:
            copy.start()
        row_of = lax.broadcasted_iota(jnp.int32, (GROUP, GROUP), 0)
        column_of = lax.broadcasted_iota(jnp.int32, (GROUP, GROUP), 1)
        same = lax.div(row_of, SEQ) == lax.div(column_of, SEQ)
        earlier = jnp.logical_and(same, row_of < column_of).astype(BF)
        chosen = (share[...] >= 0).astype(F32)
        place = jnp.dot(chosen.astype(BF), earlier, preferred_element_type=F32)
        sequence = lax.div(lax.broadcasted_iota(jnp.int32, place.shape, 1), SEQ).astype(F32)
        keys[...] = jnp.where(chosen > 0, place + sequence * self.capacity, -1.0)
        for copy in weight_copies:
            copy.wait()
        twice = peers * window - self.eff
        if twice:

            @pl.when(me == peers - 1)
            def _():
                gate[:, pl.ds(0, twice)] = jnp.zeros((D, twice), BF)
                up[:, pl.ds(0, twice)] = jnp.zeros((D, twice), BF)
                down[pl.ds(0, twice), :] = jnp.zeros((twice, D), BF)

        for k in range(supers):
            slot = k % 2
            rows_in, grad_rows, ab_grad, scaled, shared_grad, shared_inner = (
                buffer.at[slot] for buffer in kept
            )
            if k >= 2:
                for n in range(len(kept)):
                    keep(n, k - 2).wait()
            for j in range(2):
                key = keys[pl.ds(2 * k + j, 1), :]
                number = lax.broadcasted_iota(jnp.int32, (slots, GROUP), 0).astype(F32)
                pick = (number == key).astype(F32)
                picks[j] = pick.astype(BF)
                picks_t[j] = pick.T.astype(BF)
                weight = share[pl.ds(2 * k + j, 1), :]
                share_rows[pl.ds(j * slots, slots), :] = jnp.sum(
                    pick * weight, axis=1, keepdims=True
                )
            for copy in load(k):
                copy.wait()
            for source, target in ((hidden_in, rows_in), (grad_in, grad_rows)):
                for j in range(2):

                    @tiles(D, 2048)
                    def _(columns):
                        target[pl.ds(j * slots, slots), columns] = jnp.dot(
                            picks[j],
                            source[pl.ds(j * GROUP, GROUP), columns],
                            preferred_element_type=F32,
                        ).astype(BF)

                yield
            for weight, target in ((gate, a_pre), (up, b_pre)):

                @tiles(window, window)
                def _(columns):
                    target[:, columns] = jnp.dot(
                        rows_in[...], weight[:, columns], preferred_element_type=F32
                    )

                yield

            @tiles(window, window)
            def _(columns):
                flow[:, columns] = dot_t(grad_rows[...], down[columns, :])

            yield

            @tiles(rows, 32)
            def _(block):
                a = a_pre[block, :]
                b = b_pre[block, :]
                u = flow[block, :]
                weight = share_rows[block, :]
                sigma = jax.nn.sigmoid(a)
                act = a * sigma
                inner = (act * b).astype(BF).astype(F32)
                gate_rows[block, :] = jnp.sum(inner * u, axis=1, keepdims=True)
                scaled[block, :] = (inner * weight).astype(BF)
                u = u * weight
                ab_grad[block, pl.ds(0, window)] = (
                    u * b * (sigma * (1.0 + a * (1.0 - sigma)))
                ).astype(BF)
                ab_grad[block, pl.ds(window, window)] = (u * act).astype(BF)

            for j in range(2):
                pick = picks[j].astype(F32)
                gate_grad[pl.ds(2 * k + j, 1), :] = jnp.sum(
                    pick * gate_rows[pl.ds(j * slots, slots), :], axis=0, keepdims=True
                )
            yield

            @tiles(D, 1024)
            def _(columns):
                row_grad[:, columns] = (
                    dot_t(ab_grad[:, pl.ds(0, window)], gate[columns, :])
                    + dot_t(ab_grad[:, pl.ds(window, window)], up[columns, :])
                ).astype(BF)

            yield

            @tiles(D, 2048)
            def _(columns):
                expert_out[:, columns] = jnp.dot(
                    scaled[...], down[:, columns], preferred_element_type=F32
                ).astype(BF)

            yield

            @tiles(2 * GROUP, 2 * GROUP)
            def _(block):
                shared_pre[block, :] = jnp.dot(
                    hidden_in[block, :], shared_in[...], preferred_element_type=F32
                )

            yield

            @tiles(2 * GROUP, GROUP)
            def _(block):
                u = dot_t(grad_in[block, :], shared_down[...])
                a = shared_pre[block, pl.ds(0, half)]
                b = shared_pre[block, pl.ds(half, half)]
                sigma = jax.nn.sigmoid(a)
                act = a * sigma
                shared_inner[block, :] = (act * b).astype(BF)
                shared_grad[block, pl.ds(0, half)] = (
                    u * b * (sigma * (1.0 + a * (1.0 - sigma)))
                ).astype(BF)
                shared_grad[block, pl.ds(half, half)] = (u * act).astype(BF)

            for n in range(len(kept)):
                keep(n, k).start()
            if k + 1 < supers:
                for copy in load(k + 1):
                    copy.start()
            yield
            for j in range(2):
                if k:
                    put(0, k - 1, j).wait()

                @tiles(D, 1024)
                def _(columns):
                    parts[0][j, :, columns] = (
                        jnp.dot(
                            picks_t[j],
                            row_grad[pl.ds(j * slots, slots), columns],
                            preferred_element_type=F32,
                        )
                        + dot_t(shared_grad[pl.ds(j * GROUP, GROUP), :], shared_in[columns, :])
                    ).astype(BF)

                put(0, k, j).start()
            yield
            for j in range(2):
                if k:
                    put(1, k - 1, j).wait()

                @tiles(D, 1024)
                def _(columns):
                    parts[1][j, :, columns] = (
                        jnp.dot(
                            picks_t[j],
                            expert_out[pl.ds(j * slots, slots), columns],
                            preferred_element_type=F32,
                        )
                        + jnp.dot(
                            shared_inner[pl.ds(j * GROUP, GROUP), :],
                            shared_down[:, columns],
                            preferred_element_type=F32,
                        )
                    ).astype(BF)

                put(1, k, j).start()
            yield
        for k in range(max(0, supers - 2), supers):
            for n in range(len(kept)):
                keep(n, k).wait()
        for n in range(2):
            for j in range(2):
                put(n, supers - 1, j).wait()


class AllToAll:
    def __init__(self, grid, array):
        self.grid = grid
        self.inputs = [array]
        hbm = pl.BlockSpec(memory_space=pl.ANY)
        self.in_specs, self.out_specs = [hbm], [hbm]
        self.out_shapes = [jax.ShapeDtypeStruct(array.shape, array.dtype)]
        self.scratch = [pltpu.SemaphoreType.DMA((grid.devices,))] * 2

    def steps(self, at, ins, outs, scratch):
        grid, (send_sem, recv_sem) = self.grid, scratch
        me = grid.number(at)
        yield 8

        def copy(step):
            there = lax.rem(me + step, grid.devices)
            return pltpu.make_async_remote_copy(
                src_ref=ins[0].at[there],
                dst_ref=outs[0].at[me],
                send_sem=send_sem.at[step],
                recv_sem=recv_sem.at[step],
                device_id=grid.device_id(there),
                device_id_type=MESH_ID,
            )

        own = pltpu.make_async_copy(ins[0].at[me], outs[0].at[me], recv_sem.at[0])
        own.start()
        for k in range(8):
            for step in range(1 + k, grid.devices, 8):
                copy(step).start()
            yield
        own.wait()
        for step in range(1, grid.devices):
            copy(step).wait_send()
            back = outs[0].at[lax.rem(me - step + grid.devices, grid.devices)]
            pltpu.make_async_copy(back, back, recv_sem.at[step]).wait()


def chosen_lanes(height, shift, share):
    row = lax.broadcasted_iota(jnp.int32, (height, 128), 0)
    lane = lax.broadcasted_iota(jnp.int32, (height, 128), 1)
    return jnp.logical_and(row - lane == shift, lane < share).astype(BF)


class SharedColumns:
    def __init__(self, arrays, devices):
        rows, self.width = arrays[0].shape
        self.devices, self.share = devices, self.width // devices
        vmem = pl.BlockSpec(memory_space=pltpu.VMEM)
        self.inputs = list(arrays)
        self.in_specs = [vmem] * len(arrays)
        self.out_shapes = [jax.ShapeDtypeStruct((devices, rows, 128 * len(arrays)), BF)]
        self.out_specs = [vmem]
        self.scratch = []

    def steps(self, at, ins, outs, scratch):
        share = self.share
        yield self.devices
        for k in range(self.devices):
            first = share * k // 128 * 128
            width = min(256, self.width - first)
            lanes = chosen_lanes(width, share * k - first, share)
            for n, array in enumerate(ins):
                outs[0][k, :, pl.ds(128 * n, 128)] = dot(
                    array[:, pl.ds(first, width)], lanes
                ).astype(BF)
            yield


class SharedRows:
    def __init__(self, array, width):
        devices, rows, lanes = array.shape
        self.devices, self.width, self.share = devices, width, width // devices
        vmem = pl.BlockSpec(memory_space=pltpu.VMEM)
        self.inputs, self.in_specs = [array], [vmem]
        self.out_shapes = [jax.ShapeDtypeStruct((rows, width), F32)] * (lanes // 128)
        self.out_specs = [vmem] * (lanes // 128)
        self.scratch = []

    def steps(self, at, ins, outs, scratch):
        share = self.share
        yield self.width // 128
        for w in range(self.width // 128):
            totals = [None] * len(outs)
            for k in range(128 * w // share, (128 * w + 127) // share + 1):
                row = lax.broadcasted_iota(jnp.int32, (128, 128), 0)
                lane = lax.broadcasted_iota(jnp.int32, (128, 128), 1)
                place = jnp.logical_and(row - lane == 128 * w - share * k, row < share).astype(BF)
                for n in range(len(outs)):
                    term = dot(ins[0][k, :, pl.ds(128 * n, 128)], place)
                    totals[n] = term if totals[n] is None else totals[n] + term
            for out, total in zip(outs, totals):
                out[:, pl.ds(128 * w, 128)] = total
            yield


class Exchange:
    def __init__(self, grid, arrays, views, shapes, begins=(0, 0)):
        self.grid, self.views, self.begins = grid, views, begins
        self.peers = grid.size["p"]
        self.inputs = list(arrays)
        hbm = pl.BlockSpec(memory_space=pl.ANY)
        self.in_specs = [hbm] * len(arrays)
        self.out_shapes = [
            jax.ShapeDtypeStruct((self.peers - 1,) + shape, a.dtype)
            for a, shape in zip(arrays, shapes)
        ]
        self.out_specs = [hbm] * len(arrays)
        self.scratch = [pltpu.SemaphoreType.DMA((len(arrays), self.peers - 1))] * 2

    def steps(self, at, ins, outs, scratch):
        send_sem, recv_sem = scratch
        yield 20
        copies = []
        for k in range(20):
            for n, view in enumerate(self.views):
                if self.begins[n] != k:
                    continue
                for step in range(1, self.peers):
                    there = self.grid.shift(at, {"p": step})
                    copy = pltpu.make_async_remote_copy(
                        src_ref=view(ins[n], there["p"], step),
                        dst_ref=outs[n].at[step - 1],
                        send_sem=send_sem.at[n, step - 1],
                        recv_sem=recv_sem.at[n, step - 1],
                        device_id=self.grid.mesh_id(there),
                        device_id_type=MESH_ID,
                    )
                    copy.start()
                    copies.append(copy)
            yield
        for copy in copies:
            copy.wait()


SCALE = (NOPE + ROPE) ** (-0.5)
HALF = ROPE // 2
TURN = HEADS * HALF
WIDE = HEADS * NOPE


def spread():
    row = lax.broadcasted_iota(jnp.int32, (128, TURN), 0)
    lane = lax.broadcasted_iota(jnp.int32, (128, TURN), 1)
    return (lax.rem(lane, HALF) == row).astype(BF)


def of_head(h):
    lane = lax.broadcasted_iota(jnp.int32, (MICRO * SEQ, 2 * TURN), 1)
    return jnp.bitwise_and(jnp.right_shift(lane, 5), HEADS - 1) == h


def rms_scale(values):
    return lax.rsqrt(jnp.mean(values * values, -1, keepdims=True) + EPSILON)


QUERY = WIDE + 2 * TURN
ATTN_LANE, FFN_LANE = 126, 127


def weight_buffers(weights):
    q_weight, kv_down, kv_up, out_weight = weights
    shapes = [(D, QUERY), kv_down.shape, kv_up.shape, out_weight.shape, (D, 128)]
    return [pltpu.VMEM(shape, BF) for shape in shapes] + [pltpu.SemaphoreType.DMA((5,))]


def weight_loads(sources, scratch):
    q_weight, kv_down, kv_up, out_weight = sources
    views = [q_weight.at[:, pl.ds(0, QUERY)], kv_down, kv_up, out_weight]
    views.append(q_weight.at[:, pl.ds(QUERY, 128)])
    return [
        pltpu.make_async_copy(view, scratch[n], scratch[5].at[n]) for n, view in enumerate(views)
    ]


def gain_rows(router):
    turned = router[...].astype(F32).T
    return turned[ATTN_LANE : ATTN_LANE + 1], turned[FFN_LANE : FFN_LANE + 1]


def kv_gain_row(kv_up):
    return kv_up[:, pl.ds(2 * WIDE, 128)].astype(F32).T[:1]


class AttentionForward:
    def __init__(self, tokens, routes, allowed, tables, weights, experts):
        count = MICRO * SEQ
        self.experts = experts
        self.inputs = [tokens, routes, allowed, *tables, *weights]
        vmem = pl.BlockSpec(memory_space=pltpu.VMEM)
        hbm = pl.BlockSpec(memory_space=pl.ANY)
        self.in_specs = [vmem] * 5 + [hbm] * 4
        shapes = [
            ((count, D), BF), ((experts, count), F32),
            ((count, D), BF), ((count, WIDE), BF), ((count, 2 * TURN), BF), ((count, RANK), F32),
            ((count, RANK), BF), ((count, 2 * TURN), BF), ((count, 2 * WIDE), BF),
            ((HEADS, count, count), F32), ((count, WIDE), BF), ((count, D), F32),
        ]
        self.out_shapes = [jax.ShapeDtypeStruct(shape, kind) for shape, kind in shapes]
        self.out_specs = [vmem] * len(shapes)
        self.scratch = weight_buffers(weights) + [
            pltpu.VMEM((count, RANK + 256), F32),
            pltpu.VMEM((count, 2 * TURN), F32),
        ]

    def steps(self, at, ins, outs, scratch):
        tokens, routes, allowed, cosine, sine = ins[:5]
        (
            hidden, gates, normed, q_plain, q_turned, kv_low, latent, k_turned, kv, chances,
            attended, residual,
        ) = outs
        q_weight, kv_down, kv_up, out_weight, router = scratch[:5]
        kv_raw, q_raw = scratch[6:]
        yield 16
        loads = weight_loads(ins[5:], scratch)
        for n in (4, 1, 0, 2, 3):
            loads[n].start()
        loads[4].wait()
        attn_gain, ffn_gain = gain_rows(router)
        values = tokens[...].astype(F32)
        normed[...] = (values * rms_scale(values) * attn_gain).astype(BF)
        yield
        loads[1].wait()

        @tiles(RANK + 256, RANK + 256)
        def _(columns):
            kv_raw[:, columns] = dot(normed[...], kv_down[:, columns])

        low = kv_raw[:, pl.ds(0, RANK)]
        kv_low[...] = low
        loads[2].wait()
        kv_gain = kv_gain_row(kv_up)
        latent[...] = (low * rms_scale(low) * kv_gain).astype(BF)
        first, second = kv_raw[:, pl.ds(RANK, 128)], kv_raw[:, pl.ds(RANK + 128, 128)]
        c, s = cosine[:, pl.ds(0, 128)], sine[:, pl.ds(0, 128)]
        lay = spread()
        k_turned[:, pl.ds(0, TURN)] = dot((first * c - second * s).astype(BF), lay).astype(BF)
        k_turned[:, pl.ds(TURN, TURN)] = dot((second * c + first * s).astype(BF), lay).astype(BF)
        yield
        loads[0].wait()

        for k in range(2):
            columns = pl.ds(k * WIDE // 2, WIDE // 2)
            q_plain[:, columns] = dot(normed[...], q_weight[:, columns]).astype(BF)
            yield
        q_raw[...] = dot(normed[...], q_weight[:, pl.ds(WIDE, 2 * TURN)])
        first, second = q_raw[:, pl.ds(0, TURN)], q_raw[:, pl.ds(TURN, TURN)]
        q_turned[:, pl.ds(0, TURN)] = (first * cosine[...] - second * sine[...]).astype(BF)
        q_turned[:, pl.ds(TURN, TURN)] = (second * cosine[...] + first * sine[...]).astype(BF)
        yield

        @tiles(2 * WIDE, 2048)
        def _(columns):
            kv[:, columns] = dot(latent[...], kv_up[:, columns]).astype(BF)

        yield

        def head(h):
            plain = pl.ds(pl.multiple_of(h * NOPE, NOPE), NOPE)
            keys = pl.ds(pl.multiple_of(h * 2 * NOPE, NOPE), NOPE)
            both = pl.ds(pl.multiple_of(h * 2 * NOPE + NOPE, NOPE), VDIM)
            turned = jnp.where(of_head(h), q_turned[...].astype(F32), 0.0).astype(BF)
            scores = dot_t(q_plain[:, plain], kv[:, keys]) + dot_t(turned, k_turned[...])
            scores = jnp.where(allowed[...] > 0, scores * SCALE, MASKED)
            powers = jnp.exp(scores - jnp.max(scores, -1, keepdims=True))
            chance = powers / jnp.sum(powers, -1, keepdims=True)
            chances[h] = chance
            attended[:, plain] = dot(chance.astype(BF), kv[:, both]).astype(BF)

        for k in range(0, HEADS, 4):
            pl.loop(k, k + 4)(head)
            yield
        loads[3].wait()
        for k in range(2):
            columns = pl.ds(k * D // 2, D // 2)
            residual[:, columns] = tokens[:, columns].astype(F32) + dot(
                attended[...], out_weight[:, columns]
            )
            yield
        values = residual[...]
        hidden[...] = (values * rms_scale(values) * ffn_gain).astype(BF)
        logits = dot(hidden[...], router[...])
        lane = lax.broadcasted_iota(jnp.int32, logits.shape, 1)
        chosen = lane < 0
        for k in range(TOP):
            chosen = jnp.logical_or(chosen, routes[:, pl.ds(k, 1)] == lane)
        logits = jnp.where(chosen, logits, MASKED)
        powers = jnp.where(chosen, jnp.exp(logits - jnp.max(logits, -1, keepdims=True)), 0.0)
        share = powers / jnp.sum(powers, -1, keepdims=True)
        gates[...] = jnp.where(chosen, share, -1.0).T[: self.experts]
        yield


class AttentionBackward:
    def __init__(self, cotangent, hidden_sum, gate_grad, out_sums, saved, tokens, tables, weights):
        count = MICRO * SEQ
        self.experts = gate_grad.shape[0]
        self.inputs = [cotangent, hidden_sum, gate_grad, *tables, *saved, tokens, *out_sums]
        self.inputs += weights
        vmem = pl.BlockSpec(memory_space=pltpu.VMEM)
        hbm = pl.BlockSpec(memory_space=pl.ANY)
        self.in_specs = [vmem] * (5 + 12 + 1 + MICRO) + [hbm] * 4
        self.grads = [weights[n].shape for n in (3, 2, 0, 1)]
        self.out_shapes = [jax.ShapeDtypeStruct(shape, BF) for shape in self.grads] + [
            jax.ShapeDtypeStruct((count, D), BF)
        ] * 2
        self.out_specs = [hbm] * 4 + [vmem] * 2
        widest = max(width for _, width in self.grads)
        self.scratch = weight_buffers(weights) + [
            pltpu.VMEM((2, 256, widest), BF),
            pltpu.VMEM((count, 128), F32),
            pltpu.VMEM((count, D), F32),
            pltpu.VMEM((count, D), F32),
            pltpu.VMEM((count, D), BF),
            pltpu.VMEM((count, WIDE), BF),
            pltpu.VMEM((count, QUERY), BF),
            pltpu.VMEM((count, 2 * WIDE), BF),
            pltpu.VMEM((count, RANK + 256), BF),
            pltpu.VMEM((count, 2 * TURN), F32),
            pltpu.VMEM((count, 2 * TURN), F32),
            pltpu.VMEM((D, 128), F32),
            pltpu.VMEM((128, D), F32),
            pltpu.VMEM((128, RANK), F32),
            pltpu.SemaphoreType.DMA((2,)),
        ]

    def steps(self, at, ins, outs, scratch):
        cotangent, hidden_sum, gate_grad, cosine, sine = ins[:5]
        (
            hidden, gates, normed, q_plain, q_turned, kv_low, latent, k_turned, kv, chances,
            attended, residual,
        ) = ins[5:17]
        tokens, (tokens_grad, result) = ins[17], outs[4:]
        q_weight, kv_down, kv_up, out_weight, router = scratch[:5]
        (
            buffers, turned_gates, hidden_grad, residual_grad, mixed, attended_grad, q_grad, kv_grad,
            kv_raw_grad, q_turn_grad, k_turn_grad, router_grad, gain_grads, kv_gain_grads, out_sem,
        ) = scratch[6:]
        experts = self.experts
        yield 7 + sum(shape[0] // 256 for shape in self.grads)
        loads = weight_loads(ins[18 + MICRO :], scratch)
        for n in (4, 3, 2, 0, 1):
            loads[n].start()
        for k in range(MICRO):
            piece = pl.ds(k * SEQ, SEQ)
            result[piece, :] = (residual[piece, :] + ins[18 + k][...]).astype(BF)
        gain_grads[...] = jnp.zeros_like(gain_grads)
        kv_gain_grads[...] = jnp.zeros_like(kv_gain_grads)
        share = jnp.maximum(gates[...], 0.0)
        inner = jnp.sum(share * gate_grad[...], 0, keepdims=True)
        turned_gates[...] = jnp.zeros_like(turned_gates)
        turned_gates[pl.ds(0, experts), :] = share * (gate_grad[...] - inner)
        logit_grad = turned_gates[...].T.astype(BF)
        loads[4].wait()
        attn_gain, ffn_gain = gain_rows(router)

        @tiles(D, 1024)
        def _(columns):
            router_grad[columns, :] = t_dot(hidden[:, columns], logit_grad)
            hidden_grad[:, columns] = hidden_sum[:, columns] + dot_t(
                logit_grad, router[columns, :]
            )

        def norm_back(values, gain, gradient):
            scale = rms_scale(values)
            weighted = gradient * gain
            mean = jnp.mean(weighted * values, -1, keepdims=True)
            gain_grad = jnp.sum(gradient * values * scale, 0, keepdims=True)
            return scale * weighted - values * (scale * scale * scale * mean), gain_grad

        part, gain_grads[pl.ds(FFN_LANE, 1), :] = norm_back(
            residual[...], ffn_gain, hidden_grad[...]
        )
        total = cotangent[...].astype(F32) + part
        residual_grad[...] = total
        mixed[...] = total.astype(BF)
        yield
        loads[3].wait()

        @tiles(WIDE, 1024)
        def _(columns):
            attended_grad[:, columns] = dot_t(mixed[...], out_weight[columns, :]).astype(BF)

        yield
        turn = [0]
        stores = {}

        def weight_grad(n, left, right, width, beside=None):
            rows, whole = self.grads[n]
            for k in range(rows // 256):
                slot = turn[0] % 2
                turn[0] += 1
                if slot in stores:
                    stores[slot].wait()
                piece = pl.ds(k * 256, 256)

                @tiles(width, width if width < 1024 else 1024)
                def _(columns):
                    buffers[slot, :, columns] = t_dot(left[:, piece], right[:, columns]).astype(BF)

                if beside is not None:
                    lanes = beside[k * 256 : (k + 1) * 256, :]
                    buffers[slot, :, pl.ds(width, 128)] = lanes.astype(BF)
                if whole > width + 128:
                    rest = pl.ds(width + 128, whole - width - 128)
                    buffers[slot, :, rest] = jnp.zeros((256, whole - width - 128), BF)
                stores[slot] = pltpu.make_async_copy(
                    buffers.at[slot, :, pl.ds(0, whole)], outs[n].at[piece, :], out_sem.at[slot]
                )
                stores[slot].start()
                yield

        yield from weight_grad(0, attended, mixed, D)
        q_turn_grad[...] = jnp.zeros_like(q_turn_grad)
        k_turn_grad[...] = jnp.zeros_like(k_turn_grad)

        def head(h):
            plain = pl.ds(pl.multiple_of(h * NOPE, NOPE), NOPE)
            keys = pl.ds(pl.multiple_of(h * 2 * NOPE, NOPE), NOPE)
            both = pl.ds(pl.multiple_of(h * 2 * NOPE + NOPE, NOPE), VDIM)
            chance = chances[h]
            grads = attended_grad[:, plain]
            kv_grad[:, both] = t_dot(chance.astype(BF), grads).astype(BF)
            chance_grad = dot_t(grads, kv[:, both])
            mean = jnp.sum(chance * chance_grad, -1, keepdims=True)
            score_grad = (chance * (chance_grad - mean)).astype(BF)
            q_grad[:, plain] = (dot(score_grad, kv[:, keys]) * SCALE).astype(BF)
            kv_grad[:, keys] = (t_dot(score_grad, q_plain[:, plain]) * SCALE).astype(BF)
            mine = of_head(h)
            turned = jnp.where(mine, q_turned[...].astype(F32), 0.0).astype(BF)
            q_turn_grad[...] += jnp.where(mine, dot(score_grad, k_turned[...]), 0.0) * SCALE
            k_turn_grad[...] += t_dot(score_grad, turned) * SCALE

        for k in range(0, HEADS, 4):
            pl.loop(k, k + 4)(head)
            yield
        first, second = q_turn_grad[:, pl.ds(0, TURN)], q_turn_grad[:, pl.ds(TURN, TURN)]
        c, s = cosine[...], sine[...]
        q_grad[:, pl.ds(WIDE, TURN)] = (first * c + second * s).astype(BF)
        q_grad[:, pl.ds(WIDE + TURN, TURN)] = (second * c - first * s).astype(BF)
        lay = spread()

        def gathered(columns):
            values = k_turn_grad[:, columns]
            high = values.astype(BF)
            low = (values - high.astype(F32)).astype(BF)
            return dot_t(high, lay) + dot_t(low, lay)

        first, second = gathered(pl.ds(0, TURN)), gathered(pl.ds(TURN, TURN))
        c, s = cosine[:, pl.ds(0, 128)], sine[:, pl.ds(0, 128)]
        kv_raw_grad[:, pl.ds(RANK, 128)] = (first * c + second * s).astype(BF)
        kv_raw_grad[:, pl.ds(RANK + 128, 128)] = (second * c - first * s).astype(BF)
        loads[2].wait()
        latent_grad = dot_t(kv_grad[...], kv_up[:, pl.ds(0, 2 * WIDE)])
        part, kv_gain_grads[pl.ds(0, 1), :] = norm_back(
            kv_low[...], kv_gain_row(kv_up), latent_grad
        )
        kv_raw_grad[:, pl.ds(0, RANK)] = part.astype(BF)
        loads[0].wait()
        loads[1].wait()

        @tiles(D, 512)
        def _(columns):
            hidden_grad[:, columns] = dot_t(q_grad[...], q_weight[columns, :]) + dot_t(
                kv_raw_grad[...], kv_down[columns, :]
            )

        yield
        part, gain_grads[pl.ds(ATTN_LANE, 1), :] = norm_back(
            tokens[...].astype(F32), attn_gain, hidden_grad[...]
        )
        tokens_grad[...] = (residual_grad[...] + part).astype(BF)
        router_grad[...] += gain_grads[...].T
        yield from weight_grad(1, latent, kv_grad, 2 * WIDE, kv_gain_grads[...].T)
        yield from weight_grad(2, normed, q_grad, QUERY, router_grad)
        yield from weight_grad(3, normed, kv_raw_grad, RANK + 256)
        for store in stores.values():
            store.wait()


class WeightGrads:
    TILE = 256

    def __init__(self, grid, kept, extent):
        self.grid, self.extent, self.chunks = grid, extent, len(kept)
        self.inputs = [array for entry in kept for array in entry]
        rows, grad_rows, ab_grad, scaled, shared_grad, shared_inner, hidden, grad = kept[0]
        self.window = scaled.shape[1]
        hbm = pl.BlockSpec(memory_space=pl.ANY)
        self.in_specs = [hbm] * len(self.inputs)
        peers = grid.size["p"]
        window, tile = self.window, self.TILE
        self.out_shapes = [
            jax.ShapeDtypeStruct((extent, 2 * window), F32),
            jax.ShapeDtypeStruct((window, extent), F32),
            jax.ShapeDtypeStruct((peers - 1, extent, 2 * window), BF),
            jax.ShapeDtypeStruct((peers - 1, window, extent), BF),
            jax.ShapeDtypeStruct((D, shared_grad.shape[1]), BF),
            jax.ShapeDtypeStruct((shared_inner.shape[1], D), F32),
        ]
        self.out_specs = [hbm] * 6
        self.jobs = [(0, 2, True), (1, 3, False), (6, 4, True), (7, 5, False)]
        self.scratch = []
        for streamed, resident, left in self.jobs:
            a, b = kept[0][streamed], kept[0][resident]
            self.scratch.append(pltpu.VMEM((self.chunks,) + b.shape, BF))
            self.scratch.append(pltpu.VMEM((2, self.chunks, a.shape[0], tile), BF))
            shape = (tile, b.shape[1]) if left else (b.shape[1], tile)
            self.scratch.append(pltpu.VMEM((2,) + shape, F32))
            self.scratch.append(pltpu.VMEM((2,) + shape, BF))
        self.scratch += [
            pltpu.SemaphoreType.DMA((4, self.chunks)),
            pltpu.SemaphoreType.DMA((4, 2, self.chunks)),
            pltpu.SemaphoreType.DMA((4, 2)),
        ]

    def steps(self, at, ins, outs, scratch):
        tile, extent, chunks = self.TILE, self.extent, self.chunks
        peers = self.grid.size["p"]
        kept = [ins[c * 8 : (c + 1) * 8] for c in range(chunks)]
        whole_sem, tile_sem, out_sem = scratch[16:]
        own_ab, own_down, sent_ab, sent_down, shared_in, shared_down = outs

        def whole(job, c):
            return pltpu.make_async_copy(
                kept[c][self.jobs[job][1]], scratch[4 * job].at[c], whole_sem.at[job, c]
            )

        work = []
        per_peer = extent // tile
        for step in range(peers):
            for job in range(2):
                for k in range(per_peer):
                    piece = pl.ds(k * tile, tile)
                    if step == 0:
                        target = own_ab.at[piece, :] if job == 0 else own_down.at[:, piece]
                    elif job == 0:
                        target = sent_ab.at[step - 1, piece, :]
                    else:
                        target = sent_down.at[step - 1, :, piece]
                    peer = self.grid.shift(at, {"p": step})["p"]
                    first = pl.multiple_of(peer * extent + k * tile, tile)
                    work.append((job, first, target, step == 0))
        for k in range(D // tile):
            piece = pl.ds(k * tile, tile)
            work.append((2, k * tile, shared_in.at[piece, :], False))
            work.append((3, k * tile, shared_down.at[:, piece], True))
        work.sort(key=lambda entry: entry[0] >= 2)
        turns = [0] * 4
        numbered = []
        for job, first, target, wide in work:
            numbered.append((job, first, target, wide, turns[job]))
            turns[job] += 1
        yield len(work)

        def fetch(number, c):
            job, first, _, _, turn = numbered[number]
            return pltpu.make_async_copy(
                kept[c][self.jobs[job][0]].at[:, pl.ds(first, tile)],
                scratch[4 * job + 1].at[turn % 2, c],
                tile_sem.at[job, turn % 2, c],
            )

        def store(number):
            job, _, target, wide, turn = numbered[number]
            source = scratch[4 * job + (2 if wide else 3)].at[turn % 2]
            return pltpu.make_async_copy(source, target, out_sem.at[job, turn % 2])

        for c in range(chunks):
            for job in range(2):
                whole(job, c).start()
            fetch(0, c).start()
            for job in range(2, 4):
                whole(job, c).start()
        begun = set()
        last = {}
        for number, (job, _, _, wide, turn) in enumerate(numbered):
            if number + 1 < len(numbered):
                for c in range(chunks):
                    fetch(number + 1, c).start()
            if job not in begun:
                begun.add(job)
                for c in range(chunks):
                    whole(job, c).wait()
            for c in range(chunks):
                fetch(number, c).wait()
            if (job, turn % 2) in last:
                store(last[job, turn % 2]).wait()
            last[job, turn % 2] = number
            resident, streamed = scratch[4 * job], scratch[4 * job + 1].at[turn % 2]
            result = scratch[4 * job + (2 if wide else 3)].at[turn % 2]
            left = self.jobs[job][2]

            @tiles(resident.shape[2], resident.shape[2])
            def _(columns):
                total = None
                for c in range(chunks):
                    if left:
                        term = t_dot(streamed[c], resident[c, :, columns])
                    else:
                        term = t_dot(resident[c, :, columns], streamed[c])
                    total = term if total is None else total + term
                if left:
                    result[:, columns] = total.astype(result.dtype)
                else:
                    result[columns, :] = total.astype(result.dtype)

            store(number).start()
            yield
        for number in last.values():
            store(number).wait()


class Assemble:
    TILE = 128

    def __init__(self, grid, own_ab, own_down, got_ab, got_down, eff):
        self.grid, self.eff = grid, eff
        self.extent = own_ab.shape[0]
        self.window = own_down.shape[0]
        self.peers = 1 + len(got_ab)
        self.inputs = [own_ab, own_down, *got_ab, *got_down]
        hbm = pl.BlockSpec(memory_space=pl.ANY)
        self.in_specs = [hbm] * len(self.inputs)
        self.out_shapes = [
            jax.ShapeDtypeStruct((self.extent, eff), F32),
            jax.ShapeDtypeStruct((self.extent, eff), F32),
            jax.ShapeDtypeStruct((eff, self.extent), F32),
        ]
        self.out_specs = [hbm] * 3
        tile, window = self.TILE, self.window
        self.scratch = [
            pltpu.VMEM((2, tile, 2 * window), F32),
            pltpu.VMEM((2, window, tile), F32),
            pltpu.VMEM((2, self.peers - 1, tile, 2 * window), BF),
            pltpu.VMEM((2, self.peers - 1, window, tile), BF),
            pltpu.VMEM((2, 2, tile, eff), F32),
            pltpu.VMEM((2, eff, tile), F32),
            pltpu.SemaphoreType.DMA((2, 2, self.peers)),
            pltpu.SemaphoreType.DMA((2, 3)),
        ]

    def steps(self, at, ins, outs, scratch):
        tile, window, peers, eff = self.TILE, self.window, self.peers, self.eff
        own = ins[:2]
        got = (ins[2 : 1 + peers], ins[1 + peers :])
        own_tiles, got_tiles = scratch[:2], scratch[2:4]
        both, down, in_sem, out_sem = scratch[4:]
        count = self.extent // tile
        yield 2 * count
        work = [(job, k) for job in range(2) for k in range(count)]

        def piece_of(array, job, k):
            piece = pl.ds(k * tile, tile)
            return array.at[piece, :] if job == 0 else array.at[:, piece]

        def fetch(job, k):
            copies = []
            for source in range(peers):
                array = own[job] if source == 0 else got[job][source - 1]
                target = own_tiles[job].at[k % 2]
                if source:
                    target = got_tiles[job].at[k % 2, source - 1]
                copies.append(
                    pltpu.make_async_copy(
                        piece_of(array, job, k), target, in_sem.at[job, k % 2, source]
                    )
                )
            return copies

        def store(job, k):
            if job:
                return [
                    pltpu.make_async_copy(
                        down.at[k % 2], piece_of(outs[2], 1, k), out_sem.at[k % 2, 2]
                    )
                ]
            return [
                pltpu.make_async_copy(
                    both.at[k % 2, n], piece_of(outs[n], 0, k), out_sem.at[k % 2, n]
                )
                for n in range(2)
            ]

        for copy in fetch(*work[0]):
            copy.start()
        for number, (job, k) in enumerate(work):
            if number + 1 < len(work):
                for copy in fetch(*work[number + 1]):
                    copy.start()
            for copy in fetch(job, k):
                copy.wait()
            if k >= 2:
                for copy in store(job, k - 2):
                    copy.wait()
            for peer in range(peers):
                first = peer * window
                width = min(window, eff - first)
                skip = window - width
                for source in range(peers):

                    @pl.when(lax.rem(at["p"] - peer + peers, peers) == source)
                    def _():
                        if source:
                            view = got_tiles[job].at[k % 2, source - 1]
                        else:
                            view = own_tiles[job].at[k % 2]
                        if job:
                            down[k % 2, pl.ds(first, width), :] = view[
                                pl.ds(skip, width), :
                            ].astype(F32)
                        else:
                            for n in range(2):
                                both[k % 2, n, :, pl.ds(first, width)] = view[
                                    :, pl.ds(n * window + skip, width)
                                ].astype(F32)

            for copy in store(job, k):
                copy.start()
            yield
        for job in range(2):
            for k in range(max(0, count - 2), count):
                for copy in store(job, k):
                    copy.wait()


def gather_all(grid, arrays, items, collective_id):
    return together(grid, [Gather(grid, arrays, items)], collective_id, "gather_all")[0]


def position_tables():
    frequency = ROPE_BASE ** (-2.0 * np.arange(HALF) / ROPE)
    angles = np.tile(np.arange(SEQ)[:, None] * frequency[None, :], (MICRO, HEADS))
    return [jnp.asarray(np.cos(angles), F32), jnp.asarray(np.sin(angles), F32)]


def capacity_for(expert_count):
    return min(SEQ, ((4 * SEQ * TOP + 3 * expert_count - 1) // (3 * expert_count) + 7) // 8 * 8)


def dot(left, right):
    return jnp.dot(left, right, preferred_element_type=F32)


def dot_t(left, right):
    return lax.dot_general(left, right, (((1,), (1,)), ((), ())), preferred_element_type=F32)


def t_dot(left, right):
    return lax.dot_general(left, right, (((0,), (0,)), ((), ())), preferred_element_type=F32)


PIECES = 4


def finish_kernel(copied, experts, *refs):
    q_sum, down_sum, up_sum = refs[:3]
    sources = refs[3 : 3 + copied]
    q_out, down_out, up_out, gains_out, kv_gain_out, router_out = refs[3 + copied : 9 + copied]
    targets = refs[9 + copied : 9 + 2 * copied]
    held = refs[9 + 2 * copied : 9 + 3 * copied]
    in_sem, out_sem = refs[9 + 3 * copied :]
    arriving, leaving = [], []
    for n, source in enumerate(sources):
        part = source.shape[0] // PIECES
        for k in range(PIECES):
            piece = pl.ds(k * part, part)
            into = pltpu.make_async_copy(source.at[piece, :], held[n].at[piece, :], in_sem.at[n, k])
            into.start()
            arriving.append(into)
            leaving.append(
                pltpu.make_async_copy(
                    held[n].at[piece, :], targets[n].at[piece, :], out_sem.at[n, k]
                )
            )
    for h in range(0, HEADS, 2):
        pieces = []
        for head in (h, h + 1):
            pieces.append(q_sum[:, head * NOPE : (head + 1) * NOPE])
            for half in range(2):
                first = WIDE + half * TURN + head * HALF
                pieces.append(q_sum[:, first : first + HALF])
        width = 2 * (NOPE + ROPE)
        q_out[:, pl.ds(h * (NOPE + ROPE), width)] = jnp.concatenate(pieces, 1)
    down_out[...] = jnp.concatenate(
        [down_sum[:, : RANK + HALF], down_sum[:, RANK + 128 : RANK + 128 + HALF]], 1
    )
    up_out[...] = up_sum[:, : 2 * WIDE]
    beside = q_sum[:, QUERY:].T
    gains_out[...] = beside[ATTN_LANE:]
    router_out[...] = beside[:experts]
    kv_gain_out[...] = up_sum[:, 2 * WIDE : 2 * WIDE + 128].T[:1]
    for into, out in zip(arriving, leaving):
        into.wait()
        out.start()
    for out in leaving:
        out.wait()


def finished(q_sum, down_sum, up_sum, plain, experts):
    rows, up_rows = q_sum.shape[0], up_sum.shape[0]
    vmem = pl.BlockSpec(memory_space=pltpu.VMEM)
    hbm = pl.BlockSpec(memory_space=pl.ANY)
    shapes = [
        (rows, HEADS * (NOPE + ROPE)), (rows, RANK + ROPE), (up_rows, 2 * WIDE), (2, rows),
        (1, up_rows), (experts, rows),
    ]
    return pl.pallas_call(
        functools.partial(finish_kernel, len(plain), experts),
        out_shape=[jax.ShapeDtypeStruct(shape, F32) for shape in shapes]
        + [jax.ShapeDtypeStruct(array.shape, array.dtype) for array in plain],
        in_specs=[vmem] * 3 + [hbm] * len(plain),
        out_specs=[vmem] * 6 + [hbm] * len(plain),
        scratch_shapes=[pltpu.VMEM(array.shape, array.dtype) for array in plain]
        + [pltpu.SemaphoreType.DMA((len(plain), PIECES))] * 2,
        compiler_params=pltpu.CompilerParams(vmem_limit_bytes=62 * 2**20),
        name="finish",
    )(q_sum, down_sum, up_sum, *plain)


def prepare_kernel(q_weight, kv_down, kv_up, router, gains, kv_gain, shared_down, q_out, down_out, up_out, shared_out):
    rows = q_weight.shape[0]
    values = q_weight[...].astype(F32)
    head = NOPE + ROPE
    for h in range(0, HEADS, 2):
        pair = [values[:, k * head : k * head + NOPE] for k in (h, h + 1)]
        q_out[:, pl.ds(h * NOPE, 2 * NOPE)] = jnp.concatenate(pair, 1).astype(BF)
    for half in range(2):
        for h in range(0, HEADS, 4):
            starts = [k * head + NOPE + half * HALF for k in range(h, h + 4)]
            pieces = [values[:, start : start + HALF] for start in starts]
            first = WIDE + half * TURN + h * HALF
            q_out[:, pl.ds(first, 4 * HALF)] = jnp.concatenate(pieces, 1).astype(BF)
    experts = router.shape[1]
    beside = [
        router[...].astype(F32),
        jnp.zeros((rows, ATTN_LANE - experts), F32),
        gains[...].astype(F32).T,
    ]
    q_out[:, pl.ds(QUERY, 128)] = jnp.concatenate(beside, 1).astype(BF)
    low = kv_down[...].astype(F32)
    gap = jnp.zeros((rows, 128 - HALF), F32)
    down_out[:, pl.ds(0, RANK)] = kv_down[:, pl.ds(0, RANK)]
    for half in range(2):
        first = RANK + half * HALF
        down_out[:, pl.ds(RANK + half * 128, 128)] = jnp.concatenate(
            [low[:, first : first + HALF], gap], 1
        ).astype(BF)
    up_out[:, pl.ds(0, 2 * WIDE)] = kv_up[...]
    up_rows, room = kv_up.shape[0], up_out.shape[1] - 2 * WIDE
    up_out[:, pl.ds(2 * WIDE, room)] = jnp.concatenate(
        [kv_gain[...].astype(F32).T, jnp.zeros((up_rows, room - 1), F32)], 1
    ).astype(BF)
    share = shared_down.shape[0]
    shared_out[pl.ds(0, share), :] = shared_down[...]
    left = shared_out.shape[0] - share
    shared_out[pl.ds(share, left), :] = jnp.zeros((left, D), BF)


def prepared(q_weight, kv_down, kv_up, router, gains, kv_gain, shared_down, up_room, room):
    rows, up_rows = q_weight.shape[0], kv_up.shape[0]
    vmem = pl.BlockSpec(memory_space=pltpu.VMEM)
    shapes = [
        (rows, QUERY + 128), (rows, RANK + 256), (up_rows, 2 * WIDE + up_room), (room, D),
    ]
    return pl.pallas_call(
        prepare_kernel,
        out_shape=[jax.ShapeDtypeStruct(shape, BF) for shape in shapes],
        in_specs=[vmem] * 7,
        out_specs=[vmem] * 4,
        compiler_params=pltpu.CompilerParams(vmem_limit_bytes=62 * 2**20),
        name="prepare",
    )(q_weight, kv_down, kv_up, router, gains, kv_gain, shared_down)


def plain_weight_grads(grid, kept, extent):
    me = lax.axis_index("dp")
    peers = grid.size["p"]

    def total(left, right):
        return functools.reduce(jnp.add, [t_dot(entry[left], entry[right]) for entry in kept])

    def share_of(array, step, axis):
        peer = lax.rem(me + step, peers)
        return lax.dynamic_slice_in_dim(array, peer * extent, extent, axis)

    both, down = total(0, 2), total(3, 1)
    steps = range(1, peers)
    return (
        share_of(both, 0, 0),
        share_of(down, 0, 1),
        jnp.stack([share_of(both, step, 0) for step in steps]).astype(BF),
        jnp.stack([share_of(down, step, 1) for step in steps]).astype(BF),
        total(6, 4).astype(BF),
        total(5, 7),
    )


def body(
    grid,
    tokens,
    cotangent,
    routes,
    segments,
    attn_gain,
    q_weight,
    kv_down,
    kv_gain,
    kv_up,
    out_weight,
    ffn_gain,
    router,
    shared_gate,
    shared_up,
    shared_down,
    expert_gate,
    expert_up,
    expert_down,
):
    devices = grid.devices
    dp_size = grid.size["p"]
    experts = router.shape[1]
    count = MICRO * SEQ
    eff = expert_gate.shape[2]
    extent = expert_gate.shape[1]
    window = -(-eff // (128 * dp_size)) * 128
    own = (expert_gate[0], expert_up[0], expert_down[0])

    rows = q_weight.shape[0]
    up_rows = kv_up.shape[0]
    up_room = 128 * max(1, 16 // up_rows)
    room = 128
    q_sent, down_sent, up_wide, shared_part = prepared(
        q_weight,
        kv_down,
        kv_up,
        router,
        jnp.stack([attn_gain, ffn_gain]),
        kv_gain[None],
        shared_down,
        up_room,
        room,
    )
    up_sent = up_wide if up_rows % 16 == 0 else up_wide.reshape(16, -1)

    share = shared_gate.shape[1] // devices
    first, second, third = ("q", "r", "p"), ("q", "p", "r"), ("p", "q", "r")

    def columns_of(ref, peer, step):
        return ref.at[:, pl.ds(window_start(peer, dp_size, window, eff), window)]

    def rows_of(ref, peer, step):
        return ref.at[pl.ds(window_start(peer, dp_size, window, eff), window), :]

    gathered, windows_in, (shared_sent,) = together(
        grid,
        [
            Gather(
                grid,
                [q_sent, down_sent, up_sent, out_weight],
                [
                    (0, 0, q_sent.shape[1], third),
                    (1, 0, down_sent.shape[1], third),
                    (2, 0, up_sent.shape[1], ("r", "p", "q")),
                    (3, 0, D // 2, first),
                    (3, D // 2, D // 2, second),
                ],
            ),
            Exchange(grid, own[:2], [columns_of] * 2, [(extent, window)] * 2, (2, 5)),
            SharedColumns([shared_gate, shared_up], devices),
        ],
        0,
        "gather_attention",
    )
    weights = [
        gathered[0].reshape(D, -1),
        gathered[1].reshape(D, -1),
        gathered[2].reshape(RANK, -1),
        gathered[3].reshape(-1, D),
    ]

    token_rows = tokens.reshape(count, D)
    grad_out = cotangent.reshape(count, D)
    tables = position_tables()
    numbers = segments.reshape(1, -1) + 4 * (jnp.arange(count, dtype=jnp.int32) // SEQ)[None, :]
    places = jnp.arange(count, dtype=jnp.int32)
    allowed = (numbers == numbers.T) & (places[:, None] >= places[None, :])

    def half_orders(a):
        return [(a, 0, D // 2, first), (a, D // 2, D // 2, second)]

    (grad_first,), saved, windows_down, (shared_in,) = together(
        grid,
        [
            Gather(
                grid, [grad_out[:SEQ]], [(0, 0, 1536, third), (0, 1536, 512, ("p", "r", "q"))]
            ),
            AttentionForward(
                token_rows,
                routes.reshape(count, TOP),
                allowed.astype(F32),
                tables,
                weights,
                experts,
            ),
            Exchange(grid, own[2:], [rows_of], [(window, extent)], (2,)),
            AllToAll(grid, shared_sent),
        ],
        6,
        "attention_forward",
    )
    hidden, dense_gates = saved[0], saved[1]

    shared_in = shared_in.reshape(D, 2 * room)

    half = D // 2
    capacity = capacity_for(experts)
    expert = lax.axis_index("expert")
    own_weights = (own, (*windows_in, *windows_down), shared_in, shared_part)

    def gather_of(chunk):
        piece = slice(chunk * SEQ, (chunk + 1) * SEQ)
        sent = [hidden[piece], dense_gates[:, piece]]
        orders = half_orders(0) + [(1, 0, SEQ, first)]
        if chunk:
            sent.append(grad_out[piece])
            orders += half_orders(2)
        return Gather(grid, sent, orders)

    kept_hidden, kept_grad = [], []

    def experts_of(hidden_all, gates_all, grad_all):
        kept_hidden.append(hidden_all)
        kept_grad.append(grad_all)
        share = lax.dynamic_index_in_dim(gates_all, expert, 1, keepdims=False)
        return Experts(
            grid,
            hidden_all.reshape(-1, D),
            grad_all.reshape(-1, D),
            share.reshape(-1, GROUP),
            own_weights,
            capacity,
        )

    def sums_of(done):
        hidden_part, out_part, gate_grad = done[:3]
        mine = (jnp.arange(experts, dtype=jnp.int32) == expert)[None, :, None]
        gate_grad = jnp.where(mine, gate_grad.reshape(devices, 1, SEQ), 0.0)
        shape = (devices, SEQ, D)
        return [hidden_part.reshape(shape), gate_grad, out_part.reshape(shape)]

    def kept_of(done):
        flat = [(h.reshape(-1, D), g.reshape(-1, D)) for h, g in zip(kept_hidden, kept_grad)]
        return [tuple(entry[3:]) + pair for entry, pair in zip(done, flat)]

    over = [(0, 0, half, ("p", "r")), (0, half, half, ("r", "p"))]
    over_gates = [(1, 0, SEQ, ("p", "r"))]
    if devices <= 32:
        (gathered,) = together(grid, [gather_of(0)], 1, "gather_first")
        gathered, done_0 = together(
            grid,
            [gather_of(1), experts_of(*gathered, grad_first)],
            2,
            "gather_second_experts_first",
        )
        windows = [(0, 0, D), (1, 0, SEQ), (2, 0, half), (2, half, half)]
        everything = over + over_gates
        for a in (2, 3):
            everything += [(a, 0, half // 2, ("p", "r")), (a, half // 2, half // 2, ("r", "p"))]
        sums_0, done_1 = together(
            grid,
            [Scatter(grid, sums_of(done_0), everything, [[0, 1], [2], [3]], windows), experts_of(*gathered)],
            3,
            "scatter_first_experts_second",
        )
        kept = kept_of((done_0, done_1))
        sums_1, weight_grads = together(
            grid,
            [
                Scatter(grid, sums_of(done_1), everything, [[0, 1], [2], [3]], windows),
                WeightGrads(grid, kept, extent),
            ],
            4,
            "scatter_second_weight_grads",
        )
        sums = (sums_0, sums_1)
    else:
        sums, done = [], []
        for chunk in range(MICRO):
            part = gather_of(chunk)
            if chunk:
                before = tuple(sums[-1])
                *part.inputs, sums[-1] = lax.optimization_barrier((*part.inputs, before))
            (gathered,) = together(grid, [part], 1 + 7 * chunk, "gather")
            part = experts_of(*gathered, *([] if chunk else [grad_first]))
            (now,) = together(grid, [part], None, "experts")
            parts = sums_of(now)
            (hidden_gates,) = together(
                grid, [Scatter(grid, parts[:2], over + over_gates, [[0, 1]])], 2, "scatter_hidden"
            )
            (out_sum,) = together(grid, [Scatter(grid, parts[2:], over, [[0]])], 3, "scatter_out")
            sums.append((*hidden_gates, *out_sum))
            done.append(now)
        weight_grads = plain_weight_grads(grid, kept_of(done), extent)
    hidden_sum = jnp.concatenate([entry[0] for entry in sums], 0)
    gate_grad = jnp.concatenate([entry[1] for entry in sums], 1)
    out_sums = [entry[2] for entry in sums]
    own_ab, own_down, sent_ab, sent_down, shared_in_grad, shared_down_grad = weight_grads

    def sent_to(ref, peer, step):
        return ref.at[step - 1]

    attention_grads, (got_ab, got_down), (shared_back,) = together(
        grid,
        [
            AttentionBackward(
                grad_out, hidden_sum, gate_grad, out_sums, saved, token_rows, tables, weights
            ),
            Exchange(
                grid,
                [sent_ab, sent_down],
                [sent_to] * 2,
                [(extent, 2 * window), (window, extent)],
            ),
            AllToAll(grid, shared_in_grad.reshape(devices, -1, 2 * room)),
        ],
        7,
        "attention_backward",
    )
    (
        out_weight_grad, kv_up_grad, q_weight_grad, kv_down_grad, tokens_grad, result,
    ) = attention_grads
    shared_down_grad = shared_down_grad[:share]

    def halves(a, columns):
        part = columns // 256 * 128
        return [(a, 0, part, ("p", "r")), (a, part, columns - part, ("r", "p"))]

    attention_sums = Scatter(
        grid,
        [
            q_weight_grad.reshape((devices,) + q_sent.shape),
            kv_down_grad.reshape((devices,) + down_sent.shape),
            kv_up_grad.reshape((devices,) + up_sent.shape),
            out_weight_grad.reshape((devices,) + out_weight.shape),
        ],
        halves(0, q_sent.shape[1])
        + halves(1, down_sent.shape[1])
        + halves(2, up_sent.shape[1])
        + halves(3, out_weight.shape[1]),
        [[0], [3], [2], [1]],
    )
    experts_grads = Assemble(
        grid,
        own_ab,
        own_down,
        [got_ab[step] for step in range(dp_size - 1)],
        [got_down[step] for step in range(dp_size - 1)],
        eff,
    )
    (
        (q_sum, down_sum, up_sum, out_weight_sum), experts_grads,
        (shared_gate_grad, shared_up_grad),
    ) = together(
        grid,
        [attention_sums, experts_grads, SharedRows(shared_back, shared_gate.shape[1])],
        5,
        "scatter_attention_assemble",
    )
    (
        q_grad, down_grad, up_grad, gain_grads, kv_gain_grad, router_grad, result, tokens_grad,
        out_weight_grad, shared_gate_grad, shared_up_grad, gate_grad, expert_up_grad,
        expert_down_grad,
    ) = finished(
        q_sum,
        down_sum,
        up_sum.reshape(up_rows, -1),
        [
            result, tokens_grad, out_weight_sum, shared_gate_grad, shared_up_grad, *experts_grads,
        ],
        experts,
    )
    return (
        result.reshape(tokens.shape),
        tokens_grad.reshape(tokens.shape),
        gain_grads[0],
        q_grad,
        down_grad,
        kv_gain_grad[0],
        up_grad,
        out_weight_grad,
        gain_grads[1],
        router_grad.T,
        shared_gate_grad,
        shared_up_grad,
        shared_down_grad,
        gate_grad[None],
        expert_up_grad[None],
        expert_down_grad[None],
    )


def solution(mesh):
    return jax.shard_map(
        functools.partial(body, Grid(mesh)),
        mesh=mesh,
        in_specs=(
            P(None, ("dp", "expert"), None, None),
            P(None, ("dp", "expert"), None, None),
            P(None, ("dp", "expert"), None, None),
            P(None, ("dp", "expert"), None),
            P(("dp", "expert")),
            P(("dp", "expert"), None),
            P(("dp", "expert"), None),
            P(("dp", "expert")),
            P(("dp", "expert"), None),
            P(("dp", "expert"), None),
            P(("dp", "expert")),
            P(("dp", "expert"), None),
            P(("dp", "expert"), None),
            P(("dp", "expert"), None),
            P(("dp", "expert"), None),
            P("expert", "dp", None),
            P("expert", "dp", None),
            P("expert", None, "dp"),
        ),
        out_specs=(
            P(None, ("dp", "expert"), None, None),
            P(None, ("dp", "expert"), None, None),
            P(("dp", "expert")),
            P(("dp", "expert"), None),
            P(("dp", "expert"), None),
            P(("dp", "expert")),
            P(("dp", "expert"), None),
            P(("dp", "expert"), None),
            P(("dp", "expert")),
            P(("dp", "expert"), None),
            P(("dp", "expert"), None),
            P(("dp", "expert"), None),
            P(("dp", "expert"), None),
            P("expert", "dp", None),
            P("expert", "dp", None),
            P("expert", None, "dp"),
        ),
        check_vma=False,
    )
```
